32 devices in a mesh: seq: 16 (over z, y, core), head: 2 (over x).
Axes of the slice: x: 2, y: 2, z: 4, core: 2. Of those that a mesh axis runs over, the one named last changes fastest.
Arguments:
- prefill_input: bfloat16 [4096, 8192], P('seq', 'head'), may hold values from -6 to 6
- prefill_step: float32 [4096, 128], P('seq', 'head'), may hold values from 0 to 4096, as said below
- write_proj: bfloat16 [4096, 1024], P('seq', 'head'), may hold values from -2.5 to 2.5
- read_proj: bfloat16 [4096, 1024], P('seq', 'head'), may hold values from -0.5 to 0.5
- decay_rate: float32 [128], P('head'), may hold values from 0 to 1, as said below
- skip_gain: float32 [128], P('head'), may hold values from 0.5 to 2
- resident_state: bfloat16 [16, 128, 64, 128], P('seq', 'head'), may hold values from -6 to 6
- owner_slot: int32 [16], replicated, may hold values from 0 to 15, each once
- draft_ids: int32 [16, 8], replicated, may hold values from 0 to 15
- accepted_len: int32 [16], replicated, may hold values from 0 to 8
- draft_input: bfloat16 [256, 8192], P('seq', 'head'), may hold values from -6 to 6
- draft_gate: bfloat16 [256, 8192], P('seq', 'head'), may hold values from -6 to 6
- draft_write: bfloat16 [256, 1024], P('seq', 'head'), may hold values from -2.5 to 2.5
- draft_read: bfloat16 [256, 1024], P('seq', 'head'), may hold values from -0.5 to 0.5
- draft_step: float32 [256, 128], P('seq', 'head'), may hold values from 0.05 to 1
- norm_gain: float32 [8192], P('head'), may hold values from 0.5 to 1.5
- out_weight: bfloat16 [8192, 8192], P('head', 'seq'), may hold values from -0.0625 to 0.0625
Outputs:
- prefill_out: bfloat16 [4096, 8192], P('seq', 'head')
- new_state: bfloat16 [16, 128, 64, 128], P('seq', 'head')
- verify_out: bfloat16 [128, 8192], P('head', 'seq')
- prompt_state: bfloat16 [128, 8192], P('head', 'seq')
The draws below stay inside these ranges and needn't reach their ends.
Inputs may be any that keep to these rules, and one draw needn't show every extreme that they name: owner_slot holds every slot once. `decay_rate`: positive. `prefill_step`: positive.
All inputs are finite; a program needn't handle non-finite values.
Results may differ from the reference program's by a relative error of at most 0.005.
Values may be sent and summed in bfloat16 or wider, within the bound.
No kernel may reach another device: no remote copies, remote signals or barrier semaphores. Data moves between devices by JAX's collectives and lax.ppermute only.
A program may use at most 128 MiB of HBM per device.

```python
import math
import jax
import jax.numpy as jnp
from jax import lax

GROUPS = 8
HEAD_COUNT = 128
HEAD_DIM = 64
STATE_SIZE = 128
BLOCK_LEN = 256
TOK_DEV = 256
TOKENS = 4096
DRAFT_LEN = 8
CANDIDATES = 16
REQUESTS = 16
MODEL_DIM = 8192
VERIFY_ROWS = 128


def rate_table(key):
    kind = jax.random.uniform(jax.random.fold_in(key, 11), (HEAD_COUNT,))
    fast = jnp.exp(jax.random.uniform(jax.random.fold_in(key, 12), (HEAD_COUNT,), minval=jnp.log(0.4), maxval=jnp.log(0.8)))
    slow = jnp.exp(jax.random.uniform(jax.random.fold_in(key, 13), (HEAD_COUNT,), minval=jnp.log(0.1), maxval=jnp.log(0.4))) / (0.05 * TOKENS)
    share = 0.5
    return jnp.where(kind < share, fast, slow).astype(jnp.float32)


def contiguous_cluster_chart(key):
    spots = jax.random.randint(jax.random.fold_in(key, 21), (2,), 0, TOKENS)
    agreement_indicator = jnp.any(jnp.arange(TOKENS)[:, None] == spots[None, :], axis=1)
    loss = jax.random.uniform(jax.random.fold_in(key, 22), (TOKENS, HEAD_COUNT), minval=0.22, maxval=0.69)
    return (agreement_indicator, loss / rate_table(key)[None, :])


def draw_decay_rate(key, part):
    return rate_table(key)


def draw_prefill_step(key, part):
    agreement_indicator, contiguous_cluster = contiguous_cluster_chart(key)
    device_level = jax.random.uniform(jax.random.fold_in(key, 31), (TOKENS // TOK_DEV, HEAD_COUNT), minval=jnp.log(0.5), maxval=jnp.log(1.5))
    rough = jax.random.uniform(jax.random.fold_in(key, 32), (TOKENS, HEAD_COUNT), minval=jnp.log(0.5), maxval=jnp.log(2.0))
    starting_displacement = 0.05 * jnp.exp(jnp.repeat(device_level, TOK_DEV, axis=0) + rough)
    return jnp.where(agreement_indicator[:, None], contiguous_cluster, starting_displacement).astype(jnp.float32)


def draw_prefill_input(key, part):
    agreement_indicator, contiguous_cluster = contiguous_cluster_chart(key)
    noise = jax.random.truncated_normal(jax.random.fold_in(key, 41), -6.0, 6.0, (TOKENS, HEAD_COUNT, HEAD_DIM), jnp.float32)
    reduction_multiplier = jnp.where(agreement_indicator[:, None], 0.05 / contiguous_cluster, 1.0)
    return (noise * reduction_multiplier[:, :, None]).reshape(TOKENS, HEAD_COUNT * HEAD_DIM).astype(jnp.bfloat16)


def set_ends(result, own_key, smallest, largest):
    spot = [jax.random.randint(jax.random.fold_in(own_key, axis), (), 0, length) for axis, length in enumerate(result.shape)]
    longest = result.shape.index(max(result.shape))
    neighbour = spot[:longest] + [(spot[longest] + 1) % result.shape[longest]] + spot[longest + 1:]
    return result.at[tuple(spot)].set(smallest).at[tuple(neighbour)].set(largest)


def block_scale(own_key, dims, cuts, least, top_value):
    level, own = 1.0, jax.random.fold_in(own_key, 6)
    for axis_at, blocks in cuts:
        heights = jnp.exp(jax.random.uniform(jax.random.fold_in(own, axis_at), (blocks,), jnp.float32, least / len(cuts), top_value / len(cuts)))
        level = level * jnp.repeat(heights, dims[axis_at] // blocks).reshape([-1 if axis == axis_at else 1 for axis in range(len(dims))])
    return level


def centred(own_key, shape, deviation, most, pieces=(), kind=jnp.bfloat16):
    values = jax.random.normal(own_key, shape, jnp.float32) * deviation
    if len(pieces) > 0:
        values = block_scale(own_key, shape, pieces, -0.22, 0.18) * values
    return jnp.clip(values, min=-most, max=most).astype(kind)


def setup_inputs(seed: int = 0) -> dict:
    arg_keys = jax.random.split(jax.random.key(seed), 18)
    return {
        "prefill_input": draw_prefill_input(jax.random.fold_in(arg_keys[17], 71), 0),
        "prefill_step": draw_prefill_step(jax.random.fold_in(arg_keys[17], 71), 0),
        "write_proj": centred(arg_keys[2], (TOKENS, GROUPS * STATE_SIZE), 0.3, 2.5, ((0, 16), (1, 2))),
        "read_proj": centred(arg_keys[3], (TOKENS, GROUPS * STATE_SIZE), STATE_SIZE ** -0.5, 0.5, ((0, 16), (1, 2))),
        "decay_rate": draw_decay_rate(jax.random.fold_in(arg_keys[17], 71), 0),
        "skip_gain": jnp.clip(jnp.exp(math.log(2.0) - 1.3862944 * jax.random.uniform(arg_keys[5], (HEAD_COUNT,), jnp.float32) ** block_scale(arg_keys[5], (HEAD_COUNT,), ((0, 2),), -0.2, 0.2)), 0.5, 2.0),
        "resident_state": centred(arg_keys[6], (REQUESTS, HEAD_COUNT, HEAD_DIM, STATE_SIZE), 1.0, 6.0, ((0, 16), (1, 2))),
        "owner_slot": jax.random.permutation(arg_keys[7], REQUESTS).astype(jnp.int32),
        "draft_ids": set_ends(jax.random.randint(arg_keys[8], (REQUESTS, DRAFT_LEN), 0, CANDIDATES), jax.random.fold_in(arg_keys[8], 1), 0, CANDIDATES - 1).astype(jnp.int32),
        "accepted_len": set_ends(jax.random.randint(arg_keys[9], (REQUESTS,), 0, DRAFT_LEN + 1), jax.random.fold_in(arg_keys[9], 1), 0, DRAFT_LEN).astype(jnp.int32),
        "draft_input": centred(arg_keys[10], (REQUESTS * CANDIDATES, HEAD_COUNT * HEAD_DIM), 1.0, 6.0, ((0, 16), (1, 2))),
        "draft_gate": centred(arg_keys[11], (REQUESTS * CANDIDATES, HEAD_COUNT * HEAD_DIM), 1.0, 6.0, ((0, 16), (1, 2))),
        "draft_write": centred(arg_keys[12], (REQUESTS * CANDIDATES, GROUPS * STATE_SIZE), 0.3, 2.5, ((0, 16), (1, 2))),
        "draft_read": centred(arg_keys[13], (REQUESTS * CANDIDATES, GROUPS * STATE_SIZE), STATE_SIZE ** -0.5, 0.5, ((0, 16), (1, 2))),
        "draft_step": jnp.clip(jnp.exp(math.log(1.0) - 2.9957323 * jax.random.uniform(arg_keys[14], (REQUESTS * CANDIDATES, HEAD_COUNT), jnp.float32) ** block_scale(arg_keys[14], (REQUESTS * CANDIDATES, HEAD_COUNT), ((0, 16), (1, 2)), -0.2, 0.2)), 0.05, 1.0),
        "norm_gain": jnp.clip(1.0 + 0.1 * jax.random.normal(arg_keys[15], (HEAD_COUNT * HEAD_DIM,), jnp.float32), 0.5, 1.5),
        "out_weight": centred(arg_keys[16], (HEAD_COUNT * HEAD_DIM, MODEL_DIM), (HEAD_COUNT * HEAD_DIM) ** -0.5, 0.0625, ((0, 2), (1, 16))),
    }


PRECISE = lax.Precision.HIGHEST
EPSILON = 1e-05

def block_pass(block_input, block_step, block_write, block_read, rate, groups):
    span_len = block_input.shape[0]
    head_total = block_input.shape[1]
    per_group = head_total // groups
    log_decay = -block_step * rate[None, :]
    running = jnp.cumsum(log_decay, axis=0)
    scores = jnp.einsum('tgn,jgn->gtj', block_read.astype(jnp.float32), block_write.astype(jnp.float32))
    position = jnp.arange(span_len, dtype=jnp.int32)
    causal = position[:, None] >= position[None, :]
    running_t = running.T.reshape(groups, per_group, span_len)
    log_gap = running_t[:, :, :, None] - running_t[:, :, None, :]
    decayed = jnp.exp(jnp.where(causal[None, None], log_gap, -jnp.inf))
    step_t = block_step.T.reshape(groups, per_group, 1, span_len)
    mixing = (scores[:, None] * decayed * step_t).astype(jnp.bfloat16)
    incoming_vectors = block_input.reshape(span_len, groups, per_group, HEAD_DIM)
    intra_part = jnp.einsum('gktj,jgkp->tgkp', mixing.astype(jnp.float32), incoming_vectors.astype(jnp.float32))
    intra_part = intra_part.reshape(span_len, head_total, HEAD_DIM)
    to_end = jnp.exp(running[-1][None, :] - running) * block_step
    weighted = (block_input.astype(jnp.float32) * to_end[:, :, None]).astype(jnp.bfloat16)
    weighted = weighted.reshape(span_len, groups, per_group, HEAD_DIM)
    local_state = jnp.einsum('tgkp,tgn->gkpn', weighted.astype(jnp.float32), block_write.astype(jnp.float32))
    return (intra_part, local_state.reshape(head_total, HEAD_DIM, STATE_SIZE), running)

def read_state(block_read, state_now, running, groups):
    span_len = block_read.shape[0]
    head_total = state_now.shape[0]
    per_group = head_total // groups
    grouped = state_now.astype(jnp.bfloat16).reshape(groups, per_group, HEAD_DIM, STATE_SIZE)
    inter_part = jnp.einsum('tgn,gkpn->tgkp', block_read.astype(jnp.float32), grouped.astype(jnp.float32))
    return inter_part.reshape(span_len, head_total, HEAD_DIM) * jnp.exp(running)[:, :, None]

def verify_slot(start_state, rows_input, rows_gate, rows_write, rows_read, rows_step, kept_len, rate, skip, gain, groups):
    span_len = rows_input.shape[0]
    head_total = start_state.shape[0]
    per_group = head_total // groups
    log_decay = -rows_step * rate[None, :]
    running = jnp.cumsum(log_decay, axis=0)
    incoming_vectors = rows_input.astype(jnp.float32).reshape(span_len, groups, per_group, HEAD_DIM)
    write_rows = rows_write.astype(jnp.float32).reshape(span_len, groups, STATE_SIZE)
    read_rows = rows_read.astype(jnp.float32).reshape(span_len, groups, STATE_SIZE)
    scores = jnp.einsum('tgn,jgn->gtj', read_rows, write_rows, precision=PRECISE)
    position = jnp.arange(span_len, dtype=jnp.int32)
    causal = position[:, None] >= position[None, :]
    running_t = running.T.reshape(groups, per_group, span_len)
    log_gap = running_t[:, :, :, None] - running_t[:, :, None, :]
    decayed = jnp.exp(jnp.where(causal[None, None], log_gap, -jnp.inf))
    mixing = scores[:, None] * decayed * rows_step.T.reshape(groups, per_group, 1, span_len)
    intra_part = jnp.einsum('gktj,jgkp->tgkp', mixing, incoming_vectors, precision=PRECISE)
    grouped = start_state.reshape(groups, per_group, HEAD_DIM, STATE_SIZE)
    inter_part = jnp.einsum('tgn,gkpn->tgkp', read_rows, grouped, precision=PRECISE)
    inter_part = inter_part * jnp.exp(running).reshape(span_len, groups, per_group)[..., None]
    direct = intra_part + inter_part + skip.reshape(groups, per_group)[None, :, :, None] * incoming_vectors
    gates = rows_gate.astype(jnp.float32).reshape(span_len, groups, per_group, HEAD_DIM)
    gated = direct * jax.nn.silu(gates)
    flattened = gated.reshape(span_len, groups, per_group * HEAD_DIM)
    mean_square = lax.optimization_barrier(jnp.mean(flattened * flattened, axis=2, keepdims=True))
    hidden = flattened * lax.rsqrt(mean_square + EPSILON) * gain.reshape(groups, per_group * HEAD_DIM)[None]
    hidden = hidden.astype(jnp.bfloat16).reshape(span_len, head_total * HEAD_DIM)
    is_live = position < kept_len
    reach_log = lax.optimization_barrier(jnp.sum(jnp.where(is_live[:, None], log_decay, 0.0), axis=0))
    tail_weight = jnp.exp(jnp.where(is_live[:, None], reach_log[None, :] - running, -jnp.inf)) * rows_step
    weighted = incoming_vectors * tail_weight.reshape(span_len, groups, per_group)[..., None]
    added = jnp.einsum('tgkp,tgn->gkpn', weighted, write_rows, precision=PRECISE)
    added = added.reshape(head_total, HEAD_DIM, STATE_SIZE)
    new_state = (start_state * jnp.exp(reach_log)[:, None, None] + added).astype(jnp.bfloat16)
    return (hidden, new_state)

def reference(prefill_input, prefill_step, write_proj, read_proj, decay_rate, skip_gain, resident_state, owner_slot, draft_ids, accepted_len, draft_input, draft_gate, draft_write, draft_read, draft_step, norm_gain, out_weight):
    blocks = TOKENS // BLOCK_LEN
    incoming_vectors = prefill_input.reshape(blocks, BLOCK_LEN, HEAD_COUNT, HEAD_DIM)
    steps = prefill_step.reshape(blocks, BLOCK_LEN, HEAD_COUNT)
    writes = write_proj.reshape(blocks, BLOCK_LEN, GROUPS, STATE_SIZE)
    reads = read_proj.reshape(blocks, BLOCK_LEN, GROUPS, STATE_SIZE)

    def advance(state_now, block_data):
        block_input, block_step, block_write, block_read = block_data
        intra_part, local_state, running = block_pass(block_input, block_step, block_write, block_read, decay_rate, GROUPS)
        inter_part = read_state(block_read, state_now, running, GROUPS)
        output = (intra_part + inter_part + skip_gain[None, :, None] * block_input.astype(jnp.float32)).astype(jnp.bfloat16)
        state_now = state_now * jnp.exp(running[-1])[:, None, None] + local_state
        return (state_now, output)
    zero_state = jnp.zeros((HEAD_COUNT, HEAD_DIM, STATE_SIZE), jnp.float32)
    final_state, output_blocks = lax.scan(advance, zero_state, (incoming_vectors, steps, writes, reads))
    prefill_out = output_blocks.reshape(TOKENS, HEAD_COUNT * HEAD_DIM)
    prompt_state = final_state.astype(jnp.bfloat16)
    slot_index = jnp.arange(REQUESTS, dtype=jnp.int32)

    def one_slot(slot_id):
        request = jnp.sum(jnp.where(owner_slot == slot_id, slot_index, 0))
        picked = slot_index == request
        chosen = lax.optimization_barrier(jnp.sum(jnp.where(picked[:, None], draft_ids, 0), axis=0))
        kept_len = jnp.sum(jnp.where(picked, accepted_len, 0))
        row_index = (slot_id * CANDIDATES + chosen).astype(jnp.int32)
        start_state = jnp.where(owner_slot[0] == slot_id, prompt_state, resident_state[slot_id]).astype(jnp.float32)
        return verify_slot(start_state, draft_input[row_index], draft_gate[row_index], draft_write[row_index], draft_read[row_index], draft_step[row_index], kept_len, decay_rate, skip_gain, norm_gain, GROUPS)
    hidden, new_state = lax.map(one_slot, slot_index)
    verify_out = jnp.dot(hidden.reshape(VERIFY_ROWS, HEAD_COUNT * HEAD_DIM), out_weight, preferred_element_type=jnp.float32).astype(jnp.bfloat16)
    return (prefill_out, new_state, verify_out, prompt_state.reshape(HEAD_COUNT, HEAD_DIM * STATE_SIZE))
```

```python
import jax
import jax.numpy as jnp
from jax import lax
from jax.sharding import PartitionSpec as P

HEAD_DIM = 64
STATE_SIZE = 128
BLOCK_LEN = 256


PRECISE = lax.Precision.HIGHEST
EPSILON = 1e-05


def tree_factors(count):
    factors = []
    if count > 1:
        factors.append(2)
        count //= 2
    inner = 1
    while inner * inner * 4 <= count:
        inner *= 2
    for factor in (inner, count // inner):
        if factor > 1:
            factors.append(factor)
    return factors


def tree_stages(count):
    stages, stride = [], 1
    for factor in tree_factors(count):
        stages.append((factor, stride))
        stride *= factor
    assert stride == count
    return stages


def partner(index, stage, offset):
    factor, stride = stage
    return index ^ (offset * stride)


def swap(value, axis, stage, offset):
    count = lax.axis_size(axis)
    return lax.ppermute(
        value, axis, [(source, partner(source, stage, offset)) for source in range(count)]
    )


def in_order(parts, place):
    if len(parts) == 2:
        first = jnp.where(place == 0, parts[0], parts[1])
        second = jnp.where(place == 0, parts[1], parts[0])
        return jnp.stack([first, second])
    stacked = jnp.stack(parts)
    order = place ^ jnp.arange(len(parts), dtype=jnp.int32)
    return jnp.take(stacked, order, axis=0)


def gather_slots(part, axis):
    here = lax.axis_index(axis)
    stages = tree_stages(lax.axis_size(axis))
    ndim = part.ndim
    for level, stage in enumerate(reversed(stages)):
        factor, stride = stage
        place = (here // stride) % factor
        parts = [part] + [swap(part, axis, stage, k) for k in range(1, factor)]
        part = jnp.moveaxis(in_order(parts, place), 0, level)
    return part.reshape((-1,) + part.shape[part.ndim - ndim:])


def spread_rows(weights, start, length):
    rows = jnp.repeat(weights, HEAD_DIM, axis=-1)
    return lax.dynamic_slice_in_dim(rows, start, length, rows.ndim - 1)[..., None]


def scan_states(local_rows, device_log, axis):
    count, here = lax.axis_size(axis), lax.axis_index(axis)
    logs = gather_slots(device_log, axis)
    stages = tree_stages(count)
    device = jnp.arange(count, dtype=jnp.int32)
    total, start, held = local_rows, 0, []
    for factor, stride in stages:
        stage = (factor, stride)
        place = (here // stride) % factor
        base = here // (stride * factor) * (stride * factor)
        length = total.shape[0] // factor
        pieces = total.astype(jnp.bfloat16).reshape(factor, length, STATE_SIZE)
        parts = [lax.dynamic_index_in_dim(total.reshape(factor, length, STATE_SIZE), place, 0, keepdims=False)]
        for k in range(1, factor):
            sent = lax.dynamic_index_in_dim(pieces, place ^ k, 0, keepdims=False)
            parts.append(swap(sent, axis, stage, k).astype(jnp.float32))
        start = start + place * length
        segment = (device - base) // stride
        inside = (device >= base) & (device < base + stride * factor)
        spots = place ^ jnp.arange(factor, dtype=jnp.int32)
        targets = jnp.concatenate([spots, jnp.full((1,), factor, jnp.int32)])
        between = (
            inside[None, None, :]
            & (segment[None, None, :] > spots[None, :, None])
            & (segment[None, None, :] < targets[:, None, None])
        )
        reach = jnp.sum(jnp.where(between[..., None], logs[None, None], 0.0), axis=2)
        earlier = spots[None, :] < targets[:, None]
        weights = jnp.where(earlier[..., None], jnp.exp(reach), 0.0)
        ahead = inside[None, :] & (segment[None, :] < targets[:, None])
        carry = jnp.exp(jnp.sum(jnp.where(ahead[..., None], logs[None], 0.0), axis=1))
        weights = spread_rows(weights, start, length)
        carry = spread_rows(carry, start, length)
        sums = [
            sum(weights[target, k] * parts[k] for k in range(factor)) for target in range(factor + 1)
        ]
        total = sums[factor]
        held.append((stage, place, sums[:factor], carry))
    final = total.astype(jnp.bfloat16)
    entering = None
    for stage, place, sums, carry in reversed(held):
        factor, stride = stage
        if entering is not None:
            sums = [carry[k] * entering.astype(jnp.float32) + sums[k] for k in range(factor)]
        sums = [part.astype(jnp.bfloat16) for part in sums]
        parts = [sums[0]] + [swap(sums[k], axis, stage, k) for k in range(1, factor)]
        entering = in_order(parts, place).reshape(-1, STATE_SIZE)
    for stage, place, _, _ in reversed(held):
        factor, stride = stage
        parts = [final] + [swap(final, axis, stage, k) for k in range(1, factor)]
        final = in_order(parts, place).reshape(-1, STATE_SIZE)
    return (entering, final)


def scatter_sum(whole, axis):
    count, here = lax.axis_size(axis), lax.axis_index(axis)
    blocks = whole.reshape((count, -1) + whole.shape[1:])
    total = lax.dynamic_index_in_dim(blocks, here, 0, keepdims=False)
    for k in range(1, count):
        sent = lax.dynamic_index_in_dim(blocks, here ^ k, 0, keepdims=False)
        total = total + swap(sent, axis, (count, 1), k)
    return total


def local_block(block_input, block_step, block_write, block_read, rate, groups):
    span_len = block_input.shape[0]
    head_total = rate.shape[0]
    per_group = head_total // groups
    log_decay = -block_step * rate[None, :]
    running = jnp.cumsum(log_decay, axis=0)
    write_rows = block_write.reshape(span_len, groups, STATE_SIZE)
    read_rows = block_read.reshape(span_len, groups, STATE_SIZE)
    scores = jnp.einsum("tgn,jgn->gtj", read_rows, write_rows, preferred_element_type=jnp.float32)
    position = jnp.arange(span_len, dtype=jnp.int32)
    causal = position[:, None] >= position[None, :]
    running_t = running.T.reshape(groups, per_group, span_len)
    log_gap = running_t[:, :, :, None] - running_t[:, :, None, :]
    decayed = jnp.exp(jnp.where(causal[None, None], log_gap, -jnp.inf))
    step_t = block_step.T.reshape(groups, per_group, 1, span_len)
    mixing = (scores[:, None] * decayed * step_t).astype(jnp.bfloat16)
    incoming_vectors = block_input.reshape(span_len, groups, per_group, HEAD_DIM)
    intra_part = jnp.einsum(
        "gktj,jgkp->tgkp", mixing, incoming_vectors, preferred_element_type=jnp.float32
    )
    intra_part = intra_part.reshape(span_len, head_total, HEAD_DIM)
    to_end = jnp.exp(running[-1][None, :] - running) * block_step
    weighted = (
        incoming_vectors.astype(jnp.float32)
        * to_end.reshape(span_len, groups, per_group)[..., None]
    ).astype(jnp.bfloat16)
    local_state = jnp.einsum(
        "tgkp,tgn->gkpn", weighted, write_rows, preferred_element_type=jnp.float32
    )
    return (intra_part, local_state.reshape(head_total, HEAD_DIM, STATE_SIZE), running)


def read_state(block_read, state_now, running, groups):
    span_len = block_read.shape[0]
    head_total = state_now.shape[0]
    per_group = head_total // groups
    grouped = state_now.astype(jnp.bfloat16).reshape(groups, per_group, HEAD_DIM, STATE_SIZE)
    read_rows = block_read.reshape(span_len, groups, STATE_SIZE)
    inter_part = jnp.einsum(
        "tgn,gkpn->tgkp", read_rows, grouped, preferred_element_type=jnp.float32
    )
    return inter_part.reshape(span_len, head_total, HEAD_DIM) * jnp.exp(running)[:, :, None]


def verify_slot(
    start_state,
    rows_input,
    rows_gate,
    rows_write,
    rows_read,
    rows_step,
    kept_len,
    rate,
    skip,
    gain,
    groups,
):
    span_len = rows_input.shape[0]
    head_total = start_state.shape[0]
    per_group = head_total // groups
    log_decay = -rows_step * rate[None, :]
    running = jnp.cumsum(log_decay, axis=0)
    incoming_vectors = rows_input.astype(jnp.float32).reshape(span_len, groups, per_group, HEAD_DIM)
    write_rows = rows_write.astype(jnp.float32).reshape(span_len, groups, STATE_SIZE)
    read_rows = rows_read.astype(jnp.float32).reshape(span_len, groups, STATE_SIZE)
    scores = jnp.einsum("tgn,jgn->gtj", read_rows, write_rows, precision=PRECISE)
    position = jnp.arange(span_len, dtype=jnp.int32)
    causal = position[:, None] >= position[None, :]
    running_t = running.T.reshape(groups, per_group, span_len)
    log_gap = running_t[:, :, :, None] - running_t[:, :, None, :]
    decayed = jnp.exp(jnp.where(causal[None, None], log_gap, -jnp.inf))
    mixing = scores[:, None] * decayed * rows_step.T.reshape(groups, per_group, 1, span_len)
    intra_part = jnp.einsum("gktj,jgkp->tgkp", mixing, incoming_vectors, precision=PRECISE)
    grouped = start_state.reshape(groups, per_group, HEAD_DIM, STATE_SIZE)
    inter_part = jnp.einsum("tgn,gkpn->tgkp", read_rows, grouped, precision=PRECISE)
    inter_part = inter_part * jnp.exp(running).reshape(span_len, groups, per_group)[..., None]
    direct = (
        intra_part
        + inter_part
        + skip.reshape(groups, per_group)[None, :, :, None] * incoming_vectors
    )
    gates = rows_gate.astype(jnp.float32).reshape(span_len, groups, per_group, HEAD_DIM)
    gated = direct * jax.nn.silu(gates)
    flattened = gated.reshape(span_len, groups, per_group * HEAD_DIM)
    mean_square = jnp.mean(flattened * flattened, axis=2, keepdims=True)
    hidden = (
        flattened
        * lax.rsqrt(mean_square + EPSILON)
        * gain.reshape(groups, per_group * HEAD_DIM)[None]
    )
    hidden = hidden.astype(jnp.bfloat16).reshape(span_len, head_total * HEAD_DIM)
    is_live = position < kept_len
    reach_log = jnp.sum(jnp.where(is_live[:, None], log_decay, 0.0), axis=0)
    tail_weight = (
        jnp.exp(jnp.where(is_live[:, None], reach_log[None, :] - running, -jnp.inf)) * rows_step
    )
    weighted = incoming_vectors * tail_weight.reshape(span_len, groups, per_group)[..., None]
    added = jnp.einsum("tgkp,tgn->gkpn", weighted, write_rows, precision=PRECISE)
    added = added.reshape(head_total, HEAD_DIM, STATE_SIZE)
    new_state = (start_state * jnp.exp(reach_log)[:, None, None] + added).astype(jnp.bfloat16)
    return (hidden, new_state)


def on_device(
    prefill_input,
    prefill_step,
    write_proj,
    read_proj,
    decay_rate,
    skip_gain,
    resident_state,
    owner_slot,
    draft_ids,
    accepted_len,
    draft_input,
    draft_gate,
    draft_write,
    draft_read,
    draft_step,
    norm_gain,
    out_weight,
):
    local_heads = decay_rate.shape[0]
    local_groups = write_proj.shape[1] // STATE_SIZE
    assert prefill_input.shape[0] == BLOCK_LEN
    intra_part, local_state, running = local_block(
        prefill_input, prefill_step, write_proj, read_proj, decay_rate, local_groups
    )
    entering, final = scan_states(
        local_state.reshape(local_heads * HEAD_DIM, STATE_SIZE), running[-1], "seq"
    )
    state_shape = (local_heads, HEAD_DIM, STATE_SIZE)
    inter_part = read_state(read_proj, entering.reshape(state_shape), running, local_groups)
    skip_part = skip_gain[None, :, None] * prefill_input.reshape(
        BLOCK_LEN, local_heads, HEAD_DIM
    ).astype(jnp.float32)
    prefill_out = (intra_part + inter_part + skip_part).astype(jnp.bfloat16)
    prefill_out = prefill_out.reshape(BLOCK_LEN, local_heads * HEAD_DIM)
    seq_count = lax.axis_size("seq")
    sequence_index = lax.axis_index("seq")
    prompt_state = final.reshape(state_shape)
    slice_width = HEAD_DIM * STATE_SIZE // seq_count
    flat_state = prompt_state.reshape(local_heads, HEAD_DIM * STATE_SIZE)
    state_slice = lax.dynamic_slice_in_dim(flat_state, sequence_index * slice_width, slice_width, 1)
    slot_index = jnp.arange(owner_slot.shape[0], dtype=jnp.int32)
    request = jnp.sum(jnp.where(owner_slot == sequence_index, slot_index, 0))
    picked = slot_index == request
    chosen = jnp.sum(jnp.where(picked[:, None], draft_ids, 0), axis=0)
    kept_len = jnp.sum(jnp.where(picked, accepted_len, 0))
    start_state = jnp.where(
        owner_slot[0] == sequence_index, prompt_state, resident_state[0]
    ).astype(jnp.float32)
    selector = chosen[:, None] == jnp.arange(draft_input.shape[0], dtype=jnp.int32)[None, :]
    pick_low = selector.astype(jnp.bfloat16)
    pick_high = selector.astype(jnp.float32)
    rows_input = jnp.dot(pick_low, draft_input, preferred_element_type=jnp.float32).astype(
        jnp.bfloat16
    )
    rows_gate = jnp.dot(pick_low, draft_gate, preferred_element_type=jnp.float32).astype(
        jnp.bfloat16
    )
    rows_write = jnp.dot(pick_low, draft_write, preferred_element_type=jnp.float32).astype(
        jnp.bfloat16
    )
    rows_read = jnp.dot(pick_low, draft_read, preferred_element_type=jnp.float32).astype(
        jnp.bfloat16
    )
    rows_step = jnp.dot(pick_high, draft_step, precision=PRECISE)
    hidden, new_state = verify_slot(
        start_state,
        rows_input,
        rows_gate,
        rows_write,
        rows_read,
        rows_step,
        kept_len,
        decay_rate,
        skip_gain,
        norm_gain,
        local_groups,
    )
    gathered = gather_slots(hidden, "seq")
    partial_out = jnp.dot(
        gathered.reshape(-1, gathered.shape[-1]), out_weight, preferred_element_type=jnp.float32
    )
    verify_out = scatter_sum(partial_out, "head").astype(jnp.bfloat16)
    return (prefill_out, new_state[None], verify_out, state_slice)


def solution(mesh):
    return jax.shard_map(
        on_device,
        mesh=mesh,
        in_specs=(
            P("seq", "head"),
            P("seq", "head"),
            P("seq", "head"),
            P("seq", "head"),
            P("head"),
            P("head"),
            P("seq", "head", None, None),
            P(),
            P(),
            P(),
            P("seq", "head"),
            P("seq", "head"),
            P("seq", "head"),
            P("seq", "head"),
            P("seq", "head"),
            P("head"),
            P("head", "seq"),
        ),
        out_specs=(
            P("seq", "head"),
            P("seq", "head", None, None),
            P("head", "seq"),
            P("head", "seq"),
        ),
        check_vma=False,
    )
```

```python
import functools

import jax
import jax.numpy as jnp
from jax import lax
from jax.experimental import pallas as pl
from jax.experimental.pallas import tpu as pltpu
from jax.sharding import PartitionSpec as P

HEAD_DIM = 64
STATE_SIZE = 128
BLOCK_LEN = 256
DRAFTS = 8
EPSILON = 1e-05
EXTRA = 32
UP_ROWS = STATE_SIZE + EXTRA
READ_AT = STATE_SIZE + 16
LOG_AT = STATE_SIZE + 24
DOWN_ROWS = STATE_SIZE + 16

F32 = jnp.float32
BF16 = jnp.bfloat16


def tree_stages(count):
    factors, rest = [], count
    if rest > 1:
        factors.append(2)
        rest //= 2
    inner = 1
    while inner * inner * 4 <= rest:
        inner *= 2
    factors += [inner, rest // inner]
    stages, stride = [], 1
    for factor in factors:
        stages.append((factor, stride))
        stride *= factor
    assert stride == count
    return stages


def swap(value, axis, stage, offset):
    count, stride = lax.axis_size(axis), stage[1]
    return lax.ppermute(value, axis, [(k, k ^ (offset * stride)) for k in range(count)])


def place_of(stage):
    factor, stride = stage
    return lax.rem(lax.div(lax.axis_index("seq"), stride), factor)


def dot(a, b, dims=((1,), (0,))):
    return lax.dot_general(a, b, (dims, ((), ())), preferred_element_type=F32)


def split(value, parts):
    found = []
    for _ in range(parts):
        part = value.astype(BF16).astype(F32)
        found.append(part)
        value = value - part
    return found


def head_mask(rows, heads, lanes, lane0):
    row = lax.broadcasted_iota(jnp.int32, (rows, lanes), 0) & (heads - 1)
    head = lax.shift_right_logical(lax.broadcasted_iota(jnp.int32, (rows, lanes), 1) + lane0, 6)
    return jnp.where(row == head, 1.0, 0.0).astype(BF16)


def window(start, size):
    return pl.ds(pl.multiple_of(start, size), size)


def call(kernel, name, outs, args, smem=(), scratch=(), flops=0, exps=0, vmem=40):
    in_specs = [
        pl.BlockSpec(memory_space=pltpu.SMEM if k in smem else pltpu.VMEM) for k in range(len(args))
    ]
    moved = sum(a.size * a.dtype.itemsize for a in args)
    moved += sum(o.size * o.dtype.itemsize for o in outs)
    return pl.pallas_call(
        kernel,
        name=name,
        out_shape=outs,
        in_specs=in_specs,
        out_specs=[pl.BlockSpec(memory_space=pltpu.VMEM)] * len(outs),
        scratch_shapes=list(scratch),
        compiler_params=pltpu.CompilerParams(vmem_limit_bytes=vmem * 1024 * 1024),
        cost_estimate=pl.CostEstimate(flops=flops, bytes_accessed=moved, transcendentals=exps),
    )(*args)


def shape(dims, dtype):
    return jax.ShapeDtypeStruct(dims, dtype)


def open_kernel(
    stage,
    step_ref,
    rate_ref,
    skip_ref,
    x_ref,
    write_ref,
    owner_ref,
    ids_ref,
    kept_ref,
    din_ref,
    dgate_ref,
    dwrite_ref,
    dread_ref,
    dstep_ref,
    own_ref,
    sent_ref,
    run_ref,
    runt_ref,
    stept_ref,
    reach_ref,
    q1_ref,
    q2_ref,
    vread_ref,
    vwrite_ref,
    tail_ref,
    extra_ref,
):
    span, heads = step_ref.shape
    lanes = x_ref.shape[1]
    groups = write_ref.shape[1] // STATE_SIZE
    per_group = heads // groups
    wide = per_group * HEAD_DIM
    here = lax.axis_index("seq")
    place = place_of(stage)

    step = step_ref[...]
    log_decay = -step * rate_ref[...]
    lower = lax.broadcasted_iota(jnp.int32, (span, span), 0) >= lax.broadcasted_iota(
        jnp.int32, (span, span), 1
    )
    lower = jnp.where(lower, 1.0, 0.0).astype(BF16)
    running = sum(dot(lower, part.astype(BF16)) for part in split(log_decay, 3))
    total = running[span - 1 : span, :]
    to_end = jnp.exp(total - running) * step
    both = jnp.concatenate([running, step], axis=1)
    if 2 * heads < 128:
        both = jnp.concatenate([both, jnp.zeros((span, 128 - 2 * heads), F32)], axis=1)
    turned = both.T
    runt_ref[...] = turned[:heads]
    stept_ref[...] = turned[heads : 2 * heads]
    for g in range(groups):
        run_ref[g] = running[:, g * per_group : (g + 1) * per_group]
    reach_ref[...] = jnp.concatenate(split(jnp.exp(running), 2), axis=1).astype(BF16)
    end_parts = jnp.concatenate(split(to_end, 2), axis=1).astype(BF16)

    slots = owner_ref.shape[0]
    request = lax.fori_loop(
        0, slots, lambda r, found: jnp.where(owner_ref[r] == here, r, found), jnp.int32(0)
    )
    kept = kept_ref[request]
    candidates = din_ref.shape[0]
    row = lax.broadcasted_iota(jnp.int32, (DRAFTS, candidates), 0)
    col = lax.broadcasted_iota(jnp.int32, (DRAFTS, candidates), 1)
    pick = jnp.zeros((DRAFTS, candidates), F32)
    for i in range(DRAFTS):
        pick = jnp.where((row == i) & (col == ids_ref[request, i]), 1.0, pick)
    pick = pick.astype(BF16)
    vin = dot(pick, din_ref[...])
    vgate = dot(pick, dgate_ref[...])
    vwrite = dot(pick, dwrite_ref[...]).astype(BF16)
    vread = dot(pick, dread_ref[...]).astype(BF16)
    vwrite_ref[...] = vwrite
    vread_ref[...] = vread
    vstep = sum(dot(pick, part.astype(BF16)) for part in split(dstep_ref[...], 3))
    vlog = -vstep * rate_ref[...]
    index = lax.broadcasted_iota(jnp.int32, (DRAFTS, heads), 0)
    acc = jnp.zeros((1, heads), F32)
    vrun = jnp.zeros((DRAFTS, heads), F32)
    reach = jnp.zeros((1, heads), F32)
    for i in range(DRAFTS):
        acc = acc + vlog[i : i + 1]
        vrun = jnp.where(index == i, acc, vrun)
        reach = jnp.where(i < kept, acc, reach)
    others = jnp.where(index == 0, total, jnp.where(index == 1, skip_ref[...], reach))
    stacked = split(jnp.concatenate([vrun, vstep, others], axis=0), 3)
    stacked = jnp.concatenate(stacked, axis=0).astype(BF16)
    row = lax.broadcasted_iota(jnp.int32, (DRAFTS, wide), 0)
    is_owner = owner_ref[0] == here
    for g in range(groups):
        at = slice(g * wide, (g + 1) * wide)
        spread = dot(stacked, head_mask(heads, heads, wide, g * wide))
        spread = spread[0:24] + spread[24:48] + spread[48:72]
        vrun_l, vstep_l = spread[0:8], spread[8:16]
        total_l, skip_l, reach_l = spread[16:17], spread[17:18], spread[18:19]
        vin_g = vin[:, at]
        vr = vread[:, g * STATE_SIZE : (g + 1) * STATE_SIZE]
        vw = vwrite[:, g * STATE_SIZE : (g + 1) * STATE_SIZE]
        scores = dot(vr, vw, ((1,), (1,)))
        direct = skip_l * vin_g
        for j in range(DRAFTS):
            decay = jnp.exp(jnp.where(row >= j, vrun_l - vrun_l[j : j + 1], -jnp.inf))
            direct = direct + decay * scores[:, j : j + 1] * (vstep_l[j : j + 1] * vin_g[j : j + 1])
        gate = vgate[:, at]
        gate = gate / (1.0 + jnp.exp(-gate))
        q1 = direct * gate
        q2 = jnp.exp(vrun_l) * gate
        q1_ref[:, at] = q1
        q2_ref[:, at] = q2
        live = jnp.exp(jnp.where(row < kept, reach_l - vrun_l, -jnp.inf)) * vstep_l * vin_g
        keep_l = jnp.concatenate(
            split(jnp.exp(reach_l), 3) + [jnp.zeros((5, wide), F32)], axis=0
        )
        tail_ref[:, at] = jnp.concatenate(split(live, 3) + [keep_l], axis=0).astype(BF16)
        read_l = jnp.concatenate([vr.astype(F32)] * (wide // STATE_SIZE), axis=1)
        mine = jnp.concatenate([q1, q2, read_l], axis=0)
        mine = jnp.where(is_owner, mine, 0.0)
        logs = jnp.concatenate(split(total_l, 3) + [jnp.zeros((5, wide), F32)], axis=0)
        extra_ref[:, at] = jnp.concatenate([mine, logs], axis=0).astype(BF16)

    half = lanes // 2
    chunk = min(wide, half)
    for k, out_ref in ((1, sent_ref), (0, own_ref)):
        start = (place ^ k) * half
        out_ref[STATE_SIZE:, :] = extra_ref[:, window(start, half)]
        for at in range(0, half, chunk):
            lane0 = start + at
            group = lax.div(lane0, wide)
            scale = dot(end_parts, head_mask(2 * heads, heads, chunk, lane0))
            weighted = (x_ref[:, window(lane0, chunk)].astype(F32) * scale).astype(BF16)
            writes = write_ref[:, window(group * STATE_SIZE, STATE_SIZE)]
            writes = writes.astype(F32).T.astype(BF16)
            out_ref[:STATE_SIZE, at : at + chunk] = dot(writes, weighted).astype(BF16)


def logs_of(block):
    return block[0:1].astype(F32) + block[1:2].astype(F32) + block[2:3].astype(F32)


def weights_of(logs, place, target):
    spots = [place ^ k for k in range(len(logs))]
    found = []
    for k, spot in enumerate(spots):
        between = jnp.zeros_like(logs[0])
        for other, log in zip(spots, logs):
            if other is not spot:
                between = between + jnp.where((spot < other) & (other < target), log, 0.0)
        found.append(jnp.where(spot < target, jnp.exp(between), 0.0))
    return found


def carry_of(logs, place, target):
    ahead = jnp.zeros_like(logs[0])
    for k, log in enumerate(logs):
        ahead = ahead + jnp.where((place ^ k) < target, log, 0.0)
    return jnp.exp(ahead)


def up_kernel(stage, following, count, *refs):
    parts, outs = refs[:count], refs[count:]
    place, target = place_of(stage), place_of(following)
    width = outs[0].shape[1]
    chunk = min(256, width)
    order = list(range(1, len(outs))) + [0]
    for k in order:
        for at in range(0, width, chunk):
            start = at if len(outs) == 1 else (target ^ k) * width + at
            at_in = window(start, chunk)
            logs = [logs_of(part[LOG_AT:UP_ROWS, at_in]) for part in parts]
            scale = weights_of(logs, place, count)
            state = sum(
                w * part[:STATE_SIZE, at_in].astype(F32) for w, part in zip(scale, parts)
            )
            outs[k][:STATE_SIZE, at : at + chunk] = state.astype(BF16)
            mine = sum(part[STATE_SIZE:UP_ROWS, at_in].astype(F32) for part in parts)
            total = jnp.concatenate(
                split(sum(logs), 3) + [jnp.zeros((5, chunk), F32)], axis=0
            )
            outs[k][STATE_SIZE:, at : at + chunk] = jnp.concatenate(
                [mine[:24], total], axis=0
            ).astype(BF16)


def top_kernel(stage, count, *refs):
    parts, outs, prompt_ref = refs[:count], refs[count:-1], refs[-1]
    place = place_of(stage)
    width = prompt_ref.shape[1]
    logs = [logs_of(part[LOG_AT:UP_ROWS, :]) for part in parts]
    states = [part[:STATE_SIZE, :].astype(F32) for part in parts]
    final = sum(w * s for w, s in zip(weights_of(logs, place, count), states)).astype(BF16)
    prompt_ref[...] = final
    mine = sum(part[STATE_SIZE:LOG_AT, :].astype(F32) for part in parts)
    reads = mine[16:24, :STATE_SIZE].astype(BF16)
    gated = mine[0:8] + mine[8:16] * dot(reads, final)
    gated = jnp.concatenate(split(gated, 2), axis=0).astype(BF16)
    for k in list(range(1, len(outs))) + [0]:
        scale = weights_of(logs, place, place ^ k)
        outs[k][:STATE_SIZE, :] = sum(w * s for w, s in zip(scale, states)).astype(BF16)
        outs[k][STATE_SIZE:, :] = gated


def down_kernel(stage, above, above_count, count, *refs):
    pieces, parts = refs[:above_count], refs[above_count : above_count + count]
    outs = refs[above_count + count :]
    place, source = place_of(stage), place_of(above)
    width = pieces[0].shape[1]
    chunk = min(256, width)
    for k in list(range(1, len(outs))) + [0]:
        for piece in range(above_count):
            for at in range(0, width, chunk):
                start = at if above_count == 1 else (source ^ piece) * width + at
                at_out = window(start, chunk)
                block = pieces[piece][:, at : at + chunk]
                logs = [logs_of(part[LOG_AT:UP_ROWS, at_out]) for part in parts]
                state = carry_of(logs, place, place ^ k) * block[:STATE_SIZE].astype(F32)
                for w, part in zip(weights_of(logs, place, place ^ k), parts):
                    state = state + w * part[:STATE_SIZE, at_out].astype(F32)
                outs[k][:STATE_SIZE, at_out] = state.astype(BF16)
                outs[k][STATE_SIZE:, at_out] = block[STATE_SIZE:]


def intra_kernel(run_ref, runt_ref, stept_ref, skip_ref, x_ref, write_ref, read_ref, out_ref):
    span = x_ref.shape[0]
    heads = runt_ref.shape[0]
    mid = span // 2
    scores = dot(read_ref[...], write_ref[...], ((1,), (1,)))
    row = lax.broadcasted_iota(jnp.int32, (mid, mid), 0)
    causal = row >= lax.broadcasted_iota(jnp.int32, (mid, mid), 1)
    running = run_ref[0]
    spread = jnp.concatenate(split(skip_ref[...], 3) + [jnp.zeros((5, heads), F32)], axis=0)
    spread = dot(spread.astype(BF16), head_mask(heads, heads, x_ref.shape[1], 0))
    skip = spread[0:1] + spread[1:2] + spread[2:3]
    for pair in range(heads // 2):
        found = []
        for h in (2 * pair, 2 * pair + 1):
            x = x_ref[:, h * HEAD_DIM : (h + 1) * HEAD_DIM]
            t_run, j_run = running[:, h : h + 1], runt_ref[h : h + 1, :]
            step = stept_ref[h : h + 1, :]

            def mixed(rows, cols, masked):
                gap = t_run[rows] - j_run[:, cols]
                if masked:
                    gap = jnp.where(causal, gap, -jnp.inf)
                return (scores[rows, cols] * jnp.exp(gap) * step[:, cols]).astype(BF16)

            low, high = slice(0, mid), slice(mid, span)
            top = dot(mixed(low, low, True), x[low])
            bottom = dot(mixed(high, low, False), x[low]) + dot(mixed(high, high, True), x[high])
            found.append(jnp.concatenate([top, bottom], axis=0))
        at = slice(pair * 2 * HEAD_DIM, (pair + 1) * 2 * HEAD_DIM)
        both = jnp.concatenate(found, axis=1)
        out_ref[:, at] = both + skip[:, at] * x_ref[:, at].astype(F32)


def intra(run, runt, stept, skip, x, write, read, first, number):
    span, lanes = x.shape
    groups, _, per_group = run.shape
    wide = per_group * HEAD_DIM
    return pl.pallas_call(
        intra_kernel,
        name="intra",
        grid=(number,),
        out_shape=shape((span, number * wide), F32),
        in_specs=[
            pl.BlockSpec((1, span, per_group), lambda g: (g + first, 0, 0)),
            pl.BlockSpec((per_group, span), lambda g: (g + first, 0)),
            pl.BlockSpec((per_group, span), lambda g: (g + first, 0)),
            pl.BlockSpec((None, 1, per_group), lambda g: (g + first, 0, 0)),
            pl.BlockSpec((span, wide), lambda g: (0, g + first)),
            pl.BlockSpec((span, STATE_SIZE), lambda g: (0, g + first)),
            pl.BlockSpec((span, STATE_SIZE), lambda g: (0, g + first)),
        ],
        out_specs=pl.BlockSpec((span, wide), lambda g: (0, g)),
        compiler_params=pltpu.CompilerParams(vmem_limit_bytes=32 * 1024 * 1024),
        cost_estimate=pl.CostEstimate(
            flops=number * per_group * span * span * HEAD_DIM * 2,
            bytes_accessed=number * wide * span * 6,
            transcendentals=number * per_group * span * span * 3 // 4,
        ),
    )(run, runt, stept, skip.reshape(groups, 1, per_group), x, write, read)


def finish_kernel(stage, shares, *refs):
    reach_ref, read_ref, own_ref, got_ref = refs[:4]
    base_refs, out_ref = refs[4:-1], refs[-1]
    place = place_of(stage)
    heads = reach_ref.shape[1] // 2
    lanes = out_ref.shape[1]
    wide = lanes // (read_ref.shape[1] // STATE_SIZE)
    half = lanes // 2
    chunk = min(512, half)
    per_base = lanes // shares
    reach = reach_ref[...]
    for lane0 in range(0, lanes, chunk):
        group = lane0 // wide
        at = lane0 % half
        mine = place == lane0 // half
        entering = jnp.where(
            mine, own_ref[:STATE_SIZE, at : at + chunk], got_ref[:STATE_SIZE, at : at + chunk]
        )
        reads = read_ref[:, group * STATE_SIZE : (group + 1) * STATE_SIZE]
        inter = dot(reads, entering) * dot(reach, head_mask(2 * heads, heads, chunk, lane0))
        base = base_refs[lane0 // per_base]
        base_at = lane0 % per_base
        total = inter + base[:, base_at : base_at + chunk]
        out_ref[:, lane0 : lane0 + chunk] = total.astype(BF16)


def resident_kernel(state_ref, vread_ref, q1_ref, q2_ref, gain_ref, out_ref):
    drawn = dot(vread_ref[...], state_ref[...], ((1,), (1,)))
    gated = q1_ref[...] + q2_ref[...] * drawn
    out_ref[...] = normed(gated, gain_ref[...]).astype(BF16)


def normed(gated, gain):
    mean_square = jnp.mean(gated * gated, axis=1, keepdims=True)
    return gated * lax.rsqrt(mean_square + EPSILON) * gain


def resident_hidden(state, vread, q1, q2, gain):
    lanes = state.shape[0]
    groups = vread.shape[1] // STATE_SIZE
    wide = lanes // groups
    return pl.pallas_call(
        resident_kernel,
        name="resident_hidden",
        grid=(groups,),
        out_shape=shape((DRAFTS, lanes), BF16),
        in_specs=[
            pl.BlockSpec((wide, STATE_SIZE), lambda g: (g, 0)),
            pl.BlockSpec((DRAFTS, STATE_SIZE), lambda g: (0, g)),
            pl.BlockSpec((DRAFTS, wide), lambda g: (0, g)),
            pl.BlockSpec((DRAFTS, wide), lambda g: (0, g)),
            pl.BlockSpec((1, wide), lambda g: (0, g)),
        ],
        out_specs=pl.BlockSpec((DRAFTS, wide), lambda g: (0, g)),
        compiler_params=pltpu.CompilerParams(vmem_limit_bytes=32 * 1024 * 1024),
        cost_estimate=pl.CostEstimate(
            flops=2 * DRAFTS * lanes * STATE_SIZE,
            bytes_accessed=lanes * STATE_SIZE * 2,
            transcendentals=0,
        ),
    )(state, vread, q1, q2, gain)


def project_kernel(stages, head_count, *refs):
    owner_ref, own_rows, got_rows, own_ref, got_ref, gain_ref, weight_ref = refs[:7]
    outs = refs[7 : 7 + head_count]
    gated_ref, left_ref, total_ref = refs[7 + head_count :]
    group, groups = pl.program_id(0), pl.num_programs(0)
    here, head = lax.axis_index("seq"), lax.axis_index("head")
    place = place_of(stages[0])
    half = own_ref.shape[1]
    wide = weight_ref.shape[0]
    rows = own_rows.shape[0]

    @pl.when(group == 0)
    def _():
        for k, ref in enumerate((own_ref, got_ref)):
            both = ref[...].astype(F32)
            gated_ref[:, window((place ^ k) * half, half)] = both[0:8] + both[8:16]

    hidden = normed(gated_ref[:, window(group * wide, wide)], gain_ref[...])
    left_ref[0:rows, :] = own_rows[...]
    left_ref[rows : 2 * rows, :] = got_rows[...]
    left_ref[2 * rows :, :] = jnp.concatenate([hidden, jnp.zeros_like(hidden)], axis=0).astype(BF16)
    share = dot(left_ref[...], weight_ref[...])

    @pl.when(group == 0)
    def _():
        total_ref[...] = share

    @pl.when(group > 0)
    def _():
        total_ref[...] += share

    @pl.when(group == groups - 1)
    def _():
        slots = 2 * rows // DRAFTS
        per_head = slots // head_count
        offsets = [0]
        for factor, stride in reversed(stages):
            offsets = [a + k * stride for k in range(factor) for a in offsets]
        owner = owner_ref[0]
        tail = total_ref[2 * rows : 2 * rows + DRAFTS, :]
        for k in range(head_count):
            first = (head ^ k) * per_head
            for slot in range(per_head):
                at = slice(slot * DRAFTS, (slot + 1) * DRAFTS)

                offset = here ^ (first + slot)
                block = jnp.int32(0)
                for position, value in enumerate(offsets):
                    block = jnp.where(offset == value, position, block)
                from_block = total_ref[window(block * DRAFTS, DRAFTS), :]
                outs[k][at, :] = jnp.where(owner == first + slot, tail, from_block)


def project(stages, owner, own_rows, got_rows, own, got, gain, weight, head_count):
    lanes, cols = weight.shape
    rows = own_rows.shape[0]
    wide = gain.shape[1] // (gain.shape[1] // 1024)
    gated_at = STATE_SIZE // 16
    half = lanes // 2
    return pl.pallas_call(
        functools.partial(project_kernel, stages, head_count),
        name="project",
        grid=(lanes // wide,),
        out_shape=[shape((2 * rows // head_count, cols), F32)] * head_count,
        in_specs=[
            pl.BlockSpec(memory_space=pltpu.SMEM),
            pl.BlockSpec((rows, wide), lambda g: (0, g)),
            pl.BlockSpec((rows, wide), lambda g: (0, g)),
            pl.BlockSpec((16, half), lambda g: (gated_at, 0)),
            pl.BlockSpec((16, half), lambda g: (gated_at, 0)),
            pl.BlockSpec((1, wide), lambda g: (0, g)),
            pl.BlockSpec((wide, cols), lambda g: (g, 0)),
        ],
        out_specs=[pl.BlockSpec((2 * rows // head_count, cols), lambda g: (0, 0))] * head_count,
        scratch_shapes=[
            pltpu.VMEM((DRAFTS, lanes), F32),
            pltpu.VMEM((2 * rows + 16, wide), BF16),
            pltpu.VMEM((2 * rows + 16, cols), F32),
        ],
        compiler_params=pltpu.CompilerParams(vmem_limit_bytes=32 * 1024 * 1024),
        cost_estimate=pl.CostEstimate(
            flops=2 * (2 * rows + 16) * lanes * cols,
            bytes_accessed=lanes * cols * 2,
            transcendentals=0,
        ),
    )(owner, own_rows, got_rows, own, got, gain, weight)


def states_kernel(
    stages, scattered, owner_ref, resident_ref, own_ref, got_ref, tail_ref, vwrite_ref, new_ref, slice_ref, turned_ref
):
    here = lax.axis_index("seq")
    lanes = resident_ref.shape[0]
    groups = vwrite_ref.shape[1] // STATE_SIZE
    wide = lanes // groups
    half = lanes // 2
    blocks, width = [(0, 0)], half
    for stage in reversed(scattered):
        blocks = [(a[0] | (k * stage[1]), a[1]) for k in range(stage[0]) for a in blocks]
    width = half // len(blocks)
    for k, ref in enumerate((own_ref, got_ref)):
        for position, (offset, _) in enumerate(blocks):
            spot = here ^ (offset | k)
            lane = lax.rem(spot, 2) * half
            size = half
            for factor, stride in scattered:
                size = size // factor
                lane = lane + lax.rem(lax.div(spot, stride), factor) * size
            block = ref[:, position * width : (position + 1) * width]
            turned_ref[window(lane, width), :] = block.astype(F32).T
    per_slice = slice_ref.shape[1] // STATE_SIZE
    heads = slice_ref.shape[0]
    for k in range(per_slice):
        picked = turned_ref[pl.ds(here * per_slice + k, heads, stride=HEAD_DIM), :]
        slice_ref[:, k * STATE_SIZE : (k + 1) * STATE_SIZE] = picked.astype(BF16)
    is_owner = owner_ref[0] == here
    row = lax.broadcasted_iota(jnp.int32, (32, STATE_SIZE), 0)
    ones = jnp.where((row >= 24) & (row < 27), 1.0, 0.0)
    chunk = min(512, wide)
    for at in range(0, lanes, chunk):
        group = at // wide
        writes = vwrite_ref[:, group * STATE_SIZE : (group + 1) * STATE_SIZE].astype(F32)
        writes = jnp.concatenate([writes, writes, writes, jnp.zeros_like(writes)], axis=0)
        right = jnp.concatenate([writes, ones], axis=1).astype(BF16)
        left = tail_ref[:, at : at + chunk].astype(F32).T.astype(BF16)
        both = dot(left, right)
        start = jnp.where(
            is_owner, turned_ref[at : at + chunk, :], resident_ref[at : at + chunk, :].astype(F32)
        )
        new = start * both[:, STATE_SIZE:] + both[:, :STATE_SIZE]
        new_ref[at : at + chunk, :] = new.astype(BF16)


def on_device(
    prefill_input,
    prefill_step,
    write_proj,
    read_proj,
    decay_rate,
    skip_gain,
    resident_state,
    owner_slot,
    draft_ids,
    accepted_len,
    draft_input,
    draft_gate,
    draft_write,
    draft_read,
    draft_step,
    norm_gain,
    out_weight,
):
    span, lanes = prefill_input.shape
    assert span == BLOCK_LEN
    heads = decay_rate.shape[0]
    groups = write_proj.shape[1] // STATE_SIZE
    per_group = heads // groups
    half = lanes // 2
    seq_count, head_count = lax.axis_size("seq"), lax.axis_size("head")
    stages = tree_stages(seq_count)
    core, line, last = stages
    slots = owner_slot.shape[0]
    assert core[0] == 2 and slots == seq_count
    rate, skip, gain = decay_rate[None], skip_gain[None], norm_gain[None]
    resident = resident_state.reshape(lanes, STATE_SIZE)

    opened = call(
        functools.partial(open_kernel, core),
        "open_block",
        [
            shape((UP_ROWS, half), BF16),
            shape((UP_ROWS, half), BF16),
            shape((groups, span, per_group), F32),
            shape((heads, span), F32),
            shape((heads, span), F32),
            shape((span, 2 * heads), BF16),
            shape((DRAFTS, lanes), F32),
            shape((DRAFTS, lanes), F32),
            shape((DRAFTS, groups * STATE_SIZE), BF16),
            shape((DRAFTS, groups * STATE_SIZE), BF16),
            shape((32, lanes), BF16),
        ],
        (
            prefill_step, rate, skip, prefill_input, write_proj, owner_slot, draft_ids, accepted_len,
            draft_input, draft_gate, draft_write, draft_read, draft_step,
        ),
        smem=(5, 6, 7),
        scratch=[pltpu.VMEM((EXTRA, lanes), BF16)],
        flops=2 * span * lanes * STATE_SIZE * 2,
    )
    own, sent, run, runt, stept, reach, q1, q2, vread, vwrite, tail = opened
    core_parts = [own, swap(sent, "seq", core, 1)]

    line_width = half // line[0]
    split_last = line_width % (last[0] * 128) == 0
    last_width = line_width // last[0] if split_last else line_width
    outs = call(
        functools.partial(up_kernel, core, line, 2),
        "up_line",
        [shape((UP_ROWS, line_width), BF16)] * line[0],
        core_parts,
        flops=half * UP_ROWS * 4,
    )
    line_parts = [outs[0]] + [swap(outs[k], "seq", line, k) for k in range(1, line[0])]
    outs = call(
        functools.partial(up_kernel, line, last, line[0]),
        "up_last",
        [shape((UP_ROWS, last_width), BF16)] * (last[0] if split_last else 1),
        line_parts,
        flops=line_width * UP_ROWS * 4,
    )
    last_parts = [outs[0]] + [
        swap(outs[k if split_last else 0], "seq", last, k) for k in range(1, last[0])
    ]
    *outs, prompt = call(
        functools.partial(top_kernel, last, last[0]),
        "top",
        [shape((DOWN_ROWS, last_width), BF16)] * (last[0] if split_last else 1)
        + [shape((STATE_SIZE, last_width), BF16)],
        last_parts,
        flops=last_width * UP_ROWS * 16,
    )

    pieces = [outs[0]] + [swap(out, "seq", last, k) for k, out in enumerate(outs) if k > 0]
    outs = call(
        functools.partial(down_kernel, line, last, len(pieces), line[0]),
        "down_line",
        [shape((DOWN_ROWS, line_width), BF16)] * line[0],
        pieces + line_parts,
        flops=line_width * UP_ROWS * 8,
    )
    pieces = [outs[0]] + [swap(outs[k], "seq", line, k) for k in range(1, line[0])]
    outs = call(
        functools.partial(down_kernel, core, line, line[0], 2),
        "down_core",
        [shape((DOWN_ROWS, half), BF16)] * 2,
        pieces + core_parts,
        flops=half * UP_ROWS * 8,
    )
    entering = [outs[0], swap(outs[1], "seq", core, 1)]

    number = max(1, groups // 2)
    bases = [
        intra(run, runt, stept, skip, prefill_input, write_proj, read_proj, first, number)
        for first in range(0, groups, number)
    ]
    (prefill_out,) = call(
        functools.partial(finish_kernel, core, len(bases)),
        "finish",
        [shape((span, lanes), BF16)],
        (reach, read_proj, *entering, *bases),
        flops=2 * span * lanes * STATE_SIZE,
    )

    scattered = [line, last] if split_last else [line]
    for stage in reversed(scattered):
        parts = [prompt] + [swap(prompt, "seq", stage, k) for k in range(1, stage[0])]
        prompt = jnp.concatenate(parts, axis=1)
    prompts = [prompt, swap(prompt, "seq", core, 1)]
    new_state, state_slice = call(
        functools.partial(states_kernel, stages, scattered),
        "states",
        [
            shape((lanes, STATE_SIZE), BF16),
            shape((heads, HEAD_DIM // seq_count * STATE_SIZE), BF16),
        ],
        (owner_slot, resident, *prompts, tail, vwrite),
        smem=(0,),
        scratch=[pltpu.VMEM((lanes, STATE_SIZE), F32)],
        flops=2 * lanes * STATE_SIZE * 64,
    )

    hidden = resident_hidden(resident, vread, q1, q2, gain)
    for stage in (last, line):
        parts = [hidden] + [swap(hidden, "seq", stage, k) for k in range(1, stage[0])]
        hidden = jnp.concatenate(parts, axis=0)
    shares = project(
        stages, owner_slot, hidden, swap(hidden, "seq", core, 1), *entering, gain, out_weight, head_count
    )
    verify_out = shares[0]
    for k in range(1, head_count):
        verify_out = verify_out + swap(shares[k], "head", (head_count, 1), k)
    return (
        prefill_out,
        new_state.reshape(1, heads, HEAD_DIM, STATE_SIZE),
        verify_out.astype(BF16),
        state_slice,
    )


def solution(mesh):
    return jax.shard_map(
        on_device,
        mesh=mesh,
        in_specs=(
            P("seq", "head"),
            P("seq", "head"),
            P("seq", "head"),
            P("seq", "head"),
            P("head"),
            P("head"),
            P("seq", "head", None, None),
            P(),
            P(),
            P(),
            P("seq", "head"),
            P("seq", "head"),
            P("seq", "head"),
            P("seq", "head"),
            P("seq", "head"),
            P("head"),
            P("head", "seq"),
        ),
        out_specs=(
            P("seq", "head"),
            P("seq", "head", None, None),
            P("head", "seq"),
            P("head", "seq"),
        ),
        check_vma=False,
    )
```

```python
import functools

import jax
import jax.numpy as jnp
from jax import lax
from jax.experimental import pallas as pl
from jax.experimental.pallas import tpu as pltpu
from jax.sharding import PartitionSpec as P

HEAD_DIM = 64
STATE_SIZE = 128
BLOCK_LEN = 256
DRAFTS = 8
EPSILON = 1e-05
EXTRA = 32
UP_ROWS = STATE_SIZE + EXTRA
READ_AT = STATE_SIZE + 16
LOG_AT = STATE_SIZE + 24
DOWN_ROWS = STATE_SIZE + 16

F32 = jnp.float32
BF16 = jnp.bfloat16


def tree_stages(count):
    factors, rest = [], count
    if rest > 1:
        factors.append(2)
        rest //= 2
    inner = 1
    while inner * inner * 4 <= rest:
        inner *= 2
    factors += [inner, rest // inner]
    stages, stride = [], 1
    for factor in factors:
        stages.append((factor, stride))
        stride *= factor
    assert stride == count
    return stages


def swap(value, axis, stage, offset):
    count, stride = lax.axis_size(axis), stage[1]
    return lax.ppermute(value, axis, [(k, k ^ (offset * stride)) for k in range(count)])


def place_of(stage):
    factor, stride = stage
    return lax.rem(lax.div(lax.axis_index("seq"), stride), factor)


def dot(a, b, dims=((1,), (0,))):
    return lax.dot_general(a, b, (dims, ((), ())), preferred_element_type=F32)


def split(value, parts):
    found = []
    for _ in range(parts):
        part = value.astype(BF16).astype(F32)
        found.append(part)
        value = value - part
    return found


def head_mask(rows, heads, lanes, lane0):
    row = lax.broadcasted_iota(jnp.int32, (rows, lanes), 0) & (heads - 1)
    head = lax.shift_right_logical(lax.broadcasted_iota(jnp.int32, (rows, lanes), 1) + lane0, 6)
    return jnp.where(row == head, 1.0, 0.0).astype(BF16)


def window(start, size):
    return pl.ds(pl.multiple_of(start, size), size)


def ordered(kernel, count):
    return lambda *refs: kernel(*refs[count:])


ANYWHERE = pl.BlockSpec(memory_space=pl.ANY)
WHOLE = pl.BlockSpec(memory_space=pltpu.VMEM)
IN_HBM = pl.BlockSpec(memory_space=pltpu.HBM)


def call(
    kernel, name, outs, args, specs=None, out_specs=None, grid=(), after=(), scratch=(), alias=None,
    flops=0, exps=0, moved=None, vmem=32,
):
    if specs is None:
        specs = [WHOLE] * len(args)
    if out_specs is None:
        out_specs = [WHOLE] * len(outs)
    if moved is None:
        moved = sum(a.size * a.dtype.itemsize for a in (*args, *outs))
    first = len(after)
    return pl.pallas_call(
        ordered(kernel, first),
        name=name,
        grid=grid,
        out_shape=outs,
        in_specs=[ANYWHERE] * first + specs,
        out_specs=out_specs,
        scratch_shapes=list(scratch),
        input_output_aliases={first + k: v for k, v in (alias or {}).items()},
        compiler_params=pltpu.CompilerParams(vmem_limit_bytes=vmem * 1024 * 1024),
        cost_estimate=pl.CostEstimate(flops=flops, bytes_accessed=moved, transcendentals=exps),
    )(*after, *args)


def in_hbm(value):
    return pltpu.with_memory_space_constraint(value, pltpu.HBM)


def shape(dims, dtype):
    return jax.ShapeDtypeStruct(dims, dtype)


def open_kernel(stage, count, *refs):
    sources, rest = refs[:count], refs[count:]
    outs, scratch = rest[:13], rest[13:]
    own_ref, sent_ref, run_ref, runt_ref, stept_ref, reach_ref, skip_out = outs[:7]
    q1_ref, q2_ref, vread_ref, vwrite_ref, tail_ref, owner_out = outs[7:]
    extra_ref, sems, held = scratch[0], scratch[1], scratch[2:]
    fetches = [
        pltpu.make_async_copy(source, target, sems.at[k])
        for k, (source, target) in enumerate(zip(sources, held))
    ]
    for fetch in fetches:
        fetch.start()
    for fetch in fetches[:-2]:
        fetch.wait()
    turned_ref, rate_ref, skip_ref, owner_ref, ids_ref, kept_ref = held[:6]
    din_ref, dgate_ref, dwrite_ref, dread_ref, dstep_ref, write_ref, x_ref = held[6:]
    heads, span = turned_ref.shape
    lanes = x_ref.shape[1]
    groups = write_ref.shape[1] // STATE_SIZE
    per_group = heads // groups
    wide = per_group * HEAD_DIM
    here = lax.axis_index("seq")
    place = place_of(stage)
    owner_out[...] = jnp.zeros(owner_out.shape, jnp.int32) + owner_ref[0]

    step_rows = turned_ref[...]
    stept_ref[...] = step_rows
    pad = (-heads) % 128
    if pad:
        step_rows = jnp.concatenate([step_rows, jnp.zeros((pad, span), F32)], axis=0)
    step = step_rows.T[:, :heads]
    log_decay = -step * rate_ref[...]
    lower = lax.broadcasted_iota(jnp.int32, (span, span), 0) >= lax.broadcasted_iota(
        jnp.int32, (span, span), 1
    )
    lower = jnp.where(lower, 1.0, 0.0).astype(BF16)
    running = sum(dot(lower, part.astype(BF16)) for part in split(log_decay, 3))
    total = running[span - 1 : span, :]
    to_end = jnp.exp(total - running) * step
    wide_run = running
    if pad:
        wide_run = jnp.concatenate([running, jnp.zeros((span, pad), F32)], axis=1)
    runt_ref[...] = wide_run.T[:heads]
    for g in range(groups):
        run_ref[g] = running[:, g * per_group : (g + 1) * per_group]
    reach_ref[...] = jnp.concatenate(split(jnp.exp(running), 2), axis=1).astype(BF16)
    end_parts = jnp.concatenate(split(to_end, 2), axis=1).astype(BF16)

    slots = owner_ref.shape[0]
    request = lax.fori_loop(
        0, slots, lambda r, found: jnp.where(owner_ref[r] == here, r, found), jnp.int32(0)
    )
    kept = kept_ref[request]
    candidates = din_ref.shape[0]
    row = lax.broadcasted_iota(jnp.int32, (DRAFTS, candidates), 0)
    col = lax.broadcasted_iota(jnp.int32, (DRAFTS, candidates), 1)
    pick = jnp.zeros((DRAFTS, candidates), F32)
    for i in range(DRAFTS):
        pick = jnp.where((row == i) & (col == ids_ref[i, request]), 1.0, pick)
    pick = pick.astype(BF16)
    vin = dot(pick, din_ref[...])
    vgate = dot(pick, dgate_ref[...])
    vwrite = dot(pick, dwrite_ref[...]).astype(BF16)
    vread = dot(pick, dread_ref[...]).astype(BF16)
    vwrite_ref[...] = vwrite
    vread_ref[...] = vread
    vstep = sum(dot(pick, part.astype(BF16)) for part in split(dstep_ref[...], 3))
    vlog = -vstep * rate_ref[...]
    index = lax.broadcasted_iota(jnp.int32, (DRAFTS, heads), 0)
    acc = jnp.zeros((1, heads), F32)
    vrun = jnp.zeros((DRAFTS, heads), F32)
    reach = jnp.zeros((1, heads), F32)
    for i in range(DRAFTS):
        acc = acc + vlog[i : i + 1]
        vrun = jnp.where(index == i, acc, vrun)
        reach = jnp.where(i < kept, acc, reach)
    others = jnp.where(index == 0, total, jnp.where(index == 1, skip_ref[...], reach))
    stacked = split(jnp.concatenate([vrun, vstep, others], axis=0), 3)
    stacked = jnp.concatenate(stacked, axis=0).astype(BF16)
    row = lax.broadcasted_iota(jnp.int32, (DRAFTS, wide), 0)
    is_owner = owner_ref[0] == here
    for g in range(groups):
        at = slice(g * wide, (g + 1) * wide)
        spread = dot(stacked, head_mask(heads, heads, wide, g * wide))
        spread = spread[0:24] + spread[24:48] + spread[48:72]
        vrun_l, vstep_l = spread[0:8], spread[8:16]
        total_l, skip_l, reach_l = spread[16:17], spread[17:18], spread[18:19]
        skip_out[:, at] = skip_l
        vin_g = vin[:, at]
        vr = vread[:, g * STATE_SIZE : (g + 1) * STATE_SIZE]
        vw = vwrite[:, g * STATE_SIZE : (g + 1) * STATE_SIZE]
        scores = dot(vr, vw, ((1,), (1,)))
        direct = skip_l * vin_g
        for j in range(DRAFTS):
            decay = jnp.exp(jnp.where(row >= j, vrun_l - vrun_l[j : j + 1], -jnp.inf))
            direct = direct + decay * scores[:, j : j + 1] * (vstep_l[j : j + 1] * vin_g[j : j + 1])
        gate = vgate[:, at]
        gate = gate / (1.0 + jnp.exp(-gate))
        q1 = direct * gate
        q2 = jnp.exp(vrun_l) * gate
        q1_ref[:, at] = q1
        q2_ref[:, at] = q2
        live = jnp.exp(jnp.where(row < kept, reach_l - vrun_l, -jnp.inf)) * vstep_l * vin_g
        keep_l = jnp.concatenate(
            split(jnp.exp(reach_l), 3) + [jnp.zeros((5, wide), F32)], axis=0
        )
        tail_ref[:, at] = jnp.concatenate(split(live, 3) + [keep_l], axis=0).astype(BF16)
        read_l = jnp.concatenate([vr.astype(F32)] * (wide // STATE_SIZE), axis=1)
        mine = jnp.concatenate([q1, q2, read_l], axis=0)
        mine = jnp.where(is_owner, mine, 0.0)
        logs = jnp.concatenate(split(total_l, 3) + [jnp.zeros((5, wide), F32)], axis=0)
        extra_ref[:, at] = jnp.concatenate([mine, logs], axis=0).astype(BF16)

    for fetch in fetches[-2:]:
        fetch.wait()
    half = lanes // 2
    chunk = min(wide, half)
    for k, out_ref in ((1, sent_ref), (0, own_ref)):
        start = (place ^ k) * half
        out_ref[STATE_SIZE:, :] = extra_ref[:, window(start, half)]
        for at in range(0, half, chunk):
            lane0 = start + at
            group = lax.div(lane0, wide)
            scale = dot(end_parts, head_mask(2 * heads, heads, chunk, lane0))
            weighted = (x_ref[:, window(lane0, chunk)].astype(F32) * scale).astype(BF16)
            writes = write_ref[:, window(group * STATE_SIZE, STATE_SIZE)]
            writes = writes.astype(F32).T.astype(BF16)
            out_ref[:STATE_SIZE, at : at + chunk] = dot(writes, weighted).astype(BF16)


def logs_of(block):
    return block[0:1].astype(F32) + block[1:2].astype(F32) + block[2:3].astype(F32)


def weights_of(logs, place, target):
    spots = [place ^ k for k in range(len(logs))]
    found = []
    for k, spot in enumerate(spots):
        between = jnp.zeros_like(logs[0])
        for other, log in zip(spots, logs):
            if other is not spot:
                between = between + jnp.where((spot < other) & (other < target), log, 0.0)
        found.append(jnp.where(spot < target, jnp.exp(between), 0.0))
    return found


def carry_of(logs, place, target):
    ahead = jnp.zeros_like(logs[0])
    for k, log in enumerate(logs):
        ahead = ahead + jnp.where((place ^ k) < target, log, 0.0)
    return jnp.exp(ahead)


def up_kernel(stage, following, count, *refs):
    parts, outs = refs[:count], refs[count:]
    place, target = place_of(stage), place_of(following)
    width = outs[0].shape[1]
    chunk = min(256, width)
    order = list(range(1, len(outs))) + [0]
    for k in order:
        for at in range(0, width, chunk):
            start = at if len(outs) == 1 else (target ^ k) * width + at
            at_in = window(start, chunk)
            logs = [logs_of(part[LOG_AT:UP_ROWS, at_in]) for part in parts]
            scale = weights_of(logs, place, count)
            state = sum(
                w * part[:STATE_SIZE, at_in].astype(F32) for w, part in zip(scale, parts)
            )
            outs[k][:STATE_SIZE, at : at + chunk] = state.astype(BF16)
            mine = sum(part[STATE_SIZE:UP_ROWS, at_in].astype(F32) for part in parts)
            total = jnp.concatenate(
                split(sum(logs), 3) + [jnp.zeros((5, chunk), F32)], axis=0
            )
            outs[k][STATE_SIZE:, at : at + chunk] = jnp.concatenate(
                [mine[:24], total], axis=0
            ).astype(BF16)


def top_kernel(stage, count, *refs):
    parts, outs, prompt_ref = refs[:count], refs[count:-1], refs[-1]
    place = place_of(stage)
    width = prompt_ref.shape[1]
    logs = [logs_of(part[LOG_AT:UP_ROWS, :]) for part in parts]
    states = [part[:STATE_SIZE, :].astype(F32) for part in parts]
    final = sum(w * s for w, s in zip(weights_of(logs, place, count), states)).astype(BF16)
    prompt_ref[...] = final
    mine = sum(part[STATE_SIZE:LOG_AT, :].astype(F32) for part in parts)
    reads = mine[16:24, :STATE_SIZE].astype(BF16)
    gated = mine[0:8] + mine[8:16] * dot(reads, final)
    gated = jnp.concatenate(split(gated, 2), axis=0).astype(BF16)
    for k in list(range(1, len(outs))) + [0]:
        scale = weights_of(logs, place, place ^ k)
        outs[k][:STATE_SIZE, :] = sum(w * s for w, s in zip(scale, states)).astype(BF16)
        outs[k][STATE_SIZE:, :] = gated


def down_kernel(stage, above, above_count, count, handed, *refs):
    pieces, parts = refs[:above_count], refs[above_count : above_count + count]
    outs = refs[above_count + count :]
    if handed:
        outs[-1][...] = outs[0][...]
        outs = outs[1:-1]
    place, source = place_of(stage), place_of(above)
    width = pieces[0].shape[1]
    chunk = min(256, width)
    for k in list(range(1, len(outs))) + [0]:
        for piece in range(above_count):
            for at in range(0, width, chunk):
                start = at if above_count == 1 else (source ^ piece) * width + at
                at_out = window(start, chunk)
                block = pieces[piece][:, at : at + chunk]
                logs = [logs_of(part[LOG_AT:UP_ROWS, at_out]) for part in parts]
                state = carry_of(logs, place, place ^ k) * block[:STATE_SIZE].astype(F32)
                for w, part in zip(weights_of(logs, place, place ^ k), parts):
                    state = state + w * part[:STATE_SIZE, at_out].astype(F32)
                outs[k][:STATE_SIZE, at_out] = state.astype(BF16)
                outs[k][STATE_SIZE:, at_out] = block[STATE_SIZE:]


def intra_kernel(run_ref, runt_ref, stept_ref, skip_ref, x_ref, write_ref, read_ref, *refs):
    out_ref = refs[-1]
    span = x_ref.shape[0]
    heads = runt_ref.shape[0]
    mid = span // 2
    scores = dot(read_ref[...], write_ref[...], ((1,), (1,)))
    row = lax.broadcasted_iota(jnp.int32, (mid, mid), 0)
    causal = row >= lax.broadcasted_iota(jnp.int32, (mid, mid), 1)
    running = run_ref[0]
    low, high = slice(0, mid), slice(mid, span)
    for pair in range(heads // 2):
        found = []
        for h in (2 * pair, 2 * pair + 1):
            x = x_ref[:, h * HEAD_DIM : (h + 1) * HEAD_DIM]
            t_run, j_run = running[:, h : h + 1], runt_ref[h : h + 1, :]
            step = stept_ref[h : h + 1, :]

            def mixed(rows, cols, masked):
                gap = t_run[rows] - j_run[:, cols]
                if masked:
                    gap = jnp.where(causal, gap, -jnp.inf)
                return (scores[rows, cols] * jnp.exp(gap) * step[:, cols]).astype(BF16)

            top = dot(mixed(low, low, True), x[low])
            bottom = dot(mixed(high, low, False), x[low]) + dot(mixed(high, high, True), x[high])
            found.append(jnp.concatenate([top, bottom], axis=0))
        at = slice(pair * 2 * HEAD_DIM, (pair + 1) * 2 * HEAD_DIM)
        both = jnp.concatenate(found, axis=1)
        out_ref[:, at] = both + skip_ref[:, at] * x_ref[:, at].astype(F32)


def intra(run, runt, stept, skip, x, write, read, first, number, base, after):
    span, lanes = x.shape
    groups, _, per_group = run.shape
    wide = per_group * HEAD_DIM
    args = [run, runt, stept, skip, x, write, read]
    specs = [
        pl.BlockSpec((1, span, per_group), lambda g: (g + first, 0, 0)),
        pl.BlockSpec((per_group, span), lambda g: (g + first, 0)),
        pl.BlockSpec((per_group, span), lambda g: (g + first, 0)),
        pl.BlockSpec((1, wide), lambda g: (0, g + first)),
        pl.BlockSpec((span, wide), lambda g: (0, g + first)),
        pl.BlockSpec((span, STATE_SIZE), lambda g: (0, g + first)),
        pl.BlockSpec((span, STATE_SIZE), lambda g: (0, g + first)),
    ]
    alias = {}
    if base is not None:
        alias = {len(args): 0}
        args.append(base)
        specs.append(ANYWHERE)
    (base,) = call(
        intra_kernel,
        "intra",
        [shape((span, lanes), F32)],
        args,
        specs=specs,
        out_specs=[pl.BlockSpec((span, wide), lambda g: (0, g + first))],
        grid=(number,),
        after=after,
        alias=alias,
        flops=number * per_group * span * span * HEAD_DIM * 2,
        moved=number * wide * span * 6,
        exps=number * per_group * span * span * 3 // 4,
    )
    return base


def finish_kernel(stage, chunks, reach_ref, read_ref, own_ref, got_ref, base_ref, out_ref):
    place = place_of(stage)
    step = pl.program_id(0)
    heads = reach_ref.shape[1] // 2
    chunk = out_ref.shape[1]
    mine = place == lax.div(step, chunks // 2)
    entering = jnp.where(mine, own_ref[:STATE_SIZE, :], got_ref[:STATE_SIZE, :])
    inter = dot(read_ref[...], entering)
    inter = inter * dot(reach_ref[...], head_mask(2 * heads, heads, chunk, step * chunk))
    out_ref[...] = (inter + base_ref[...]).astype(BF16)


def finish(stage, reach, read, own, got, base, after=()):
    span, lanes = base.shape
    wide = lanes // (read.shape[1] // STATE_SIZE)
    half = lanes // 2
    chunk = min(512, half)
    chunks, halves = lanes // chunk, half // chunk
    entering = pl.BlockSpec((DOWN_ROWS, chunk), lambda c: (0, lax.rem(c, halves)))
    return call(
        functools.partial(finish_kernel, stage, chunks),
        "finish",
        [shape((span, lanes), BF16)],
        (reach, read, own, got, base),
        specs=[
            pl.BlockSpec(reach.shape, lambda c: (0, 0)),
            pl.BlockSpec((span, STATE_SIZE), lambda c: (0, lax.div(c * chunk, wide))),
            entering,
            entering,
            pl.BlockSpec((span, chunk), lambda c: (0, c)),
        ],
        out_specs=[pl.BlockSpec((span, chunk), lambda c: (0, c))],
        grid=(chunks,),
        after=after,
        flops=2 * span * lanes * STATE_SIZE,
    )[0]


def resident_kernel(state_ref, vread_ref, q1_ref, q2_ref, gain_ref, out_ref):
    drawn = dot(vread_ref[...], state_ref[...], ((1,), (1,)))
    gated = q1_ref[...] + q2_ref[...] * drawn
    out_ref[...] = normed(gated, gain_ref[...]).astype(BF16)


def normed(gated, gain):
    mean_square = jnp.mean(gated * gated, axis=1, keepdims=True)
    return gated * lax.rsqrt(mean_square + EPSILON) * gain


def resident_hidden(state, vread, q1, q2, gain, after):
    lanes = state.shape[0]
    groups = vread.shape[1] // STATE_SIZE
    wide = lanes // groups
    rows = pl.BlockSpec((DRAFTS, wide), lambda g: (0, g))
    return call(
        resident_kernel,
        "resident_hidden",
        [shape((DRAFTS, lanes), BF16)],
        (state, vread, q1, q2, gain),
        specs=[
            pl.BlockSpec((wide, STATE_SIZE), lambda g: (g, 0)),
            pl.BlockSpec((DRAFTS, STATE_SIZE), lambda g: (0, g)),
            rows,
            rows,
            pl.BlockSpec((1, wide), lambda g: (0, g)),
        ],
        out_specs=[rows],
        grid=(groups,),
        after=after,
        flops=2 * DRAFTS * lanes * STATE_SIZE,
    )[0]


def join_kernel(axis, *refs):
    out_ref = refs[-1]
    for k, ref in enumerate(refs[:-1]):
        size = ref.shape[axis]
        at = slice(k * size, (k + 1) * size)
        if axis == 0:
            out_ref[at, :] = ref[...]
        else:
            out_ref[:, at] = ref[...]


def join(parts, axis, after=()):
    dims = list(parts[0].shape)
    dims[axis] *= len(parts)
    return call(
        functools.partial(join_kernel, axis), "join", [shape(tuple(dims), parts[0].dtype)], parts, after=after
    )[0]


def project_kernel(stages, head_count, *refs):
    owner_ref, own_rows, got_rows, own_ref, got_ref, gain_ref, weight_ref = refs[:7]
    outs = refs[7 : 7 + head_count]
    gated_ref, left_ref, total_ref = refs[7 + head_count :]
    here, head = lax.axis_index("seq"), lax.axis_index("head")
    place = place_of(stages[0])
    half = own_ref.shape[1]
    lanes = weight_ref.shape[0]
    wide = min(1024, lanes)
    rows = own_rows.shape[0]
    for k, ref in enumerate((own_ref, got_ref)):
        both = ref[STATE_SIZE:, :].astype(F32)
        gated_ref[:, window((place ^ k) * half, half)] = both[0:8] + both[8:16]
    left_ref[0:rows, :] = own_rows[...]
    left_ref[rows : 2 * rows, :] = got_rows[...]
    for lane0 in range(0, lanes, wide):
        at = slice(lane0, lane0 + wide)
        hidden = normed(gated_ref[:, at], gain_ref[:, at])
        hidden = jnp.concatenate([hidden, jnp.zeros_like(hidden)], axis=0)
        left_ref[2 * rows :, at] = hidden.astype(BF16)
    total_ref[...] = dot(left_ref[...], weight_ref[...])

    slots = 2 * rows // DRAFTS
    per_head = slots // head_count
    offsets = [0]
    for factor, stride in reversed(stages):
        offsets = [a + k * stride for k in range(factor) for a in offsets]
    owner = owner_ref[...]
    tail = total_ref[2 * rows : 2 * rows + DRAFTS, :]
    for k in list(range(1, head_count)) + [0]:
        first = (head ^ k) * per_head
        for slot in range(per_head):
            at = slice(slot * DRAFTS, (slot + 1) * DRAFTS)
            offset = here ^ (first + slot)
            block = jnp.int32(0)
            for position, value in enumerate(offsets):
                block = jnp.where(offset == value, position, block)
            from_block = total_ref[window(block * DRAFTS, DRAFTS), :]
            outs[k][at, :] = jnp.where(owner == first + slot, tail, from_block)


def project(stages, owner, own_rows, got_rows, own, got, gain, weight, head_count):
    lanes, cols = weight.shape
    rows = own_rows.shape[0]
    return call(
        functools.partial(project_kernel, stages, head_count),
        "project",
        [shape((2 * rows // head_count, cols), F32)] * head_count,
        (owner, own_rows, got_rows, own, got, gain, weight),

        scratch=[
            pltpu.VMEM((DRAFTS, lanes), F32),
            pltpu.VMEM((2 * rows + 16, lanes), BF16),
            pltpu.VMEM((2 * rows + 16, cols), F32),
        ],
        flops=2 * (2 * rows + 16) * lanes * cols,
    )


def states_kernel(stages, scattered, shares, *refs):
    owner_ref, resident_ref, own_ref, got_ref, tail_ref, vwrite_ref = refs[:6]
    share_refs = refs[6 : 6 + shares]
    new_ref, slice_ref, verify_ref, turned_ref = refs[6 + shares :]
    here, step = lax.axis_index("seq"), pl.program_id(0)

    @pl.when(step == 0)
    def _():
        verify_ref[...] = sum(ref[...] for ref in share_refs).astype(BF16)

    chunk = resident_ref.shape[0]
    half = own_ref.shape[1]
    blocks = [0]
    for factor, stride in reversed(scattered):
        blocks = [a | (k * stride) for k in range(factor) for a in blocks]
    width = half // len(blocks)
    for at in range(0, chunk, width):
        lane = step * chunk + at
        spot, size = lax.div(lane, half), half
        rest = lax.rem(lane, half)
        for factor, stride in scattered:
            size = size // factor
            spot = spot | (lax.div(rest, size) * stride)
            rest = lax.rem(rest, size)
        offset = spot ^ here
        position = jnp.int32(0)
        for place, value in enumerate(blocks):
            position = jnp.where((offset & sum_of(scattered)) == value, place, position)
        found = jnp.where(
            lax.rem(offset, 2) == 0,
            own_ref[:, window(position * width, width)],
            got_ref[:, window(position * width, width)],
        )
        turned_ref[at : at + width, :] = found.astype(F32).T
    per_slice = slice_ref.shape[1] // STATE_SIZE
    heads = slice_ref.shape[0]
    for k in range(per_slice):
        picked = turned_ref[pl.ds(here * per_slice + k, heads, stride=HEAD_DIM), :]
        slice_ref[:, k * STATE_SIZE : (k + 1) * STATE_SIZE] = picked.astype(BF16)
    is_owner = owner_ref[0:1, :STATE_SIZE] == here
    row = lax.broadcasted_iota(jnp.int32, (32, STATE_SIZE), 0)
    ones = jnp.where((row >= 24) & (row < 27), 1.0, 0.0)
    writes = vwrite_ref[...].astype(F32)
    writes = jnp.concatenate([writes, writes, writes, jnp.zeros_like(writes)], axis=0)
    right = jnp.concatenate([writes, ones], axis=1).astype(BF16)
    left = tail_ref[...].astype(F32).T.astype(BF16)
    both = dot(left, right)
    start = jnp.where(is_owner, turned_ref[...], resident_ref[...].astype(F32))
    new_ref[...] = (start * both[:, STATE_SIZE:] + both[:, :STATE_SIZE]).astype(BF16)


def sum_of(stages):
    return sum((factor - 1) * stride for factor, stride in stages)


def states(stages, scattered, owner, resident, own, got, tail, vwrite, shares, seq_count):
    lanes = resident.shape[0]
    wide = lanes // (vwrite.shape[1] // STATE_SIZE)
    chunk = min(512, wide)
    heads = lanes // HEAD_DIM
    rows, cols = shares[0].shape
    fixed = pl.BlockSpec((rows, cols), lambda c: (0, 0))
    return call(
        functools.partial(states_kernel, stages, scattered, len(shares)),
        "states",
        [
            shape((lanes, STATE_SIZE), BF16),
            shape((heads, HEAD_DIM // seq_count * STATE_SIZE), BF16),
            shape((rows, cols), BF16),
        ],
        (owner, resident, own, got, tail, vwrite, *shares),
        specs=[
            WHOLE,
            pl.BlockSpec((chunk, STATE_SIZE), lambda c: (c, 0)),
            WHOLE,
            WHOLE,
            pl.BlockSpec((32, chunk), lambda c: (0, c)),
            pl.BlockSpec((DRAFTS, STATE_SIZE), lambda c: (0, lax.div(c * chunk, wide))),
        ]
        + [WHOLE] * len(shares),
        out_specs=[
            pl.BlockSpec((chunk, STATE_SIZE), lambda c: (c, 0)),
            pl.BlockSpec((chunk // HEAD_DIM, HEAD_DIM // seq_count * STATE_SIZE), lambda c: (c, 0)),
            fixed,
        ],
        grid=(lanes // chunk,),
        scratch=[pltpu.VMEM((chunk, STATE_SIZE), F32)],
        flops=2 * lanes * STATE_SIZE * 64,
    )


def on_device(
    prefill_input,
    prefill_step,
    write_proj,
    read_proj,
    decay_rate,
    skip_gain,
    resident_state,
    owner_slot,
    draft_ids,
    accepted_len,
    draft_input,
    draft_gate,
    draft_write,
    draft_read,
    draft_step,
    norm_gain,
    out_weight,
):
    span, lanes = prefill_input.shape
    assert span == BLOCK_LEN
    heads = decay_rate.shape[0]
    groups = write_proj.shape[1] // STATE_SIZE
    per_group = heads // groups
    half = lanes // 2
    seq_count, head_count = lax.axis_size("seq"), lax.axis_size("head")
    stages = tree_stages(seq_count)
    core, line, last = stages
    slots = owner_slot.shape[0]
    assert core[0] == 2 and slots == seq_count
    rate, skip, gain = decay_rate[None], skip_gain[None], norm_gain[None]
    resident = resident_state.reshape(lanes, STATE_SIZE)

    inputs = (
        prefill_step.T, rate, skip, owner_slot, draft_ids.T, accepted_len, draft_input, draft_gate,
        draft_write, draft_read, draft_step, write_proj, prefill_input,
    )
    inputs = [in_hbm(value) for value in inputs]
    opened = call(
        functools.partial(open_kernel, core, len(inputs)),
        "open_block",
        [
            shape((UP_ROWS, half), BF16),
            shape((UP_ROWS, half), BF16),
            shape((groups, span, per_group), F32),
            shape((heads, span), F32),
            shape((heads, span), F32),
            shape((span, 2 * heads), BF16),
            shape((1, lanes), F32),
            shape((DRAFTS, lanes), F32),
            shape((DRAFTS, lanes), F32),
            shape((DRAFTS, groups * STATE_SIZE), BF16),
            shape((DRAFTS, groups * STATE_SIZE), BF16),
            shape((32, lanes), BF16),
            shape((DRAFTS, out_weight.shape[1]), jnp.int32),
        ],
        inputs,
        specs=[IN_HBM] * len(inputs),
        scratch=[pltpu.VMEM((EXTRA, lanes), BF16), pltpu.SemaphoreType.DMA((len(inputs),))]
        + [
            (pltpu.SMEM if value.dtype == jnp.int32 else pltpu.VMEM)(value.shape, value.dtype)
            for value in inputs
        ],
        flops=2 * span * lanes * STATE_SIZE * 2,
    )
    prefill_input, write_proj, read_proj, resident, gain = (
        in_hbm(value) for value in (prefill_input, write_proj, read_proj, resident, gain)
    )
    own, sent, run, runt, stept, reach, skip_lanes, q1, q2, vread, vwrite, tail, owner = opened
    core_parts = [own, swap(sent, "seq", core, 1)]

    number = max(1, groups // 4)
    firsts = list(range(0, groups, number))
    base = None

    def fill(after):
        nonlocal base
        if firsts:
            base = intra(
                run, runt, stept, skip_lanes, prefill_input, write_proj, read_proj, firsts.pop(0), number,
                base, after,
            )
        return [base]

    def exchange(parts, stage):
        got = {k: swap(parts[k], "seq", stage, k) for k in range(stage[0] - 1, 0, -1)}
        return [parts[0]] + [got[k] for k in range(1, stage[0])]

    line_width = half // line[0]
    split_last = line_width % (last[0] * 128) == 0
    last_width = line_width // last[0] if split_last else line_width
    outs = call(
        functools.partial(up_kernel, core, line, 2),
        "up_line",
        [shape((UP_ROWS, line_width), BF16)] * line[0],
        core_parts,
        flops=half * UP_ROWS * 4,
    )
    line_parts = exchange(outs, line)
    hidden = resident_hidden(resident, vread, q1, q2, gain, [outs[-1]])
    hidden = join(exchange([hidden] * last[0], last), 0)
    outs = call(
        functools.partial(up_kernel, line, last, line[0]),
        "up_last",
        [shape((UP_ROWS, last_width), BF16)] * (last[0] if split_last else 1),
        line_parts,
        after=[hidden],
        flops=line_width * UP_ROWS * 4,
    )
    last_parts = exchange(outs if split_last else outs * last[0], last)
    hiddens = exchange([hidden] * line[0], line)
    fill([outs[-1]])
    filled = fill([])
    *outs, prompt = call(
        functools.partial(top_kernel, last, last[0]),
        "top",
        [shape((DOWN_ROWS, last_width), BF16)] * (last[0] if split_last else 1)
        + [shape((STATE_SIZE, last_width), BF16)],
        last_parts,
        after=filled,
        flops=last_width * UP_ROWS * 16,
    )

    pieces = exchange(outs, last) if split_last else outs
    filled = fill([outs[-1]])
    hidden = join(hiddens, 0)
    *outs, prompt = call(
        functools.partial(down_kernel, line, last, len(pieces), line[0], True),
        "down_line",
        [shape((DOWN_ROWS, line_width), BF16)] * line[0] + [shape(prompt.shape, BF16)],
        [*pieces, *line_parts, prompt],
        after=[*filled, hidden],
        flops=line_width * UP_ROWS * 8,
    )
    pieces = exchange(outs, line)
    filled = fill([outs[-1]])
    scattered = [line, last] if split_last else [line]
    if split_last:
        prompts = exchange([prompt] * last[0], last)
    outs = call(
        functools.partial(down_kernel, core, line, line[0], 2, False),
        "down_core",
        [shape((DOWN_ROWS, half), BF16)] * 2,
        pieces + core_parts,
        after=filled,
        flops=half * UP_ROWS * 8,
    )
    if split_last:
        prompt = join(prompts, 1, [outs[-1]])
    entering = exchange(outs, core)
    while firsts:
        fill([])
    prefill_out = finish(core, reach, read_proj, *entering, base)

    shares = project(
        stages, owner, hidden, swap(hidden, "seq", core, 1), *entering, norm_gain[None], out_weight, head_count
    )
    shares = [shares[0]] + [swap(shares[k], "head", (head_count, 1), k) for k in range(1, head_count)]

    prompt = join(exchange([prompt] * line[0], line), 1)
    prompts = exchange([prompt] * 2, core)
    new_state, state_slice, verify_out = states(
        stages, scattered, owner, resident, *prompts, tail, vwrite, shares, seq_count
    )
    return (
        prefill_out,
        new_state.reshape(1, heads, HEAD_DIM, STATE_SIZE),
        verify_out,
        state_slice,
    )


def solution(mesh):
    return jax.shard_map(
        on_device,
        mesh=mesh,
        in_specs=(
            P("seq", "head"),
            P("seq", "head"),
            P("seq", "head"),
            P("seq", "head"),
            P("head"),
            P("head"),
            P("seq", "head", None, None),
            P(),
            P(),
            P(),
            P("seq", "head"),
            P("seq", "head"),
            P("seq", "head"),
            P("seq", "head"),
            P("seq", "head"),
            P("head"),
            P("head", "seq"),
        ),
        out_specs=(
            P("seq", "head"),
            P("seq", "head", None, None),
            P("head", "seq"),
            P("head", "seq"),
        ),
        check_vma=False,
    )
```

```python
import functools

import jax
import jax.numpy as jnp
from jax import lax
from jax.experimental import pallas as pl
from jax.experimental.pallas import tpu as pltpu
from jax.sharding import PartitionSpec as P

HEAD_DIM = 64
STATE_SIZE = 128
BLOCK_LEN = 256
DRAFTS = 8
EPSILON = 1e-05
EXTRA = 32
UP_ROWS = STATE_SIZE + EXTRA
READ_AT = STATE_SIZE + 16
LOG_AT = STATE_SIZE + 24
DOWN_ROWS = STATE_SIZE + 16

F32 = jnp.float32
BF16 = jnp.bfloat16


def tree_stages(count):
    factors, rest = [], count
    if rest > 1:
        factors.append(2)
        rest //= 2
    inner = 1
    while inner * inner * 4 <= rest:
        inner *= 2
    factors += [inner, rest // inner]
    stages, stride = [], 1
    for factor in factors:
        stages.append((factor, stride))
        stride *= factor
    assert stride == count
    return stages


def swap(value, axis, stage, offset):
    count, stride = lax.axis_size(axis), stage[1]
    return lax.ppermute(value, axis, [(k, k ^ (offset * stride)) for k in range(count)])


def place_of(stage):
    factor, stride = stage
    return lax.rem(lax.div(lax.axis_index("seq"), stride), factor)


def dot(a, b, dims=((1,), (0,))):
    return lax.dot_general(a, b, (dims, ((), ())), preferred_element_type=F32)


def split(value, parts):
    found = []
    for _ in range(parts):
        part = value.astype(BF16).astype(F32)
        found.append(part)
        value = value - part
    return found


def head_mask(rows, heads, lanes, lane0):
    row = lax.broadcasted_iota(jnp.int32, (rows, lanes), 0) & (heads - 1)
    head = lax.shift_right_logical(lax.broadcasted_iota(jnp.int32, (rows, lanes), 1) + lane0, 6)
    return jnp.where(row == head, 1.0, 0.0).astype(BF16)


def window(start, size):
    return pl.ds(pl.multiple_of(start, size), size)


def ordered(kernel, count):
    return lambda *refs: kernel(*refs[count:])


ANYWHERE = pl.BlockSpec(memory_space=pl.ANY)
WHOLE = pl.BlockSpec(memory_space=pltpu.VMEM)
IN_HBM = pl.BlockSpec(memory_space=pltpu.HBM)


def call(
    kernel, name, outs, args, specs=None, out_specs=None, grid=(), after=(), scratch=(), alias=None,
    flops=0, exps=0, moved=None, vmem=32,
):
    if specs is None:
        specs = [WHOLE] * len(args)
    if out_specs is None:
        out_specs = [WHOLE] * len(outs)
    if moved is None:
        moved = sum(a.size * a.dtype.itemsize for a in (*args, *outs))
    first = len(after)
    return pl.pallas_call(
        ordered(kernel, first),
        name=name,
        grid=grid,
        out_shape=outs,
        in_specs=[ANYWHERE] * first + specs,
        out_specs=out_specs,
        scratch_shapes=list(scratch),
        input_output_aliases={first + k: v for k, v in (alias or {}).items()},
        compiler_params=pltpu.CompilerParams(vmem_limit_bytes=vmem * 1024 * 1024),
        cost_estimate=pl.CostEstimate(flops=flops, bytes_accessed=moved, transcendentals=exps),
    )(*after, *args)


def in_hbm(value):
    return pltpu.with_memory_space_constraint(value, pltpu.HBM)


def shape(dims, dtype):
    return jax.ShapeDtypeStruct(dims, dtype)


def open_kernel(stage, count, passed, *refs):
    sources, rest = refs[:count], refs[count:]
    outs, scratch = rest[: 13 + passed], rest[13 + passed :]
    outs, later = outs[:13], list(outs[13:])
    own_ref, sent_ref, run_ref, runt_ref, stept_ref, reach_ref, skip_out = outs[:7]
    q1_ref, q2_ref, vread_ref, vwrite_ref, tail_ref, owner_out = outs[7:]
    extra_ref, sems, held = scratch[0], scratch[1], [*scratch[2:], *later]
    fetches = [
        pltpu.make_async_copy(source, target, sems.at[k])
        for k, (source, target) in enumerate(zip(sources, held))
    ]
    for fetch in fetches:
        fetch.start()
    early = count - passed
    for fetch in fetches[:early]:
        fetch.wait()
    turned_ref, rate_ref, skip_ref, owner_ref, ids_ref, kept_ref = held[:6]
    din_ref, dgate_ref, dwrite_ref, dread_ref, dstep_ref, write_ref, x_ref = held[6:13]
    heads, span = turned_ref.shape
    lanes = x_ref.shape[1]
    groups = write_ref.shape[1] // STATE_SIZE
    per_group = heads // groups
    wide = per_group * HEAD_DIM
    here = lax.axis_index("seq")
    place = place_of(stage)
    owner_out[...] = jnp.zeros(owner_out.shape, jnp.int32) + owner_ref[0]

    step_rows = turned_ref[...]
    stept_ref[...] = step_rows
    pad = (-heads) % 128
    if pad:
        step_rows = jnp.concatenate([step_rows, jnp.zeros((pad, span), F32)], axis=0)
    step = step_rows.T[:, :heads]
    log_decay = -step * rate_ref[...]
    lower = lax.broadcasted_iota(jnp.int32, (span, span), 0) >= lax.broadcasted_iota(
        jnp.int32, (span, span), 1
    )
    lower = jnp.where(lower, 1.0, 0.0).astype(BF16)
    running = sum(dot(lower, part.astype(BF16)) for part in split(log_decay, 3))
    total = running[span - 1 : span, :]
    to_end = jnp.exp(total - running) * step
    wide_run = running
    if pad:
        wide_run = jnp.concatenate([running, jnp.zeros((span, pad), F32)], axis=1)
    runt_ref[...] = wide_run.T[:heads]
    for g in range(groups):
        run_ref[g] = running[:, g * per_group : (g + 1) * per_group]
    reach_ref[...] = jnp.concatenate(split(jnp.exp(running), 2), axis=1).astype(BF16)
    end_parts = jnp.concatenate(split(to_end, 2), axis=1).astype(BF16)

    slots = owner_ref.shape[0]
    request = lax.fori_loop(
        0, slots, lambda r, found: jnp.where(owner_ref[r] == here, r, found), jnp.int32(0)
    )
    kept = kept_ref[request]
    candidates = din_ref.shape[0]
    row = lax.broadcasted_iota(jnp.int32, (DRAFTS, candidates), 0)
    col = lax.broadcasted_iota(jnp.int32, (DRAFTS, candidates), 1)
    pick = jnp.zeros((DRAFTS, candidates), F32)
    for i in range(DRAFTS):
        pick = jnp.where((row == i) & (col == ids_ref[i, request]), 1.0, pick)
    pick = pick.astype(BF16)
    vin = dot(pick, din_ref[...])
    vgate = dot(pick, dgate_ref[...])
    vwrite = dot(pick, dwrite_ref[...]).astype(BF16)
    vread = dot(pick, dread_ref[...]).astype(BF16)
    vwrite_ref[...] = vwrite
    vread_ref[...] = vread
    vstep = sum(dot(pick, part.astype(BF16)) for part in split(dstep_ref[...], 3))
    vlog = -vstep * rate_ref[...]
    index = lax.broadcasted_iota(jnp.int32, (DRAFTS, heads), 0)
    acc = jnp.zeros((1, heads), F32)
    vrun = jnp.zeros((DRAFTS, heads), F32)
    reach = jnp.zeros((1, heads), F32)
    for i in range(DRAFTS):
        acc = acc + vlog[i : i + 1]
        vrun = jnp.where(index == i, acc, vrun)
        reach = jnp.where(i < kept, acc, reach)
    others = jnp.where(index == 0, total, jnp.where(index == 1, skip_ref[...], reach))
    stacked = split(jnp.concatenate([vrun, vstep, others], axis=0), 3)
    stacked = jnp.concatenate(stacked, axis=0).astype(BF16)
    row = lax.broadcasted_iota(jnp.int32, (DRAFTS, wide), 0)
    is_owner = owner_ref[0] == here
    for g in range(groups):
        at = slice(g * wide, (g + 1) * wide)
        spread = dot(stacked, head_mask(heads, heads, wide, g * wide))
        spread = spread[0:24] + spread[24:48] + spread[48:72]
        vrun_l, vstep_l = spread[0:8], spread[8:16]
        total_l, skip_l, reach_l = spread[16:17], spread[17:18], spread[18:19]
        skip_out[:, at] = skip_l
        vin_g = vin[:, at]
        vr = vread[:, g * STATE_SIZE : (g + 1) * STATE_SIZE]
        vw = vwrite[:, g * STATE_SIZE : (g + 1) * STATE_SIZE]
        scores = dot(vr, vw, ((1,), (1,)))
        direct = skip_l * vin_g
        for j in range(DRAFTS):
            decay = jnp.exp(jnp.where(row >= j, vrun_l - vrun_l[j : j + 1], -jnp.inf))
            direct = direct + decay * scores[:, j : j + 1] * (vstep_l[j : j + 1] * vin_g[j : j + 1])
        gate = vgate[:, at]
        gate = gate / (1.0 + jnp.exp(-gate))
        q1 = direct * gate
        q2 = jnp.exp(vrun_l) * gate
        q1_ref[:, at] = q1
        q2_ref[:, at] = q2
        live = jnp.exp(jnp.where(row < kept, reach_l - vrun_l, -jnp.inf)) * vstep_l * vin_g
        keep_l = jnp.concatenate(
            split(jnp.exp(reach_l), 3) + [jnp.zeros((5, wide), F32)], axis=0
        )
        tail_ref[:, at] = jnp.concatenate(split(live, 3) + [keep_l], axis=0).astype(BF16)
        read_l = jnp.concatenate([vr.astype(F32)] * (wide // STATE_SIZE), axis=1)
        mine = jnp.concatenate([q1, q2, read_l], axis=0)
        mine = jnp.where(is_owner, mine, 0.0)
        logs = jnp.concatenate(split(total_l, 3) + [jnp.zeros((5, wide), F32)], axis=0)
        extra_ref[:, at] = jnp.concatenate([mine, logs], axis=0).astype(BF16)

    for fetch in fetches[early : early + 2]:
        fetch.wait()
    half = lanes // 2
    chunk = min(wide, half)
    for k, out_ref in ((1, sent_ref), (0, own_ref)):
        start = (place ^ k) * half
        out_ref[STATE_SIZE:, :] = extra_ref[:, window(start, half)]
        for at in range(0, half, chunk):
            lane0 = start + at
            group = lax.div(lane0, wide)
            scale = dot(end_parts, head_mask(2 * heads, heads, chunk, lane0))
            weighted = (x_ref[:, window(lane0, chunk)].astype(F32) * scale).astype(BF16)
            writes = write_ref[:, window(group * STATE_SIZE, STATE_SIZE)]
            writes = writes.astype(F32).T.astype(BF16)
            out_ref[:STATE_SIZE, at : at + chunk] = dot(writes, weighted).astype(BF16)
    for fetch in fetches[early + 2 :]:
        fetch.wait()


def logs_of(block):
    return block[0:1].astype(F32) + block[1:2].astype(F32) + block[2:3].astype(F32)


def weights_of(logs, place, target):
    spots = [place ^ k for k in range(len(logs))]
    found = []
    for k, spot in enumerate(spots):
        between = jnp.zeros_like(logs[0])
        for other, log in zip(spots, logs):
            if other is not spot:
                between = between + jnp.where((spot < other) & (other < target), log, 0.0)
        found.append(jnp.where(spot < target, jnp.exp(between), 0.0))
    return found


def carry_of(logs, place, target):
    ahead = jnp.zeros_like(logs[0])
    for k, log in enumerate(logs):
        ahead = ahead + jnp.where((place ^ k) < target, log, 0.0)
    return jnp.exp(ahead)


def up_kernel(stage, following, count, *refs):
    parts, outs = refs[:count], refs[count:]
    place, target = place_of(stage), place_of(following)
    width = outs[0].shape[1]
    chunk = min(256, width)
    order = list(range(1, len(outs))) + [0]
    for k in order:
        for at in range(0, width, chunk):
            start = at if len(outs) == 1 else (target ^ k) * width + at
            at_in = window(start, chunk)
            logs = [logs_of(part[LOG_AT:UP_ROWS, at_in]) for part in parts]
            scale = weights_of(logs, place, count)
            state = sum(
                w * part[:STATE_SIZE, at_in].astype(F32) for w, part in zip(scale, parts)
            )
            outs[k][:STATE_SIZE, at : at + chunk] = state.astype(BF16)
            mine = sum(part[STATE_SIZE:UP_ROWS, at_in].astype(F32) for part in parts)
            total = jnp.concatenate(
                split(sum(logs), 3) + [jnp.zeros((5, chunk), F32)], axis=0
            )
            outs[k][STATE_SIZE:, at : at + chunk] = jnp.concatenate(
                [mine[:24], total], axis=0
            ).astype(BF16)


def top_kernel(stage, count, *refs):
    parts, outs, prompt_ref = refs[:count], refs[count:-1], refs[-1]
    place = place_of(stage)
    width = prompt_ref.shape[1]
    logs = [logs_of(part[LOG_AT:UP_ROWS, :]) for part in parts]
    states = [part[:STATE_SIZE, :].astype(F32) for part in parts]
    final = sum(w * s for w, s in zip(weights_of(logs, place, count), states)).astype(BF16)
    prompt_ref[...] = final
    mine = sum(part[STATE_SIZE:LOG_AT, :].astype(F32) for part in parts)
    reads = mine[16:24, :STATE_SIZE].astype(BF16)
    gated = mine[0:8] + mine[8:16] * dot(reads, final)
    gated = jnp.concatenate(split(gated, 2), axis=0).astype(BF16)
    for k in list(range(1, len(outs))) + [0]:
        scale = weights_of(logs, place, place ^ k)
        outs[k][:STATE_SIZE, :] = sum(w * s for w, s in zip(scale, states)).astype(BF16)
        outs[k][STATE_SIZE:, :] = gated


def down_kernel(stage, above, above_count, count, handed, *refs):
    pieces, parts = refs[:above_count], refs[above_count : above_count + count]
    outs = refs[above_count + count :]
    if handed:
        outs[-1][...] = outs[0][...]
        outs = outs[1:-1]
    place, source = place_of(stage), place_of(above)
    width = pieces[0].shape[1]
    chunk = min(256, width)
    for k in list(range(1, len(outs))) + [0]:
        for piece in range(above_count):
            for at in range(0, width, chunk):
                start = at if above_count == 1 else (source ^ piece) * width + at
                at_out = window(start, chunk)
                block = pieces[piece][:, at : at + chunk]
                logs = [logs_of(part[LOG_AT:UP_ROWS, at_out]) for part in parts]
                state = carry_of(logs, place, place ^ k) * block[:STATE_SIZE].astype(F32)
                for w, part in zip(weights_of(logs, place, place ^ k), parts):
                    state = state + w * part[:STATE_SIZE, at_out].astype(F32)
                outs[k][:STATE_SIZE, at_out] = state.astype(BF16)
                outs[k][STATE_SIZE:, at_out] = block[STATE_SIZE:]


def intra_kernel(group, run_ref, runt_ref, stept_ref, skip_ref, x_ref, write_ref, read_ref, *refs):
    fetch = None
    out_ref = refs[0]
    if len(refs) > 1:
        source_ref, out_ref, held_ref, sem = refs
        fetch = pltpu.make_async_copy(source_ref, held_ref, sem)
        fetch.start()
    span, heads = run_ref.shape[1:]
    mid = span // 2
    states = slice(group * STATE_SIZE, (group + 1) * STATE_SIZE)
    scores = dot(read_ref[:, states], write_ref[:, states], ((1,), (1,)))
    row = lax.broadcasted_iota(jnp.int32, (mid, mid), 0)
    causal = row >= lax.broadcasted_iota(jnp.int32, (mid, mid), 1)
    running = run_ref[group]
    low, high = slice(0, mid), slice(mid, span)
    for pair in range(heads // 2):
        found = []
        for k in (2 * pair, 2 * pair + 1):
            h = group * heads + k
            x = x_ref[:, h * HEAD_DIM : (h + 1) * HEAD_DIM]
            t_run, j_run = running[:, k : k + 1], runt_ref[h : h + 1, :]
            step = stept_ref[h : h + 1, :]

            def mixed(rows, cols, masked):
                gap = t_run[rows] - j_run[:, cols]
                if masked:
                    gap = jnp.where(causal, gap, -jnp.inf)
                return (scores[rows, cols] * jnp.exp(gap) * step[:, cols]).astype(BF16)

            top = dot(mixed(low, low, True), x[low])
            bottom = dot(mixed(high, low, False), x[low]) + dot(mixed(high, high, True), x[high])
            found.append(jnp.concatenate([top, bottom], axis=0))
        at = slice(pair * 2 * HEAD_DIM, (pair + 1) * 2 * HEAD_DIM)
        lanes = slice((group * heads + 2 * pair) * HEAD_DIM, (group * heads + 2 * pair + 2) * HEAD_DIM)
        both = jnp.concatenate(found, axis=1)
        out_ref[:, at] = both + skip_ref[:, lanes] * x_ref[:, lanes].astype(F32)
    if fetch is not None:
        fetch.wait()


def intra(group, run, runt, stept, skip, x, write, read, after, wanted=()):
    span, per_group = run.shape[1:]
    wide = per_group * HEAD_DIM
    return call(
        functools.partial(intra_kernel, group),
        "intra",
        [shape((span, wide), F32)] + [shape(value.shape, value.dtype) for value in wanted],
        (run, runt, stept, skip, x, write, read, *map(in_hbm, wanted)),
        specs=[WHOLE] * 7 + [IN_HBM] * len(wanted),
        scratch=[pltpu.SemaphoreType.DMA] * len(wanted),
        after=after,
        flops=per_group * span * span * HEAD_DIM * 2,
        moved=wide * span * 6,
        exps=per_group * span * span * 3 // 4,
    )


def finish_kernel(stage, reach_ref, read_ref, own_ref, got_ref, *refs):
    base_refs, (out_ref, token_ref, held_ref, sems) = refs[:-4], refs[-4:]
    token_ref[...] = jnp.zeros_like(token_ref)
    place = place_of(stage)
    heads = reach_ref.shape[1] // 2
    lanes = held_ref.shape[1]
    wide = lanes // len(base_refs)
    half = lanes // 2
    chunk = lanes // sems.shape[0]
    copies = []
    for k, lane0 in enumerate(range(0, lanes, chunk)):
        group, at = lane0 // wide, lane0 % half
        at_in, at_out = slice(at, at + chunk), slice(lane0, lane0 + chunk)
        entering = jnp.where(
            place == lane0 // half, own_ref[:STATE_SIZE, at_in], got_ref[:STATE_SIZE, at_in]
        )
        inter = dot(read_ref[:, group * STATE_SIZE : (group + 1) * STATE_SIZE], entering)
        inter = inter * dot(reach_ref[...], head_mask(2 * heads, heads, chunk, lane0))
        base = base_refs[group][:, lane0 % wide : lane0 % wide + chunk]
        held_ref[:, at_out] = (inter + base).astype(BF16)
        copies.append(
            pltpu.make_async_copy(held_ref.at[:, at_out], out_ref.at[:, at_out], sems.at[k])
        )
        copies[-1].start()
    for copy in copies:
        copy.wait()


def finish(stage, reach, read, own, got, bases, after):
    span = read.shape[0]
    lanes = 2 * own.shape[1]
    chunk = min(512, own.shape[1])
    return call(
        functools.partial(finish_kernel, stage),
        "finish",
        [shape((span, lanes), BF16), shape((8, 128), F32)],
        (reach, read, own, got, *bases),
        out_specs=[IN_HBM, WHOLE],
        after=after,
        scratch=[pltpu.VMEM((span, lanes), BF16), pltpu.SemaphoreType.DMA((lanes // chunk,))],
        flops=2 * span * lanes * STATE_SIZE,
    )


def resident_kernel(state_ref, vread_ref, q1_ref, q2_ref, gain_ref, out_ref):
    groups = vread_ref.shape[1] // STATE_SIZE
    wide = state_ref.shape[0] // groups
    for g in range(groups):
        at = slice(g * wide, (g + 1) * wide)
        reads = vread_ref[:, g * STATE_SIZE : (g + 1) * STATE_SIZE]
        drawn = dot(reads, state_ref[at, :], ((1,), (1,)))
        gated = q1_ref[:, at] + q2_ref[:, at] * drawn
        out_ref[:, at] = normed(gated, gain_ref[:, at]).astype(BF16)


def normed(gated, gain):
    mean_square = jnp.mean(gated * gated, axis=1, keepdims=True)
    return gated * lax.rsqrt(mean_square + EPSILON) * gain


def resident_hidden(state, vread, q1, q2, gain, after):
    lanes = state.shape[0]
    return call(
        resident_kernel,
        "resident_hidden",
        [shape((DRAFTS, lanes), BF16)],
        (state, vread, q1, q2, gain),
        after=after,
        flops=2 * DRAFTS * lanes * STATE_SIZE,
    )[0]


def join_kernel(axis, *refs):
    out_ref = refs[-1]
    for k, ref in enumerate(refs[:-1]):
        size = ref.shape[axis]
        at = slice(k * size, (k + 1) * size)
        if axis == 0:
            out_ref[at, :] = ref[...]
        else:
            out_ref[:, at] = ref[...]


def join(parts, axis, after=()):
    dims = list(parts[0].shape)
    dims[axis] *= len(parts)
    return call(
        functools.partial(join_kernel, axis), "join", [shape(tuple(dims), parts[0].dtype)], parts, after=after
    )[0]


def project_kernel(stages, head_count, *refs):
    owner_ref, own_rows, got_rows, own_ref, got_ref, gain_ref, weight_ref = refs[:7]
    outs = refs[7 : 7 + head_count]
    gated_ref, left_ref, total_ref = refs[7 + head_count :]
    here, head = lax.axis_index("seq"), lax.axis_index("head")
    place = place_of(stages[0])
    half = own_ref.shape[1]
    lanes = weight_ref.shape[0]
    wide = min(1024, lanes)
    rows = own_rows.shape[0]
    for k, ref in enumerate((own_ref, got_ref)):
        both = ref[STATE_SIZE:, :].astype(F32)
        gated_ref[:, window((place ^ k) * half, half)] = both[0:8] + both[8:16]
    left_ref[0:rows, :] = own_rows[...]
    left_ref[rows : 2 * rows, :] = got_rows[...]
    for lane0 in range(0, lanes, wide):
        at = slice(lane0, lane0 + wide)
        hidden = normed(gated_ref[:, at], gain_ref[:, at])
        hidden = jnp.concatenate([hidden, jnp.zeros_like(hidden)], axis=0)
        left_ref[2 * rows :, at] = hidden.astype(BF16)
    total_ref[...] = dot(left_ref[...], weight_ref[...])

    slots = 2 * rows // DRAFTS
    per_head = slots // head_count
    offsets = [0]
    for factor, stride in reversed(stages):
        offsets = [a + k * stride for k in range(factor) for a in offsets]
    owner = owner_ref[...]
    tail = total_ref[2 * rows : 2 * rows + DRAFTS, :]
    for k in list(range(1, head_count)) + [0]:
        first = (head ^ k) * per_head
        for slot in range(per_head):
            at = slice(slot * DRAFTS, (slot + 1) * DRAFTS)
            offset = here ^ (first + slot)
            block = jnp.int32(0)
            for position, value in enumerate(offsets):
                block = jnp.where(offset == value, position, block)
            from_block = total_ref[window(block * DRAFTS, DRAFTS), :]
            outs[k][at, :] = jnp.where(owner == first + slot, tail, from_block)


def project(stages, owner, own_rows, got_rows, own, got, gain, weight, head_count):
    lanes, cols = weight.shape
    rows = own_rows.shape[0]
    return call(
        functools.partial(project_kernel, stages, head_count),
        "project",
        [shape((2 * rows // head_count, cols), F32)] * head_count,
        (owner, own_rows, got_rows, own, got, gain, weight),

        scratch=[
            pltpu.VMEM((DRAFTS, lanes), F32),
            pltpu.VMEM((2 * rows + 16, lanes), BF16),
            pltpu.VMEM((2 * rows + 16, cols), F32),
        ],
        flops=2 * (2 * rows + 16) * lanes * cols,
    )


def states_kernel(scattered, shares, *refs):
    owner_ref, resident_ref, own_ref, got_ref, tail_ref, vwrite_ref = refs[:6]
    share_refs = refs[6 : 6 + shares]
    new_ref, slice_ref, verify_ref, turned_ref, held_ref, sems = refs[6 + shares :]
    here = lax.axis_index("seq")
    verify_ref[...] = sum(ref[...] for ref in share_refs).astype(BF16)
    lanes = resident_ref.shape[0]
    half = lanes // 2
    wide = lanes // (vwrite_ref.shape[1] // STATE_SIZE)
    blocks = [0]
    for factor, stride in reversed(scattered):
        blocks = [a | (k * stride) for k in range(factor) for a in blocks]
    width = half // len(blocks)
    chunk = lanes // sems.shape[0]
    is_owner = owner_ref[0:1, :STATE_SIZE] == here
    row = lax.broadcasted_iota(jnp.int32, (32, STATE_SIZE), 0)
    ones = jnp.where((row >= 24) & (row < 27), 1.0, 0.0)
    copies = []
    for part in range(sems.shape[0]):
        rows = slice(part * chunk, (part + 1) * chunk)
        for lane in range(part * chunk, (part + 1) * chunk, width):
            spot, size, rest = lane // half, half, lane % half
            for factor, stride in scattered:
                size = size // factor
                spot |= rest // size * stride
                rest %= size
            offset = spot ^ here
            position = jnp.int32(0)
            for place, value in enumerate(blocks):
                position = jnp.where((offset & sum_of(scattered)) == value, place, position)
            found = jnp.where(
                lax.rem(offset, 2) == 0,
                own_ref[:, window(position * width, width)],
                got_ref[:, window(position * width, width)],
            )
            turned_ref[lane : lane + width, :] = found.astype(F32).T
        group = part * chunk // wide
        writes = vwrite_ref[:, group * STATE_SIZE : (group + 1) * STATE_SIZE].astype(F32)
        writes = jnp.concatenate([writes, writes, writes, jnp.zeros_like(writes)], axis=0)
        right = jnp.concatenate([writes, ones], axis=1).astype(BF16)
        left = tail_ref[:, rows].astype(F32).T.astype(BF16)
        both = dot(left, right)
        start = jnp.where(is_owner, turned_ref[rows, :], resident_ref[rows, :].astype(F32))
        held_ref[rows, :] = (start * both[:, STATE_SIZE:] + both[:, :STATE_SIZE]).astype(BF16)
        copies.append(pltpu.make_async_copy(held_ref.at[rows, :], new_ref.at[rows, :], sems.at[part]))
        copies[-1].start()
    per_slice = slice_ref.shape[1] // STATE_SIZE
    heads = slice_ref.shape[0]
    for k in range(per_slice):
        picked = turned_ref[pl.ds(here * per_slice + k, heads, stride=HEAD_DIM), :]
        slice_ref[:, k * STATE_SIZE : (k + 1) * STATE_SIZE] = picked.astype(BF16)
    for copy in copies:
        copy.wait()


def sum_of(stages):
    return sum((factor - 1) * stride for factor, stride in stages)


def states(scattered, owner, resident, own, got, tail, vwrite, shares, seq_count):
    lanes = resident.shape[0]
    wide = lanes // (vwrite.shape[1] // STATE_SIZE)
    chunk = min(512, wide)
    return call(
        functools.partial(states_kernel, scattered, len(shares)),
        "states",
        [
            shape((lanes, STATE_SIZE), BF16),
            shape((lanes // HEAD_DIM, HEAD_DIM // seq_count * STATE_SIZE), BF16),
            shape(shares[0].shape, BF16),
        ],
        (owner, resident, own, got, tail, vwrite, *shares),
        out_specs=[IN_HBM, WHOLE, WHOLE],
        scratch=[
            pltpu.VMEM((lanes, STATE_SIZE), F32),
            pltpu.VMEM((lanes, STATE_SIZE), BF16),
            pltpu.SemaphoreType.DMA((lanes // chunk,)),
        ],
        flops=2 * lanes * STATE_SIZE * 64,
    )


def on_device(
    prefill_input,
    prefill_step,
    write_proj,
    read_proj,
    decay_rate,
    skip_gain,
    resident_state,
    owner_slot,
    draft_ids,
    accepted_len,
    draft_input,
    draft_gate,
    draft_write,
    draft_read,
    draft_step,
    norm_gain,
    out_weight,
):
    span, lanes = prefill_input.shape
    assert span == BLOCK_LEN
    heads = decay_rate.shape[0]
    groups = write_proj.shape[1] // STATE_SIZE
    per_group = heads // groups
    half = lanes // 2
    seq_count, head_count = lax.axis_size("seq"), lax.axis_size("head")
    stages = tree_stages(seq_count)
    core, line, last = stages
    slots = owner_slot.shape[0]
    assert core[0] == 2 and slots == seq_count
    rate, skip, gain = decay_rate[None], skip_gain[None], norm_gain[None]
    resident = resident_state.reshape(lanes, STATE_SIZE)

    inputs = (
        prefill_step.T, rate, skip, owner_slot, draft_ids.T, accepted_len, draft_input, draft_gate,
        draft_write, draft_read, draft_step, write_proj, prefill_input, read_proj, resident, gain,
    )
    passed = 5
    inputs = [in_hbm(value) for value in inputs]
    opened = call(
        functools.partial(open_kernel, core, len(inputs), passed),
        "open_block",
        [
            shape((UP_ROWS, half), BF16),
            shape((UP_ROWS, half), BF16),
            shape((groups, span, per_group), F32),
            shape((heads, span), F32),
            shape((heads, span), F32),
            shape((span, 2 * heads), BF16),
            shape((1, lanes), F32),
            shape((DRAFTS, lanes), F32),
            shape((DRAFTS, lanes), F32),
            shape((DRAFTS, groups * STATE_SIZE), BF16),
            shape((DRAFTS, groups * STATE_SIZE), BF16),
            shape((32, lanes), BF16),
            shape((DRAFTS, out_weight.shape[1]), jnp.int32),
        ]
        + [shape(value.shape, value.dtype) for value in inputs[-passed:]],
        inputs,
        specs=[IN_HBM] * len(inputs),
        scratch=[pltpu.VMEM((EXTRA, lanes), BF16), pltpu.SemaphoreType.DMA((len(inputs),))]
        + [
            (pltpu.SMEM if value.dtype == jnp.int32 else pltpu.VMEM)(value.shape, value.dtype)
            for value in inputs[:-passed]
        ],
        flops=2 * span * lanes * STATE_SIZE * 2,
    )
    own, sent, run, runt, stept, reach, skip_lanes, q1, q2, vread, vwrite, tail, owner = opened[:13]
    writes, x, reads, resident, gain = opened[13:]
    core_parts = [own, swap(sent, "seq", core, 1)]

    bases, fetched = [], []

    def fill(after):
        if len(bases) < groups:
            wanted = [] if bases else [out_weight]
            base, *found = intra(
                len(bases), run, runt, stept, skip_lanes, x, writes, reads, after, wanted
            )
            bases.append(base)
            fetched.extend(found)
        return bases[-1:]

    def exchange(parts, stage):
        got = {k: swap(parts[k], "seq", stage, k) for k in range(stage[0] - 1, 0, -1)}
        return [parts[0]] + [got[k] for k in range(1, stage[0])]

    line_width = half // line[0]
    split_last = line_width % (last[0] * 128) == 0
    last_width = line_width // last[0] if split_last else line_width
    outs = call(
        functools.partial(up_kernel, core, line, 2),
        "up_line",
        [shape((UP_ROWS, line_width), BF16)] * line[0],
        core_parts,
        flops=half * UP_ROWS * 4,
    )
    line_parts = exchange(outs, line)
    hidden = resident_hidden(resident, vread, q1, q2, gain, [outs[-1]])
    hidden = join(exchange([hidden] * last[0], last), 0)
    outs = call(
        functools.partial(up_kernel, line, last, line[0]),
        "up_last",
        [shape((UP_ROWS, last_width), BF16)] * (last[0] if split_last else 1),
        line_parts,
        after=[hidden],
        flops=line_width * UP_ROWS * 4,
    )
    last_parts = exchange(outs if split_last else outs * last[0], last)
    hiddens = exchange([hidden] * line[0], line)
    filled = fill([outs[-1]]) + fill(bases[-1:])
    *outs, prompt = call(
        functools.partial(top_kernel, last, last[0]),
        "top",
        [shape((DOWN_ROWS, last_width), BF16)] * (last[0] if split_last else 1)
        + [shape((STATE_SIZE, last_width), BF16)],
        last_parts,
        after=filled,
        flops=last_width * UP_ROWS * 16,
    )

    pieces = exchange(outs, last) if split_last else outs
    filled = fill([outs[-1]])
    hidden = join(hiddens, 0)
    *outs, prompt = call(
        functools.partial(down_kernel, line, last, len(pieces), line[0], True),
        "down_line",
        [shape((DOWN_ROWS, line_width), BF16)] * line[0] + [shape(prompt.shape, BF16)],
        [*pieces, *line_parts, prompt],
        after=[*filled, hidden],
        flops=line_width * UP_ROWS * 8,
    )
    pieces = exchange(outs, line)
    filled = fill([outs[-1]])
    scattered = [line, last] if split_last else [line]
    if split_last:
        prompt = join(exchange([prompt] * last[0], last), 1)
    outs = call(
        functools.partial(down_kernel, core, line, line[0], 2, False),
        "down_core",
        [shape((DOWN_ROWS, half), BF16)] * 2,
        pieces + core_parts,
        after=filled + [prompt],
        flops=half * UP_ROWS * 8,
    )
    entering = exchange(outs, core)
    while len(bases) < groups:
        fill([])

    shares = project(
        stages, owner, hidden, swap(hidden, "seq", core, 1), *entering, gain, fetched[0], head_count
    )
    prefill_out, token = finish(core, reach, reads, *entering, bases, shares[:1])
    shares = [shares[0]] + [swap(shares[k], "head", (head_count, 1), k) for k in range(1, head_count)]

    prompt = join(exchange([prompt] * line[0], line), 1, [token, *shares[1:]])
    prompts = exchange([prompt] * 2, core)
    new_state, state_slice, verify_out = states(
        scattered, owner, resident, *prompts, tail, vwrite, shares, seq_count
    )
    return (
        prefill_out,
        new_state.reshape(1, heads, HEAD_DIM, STATE_SIZE),
        verify_out,
        state_slice,
    )


def solution(mesh):
    return jax.shard_map(
        on_device,
        mesh=mesh,
        in_specs=(
            P("seq", "head"),
            P("seq", "head"),
            P("seq", "head"),
            P("seq", "head"),
            P("head"),
            P("head"),
            P("seq", "head", None, None),
            P(),
            P(),
            P(),
            P("seq", "head"),
            P("seq", "head"),
            P("seq", "head"),
            P("seq", "head"),
            P("seq", "head"),
            P("head"),
            P("head", "seq"),
        ),
        out_specs=(
            P("seq", "head"),
            P("seq", "head", None, None),
            P("head", "seq"),
            P("head", "seq"),
        ),
        check_vma=False,
    )
```

```python
import functools

import jax
import jax.numpy as jnp
from jax import lax
from jax.experimental import pallas as pl
from jax.experimental.pallas import tpu as pltpu
from jax.sharding import PartitionSpec as P

HEAD_DIM = 64
STATE_SIZE = 128
BLOCK_LEN = 256
DRAFTS = 8
EPSILON = 1e-05
EXTRA = 32
UP_ROWS = STATE_SIZE + EXTRA
READ_AT = STATE_SIZE + 16
LOG_AT = STATE_SIZE + 24
DOWN_ROWS = STATE_SIZE + 16

F32 = jnp.float32
BF16 = jnp.bfloat16


def tree_stages(count):
    factors, rest = [], count
    if rest > 1:
        factors.append(2)
        rest //= 2
    inner = 1
    while inner * inner * 4 <= rest:
        inner *= 2
    factors += [inner, rest // inner]
    stages, stride = [], 1
    for factor in factors:
        stages.append((factor, stride))
        stride *= factor
    assert stride == count
    return stages


def swap(value, axis, stage, offset):
    count, stride = lax.axis_size(axis), stage[1]
    return lax.ppermute(value, axis, [(k, k ^ (offset * stride)) for k in range(count)])


def place_of(stage):
    factor, stride = stage
    return lax.rem(lax.div(lax.axis_index("seq"), stride), factor)


def dot(a, b, dims=((1,), (0,))):
    return lax.dot_general(a, b, (dims, ((), ())), preferred_element_type=F32)


def split(value, parts):
    found = []
    for _ in range(parts):
        part = value.astype(BF16).astype(F32)
        found.append(part)
        value = value - part
    return found


def head_mask(rows, heads, lanes, lane0):
    row = lax.broadcasted_iota(jnp.int32, (rows, lanes), 0) & (heads - 1)
    head = lax.shift_right_logical(lax.broadcasted_iota(jnp.int32, (rows, lanes), 1) + lane0, 6)
    return jnp.where(row == head, 1.0, 0.0).astype(BF16)


def window(start, size):
    return pl.ds(pl.multiple_of(start, size), size)


def ordered(kernel, count):
    return lambda *refs: kernel(*refs[count:])


ANYWHERE = pl.BlockSpec(memory_space=pl.ANY)
WHOLE = pl.BlockSpec(memory_space=pltpu.VMEM)
IN_HBM = pl.BlockSpec(memory_space=pltpu.HBM)


def call(
    kernel, name, outs, args, specs=None, out_specs=None, grid=(), after=(), scratch=(), alias=None,
    flops=0, exps=0, moved=None, vmem=32,
):
    if specs is None:
        specs = [WHOLE] * len(args)
    if out_specs is None:
        out_specs = [WHOLE] * len(outs)
    if moved is None:
        moved = sum(a.size * a.dtype.itemsize for a in (*args, *outs))
    first = len(after)
    return pl.pallas_call(
        ordered(kernel, first),
        name=name,
        grid=grid,
        out_shape=outs,
        in_specs=[ANYWHERE] * first + specs,
        out_specs=out_specs,
        scratch_shapes=list(scratch),
        input_output_aliases={first + k: v for k, v in (alias or {}).items()},
        compiler_params=pltpu.CompilerParams(vmem_limit_bytes=vmem * 1024 * 1024),
        cost_estimate=pl.CostEstimate(flops=flops, bytes_accessed=moved, transcendentals=exps),
    )(*after, *args)


def in_hbm(value):
    return pltpu.with_memory_space_constraint(value, pltpu.HBM)


def shape(dims, dtype):
    return jax.ShapeDtypeStruct(dims, dtype)


def open_kernel(stage, count, passed, *refs):
    sources, rest = refs[:count], refs[count:]
    outs, scratch = rest[: 14 + passed], rest[14 + passed :]
    outs, later = outs[:14], list(outs[14:])
    sent_ref, run_ref, runt_ref, stept_ref, reach_ref, end_ref, skip_out = outs[:7]
    q1_ref, q2_ref, vread_ref, vwrite_ref, tail_ref, owner_out, extra_ref = outs[7:]
    sems, held = scratch[0], [*scratch[1:], *later]
    fetches = [
        pltpu.make_async_copy(source, target, sems.at[k])
        for k, (source, target) in enumerate(zip(sources, held))
    ]
    for fetch in fetches:
        fetch.start()
    early = count - passed
    for fetch in fetches[:early]:
        fetch.wait()
    turned_ref, rate_ref, skip_ref, owner_ref, ids_ref, kept_ref = held[:6]
    din_ref, dgate_ref, dwrite_ref, dread_ref, dstep_ref, write_ref, x_ref = held[6:13]
    heads, span = turned_ref.shape
    lanes = x_ref.shape[1]
    groups = write_ref.shape[1] // STATE_SIZE
    per_group = heads // groups
    wide = per_group * HEAD_DIM
    here = lax.axis_index("seq")
    place = place_of(stage)
    owner_out[...] = jnp.zeros(owner_out.shape, jnp.int32) + owner_ref[0]

    step_rows = turned_ref[...]
    stept_ref[...] = step_rows
    pad = (-heads) % 128
    if pad:
        step_rows = jnp.concatenate([step_rows, jnp.zeros((pad, span), F32)], axis=0)
    step = step_rows.T[:, :heads]
    log_decay = -step * rate_ref[...]
    lower = lax.broadcasted_iota(jnp.int32, (span, span), 0) >= lax.broadcasted_iota(
        jnp.int32, (span, span), 1
    )
    lower = jnp.where(lower, 1.0, 0.0).astype(BF16)
    running = sum(dot(lower, part.astype(BF16)) for part in split(log_decay, 3))
    total = running[span - 1 : span, :]
    to_end = jnp.exp(total - running) * step
    wide_run = running
    if pad:
        wide_run = jnp.concatenate([running, jnp.zeros((span, pad), F32)], axis=1)
    runt_ref[...] = wide_run.T[:heads]
    for g in range(groups):
        run_ref[g] = running[:, g * per_group : (g + 1) * per_group]
    reach_ref[...] = jnp.concatenate(split(jnp.exp(running), 2), axis=1).astype(BF16)
    end_ref[...] = jnp.concatenate(split(to_end, 2), axis=1).astype(BF16)

    slots = owner_ref.shape[0]
    request = lax.fori_loop(
        0, slots, lambda r, found: jnp.where(owner_ref[r] == here, r, found), jnp.int32(0)
    )
    kept = kept_ref[request]
    candidates = din_ref.shape[0]
    row = lax.broadcasted_iota(jnp.int32, (DRAFTS, candidates), 0)
    col = lax.broadcasted_iota(jnp.int32, (DRAFTS, candidates), 1)
    pick = jnp.zeros((DRAFTS, candidates), F32)
    for i in range(DRAFTS):
        pick = jnp.where((row == i) & (col == ids_ref[i, request]), 1.0, pick)
    pick = pick.astype(BF16)
    vin = dot(pick, din_ref[...])
    vgate = dot(pick, dgate_ref[...])
    vwrite = dot(pick, dwrite_ref[...]).astype(BF16)
    vread = dot(pick, dread_ref[...]).astype(BF16)
    vwrite_ref[...] = vwrite
    vread_ref[...] = vread
    vstep = sum(dot(pick, part.astype(BF16)) for part in split(dstep_ref[...], 3))
    vlog = -vstep * rate_ref[...]
    index = lax.broadcasted_iota(jnp.int32, (DRAFTS, heads), 0)
    acc = jnp.zeros((1, heads), F32)
    vrun = jnp.zeros((DRAFTS, heads), F32)
    reach = jnp.zeros((1, heads), F32)
    for i in range(DRAFTS):
        acc = acc + vlog[i : i + 1]
        vrun = jnp.where(index == i, acc, vrun)
        reach = jnp.where(i < kept, acc, reach)
    others = jnp.where(index == 0, total, jnp.where(index == 1, skip_ref[...], reach))
    stacked = split(jnp.concatenate([vrun, vstep, others], axis=0), 3)
    stacked = jnp.concatenate(stacked, axis=0).astype(BF16)
    row = lax.broadcasted_iota(jnp.int32, (DRAFTS, wide), 0)
    is_owner = owner_ref[0] == here
    for g in range(groups):
        at = slice(g * wide, (g + 1) * wide)
        spread = dot(stacked, head_mask(heads, heads, wide, g * wide))
        spread = spread[0:24] + spread[24:48] + spread[48:72]
        vrun_l, vstep_l = spread[0:8], spread[8:16]
        total_l, skip_l, reach_l = spread[16:17], spread[17:18], spread[18:19]
        skip_out[:, at] = skip_l
        vin_g = vin[:, at]
        vr = vread[:, g * STATE_SIZE : (g + 1) * STATE_SIZE]
        vw = vwrite[:, g * STATE_SIZE : (g + 1) * STATE_SIZE]
        scores = dot(vr, vw, ((1,), (1,)))
        direct = skip_l * vin_g
        for j in range(DRAFTS):
            decay = jnp.exp(jnp.where(row >= j, vrun_l - vrun_l[j : j + 1], -jnp.inf))
            direct = direct + decay * scores[:, j : j + 1] * (vstep_l[j : j + 1] * vin_g[j : j + 1])
        gate = vgate[:, at]
        gate = gate / (1.0 + jnp.exp(-gate))
        q1 = direct * gate
        q2 = jnp.exp(vrun_l) * gate
        q1_ref[:, at] = q1
        q2_ref[:, at] = q2
        live = jnp.exp(jnp.where(row < kept, reach_l - vrun_l, -jnp.inf)) * vstep_l * vin_g
        keep_l = jnp.concatenate(
            split(jnp.exp(reach_l), 3) + [jnp.zeros((5, wide), F32)], axis=0
        )
        tail_ref[:, at] = jnp.concatenate(split(live, 3) + [keep_l], axis=0).astype(BF16)
        read_l = jnp.concatenate([vr.astype(F32)] * (wide // STATE_SIZE), axis=1)
        mine = jnp.concatenate([q1, q2, read_l], axis=0)
        mine = jnp.where(is_owner, mine, 0.0)
        logs = jnp.concatenate(split(total_l, 3) + [jnp.zeros((5, wide), F32)], axis=0)
        extra_ref[:, at] = jnp.concatenate([mine, logs], axis=0).astype(BF16)

    for fetch in fetches[early : early + 2]:
        fetch.wait()
    fill_message(place ^ 1, end_ref, x_ref, write_ref, extra_ref, sent_ref)
    for fetch in fetches[early + 2 :]:
        fetch.wait()


def fill_message(side, end_ref, x_ref, write_ref, extra_ref, out_ref):
    heads = end_ref.shape[1] // 2
    half = out_ref.shape[1]
    wide = 2 * half // (write_ref.shape[1] // STATE_SIZE)
    chunk = min(wide, half)
    start = side * half
    out_ref[STATE_SIZE:, :] = extra_ref[:, window(start, half)]
    for at in range(0, half, chunk):
        lane0 = start + at
        group = lax.div(lane0, wide)
        scale = dot(end_ref[...], head_mask(2 * heads, heads, chunk, lane0))
        weighted = (x_ref[:, window(lane0, chunk)].astype(F32) * scale).astype(BF16)
        writes = write_ref[:, window(group * STATE_SIZE, STATE_SIZE)]
        writes = writes.astype(F32).T.astype(BF16)
        out_ref[:STATE_SIZE, at : at + chunk] = dot(writes, weighted).astype(BF16)


def own_kernel(stage, end_ref, x_ref, write_ref, extra_ref, out_ref):
    fill_message(place_of(stage), end_ref, x_ref, write_ref, extra_ref, out_ref)


def logs_of(block):
    return block[0:1].astype(F32) + block[1:2].astype(F32) + block[2:3].astype(F32)


def weights_of(logs, place, target):
    spots = [place ^ k for k in range(len(logs))]
    found = []
    for k, spot in enumerate(spots):
        between = jnp.zeros_like(logs[0])
        for other, log in zip(spots, logs):
            if other is not spot:
                between = between + jnp.where((spot < other) & (other < target), log, 0.0)
        found.append(jnp.where(spot < target, jnp.exp(between), 0.0))
    return found


def carry_of(logs, place, target):
    ahead = jnp.zeros_like(logs[0])
    for k, log in enumerate(logs):
        ahead = ahead + jnp.where((place ^ k) < target, log, 0.0)
    return jnp.exp(ahead)


def up_kernel(stage, following, count, *refs):
    parts, outs = refs[:count], refs[count:]
    place, target = place_of(stage), place_of(following)
    width = outs[0].shape[1]
    chunk = min(256, width)
    order = list(range(1, len(outs))) + [0]
    for k in order:
        for at in range(0, width, chunk):
            start = at if len(outs) == 1 else (target ^ k) * width + at
            at_in = window(start, chunk)
            logs = [logs_of(part[LOG_AT:UP_ROWS, at_in]) for part in parts]
            scale = weights_of(logs, place, count)
            state = sum(
                w * part[:STATE_SIZE, at_in].astype(F32) for w, part in zip(scale, parts)
            )
            outs[k][:STATE_SIZE, at : at + chunk] = state.astype(BF16)
            mine = sum(part[STATE_SIZE:UP_ROWS, at_in].astype(F32) for part in parts)
            total = jnp.concatenate(
                split(sum(logs), 3) + [jnp.zeros((5, chunk), F32)], axis=0
            )
            outs[k][STATE_SIZE:, at : at + chunk] = jnp.concatenate(
                [mine[:24], total], axis=0
            ).astype(BF16)


def top_kernel(stage, count, *refs):
    parts, outs, prompt_ref = refs[:count], refs[count:-1], refs[-1]
    place = place_of(stage)
    width = prompt_ref.shape[1]
    logs = [logs_of(part[LOG_AT:UP_ROWS, :]) for part in parts]
    states = [part[:STATE_SIZE, :].astype(F32) for part in parts]
    final = sum(w * s for w, s in zip(weights_of(logs, place, count), states)).astype(BF16)
    prompt_ref[...] = final
    mine = sum(part[STATE_SIZE:LOG_AT, :].astype(F32) for part in parts)
    reads = mine[16:24, :STATE_SIZE].astype(BF16)
    gated = mine[0:8] + mine[8:16] * dot(reads, final)
    gated = jnp.concatenate(split(gated, 2), axis=0).astype(BF16)
    for k in list(range(1, len(outs))) + [0]:
        scale = weights_of(logs, place, place ^ k)
        outs[k][:STATE_SIZE, :] = sum(w * s for w, s in zip(scale, states)).astype(BF16)
        outs[k][STATE_SIZE:, :] = gated


def down_kernel(stage, above, above_count, count, targets, handed, *refs):
    pieces, parts = refs[:above_count], refs[above_count : above_count + count]
    outs = refs[above_count + count :]
    if handed:
        outs[-1][...] = outs[0][...]
        outs = outs[1:-1]
    place, source = place_of(stage), place_of(above)
    width = pieces[0].shape[1]
    chunk = min(256, width)
    for k, out_ref in zip(targets, outs):
        for piece in range(above_count):
            for at in range(0, width, chunk):
                start = at if above_count == 1 else (source ^ piece) * width + at
                at_out = window(start, chunk)
                block = pieces[piece][:, at : at + chunk]
                logs = [logs_of(part[LOG_AT:UP_ROWS, at_out]) for part in parts]
                state = carry_of(logs, place, place ^ k) * block[:STATE_SIZE].astype(F32)
                for w, part in zip(weights_of(logs, place, place ^ k), parts):
                    state = state + w * part[:STATE_SIZE, at_out].astype(F32)
                out_ref[:STATE_SIZE, at_out] = state.astype(BF16)
                out_ref[STATE_SIZE:, at_out] = block[STATE_SIZE:]


def intra_kernel(group, run_ref, runt_ref, stept_ref, skip_ref, x_ref, write_ref, read_ref, *refs):
    fetch = None
    out_ref = refs[0]
    if len(refs) > 1:
        source_ref, out_ref, held_ref, sem = refs
        fetch = pltpu.make_async_copy(source_ref, held_ref, sem)
        fetch.start()
    span, heads = run_ref.shape[1:]
    mid = span // 2
    states = slice(group * STATE_SIZE, (group + 1) * STATE_SIZE)
    scores = dot(read_ref[:, states], write_ref[:, states], ((1,), (1,)))
    row = lax.broadcasted_iota(jnp.int32, (mid, mid), 0)
    causal = row >= lax.broadcasted_iota(jnp.int32, (mid, mid), 1)
    running = run_ref[group]
    low, high = slice(0, mid), slice(mid, span)
    for pair in range(heads // 2):
        found = []
        for k in (2 * pair, 2 * pair + 1):
            h = group * heads + k
            x = x_ref[:, h * HEAD_DIM : (h + 1) * HEAD_DIM]
            t_run, j_run = running[:, k : k + 1], runt_ref[h : h + 1, :]
            step = stept_ref[h : h + 1, :]

            def mixed(rows, cols, masked):
                gap = t_run[rows] - j_run[:, cols]
                if masked:
                    gap = jnp.where(causal, gap, -jnp.inf)
                return (scores[rows, cols] * jnp.exp(gap) * step[:, cols]).astype(BF16)

            top = dot(mixed(low, low, True), x[low])
            bottom = dot(mixed(high, low, False), x[low]) + dot(mixed(high, high, True), x[high])
            found.append(jnp.concatenate([top, bottom], axis=0))
        at = slice(pair * 2 * HEAD_DIM, (pair + 1) * 2 * HEAD_DIM)
        lanes = slice((group * heads + 2 * pair) * HEAD_DIM, (group * heads + 2 * pair + 2) * HEAD_DIM)
        both = jnp.concatenate(found, axis=1)
        out_ref[:, at] = both + skip_ref[:, lanes] * x_ref[:, lanes].astype(F32)
    if fetch is not None:
        fetch.wait()


def intra(group, run, runt, stept, skip, x, write, read, after, wanted=()):
    span, per_group = run.shape[1:]
    wide = per_group * HEAD_DIM
    return call(
        functools.partial(intra_kernel, group),
        "intra",
        [shape((span, wide), F32)] + [shape(value.shape, value.dtype) for value in wanted],
        (run, runt, stept, skip, x, write, read, *map(in_hbm, wanted)),
        specs=[WHOLE] * 7 + [IN_HBM] * len(wanted),
        scratch=[pltpu.SemaphoreType.DMA] * len(wanted),
        after=after,
        flops=per_group * span * span * HEAD_DIM * 2,
        moved=wide * span * 6,
        exps=per_group * span * span * 3 // 4,
    )


def finish_kernel(stage, offset, reach_ref, read_ref, entering_ref, *refs):
    base_refs, (out_ref, token_ref, held_ref, sems) = refs[:-4], refs[-4:]
    if offset:
        base_refs = base_refs[:-1]
    token_ref[...] = jnp.zeros_like(token_ref)
    side = place_of(stage) ^ offset
    heads = reach_ref.shape[1] // 2
    half = held_ref.shape[1]
    wide = 2 * half // len(base_refs)
    chunk = half // sems.shape[0]
    copies = []
    for k, at in enumerate(range(0, half, chunk)):
        found = []
        for lane0 in (at, half + at):
            group = lane0 // wide
            found.append(
                (
                    read_ref[:, group * STATE_SIZE : (group + 1) * STATE_SIZE],
                    base_refs[group][:, lane0 % wide : lane0 % wide + chunk],
                )
            )
        reads, base = (jnp.where(side == 0, a, b) for a, b in zip(*found))
        lane0 = side * half + at
        inter = dot(reads, entering_ref[:STATE_SIZE, at : at + chunk])
        inter = inter * dot(reach_ref[...], head_mask(2 * heads, heads, chunk, lane0))
        held_ref[:, at : at + chunk] = (inter + base).astype(BF16)
        copies.append(
            pltpu.make_async_copy(
                held_ref.at[:, at : at + chunk], out_ref.at[:, window(lane0, chunk)], sems.at[k]
            )
        )
        copies[-1].start()
    for copy in copies:
        copy.wait()


def finish(stage, offset, reach, read, entering, bases, out, after):
    span, half = read.shape[0], entering.shape[1]
    chunk = min(512, half)
    args = [reach, read, entering, *bases]
    specs = [WHOLE] * len(args)
    if offset:
        args.append(out)
        specs.append(IN_HBM)
    return call(
        functools.partial(finish_kernel, stage, offset),
        "finish",
        [shape((span, 2 * half), BF16), shape((8, 128), F32)],
        args,
        specs=specs,
        out_specs=[IN_HBM, WHOLE],
        after=after,
        alias={len(args) - 1: 0} if offset else None,
        scratch=[pltpu.VMEM((span, half), BF16), pltpu.SemaphoreType.DMA((half // chunk,))],
        flops=span * half * STATE_SIZE * 2,
        moved=span * half * 8,
    )


def resident_kernel(state_ref, vread_ref, q1_ref, q2_ref, gain_ref, out_ref):
    groups = vread_ref.shape[1] // STATE_SIZE
    wide = state_ref.shape[0] // groups
    for g in range(groups):
        at = slice(g * wide, (g + 1) * wide)
        reads = vread_ref[:, g * STATE_SIZE : (g + 1) * STATE_SIZE]
        drawn = dot(reads, state_ref[at, :], ((1,), (1,)))
        gated = q1_ref[:, at] + q2_ref[:, at] * drawn
        out_ref[:, at] = normed(gated, gain_ref[:, at]).astype(BF16)


def normed(gated, gain):
    mean_square = jnp.mean(gated * gated, axis=1, keepdims=True)
    return gated * lax.rsqrt(mean_square + EPSILON) * gain


def resident_hidden(state, vread, q1, q2, gain, after):
    lanes = state.shape[0]
    return call(
        resident_kernel,
        "resident_hidden",
        [shape((DRAFTS, lanes), BF16)],
        (state, vread, q1, q2, gain),
        after=after,
        flops=2 * DRAFTS * lanes * STATE_SIZE,
    )[0]


def join_kernel(axis, *refs):
    out_ref = refs[-1]
    for k, ref in enumerate(refs[:-1]):
        size = ref.shape[axis]
        at = slice(k * size, (k + 1) * size)
        if axis == 0:
            out_ref[at, :] = ref[...]
        else:
            out_ref[:, at] = ref[...]


def join(parts, axis, after=()):
    dims = list(parts[0].shape)
    dims[axis] *= len(parts)
    return call(
        functools.partial(join_kernel, axis), "join", [shape(tuple(dims), parts[0].dtype)], parts, after=after
    )[0]


def project_kernel(stage, head_count, *refs):
    owner_ref, rows_ref, own_ref, got_ref, gain_ref, weight_ref = refs[:6]
    outs = refs[6 : 6 + head_count]
    gated_ref, left_ref, total_ref, sem = refs[6 + head_count :]
    head = lax.axis_index("head")
    place = place_of(stage)
    half = own_ref.shape[1]
    lanes = weight_ref.shape[0]
    wide = min(1024, lanes)
    rows = rows_ref.shape[0]
    fetch = pltpu.make_async_copy(rows_ref, left_ref.at[0:rows, :], sem)
    fetch.start()
    for k, ref in enumerate((own_ref, got_ref)):
        both = ref[STATE_SIZE:, :].astype(F32)
        gated_ref[:, window((place ^ k) * half, half)] = both[0:8] + both[8:16]
    for lane0 in range(0, lanes, wide):
        at = slice(lane0, lane0 + wide)
        hidden = normed(gated_ref[:, at], gain_ref[:, at])
        hidden = jnp.concatenate([hidden, jnp.zeros_like(hidden)], axis=0)
        left_ref[rows:, at] = hidden.astype(BF16)
    fetch.wait()
    total_ref[...] = dot(left_ref[...], weight_ref[...])

    per_head = rows // DRAFTS // head_count
    owner = owner_ref[...]
    tail = total_ref[rows : rows + DRAFTS, :]
    for k in range(head_count):
        first = (head ^ k) * per_head
        for slot in range(per_head):
            at = slice(slot * DRAFTS, (slot + 1) * DRAFTS)
            drawn = total_ref[window((first + slot) * DRAFTS, DRAFTS), :]
            outs[k][at, :] = jnp.where(owner == first + slot, tail, drawn)


def project(stage, owner, hidden, own, got, gain, weight, head_count, after):
    lanes, cols = weight.shape
    rows = hidden.shape[0]
    return call(
        functools.partial(project_kernel, stage, head_count),
        "project",
        [shape((rows // head_count, cols), F32)] * head_count,
        (owner, in_hbm(hidden), own, got, gain, weight),
        specs=[WHOLE, IN_HBM] + [WHOLE] * 4,
        after=after,
        scratch=[
            pltpu.VMEM((DRAFTS, lanes), F32),
            pltpu.VMEM((rows + 16, lanes), BF16),
            pltpu.VMEM((rows + 16, cols), F32),
            pltpu.SemaphoreType.DMA,
        ],
        flops=2 * (rows + 16) * lanes * cols,
    )


def states_kernel(stage, scattered, offset, *refs):
    owner_ref, resident_ref, prompt_ref, tail_ref, vwrite_ref = refs[:5]
    here = lax.axis_index("seq")
    side = place_of(stage) ^ offset
    if offset:
        other_ref, _, new_ref, slice_ref, turned_ref, held_ref, sems = refs[5:]
    else:
        share_refs, (new_ref, turned_ref, verify_ref, held_ref, sems) = refs[5:-5], refs[-5:]
        verify_ref[...] = sum(ref[...] for ref in share_refs).astype(BF16)
    half = prompt_ref.shape[1]
    wide = 2 * half // (vwrite_ref.shape[1] // STATE_SIZE)
    blocks = [0]
    for factor, stride in reversed(scattered):
        blocks = [a | (k * stride) for k in range(factor) for a in blocks]
    width = half // len(blocks)
    chunk = half // sems.shape[0]
    is_owner = owner_ref[0:1, :STATE_SIZE] == here
    row = lax.broadcasted_iota(jnp.int32, (32, STATE_SIZE), 0)
    ones = jnp.where((row >= 24) & (row < 27), 1.0, 0.0)
    copies = []
    for part in range(sems.shape[0]):
        rows = slice(part * chunk, (part + 1) * chunk)
        for lane in range(part * chunk, (part + 1) * chunk, width):
            spot, size, rest = 0, half, lane
            for factor, stride in scattered:
                size = size // factor
                spot |= rest // size * stride
                rest %= size
            apart = (spot ^ here) & sum((factor - 1) * stride for factor, stride in scattered)
            position = jnp.int32(0)
            for place, value in enumerate(blocks):
                position = jnp.where(apart == value, place, position)
            found = prompt_ref[:, window(position * width, width)]
            turned_ref[lane : lane + width, :] = found.astype(F32).T
        groups = [start // wide for start in (part * chunk, half + part * chunk)]
        low, high = (vwrite_ref[:, g * STATE_SIZE : (g + 1) * STATE_SIZE] for g in groups)
        writes = jnp.where(side == 0, low, high).astype(F32)
        writes = jnp.concatenate([writes, writes, writes, jnp.zeros_like(writes)], axis=0)
        right = jnp.concatenate([writes, ones], axis=1).astype(BF16)
        at = window(side * half + part * chunk, chunk)
        left = tail_ref[:, at].astype(F32).T.astype(BF16)
        both = dot(left, right)
        start = jnp.where(is_owner, turned_ref[rows, :], resident_ref[at, :].astype(F32))
        held_ref[rows, :] = (start * both[:, STATE_SIZE:] + both[:, :STATE_SIZE]).astype(BF16)
        copies.append(pltpu.make_async_copy(held_ref.at[rows, :], new_ref.at[at, :], sems.at[part]))
        copies[-1].start()
    if offset:
        per_slice = slice_ref.shape[1] // STATE_SIZE
        heads = slice_ref.shape[0] // 2
        for k in range(per_slice):
            row = pl.ds(here * per_slice + k, heads, stride=HEAD_DIM)
            got, own = turned_ref[row, :], other_ref[row, :]
            low, high = jnp.where(side == 0, got, own), jnp.where(side == 0, own, got)
            at = slice(k * STATE_SIZE, (k + 1) * STATE_SIZE)
            slice_ref[:, at] = jnp.concatenate([low, high], axis=0).astype(BF16)
    for copy in copies:
        copy.wait()


def states(stage, scattered, owner, resident, prompts, tail, vwrite, shares, seq_count):
    lanes = resident.shape[0]
    half = lanes // 2
    chunk = min(512, half)
    args = [owner, resident, prompts[0], tail, vwrite, *shares]
    scratch = [pltpu.VMEM((half, STATE_SIZE), BF16), pltpu.SemaphoreType.DMA((half // chunk,))]
    new, turned, verify = call(
        functools.partial(states_kernel, stage, scattered, 0),
        "states",
        [
            shape((lanes, STATE_SIZE), BF16),
            shape((half, STATE_SIZE), F32),
            shape(shares[0].shape, BF16),
        ],
        args,
        out_specs=[IN_HBM, WHOLE, WHOLE],
        scratch=scratch,
        flops=lanes * STATE_SIZE * 64,
        moved=lanes * STATE_SIZE * 3,
    )
    args = [owner, resident, prompts[1], tail, vwrite, turned, new]
    new, sliced = call(
        functools.partial(states_kernel, stage, scattered, 1),
        "states",
        [
            shape((lanes, STATE_SIZE), BF16),
            shape((lanes // HEAD_DIM, HEAD_DIM // seq_count * STATE_SIZE), BF16),
        ],
        args,
        specs=[WHOLE] * 6 + [IN_HBM],
        out_specs=[IN_HBM, WHOLE],
        alias={6: 0},
        scratch=[pltpu.VMEM((half, STATE_SIZE), F32)] + scratch,
        flops=lanes * STATE_SIZE * 64,
        moved=lanes * STATE_SIZE * 3,
    )
    return new, verify, sliced


def on_device(
    prefill_input,
    prefill_step,
    write_proj,
    read_proj,
    decay_rate,
    skip_gain,
    resident_state,
    owner_slot,
    draft_ids,
    accepted_len,
    draft_input,
    draft_gate,
    draft_write,
    draft_read,
    draft_step,
    norm_gain,
    out_weight,
):
    span, lanes = prefill_input.shape
    assert span == BLOCK_LEN
    heads = decay_rate.shape[0]
    groups = write_proj.shape[1] // STATE_SIZE
    per_group = heads // groups
    half = lanes // 2
    seq_count, head_count = lax.axis_size("seq"), lax.axis_size("head")
    stages = tree_stages(seq_count)
    core, line, last = stages
    slots = owner_slot.shape[0]
    assert core[0] == 2 and slots == seq_count
    rate, skip, gain = decay_rate[None], skip_gain[None], norm_gain[None]
    resident = resident_state.reshape(lanes, STATE_SIZE)

    inputs = (
        prefill_step.T, rate, skip, owner_slot, draft_ids.T, accepted_len, draft_input, draft_gate,
        draft_write, draft_read, draft_step, write_proj, prefill_input, read_proj, resident, gain,
    )
    passed = 5
    inputs = [in_hbm(value) for value in inputs]
    opened = call(
        functools.partial(open_kernel, core, len(inputs), passed),
        "open_block",
        [
            shape((UP_ROWS, half), BF16),
            shape((groups, span, per_group), F32),
            shape((heads, span), F32),
            shape((heads, span), F32),
            shape((span, 2 * heads), BF16),
            shape((span, 2 * heads), BF16),
            shape((1, lanes), F32),
            shape((DRAFTS, lanes), F32),
            shape((DRAFTS, lanes), F32),
            shape((DRAFTS, groups * STATE_SIZE), BF16),
            shape((DRAFTS, groups * STATE_SIZE), BF16),
            shape((32, lanes), BF16),
            shape((DRAFTS, out_weight.shape[1]), jnp.int32),
            shape((EXTRA, lanes), BF16),
        ]
        + [shape(value.shape, value.dtype) for value in inputs[-passed:]],
        inputs,
        specs=[IN_HBM] * len(inputs),
        scratch=[pltpu.SemaphoreType.DMA((len(inputs),))]
        + [
            (pltpu.SMEM if value.dtype == jnp.int32 else pltpu.VMEM)(value.shape, value.dtype)
            for value in inputs[:-passed]
        ],
        flops=2 * span * lanes * STATE_SIZE * 2,
    )
    sent, run, runt, stept, reach, end, skip_lanes, q1, q2, vread, vwrite, tail, owner, extra = opened[:14]
    writes, x, reads, resident, gain = opened[14:]
    received = swap(sent, "seq", core, 1)
    (own,) = call(
        functools.partial(own_kernel, core),
        "own_message",
        [shape((UP_ROWS, half), BF16)],
        (end, x, writes, extra),
        flops=span * lanes * STATE_SIZE * 2,
    )
    core_parts = [own, received]

    bases, fetched = [], []

    def fill(after):
        if len(bases) < groups:
            wanted = [] if bases else [out_weight]
            base, *found = intra(
                len(bases), run, runt, stept, skip_lanes, x, writes, reads, after, wanted
            )
            bases.append(base)
            fetched.extend(found)
        return bases[-1:]

    def exchange(parts, stage):
        got = {k: swap(parts[k], "seq", stage, k) for k in range(stage[0] - 1, 0, -1)}
        return [parts[0]] + [got[k] for k in range(1, stage[0])]

    line_width = half // line[0]
    split_last = line_width % (last[0] * 128) == 0
    last_width = line_width // last[0] if split_last else line_width
    outs = call(
        functools.partial(up_kernel, core, line, 2),
        "up_line",
        [shape((UP_ROWS, line_width), BF16)] * line[0],
        core_parts,
        flops=half * UP_ROWS * 4,
    )
    line_parts = exchange(outs, line)
    hidden = resident_hidden(resident, vread, q1, q2, gain, [outs[-1]])
    filled = fill([hidden])
    hidden = lax.all_gather(hidden, "seq", axis=0, tiled=True)
    outs = call(
        functools.partial(up_kernel, line, last, line[0]),
        "up_last",
        [shape((UP_ROWS, last_width), BF16)] * (last[0] if split_last else 1),
        line_parts,
        after=filled,
        flops=line_width * UP_ROWS * 4,
    )
    last_parts = exchange(outs if split_last else outs * last[0], last)
    filled = fill([outs[-1]])
    *outs, prompt = call(
        functools.partial(top_kernel, last, last[0]),
        "top",
        [shape((DOWN_ROWS, last_width), BF16)] * (last[0] if split_last else 1)
        + [shape((STATE_SIZE, last_width), BF16)],
        last_parts,
        after=filled,
        flops=last_width * UP_ROWS * 16,
    )

    pieces = exchange(outs, last) if split_last else outs
    filled = fill([outs[-1]])
    *outs, prompt = call(
        functools.partial(down_kernel, line, last, len(pieces), line[0], range(line[0]), True),
        "down_line",
        [shape((DOWN_ROWS, line_width), BF16)] * line[0] + [shape(prompt.shape, BF16)],
        [*pieces, *line_parts, prompt],
        after=filled,
        flops=line_width * UP_ROWS * 8,
    )
    pieces = exchange(outs, line)
    filled = fill([outs[-1]])
    scattered = [line, last] if split_last else [line]
    if split_last:
        prompt = join(exchange([prompt] * last[0], last), 1)
    def down_core(target, after):
        return call(
            functools.partial(down_kernel, core, line, line[0], 2, (target,), False),
            "down_core",
            [shape((DOWN_ROWS, half), BF16)],
            pieces + core_parts,
            after=after,
            flops=half * UP_ROWS * 4,
        )[0]

    sent = down_core(1, filled + [prompt])
    entering = [down_core(0, [sent]), swap(sent, "seq", core, 1)]
    while len(bases) < groups:
        fill([])

    prefill_out, token = finish(core, 0, reach, reads, entering[0], bases, None, entering[:1])
    shares = project(core, owner, hidden, *entering, gain, fetched[0], head_count, [token])
    prefill_out, token = finish(
        core, 1, reach, reads, entering[1], bases, prefill_out, [shares[0], token]
    )
    shares = [shares[0]] + [swap(shares[k], "head", (head_count, 1), k) for k in range(1, head_count)]

    prompt = join(exchange([prompt] * line[0], line), 1, [token, *shares[1:]])
    prompts = exchange([prompt] * 2, core)
    new_state, verify_out, state_slice = states(
        core, scattered, owner, resident, prompts, tail, vwrite, shares, seq_count
    )
    return (
        prefill_out,
        new_state.reshape(1, heads, HEAD_DIM, STATE_SIZE),
        verify_out,
        state_slice,
    )


def solution(mesh):
    return jax.shard_map(
        on_device,
        mesh=mesh,
        in_specs=(
            P("seq", "head"),
            P("seq", "head"),
            P("seq", "head"),
            P("seq", "head"),
            P("head"),
            P("head"),
            P("seq", "head", None, None),
            P(),
            P(),
            P(),
            P("seq", "head"),
            P("seq", "head"),
            P("seq", "head"),
            P("seq", "head"),
            P("seq", "head"),
            P("head"),
            P("head", "seq"),
        ),
        out_specs=(
            P("seq", "head"),
            P("seq", "head", None, None),
            P("head", "seq"),
            P("head", "seq"),
        ),
        check_vma=False,
    )
```

```python
import functools

import jax
import jax.numpy as jnp
from jax import lax
from jax.experimental import pallas as pl
from jax.experimental.pallas import tpu as pltpu
from jax.sharding import PartitionSpec as P

HEAD_DIM = 64
STATE_SIZE = 128
BLOCK_LEN = 256
DRAFTS = 8
EPSILON = 1e-05
EXTRA = 32
UP_ROWS = STATE_SIZE + EXTRA
READ_AT = STATE_SIZE + 16
LOG_AT = STATE_SIZE + 24
DOWN_ROWS = STATE_SIZE + 16

F32 = jnp.float32
BF16 = jnp.bfloat16


def tree_stages(count):
    factors, rest = [], count
    if rest > 1:
        factors.append(2)
        rest //= 2
    inner = 1
    while inner * inner * 4 <= rest:
        inner *= 2
    factors += [inner, rest // inner]
    stages, stride = [], 1
    for factor in factors:
        stages.append((factor, stride))
        stride *= factor
    assert stride == count
    return stages


def swap(value, axis, stage, offset):
    count, stride = lax.axis_size(axis), stage[1]
    return lax.ppermute(value, axis, [(k, k ^ (offset * stride)) for k in range(count)])


def place_of(stage):
    factor, stride = stage
    return lax.rem(lax.div(lax.axis_index("seq"), stride), factor)


def dot(a, b, dims=((1,), (0,))):
    return lax.dot_general(a, b, (dims, ((), ())), preferred_element_type=F32)


def split(value, parts):
    found = []
    for _ in range(parts):
        part = value.astype(BF16).astype(F32)
        found.append(part)
        value = value - part
    return found


def head_mask(rows, heads, lanes, lane0):
    row = lax.broadcasted_iota(jnp.int32, (rows, lanes), 0) & (heads - 1)
    head = lax.shift_right_logical(lax.broadcasted_iota(jnp.int32, (rows, lanes), 1) + lane0, 6)
    return jnp.where(row == head, 1.0, 0.0).astype(BF16)


def window(start, size):
    return pl.ds(pl.multiple_of(start, size), size)


def ordered(kernel, count):
    return lambda *refs: kernel(*refs[count:])


ANYWHERE = pl.BlockSpec(memory_space=pl.ANY)
WHOLE = pl.BlockSpec(memory_space=pltpu.VMEM)
IN_HBM = pl.BlockSpec(memory_space=pltpu.HBM)


def call(
    kernel, name, outs, args, specs=None, out_specs=None, grid=(), after=(), scratch=(), alias=None,
    flops=0, exps=0, moved=None, vmem=32,
):
    if specs is None:
        specs = [WHOLE] * len(args)
    if out_specs is None:
        out_specs = [WHOLE] * len(outs)
    if moved is None:
        moved = sum(a.size * a.dtype.itemsize for a in (*args, *outs))
    first = len(after)
    return pl.pallas_call(
        ordered(kernel, first),
        name=name,
        grid=grid,
        out_shape=outs,
        in_specs=[ANYWHERE] * first + specs,
        out_specs=out_specs,
        scratch_shapes=list(scratch),
        input_output_aliases={first + k: v for k, v in (alias or {}).items()},
        compiler_params=pltpu.CompilerParams(vmem_limit_bytes=vmem * 1024 * 1024),
        cost_estimate=pl.CostEstimate(flops=flops, bytes_accessed=moved, transcendentals=exps),
    )(*after, *args)


def in_hbm(value):
    return pltpu.with_memory_space_constraint(value, pltpu.HBM)


def shape(dims, dtype):
    return jax.ShapeDtypeStruct(dims, dtype)


def open_kernel(stage, count, passed, *refs):
    sources, rest = refs[:count], refs[count:]
    outs, scratch = rest[: 14 + passed], rest[14 + passed :]
    outs, later = outs[:14], list(outs[14:])
    sent_ref, run_ref, runt_ref, stept_ref, reach_ref, end_ref, skip_out = outs[:7]
    q1_ref, q2_ref, vread_ref, vwrite_ref, tail_ref, owner_out, extra_ref = outs[7:]
    sems, held = scratch[0], [*scratch[1:], *later]
    fetches = [
        pltpu.make_async_copy(source, target, sems.at[k])
        for k, (source, target) in enumerate(zip(sources, held))
    ]
    for fetch in fetches:
        fetch.start()
    early = count - passed
    for fetch in fetches[:early]:
        fetch.wait()
    turned_ref, rate_ref, skip_ref, owner_ref, ids_ref, kept_ref = held[:6]
    din_ref, dgate_ref, dwrite_ref, dread_ref, dstep_ref, write_ref, x_ref = held[6:13]
    heads, span = turned_ref.shape
    lanes = x_ref.shape[1]
    groups = write_ref.shape[1] // STATE_SIZE
    per_group = heads // groups
    wide = per_group * HEAD_DIM
    here = lax.axis_index("seq")
    place = place_of(stage)
    owner_out[...] = jnp.zeros(owner_out.shape, jnp.int32) + owner_ref[0]

    step_rows = turned_ref[...]
    stept_ref[...] = step_rows
    pad = (-heads) % 128
    if pad:
        step_rows = jnp.concatenate([step_rows, jnp.zeros((pad, span), F32)], axis=0)
    step = step_rows.T[:, :heads]
    log_decay = -step * rate_ref[...]
    lower = lax.broadcasted_iota(jnp.int32, (span, span), 0) >= lax.broadcasted_iota(
        jnp.int32, (span, span), 1
    )
    lower = jnp.where(lower, 1.0, 0.0).astype(BF16)
    running = sum(dot(lower, part.astype(BF16)) for part in split(log_decay, 3))
    total = running[span - 1 : span, :]
    to_end = jnp.exp(total - running) * step
    wide_run = running
    if pad:
        wide_run = jnp.concatenate([running, jnp.zeros((span, pad), F32)], axis=1)
    runt_ref[...] = wide_run.T[:heads]
    for g in range(groups):
        run_ref[g] = running[:, g * per_group : (g + 1) * per_group]
    reach_ref[...] = jnp.concatenate(split(jnp.exp(running), 2), axis=1).astype(BF16)
    end_ref[...] = jnp.concatenate(split(to_end, 2), axis=1).astype(BF16)

    slots = owner_ref.shape[0]
    request = lax.fori_loop(
        0, slots, lambda r, found: jnp.where(owner_ref[r] == here, r, found), jnp.int32(0)
    )
    kept = kept_ref[request]
    candidates = din_ref.shape[0]
    row = lax.broadcasted_iota(jnp.int32, (DRAFTS, candidates), 0)
    col = lax.broadcasted_iota(jnp.int32, (DRAFTS, candidates), 1)
    pick = jnp.zeros((DRAFTS, candidates), F32)
    for i in range(DRAFTS):
        pick = jnp.where((row == i) & (col == ids_ref[i, request]), 1.0, pick)
    pick = pick.astype(BF16)
    vin = dot(pick, din_ref[...])
    vgate = dot(pick, dgate_ref[...])
    vwrite = dot(pick, dwrite_ref[...]).astype(BF16)
    vread = dot(pick, dread_ref[...]).astype(BF16)
    vwrite_ref[...] = vwrite
    vread_ref[...] = vread
    vstep = sum(dot(pick, part.astype(BF16)) for part in split(dstep_ref[...], 3))
    vlog = -vstep * rate_ref[...]
    index = lax.broadcasted_iota(jnp.int32, (DRAFTS, heads), 0)
    acc = jnp.zeros((1, heads), F32)
    vrun = jnp.zeros((DRAFTS, heads), F32)
    reach = jnp.zeros((1, heads), F32)
    for i in range(DRAFTS):
        acc = acc + vlog[i : i + 1]
        vrun = jnp.where(index == i, acc, vrun)
        reach = jnp.where(i < kept, acc, reach)
    others = jnp.where(index == 0, total, jnp.where(index == 1, skip_ref[...], reach))
    stacked = split(jnp.concatenate([vrun, vstep, others], axis=0), 3)
    stacked = jnp.concatenate(stacked, axis=0).astype(BF16)
    row = lax.broadcasted_iota(jnp.int32, (DRAFTS, wide), 0)
    is_owner = owner_ref[0] == here
    for g in range(groups):
        at = slice(g * wide, (g + 1) * wide)
        spread = dot(stacked, head_mask(heads, heads, wide, g * wide))
        spread = spread[0:24] + spread[24:48] + spread[48:72]
        vrun_l, vstep_l = spread[0:8], spread[8:16]
        total_l, skip_l, reach_l = spread[16:17], spread[17:18], spread[18:19]
        skip_out[:, at] = skip_l
        vin_g = vin[:, at]
        vr = vread[:, g * STATE_SIZE : (g + 1) * STATE_SIZE]
        vw = vwrite[:, g * STATE_SIZE : (g + 1) * STATE_SIZE]
        scores = dot(vr, vw, ((1,), (1,)))
        direct = skip_l * vin_g
        for j in range(DRAFTS):
            decay = jnp.exp(jnp.where(row >= j, vrun_l - vrun_l[j : j + 1], -jnp.inf))
            direct = direct + decay * scores[:, j : j + 1] * (vstep_l[j : j + 1] * vin_g[j : j + 1])
        gate = vgate[:, at]
        gate = gate / (1.0 + jnp.exp(-gate))
        q1 = direct * gate
        q2 = jnp.exp(vrun_l) * gate
        q1_ref[:, at] = q1
        q2_ref[:, at] = q2
        live = jnp.exp(jnp.where(row < kept, reach_l - vrun_l, -jnp.inf)) * vstep_l * vin_g
        keep_l = jnp.concatenate(
            split(jnp.exp(reach_l), 3) + [jnp.zeros((5, wide), F32)], axis=0
        )
        tail_ref[:, at] = jnp.concatenate(split(live, 3) + [keep_l], axis=0).astype(BF16)
        read_l = jnp.concatenate([vr.astype(F32)] * (wide // STATE_SIZE), axis=1)
        mine = jnp.concatenate([q1, q2, read_l], axis=0)
        mine = jnp.where(is_owner, mine, 0.0)
        logs = jnp.concatenate(split(total_l, 3) + [jnp.zeros((5, wide), F32)], axis=0)
        extra_ref[:, at] = jnp.concatenate([mine, logs], axis=0).astype(BF16)

    for fetch in fetches[early : early + 2]:
        fetch.wait()
    fill_message(place ^ 1, end_ref, x_ref, write_ref, extra_ref, sent_ref)
    for fetch in fetches[early + 2 :]:
        fetch.wait()


def fill_message(side, end_ref, x_ref, write_ref, extra_ref, out_ref):
    heads = end_ref.shape[1] // 2
    half = out_ref.shape[1]
    wide = 2 * half // (write_ref.shape[1] // STATE_SIZE)
    chunk = min(wide, half)
    start = side * half
    out_ref[STATE_SIZE:, :] = extra_ref[:, window(start, half)]
    for at in range(0, half, chunk):
        lane0 = start + at
        group = lax.div(lane0, wide)
        scale = dot(end_ref[...], head_mask(2 * heads, heads, chunk, lane0))
        weighted = (x_ref[:, window(lane0, chunk)].astype(F32) * scale).astype(BF16)
        writes = write_ref[:, window(group * STATE_SIZE, STATE_SIZE)]
        writes = writes.astype(F32).T.astype(BF16)
        out_ref[:STATE_SIZE, at : at + chunk] = dot(writes, weighted).astype(BF16)


def own_kernel(stage, end_ref, x_ref, write_ref, extra_ref, out_ref):
    fill_message(place_of(stage), end_ref, x_ref, write_ref, extra_ref, out_ref)


def logs_of(block):
    return block[0:1].astype(F32) + block[1:2].astype(F32) + block[2:3].astype(F32)


def weights_of(logs, place, target):
    spots = [place ^ k for k in range(len(logs))]
    found = []
    for k, spot in enumerate(spots):
        between = jnp.zeros_like(logs[0])
        for other, log in zip(spots, logs):
            if other is not spot:
                between = between + jnp.where((spot < other) & (other < target), log, 0.0)
        found.append(jnp.where(spot < target, jnp.exp(between), 0.0))
    return found


def carry_of(logs, place, target):
    ahead = jnp.zeros_like(logs[0])
    for k, log in enumerate(logs):
        ahead = ahead + jnp.where((place ^ k) < target, log, 0.0)
    return jnp.exp(ahead)


def up_kernel(stage, following, count, *refs):
    parts, outs = refs[:count], refs[count:]
    place, target = place_of(stage), place_of(following)
    width = outs[0].shape[1]
    chunk = min(256, width)
    order = list(range(1, len(outs))) + [0]
    for k in order:
        for at in range(0, width, chunk):
            start = at if len(outs) == 1 else (target ^ k) * width + at
            at_in = window(start, chunk)
            logs = [logs_of(part[LOG_AT:UP_ROWS, at_in]) for part in parts]
            scale = weights_of(logs, place, count)
            state = sum(
                w * part[:STATE_SIZE, at_in].astype(F32) for w, part in zip(scale, parts)
            )
            outs[k][:STATE_SIZE, at : at + chunk] = state.astype(BF16)
            mine = sum(part[STATE_SIZE:UP_ROWS, at_in].astype(F32) for part in parts)
            total = jnp.concatenate(
                split(sum(logs), 3) + [jnp.zeros((5, chunk), F32)], axis=0
            )
            outs[k][STATE_SIZE:, at : at + chunk] = jnp.concatenate(
                [mine[:24], total], axis=0
            ).astype(BF16)


def top_kernel(stage, count, *refs):
    parts, outs, prompt_ref = refs[:count], refs[count:-1], refs[-1]
    place = place_of(stage)
    width = prompt_ref.shape[1]
    logs = [logs_of(part[LOG_AT:UP_ROWS, :]) for part in parts]
    states = [part[:STATE_SIZE, :].astype(F32) for part in parts]
    final = sum(w * s for w, s in zip(weights_of(logs, place, count), states)).astype(BF16)
    prompt_ref[...] = final
    mine = sum(part[STATE_SIZE:LOG_AT, :].astype(F32) for part in parts)
    reads = mine[16:24, :STATE_SIZE].astype(BF16)
    gated = mine[0:8] + mine[8:16] * dot(reads, final)
    gated = jnp.concatenate(split(gated, 2), axis=0).astype(BF16)
    for k in list(range(1, len(outs))) + [0]:
        scale = weights_of(logs, place, place ^ k)
        outs[k][:STATE_SIZE, :] = sum(w * s for w, s in zip(scale, states)).astype(BF16)
        outs[k][STATE_SIZE:, :] = gated


def down_kernel(stage, above, above_count, count, targets, handed, *refs):
    pieces, parts = refs[:above_count], refs[above_count : above_count + count]
    outs = refs[above_count + count :]
    if handed:
        outs[-1][...] = outs[0][...]
        outs = outs[1:-1]
    place, source = place_of(stage), place_of(above)
    width = pieces[0].shape[1]
    chunk = min(256, width)
    for k, out_ref in zip(targets, outs):
        for piece in range(above_count):
            for at in range(0, width, chunk):
                start = at if above_count == 1 else (source ^ piece) * width + at
                at_out = window(start, chunk)
                block = pieces[piece][:, at : at + chunk]
                logs = [logs_of(part[LOG_AT:UP_ROWS, at_out]) for part in parts]
                state = carry_of(logs, place, place ^ k) * block[:STATE_SIZE].astype(F32)
                for w, part in zip(weights_of(logs, place, place ^ k), parts):
                    state = state + w * part[:STATE_SIZE, at_out].astype(F32)
                out_ref[:STATE_SIZE, at_out] = state.astype(BF16)
                out_ref[STATE_SIZE:, at_out] = block[STATE_SIZE:]


def intra_kernel(group, run_ref, runt_ref, stept_ref, skip_ref, x_ref, write_ref, read_ref, *refs):
    fetch = None
    out_ref = refs[0]
    if len(refs) > 1:
        source_ref, out_ref, held_ref, sem = refs
        fetch = pltpu.make_async_copy(source_ref, held_ref, sem)
        fetch.start()
    span, heads = run_ref.shape[1:]
    mid = span // 2
    states = slice(group * STATE_SIZE, (group + 1) * STATE_SIZE)
    scores = dot(read_ref[:, states], write_ref[:, states], ((1,), (1,)))
    row = lax.broadcasted_iota(jnp.int32, (mid, mid), 0)
    causal = row >= lax.broadcasted_iota(jnp.int32, (mid, mid), 1)
    running = run_ref[group]
    low, high = slice(0, mid), slice(mid, span)
    for pair in range(heads // 2):
        found = []
        for k in (2 * pair, 2 * pair + 1):
            h = group * heads + k
            x = x_ref[:, h * HEAD_DIM : (h + 1) * HEAD_DIM]
            t_run, j_run = running[:, k : k + 1], runt_ref[h : h + 1, :]
            step = stept_ref[h : h + 1, :]

            def mixed(rows, cols, masked):
                gap = t_run[rows] - j_run[:, cols]
                if masked:
                    gap = jnp.where(causal, gap, -jnp.inf)
                return (scores[rows, cols] * jnp.exp(gap) * step[:, cols]).astype(BF16)

            top = dot(mixed(low, low, True), x[low])
            bottom = dot(mixed(high, low, False), x[low]) + dot(mixed(high, high, True), x[high])
            found.append(jnp.concatenate([top, bottom], axis=0))
        at = slice(pair * 2 * HEAD_DIM, (pair + 1) * 2 * HEAD_DIM)
        lanes = slice((group * heads + 2 * pair) * HEAD_DIM, (group * heads + 2 * pair + 2) * HEAD_DIM)
        both = jnp.concatenate(found, axis=1)
        out_ref[:, at] = both + skip_ref[:, lanes] * x_ref[:, lanes].astype(F32)
    if fetch is not None:
        fetch.wait()


def intra(group, run, runt, stept, skip, x, write, read, after, wanted=()):
    span, per_group = run.shape[1:]
    wide = per_group * HEAD_DIM
    return call(
        functools.partial(intra_kernel, group),
        "intra",
        [shape((span, wide), F32)] + [shape(value.shape, value.dtype) for value in wanted],
        (run, runt, stept, skip, x, write, read, *map(in_hbm, wanted)),
        specs=[WHOLE] * 7 + [IN_HBM] * len(wanted),
        scratch=[pltpu.SemaphoreType.DMA] * len(wanted),
        after=after,
        flops=per_group * span * span * HEAD_DIM * 2,
        moved=wide * span * 6,
        exps=per_group * span * span * 3 // 4,
    )


def finish_kernel(stage, offset, reach_ref, read_ref, entering_ref, *refs):
    base_refs, (out_ref, token_ref, held_ref, sems) = refs[:-4], refs[-4:]
    if offset:
        base_refs = base_refs[:-1]
    token_ref[...] = jnp.zeros_like(token_ref)
    side = place_of(stage) ^ offset
    heads = reach_ref.shape[1] // 2
    half = held_ref.shape[1]
    wide = 2 * half // len(base_refs)
    chunk = half // sems.shape[0]
    copies = []
    for k, at in enumerate(range(0, half, chunk)):
        found = []
        for lane0 in (at, half + at):
            group = lane0 // wide
            found.append(
                (
                    read_ref[:, group * STATE_SIZE : (group + 1) * STATE_SIZE],
                    base_refs[group][:, lane0 % wide : lane0 % wide + chunk],
                )
            )
        reads, base = (jnp.where(side == 0, a, b) for a, b in zip(*found))
        lane0 = side * half + at
        inter = dot(reads, entering_ref[:STATE_SIZE, at : at + chunk])
        inter = inter * dot(reach_ref[...], head_mask(2 * heads, heads, chunk, lane0))
        held_ref[:, at : at + chunk] = (inter + base).astype(BF16)
        copies.append(
            pltpu.make_async_copy(
                held_ref.at[:, at : at + chunk], out_ref.at[:, window(lane0, chunk)], sems.at[k]
            )
        )
        copies[-1].start()
    for copy in copies:
        copy.wait()


def finish(stage, offset, reach, read, entering, bases, out, after):
    span, half = read.shape[0], entering.shape[1]
    chunk = min(512, half)
    args = [reach, read, entering, *bases]
    specs = [WHOLE] * len(args)
    if offset:
        args.append(out)
        specs.append(IN_HBM)
    return call(
        functools.partial(finish_kernel, stage, offset),
        "finish",
        [shape((span, 2 * half), BF16), shape((8, 128), F32)],
        args,
        specs=specs,
        out_specs=[IN_HBM, WHOLE],
        after=after,
        alias={len(args) - 1: 0} if offset else None,
        scratch=[pltpu.VMEM((span, half), BF16), pltpu.SemaphoreType.DMA((half // chunk,))],
        moved=1,
    )


def resident_kernel(state_ref, vread_ref, q1_ref, q2_ref, gain_ref, out_ref):
    groups = vread_ref.shape[1] // STATE_SIZE
    wide = state_ref.shape[0] // groups
    for g in range(groups):
        at = slice(g * wide, (g + 1) * wide)
        reads = vread_ref[:, g * STATE_SIZE : (g + 1) * STATE_SIZE]
        drawn = dot(reads, state_ref[at, :], ((1,), (1,)))
        gated = q1_ref[:, at] + q2_ref[:, at] * drawn
        out_ref[:, at] = normed(gated, gain_ref[:, at]).astype(BF16)


def normed(gated, gain):
    mean_square = jnp.mean(gated * gated, axis=1, keepdims=True)
    return gated * lax.rsqrt(mean_square + EPSILON) * gain


def resident_hidden(state, vread, q1, q2, gain, after):
    lanes = state.shape[0]
    return call(
        resident_kernel,
        "resident_hidden",
        [shape((DRAFTS, lanes), BF16)],
        (state, vread, q1, q2, gain),
        after=after,
        flops=2 * DRAFTS * lanes * STATE_SIZE,
    )[0]


def hand_on(value, after):
    def copy(value_ref, out_ref):
        out_ref[...] = value_ref[...]

    return call(copy, "hand_on", [shape(value.shape, value.dtype)], [value], after=after)[0]


def join_kernel(axis, *refs):
    out_ref = refs[-1]
    for k, ref in enumerate(refs[:-1]):
        size = ref.shape[axis]
        at = slice(k * size, (k + 1) * size)
        if axis == 0:
            out_ref[at, :] = ref[...]
        else:
            out_ref[:, at] = ref[...]


def join(parts, axis, after=()):
    dims = list(parts[0].shape)
    dims[axis] *= len(parts)
    return call(
        functools.partial(join_kernel, axis), "join", [shape(tuple(dims), parts[0].dtype)], parts, after=after, moved=1
    )[0]


def project_kernel(stages, head_count, *refs):
    owner_ref, own_rows, got_rows, own_ref, got_ref, gain_ref, weight_ref = refs[:7]
    outs = refs[7 : 7 + head_count]
    gated_ref, left_ref, total_ref = refs[7 + head_count :]
    here, head = lax.axis_index("seq"), lax.axis_index("head")
    place = place_of(stages[0])
    half = own_ref.shape[1]
    lanes = weight_ref.shape[0]
    wide = min(1024, lanes)
    rows = own_rows.shape[0]
    for k, ref in enumerate((own_ref, got_ref)):
        both = ref[STATE_SIZE:, :].astype(F32)
        gated_ref[:, window((place ^ k) * half, half)] = both[0:8] + both[8:16]
    left_ref[0:rows, :] = own_rows[...]
    left_ref[rows : 2 * rows, :] = got_rows[...]
    for lane0 in range(0, lanes, wide):
        at = slice(lane0, lane0 + wide)
        hidden = normed(gated_ref[:, at], gain_ref[:, at])
        hidden = jnp.concatenate([hidden, jnp.zeros_like(hidden)], axis=0)
        left_ref[2 * rows :, at] = hidden.astype(BF16)
    total_ref[...] = dot(left_ref[...], weight_ref[...])

    per_head = 2 * rows // DRAFTS // head_count
    offsets = [0]
    for factor, stride in reversed(stages):
        offsets = [a + k * stride for k in range(factor) for a in offsets]
    owner = owner_ref[...]
    tail = total_ref[2 * rows : 2 * rows + DRAFTS, :]
    for k in range(head_count):
        first = (head ^ k) * per_head
        for slot in range(per_head):
            at = slice(slot * DRAFTS, (slot + 1) * DRAFTS)
            offset = here ^ (first + slot)
            block = jnp.int32(0)
            for position, value in enumerate(offsets):
                block = jnp.where(offset == value, position, block)
            drawn = total_ref[window(block * DRAFTS, DRAFTS), :]
            outs[k][at, :] = jnp.where(owner == first + slot, tail, drawn)


def project(stages, owner, own_rows, got_rows, own, got, gain, weight, head_count, after):
    lanes, cols = weight.shape
    rows = 2 * own_rows.shape[0]
    return call(
        functools.partial(project_kernel, stages, head_count),
        "project",
        [shape((rows // head_count, cols), F32)] * head_count,
        (owner, own_rows, got_rows, own, got, gain, weight),
        after=after,
        scratch=[
            pltpu.VMEM((DRAFTS, lanes), F32),
            pltpu.VMEM((rows + 16, lanes), BF16),
            pltpu.VMEM((rows + 16, cols), F32),
        ],
        moved=1,
    )


def states_kernel(stage, scattered, offset, *refs):
    owner_ref, resident_ref, prompt_ref, tail_ref, vwrite_ref = refs[:5]
    here = lax.axis_index("seq")
    side = place_of(stage) ^ offset
    if offset:
        other_ref, _, new_ref, slice_ref, turned_ref, held_ref, sems = refs[5:]
    else:
        share_refs, (new_ref, turned_ref, verify_ref, held_ref, sems) = refs[5:-5], refs[-5:]
        verify_ref[...] = sum(ref[...] for ref in share_refs).astype(BF16)
    half = prompt_ref.shape[1]
    wide = 2 * half // (vwrite_ref.shape[1] // STATE_SIZE)
    blocks = [0]
    for factor, stride in scattered:
        blocks = [a | (k * stride) for k in range(factor) for a in blocks]
    width = half // len(blocks)
    chunk = half // sems.shape[0]
    is_owner = owner_ref[0:1, :STATE_SIZE] == here
    row = lax.broadcasted_iota(jnp.int32, (32, STATE_SIZE), 0)
    ones = jnp.where((row >= 24) & (row < 27), 1.0, 0.0)
    copies = []
    for part in range(sems.shape[0]):
        rows = slice(part * chunk, (part + 1) * chunk)
        for lane in range(part * chunk, (part + 1) * chunk, width):
            spot, size, rest = 0, half, lane
            for factor, stride in scattered:
                size = size // factor
                spot |= rest // size * stride
                rest %= size
            apart = (spot ^ here) & sum((factor - 1) * stride for factor, stride in scattered)
            position = jnp.int32(0)
            for place, value in enumerate(blocks):
                position = jnp.where(apart == value, place, position)
            found = prompt_ref[:, window(position * width, width)]
            turned_ref[lane : lane + width, :] = found.astype(F32).T
        groups = [start // wide for start in (part * chunk, half + part * chunk)]
        low, high = (vwrite_ref[:, g * STATE_SIZE : (g + 1) * STATE_SIZE] for g in groups)
        writes = jnp.where(side == 0, low, high).astype(F32)
        writes = jnp.concatenate([writes, writes, writes, jnp.zeros_like(writes)], axis=0)
        right = jnp.concatenate([writes, ones], axis=1).astype(BF16)
        at = window(side * half + part * chunk, chunk)
        left = tail_ref[:, at].astype(F32).T.astype(BF16)
        both = dot(left, right)
        start = jnp.where(is_owner, turned_ref[rows, :], resident_ref[at, :].astype(F32))
        held_ref[rows, :] = (start * both[:, STATE_SIZE:] + both[:, :STATE_SIZE]).astype(BF16)
        copies.append(pltpu.make_async_copy(held_ref.at[rows, :], new_ref.at[at, :], sems.at[part]))
        copies[-1].start()
    if offset:
        per_slice = slice_ref.shape[1] // STATE_SIZE
        heads = slice_ref.shape[0] // 2
        for k in range(per_slice):
            row = pl.ds(here * per_slice + k, heads, stride=HEAD_DIM)
            got, own = turned_ref[row, :], other_ref[row, :]
            low, high = jnp.where(side == 0, got, own), jnp.where(side == 0, own, got)
            at = slice(k * STATE_SIZE, (k + 1) * STATE_SIZE)
            slice_ref[:, at] = jnp.concatenate([low, high], axis=0).astype(BF16)
    for copy in copies:
        copy.wait()


def states(stage, scattered, owner, resident, prompts, tail, vwrite, shares, seq_count):
    lanes = resident.shape[0]
    half = lanes // 2
    chunk = min(512, half)
    args = [owner, resident, prompts[0], tail, vwrite, *shares]
    scratch = [pltpu.VMEM((half, STATE_SIZE), BF16), pltpu.SemaphoreType.DMA((half // chunk,))]
    new, turned, verify = call(
        functools.partial(states_kernel, stage, scattered, 0),
        "states",
        [
            shape((lanes, STATE_SIZE), BF16),
            shape((half, STATE_SIZE), F32),
            shape(shares[0].shape, BF16),
        ],
        args,
        out_specs=[IN_HBM, WHOLE, WHOLE],
        scratch=scratch,
        flops=lanes * STATE_SIZE * 64,
        moved=lanes * STATE_SIZE * 3,
    )
    args = [owner, resident, prompts[1], tail, vwrite, turned, new]
    new, sliced = call(
        functools.partial(states_kernel, stage, scattered, 1),
        "states",
        [
            shape((lanes, STATE_SIZE), BF16),
            shape((lanes // HEAD_DIM, HEAD_DIM // seq_count * STATE_SIZE), BF16),
        ],
        args,
        specs=[WHOLE] * 6 + [IN_HBM],
        out_specs=[IN_HBM, WHOLE],
        alias={6: 0},
        scratch=[pltpu.VMEM((half, STATE_SIZE), F32)] + scratch,
        flops=lanes * STATE_SIZE * 64,
        moved=lanes * STATE_SIZE * 3,
    )
    return new, verify, sliced


def on_device(
    prefill_input,
    prefill_step,
    write_proj,
    read_proj,
    decay_rate,
    skip_gain,
    resident_state,
    owner_slot,
    draft_ids,
    accepted_len,
    draft_input,
    draft_gate,
    draft_write,
    draft_read,
    draft_step,
    norm_gain,
    out_weight,
):
    span, lanes = prefill_input.shape
    assert span == BLOCK_LEN
    heads = decay_rate.shape[0]
    groups = write_proj.shape[1] // STATE_SIZE
    per_group = heads // groups
    half = lanes // 2
    seq_count, head_count = lax.axis_size("seq"), lax.axis_size("head")
    stages = tree_stages(seq_count)
    core, line, last = stages
    slots = owner_slot.shape[0]
    assert core[0] == 2 and slots == seq_count
    rate, skip, gain = decay_rate[None], skip_gain[None], norm_gain[None]
    resident = resident_state.reshape(lanes, STATE_SIZE)

    inputs = (
        prefill_step.T, rate, skip, owner_slot, draft_ids.T, accepted_len, draft_input, draft_gate,
        draft_write, draft_read, draft_step, write_proj, prefill_input, read_proj, resident, gain,
    )
    passed = 5
    inputs = [in_hbm(value) for value in inputs]
    opened = call(
        functools.partial(open_kernel, core, len(inputs), passed),
        "open_block",
        [
            shape((UP_ROWS, half), BF16),
            shape((groups, span, per_group), F32),
            shape((heads, span), F32),
            shape((heads, span), F32),
            shape((span, 2 * heads), BF16),
            shape((span, 2 * heads), BF16),
            shape((1, lanes), F32),
            shape((DRAFTS, lanes), F32),
            shape((DRAFTS, lanes), F32),
            shape((DRAFTS, groups * STATE_SIZE), BF16),
            shape((DRAFTS, groups * STATE_SIZE), BF16),
            shape((32, lanes), BF16),
            shape((DRAFTS, out_weight.shape[1]), jnp.int32),
            shape((EXTRA, lanes), BF16),
        ]
        + [shape(value.shape, value.dtype) for value in inputs[-passed:]],
        inputs,
        specs=[IN_HBM] * len(inputs),
        scratch=[pltpu.SemaphoreType.DMA((len(inputs),))]
        + [
            (pltpu.SMEM if value.dtype == jnp.int32 else pltpu.VMEM)(value.shape, value.dtype)
            for value in inputs[:-passed]
        ],
        flops=2 * span * lanes * STATE_SIZE * 2,
    )
    sent, run, runt, stept, reach, end, skip_lanes, q1, q2, vread, vwrite, tail, owner, extra = opened[:14]
    writes, x, reads, resident, gain = opened[14:]
    received = swap(sent, "seq", core, 1)
    (own,) = call(
        functools.partial(own_kernel, core),
        "own_message",
        [shape((UP_ROWS, half), BF16)],
        (end, x, writes, extra),
        flops=span * lanes * STATE_SIZE * 2,
    )
    core_parts = [own, received]
    hidden = resident_hidden(resident, vread, q1, q2, gain, [own])

    bases, fetched = [], []

    def fill(after):
        if len(bases) < groups:
            wanted = [] if bases else [out_weight]
            base, *found = intra(
                len(bases), run, runt, stept, skip_lanes, x, writes, reads, after, wanted
            )
            bases.append(base)
            fetched.extend(found)
        return bases[-1:]

    def exchange(parts, stage):
        got = {k: swap(parts[k], "seq", stage, k) for k in range(stage[0] - 1, 0, -1)}
        return [parts[0]] + [got[k] for k in range(1, stage[0])]

    line_width = half // line[0]
    split_last = line_width % (last[0] * 128) == 0
    last_width = line_width // last[0] if split_last else line_width
    outs = call(
        functools.partial(up_kernel, core, line, 2),
        "up_line",
        [shape((UP_ROWS, line_width), BF16)] * line[0],
        core_parts,
        after=[hidden],
        flops=half * UP_ROWS * 4,
    )
    line_parts = exchange(outs, line)
    hiddens = exchange([hand_on(hidden, [outs[-1]])] * last[0], last)
    filled = fill([outs[-1]])
    hidden = join(hiddens, 0)
    outs = call(
        functools.partial(up_kernel, line, last, line[0]),
        "up_last",
        [shape((UP_ROWS, last_width), BF16)] * (last[0] if split_last else 1),
        line_parts,
        after=filled + [hidden],
        flops=line_width * UP_ROWS * 4,
    )
    last_parts = exchange(outs if split_last else outs * last[0], last)
    hiddens = exchange([hand_on(hidden, [outs[-1]])] * line[0], line)
    filled = fill([outs[-1]])
    *outs, prompt = call(
        functools.partial(top_kernel, last, last[0]),
        "top",
        [shape((DOWN_ROWS, last_width), BF16)] * (last[0] if split_last else 1)
        + [shape((STATE_SIZE, last_width), BF16)],
        last_parts,
        after=filled,
        flops=last_width * UP_ROWS * 16,
    )

    pieces = exchange(outs, last) if split_last else outs
    hidden = join(hiddens, 0, [outs[-1]])
    filled = fill([outs[-1], hidden])
    prompt = join(exchange([prompt] * line[0], line), 1)
    *outs, prompt = call(
        functools.partial(down_kernel, line, last, len(pieces), line[0], range(line[0]), True),
        "down_line",
        [shape((DOWN_ROWS, line_width), BF16)] * line[0] + [shape(prompt.shape, BF16)],
        [*pieces, *line_parts, prompt],
        after=filled,
        flops=line_width * UP_ROWS * 8,
    )
    pieces = exchange(outs, line)
    filled = fill([outs[-1]])
    scattered = [line, last] if split_last else [line]
    prompts = exchange([prompt] * last[0], last) if split_last else [prompt]
    def down_core(target, after):
        return call(
            functools.partial(down_kernel, core, line, line[0], 2, (target,), False),
            "down_core",
            [shape((DOWN_ROWS, half), BF16)],
            pieces + core_parts,
            after=after,
            moved=1,
        )[0]

    sent = down_core(1, filled + [prompts[k] for k in (1, last[0] - 1) if split_last])
    entering = [down_core(0, [sent]), swap(sent, "seq", core, 1)]
    while len(bases) < groups:
        fill([])

    prefill_out, token = finish(core, 0, reach, reads, entering[0], bases, None, entering[:1])
    shares = project(
        stages, owner, hidden, swap(hidden, "seq", core, 1), *entering, gain, fetched[0], head_count, [token]
    )
    prefill_out, token = finish(
        core, 1, reach, reads, entering[1], bases, prefill_out, [shares[0], token]
    )
    shares = [shares[0]] + [swap(shares[k], "head", (head_count, 1), k) for k in range(1, head_count)]

    prompt = join(prompts, 1, [token, *shares[1:]])
    prompts = exchange([prompt] * 2, core)
    new_state, verify_out, state_slice = states(
        core, scattered, owner, resident, prompts, tail, vwrite, shares, seq_count
    )
    return (
        prefill_out,
        new_state.reshape(1, heads, HEAD_DIM, STATE_SIZE),
        verify_out,
        state_slice,
    )


def solution(mesh):
    return jax.shard_map(
        on_device,
        mesh=mesh,
        in_specs=(
            P("seq", "head"),
            P("seq", "head"),
            P("seq", "head"),
            P("seq", "head"),
            P("head"),
            P("head"),
            P("seq", "head", None, None),
            P(),
            P(),
            P(),
            P("seq", "head"),
            P("seq", "head"),
            P("seq", "head"),
            P("seq", "head"),
            P("seq", "head"),
            P("head"),
            P("head", "seq"),
        ),
        out_specs=(
            P("seq", "head"),
            P("seq", "head", None, None),
            P("head", "seq"),
            P("head", "seq"),
        ),
        check_vma=False,
    )
```

```python
import functools

import jax
import jax.numpy as jnp
from jax import lax
from jax.experimental import pallas as pl
from jax.experimental.pallas import tpu as pltpu
from jax.sharding import PartitionSpec as P

HEAD_DIM = 64
STATE_SIZE = 128
BLOCK_LEN = 256
DRAFTS = 8
EPSILON = 1e-05
EXTRA = 32
UP_ROWS = STATE_SIZE + EXTRA
READ_AT = STATE_SIZE + 16
LOG_AT = STATE_SIZE + 24
DOWN_ROWS = STATE_SIZE + 16

F32 = jnp.float32
BF16 = jnp.bfloat16


def tree_stages(count):
    factors, rest = [], count
    if rest > 1:
        factors.append(2)
        rest //= 2
    inner = 1
    while inner * inner * 4 <= rest:
        inner *= 2
    factors += [inner, rest // inner]
    stages, stride = [], 1
    for factor in factors:
        stages.append((factor, stride))
        stride *= factor
    assert stride == count
    return stages


def swap(value, axis, stage, offset):
    count, stride = lax.axis_size(axis), stage[1]
    return lax.ppermute(value, axis, [(k, k ^ (offset * stride)) for k in range(count)])


def place_of(stage):
    factor, stride = stage
    return lax.rem(lax.div(lax.axis_index("seq"), stride), factor)


def dot(a, b, dims=((1,), (0,))):
    return lax.dot_general(a, b, (dims, ((), ())), preferred_element_type=F32)


def split(value, parts):
    found = []
    for _ in range(parts):
        part = value.astype(BF16).astype(F32)
        found.append(part)
        value = value - part
    return found


def head_mask(rows, heads, lanes, lane0):
    row = lax.broadcasted_iota(jnp.int32, (rows, lanes), 0) & (heads - 1)
    head = lax.shift_right_logical(lax.broadcasted_iota(jnp.int32, (rows, lanes), 1) + lane0, 6)
    return jnp.where(row == head, 1.0, 0.0).astype(BF16)


def window(start, size):
    return pl.ds(pl.multiple_of(start, size), size)


def ordered(kernel, count):
    return lambda *refs: kernel(*refs[count:])


ANYWHERE = pl.BlockSpec(memory_space=pl.ANY)
WHOLE = pl.BlockSpec(memory_space=pltpu.VMEM)
IN_HBM = pl.BlockSpec(memory_space=pltpu.HBM)


def call(
    kernel, name, outs, args, specs=None, out_specs=None, grid=(), after=(), scratch=(), alias=None,
    flops=0, exps=0, moved=None, vmem=32,
):
    if specs is None:
        specs = [WHOLE] * len(args)
    if out_specs is None:
        out_specs = [WHOLE] * len(outs)
    if moved is None:
        moved = sum(a.size * a.dtype.itemsize for a in (*args, *outs))
    first = len(after)
    return pl.pallas_call(
        ordered(kernel, first),
        name=name,
        grid=grid,
        out_shape=outs,
        in_specs=[ANYWHERE] * first + specs,
        out_specs=out_specs,
        scratch_shapes=list(scratch),
        input_output_aliases={first + k: v for k, v in (alias or {}).items()},
        compiler_params=pltpu.CompilerParams(vmem_limit_bytes=vmem * 1024 * 1024),
        cost_estimate=pl.CostEstimate(flops=flops, bytes_accessed=moved, transcendentals=exps),
    )(*after, *args)


def in_hbm(value):
    return pltpu.with_memory_space_constraint(value, pltpu.HBM)


def shape(dims, dtype):
    return jax.ShapeDtypeStruct(dims, dtype)


def open_kernel(stage, count, passed, *refs):
    sources, rest = refs[:count], refs[count:]
    outs, scratch = rest[: 9 + passed], rest[9 + passed :]
    outs, later = outs[:9], list(outs[9:])
    sent_ref, run_ref, runt_ref, stept_ref, reach_ref, end_ref, pick_ref, kept_out, owner_out = outs
    sems, held = scratch[0], [*scratch[1:], *later]
    fetches = [
        pltpu.make_async_copy(source, target, sems.at[k])
        for k, (source, target) in enumerate(zip(sources, held))
    ]
    for fetch in fetches:
        fetch.start()
    early = count - passed
    for fetch in fetches[:early]:
        fetch.wait()
    turned_ref, rate_ref, owner_ref, ids_ref, kept_ref, write_ref, x_ref = held[:7]
    heads, span = turned_ref.shape
    groups = write_ref.shape[1] // STATE_SIZE
    per_group = heads // groups
    here = lax.axis_index("seq")
    place = place_of(stage)

    step_rows = turned_ref[...]
    stept_ref[...] = step_rows
    pad = (-heads) % 128
    if pad:
        step_rows = jnp.concatenate([step_rows, jnp.zeros((pad, span), F32)], axis=0)
    step = step_rows.T[:, :heads]
    log_decay = -step * rate_ref[...]
    lower = lax.broadcasted_iota(jnp.int32, (span, span), 0) >= lax.broadcasted_iota(
        jnp.int32, (span, span), 1
    )
    lower = jnp.where(lower, 1.0, 0.0).astype(BF16)
    running = sum(dot(lower, part.astype(BF16)) for part in split(log_decay, 3))
    to_end = jnp.exp(running[span - 1 : span, :] - running) * step
    end_ref[...] = jnp.concatenate(split(to_end, 2), axis=1).astype(BF16)

    for fetch in fetches[early : early + 2]:
        fetch.wait()
    fill_message(place ^ 1, end_ref, x_ref, write_ref, sent_ref)

    wide_run = running
    if pad:
        wide_run = jnp.concatenate([running, jnp.zeros((span, pad), F32)], axis=1)
    runt_ref[...] = wide_run.T[:heads]
    for g in range(groups):
        run_ref[g] = running[:, g * per_group : (g + 1) * per_group]
    reach_ref[...] = jnp.concatenate(split(jnp.exp(running), 2), axis=1).astype(BF16)

    slots = owner_ref.shape[0]
    request = lax.fori_loop(
        0, slots, lambda r, found: jnp.where(owner_ref[r] == here, r, found), jnp.int32(0)
    )
    row = lax.broadcasted_iota(jnp.int32, pick_ref.shape, 0)
    col = lax.broadcasted_iota(jnp.int32, pick_ref.shape, 1)
    pick = jnp.zeros(pick_ref.shape, F32)
    for i in range(DRAFTS):
        pick = jnp.where((row == i) & (col == ids_ref[i, request]), 1.0, pick)
    pick_ref[...] = pick
    kept_out[...] = jnp.zeros(kept_out.shape, jnp.int32) + kept_ref[request]
    owner_out[...] = jnp.zeros(owner_out.shape, jnp.int32) + owner_ref[0]
    for fetch in fetches[early + 2 :]:
        fetch.wait()


def draft_kernel(
    stage,
    pick_ref,
    kept_ref,
    owner_ref,
    runt_ref,
    rate_ref,
    skip_ref,
    din_ref,
    dgate_ref,
    dwrite_ref,
    dread_ref,
    dstep_ref,
    own_ref,
    sent_ref,
    skip_out,
    q1_ref,
    q2_ref,
    vread_ref,
    vwrite_ref,
    tail_ref,
    extra_ref,
):
    heads, span = runt_ref.shape
    lanes = din_ref.shape[1]
    groups = dwrite_ref.shape[1] // STATE_SIZE
    wide = lanes // groups
    here = lax.axis_index("seq")
    place = place_of(stage)
    pick = pick_ref[...].astype(BF16)
    vin = dot(pick, din_ref[...])
    vgate = dot(pick, dgate_ref[...])
    vwrite = dot(pick, dwrite_ref[...]).astype(BF16)
    vread = dot(pick, dread_ref[...]).astype(BF16)
    vwrite_ref[...] = vwrite
    vread_ref[...] = vread
    vstep = sum(dot(pick, part.astype(BF16)) for part in split(dstep_ref[...], 3))
    vlog = -vstep * rate_ref[...]
    index = lax.broadcasted_iota(jnp.int32, (DRAFTS, heads), 0)
    kept_heads = kept_ref[:, :1]
    acc = jnp.zeros((1, heads), F32)
    vrun = jnp.zeros((DRAFTS, heads), F32)
    reach = jnp.zeros((1, heads), F32)
    for i in range(DRAFTS):
        acc = acc + vlog[i : i + 1]
        vrun = jnp.where(index == i, acc, vrun)
        reach = jnp.where(i < kept_heads[0:1], acc, reach)
    total = runt_ref[:, span - 128 :]
    if heads < 128:
        total = jnp.concatenate([total, jnp.zeros((128 - heads, 128), F32)], axis=0)
    total = total.T[127:128, :heads]
    others = jnp.where(index == 0, total, jnp.where(index == 1, skip_ref[...], reach))
    stacked = split(jnp.concatenate([vrun, vstep, others], axis=0), 3)
    stacked = jnp.concatenate(stacked, axis=0).astype(BF16)
    row = lax.broadcasted_iota(jnp.int32, (DRAFTS, wide), 0)
    kept = kept_ref[:, :1]
    is_owner = owner_ref[0:1, :1] == here
    for g in range(groups):
        at = slice(g * wide, (g + 1) * wide)
        spread = dot(stacked, head_mask(heads, heads, wide, g * wide))
        spread = spread[0:24] + spread[24:48] + spread[48:72]
        vrun_l, vstep_l = spread[0:8], spread[8:16]
        total_l, skip_l, reach_l = spread[16:17], spread[17:18], spread[18:19]
        skip_out[:, at] = skip_l
        vin_g = vin[:, at]
        vr = vread[:, g * STATE_SIZE : (g + 1) * STATE_SIZE]
        vw = vwrite[:, g * STATE_SIZE : (g + 1) * STATE_SIZE]
        scores = dot(vr, vw, ((1,), (1,)))
        direct = skip_l * vin_g
        for j in range(DRAFTS):
            decay = jnp.exp(jnp.where(row >= j, vrun_l - vrun_l[j : j + 1], -jnp.inf))
            direct = direct + decay * scores[:, j : j + 1] * (vstep_l[j : j + 1] * vin_g[j : j + 1])
        gate = vgate[:, at]
        gate = gate / (1.0 + jnp.exp(-gate))
        q1 = direct * gate
        q2 = jnp.exp(vrun_l) * gate
        q1_ref[:, at] = q1
        q2_ref[:, at] = q2
        live = jnp.exp(jnp.where(row < kept, reach_l - vrun_l, -jnp.inf)) * vstep_l * vin_g
        keep_l = jnp.concatenate(
            split(jnp.exp(reach_l), 3) + [jnp.zeros((5, wide), F32)], axis=0
        )
        tail_ref[:, at] = jnp.concatenate(split(live, 3) + [keep_l], axis=0).astype(BF16)
        read_l = jnp.concatenate([vr.astype(F32)] * (wide // STATE_SIZE), axis=1)
        mine = jnp.concatenate([q1, q2, read_l], axis=0)
        mine = jnp.where(is_owner, mine, 0.0)
        logs = jnp.concatenate(split(total_l, 3) + [jnp.zeros((5, wide), F32)], axis=0)
        extra_ref[:, at] = jnp.concatenate([mine, logs], axis=0).astype(BF16)
    half = lanes // 2
    own_ref[...] = extra_ref[:, window(place * half, half)]
    sent_ref[...] = extra_ref[:, window((place ^ 1) * half, half)]


def fill_message(side, end_ref, x_ref, write_ref, out_ref):
    heads = end_ref.shape[1] // 2
    half = out_ref.shape[1]
    wide = 2 * half // (write_ref.shape[1] // STATE_SIZE)
    chunk = min(wide, half)
    start = side * half
    for at in range(0, half, chunk):
        lane0 = start + at
        group = lax.div(lane0, wide)
        scale = dot(end_ref[...], head_mask(2 * heads, heads, chunk, lane0))
        weighted = (x_ref[:, window(lane0, chunk)].astype(F32) * scale).astype(BF16)
        writes = write_ref[:, window(group * STATE_SIZE, STATE_SIZE)]
        writes = writes.astype(F32).T.astype(BF16)
        out_ref[:, at : at + chunk] = dot(writes, weighted).astype(BF16)


def own_kernel(stage, end_ref, x_ref, write_ref, out_ref):
    fill_message(place_of(stage), end_ref, x_ref, write_ref, out_ref)


def state_of(part, at):
    return part[0][:STATE_SIZE, at].astype(F32)


def extra_of(part, at):
    return (part[1][:, at] if part[2] else part[0][STATE_SIZE:UP_ROWS, at]).astype(F32)


def logs_of(part, at):
    found = extra_of(part, at)[LOG_AT - STATE_SIZE :]
    return found[0:1] + found[1:2] + found[2:3]


def turned(parts):
    return [parts[0], *parts[:0:-1]]


def paired(refs, apart):
    if apart:
        return [(refs[k], refs[k + 1], True) for k in range(0, len(refs), 2)]
    return [(ref, None, False) for ref in refs]


def weights_of(logs, place, target):
    spots = [place ^ k for k in range(len(logs))]
    found = []
    for k, spot in enumerate(spots):
        between = jnp.zeros_like(logs[0])
        for other, log in zip(spots, logs):
            if other is not spot:
                between = between + jnp.where((spot < other) & (other < target), log, 0.0)
        found.append(jnp.where(spot < target, jnp.exp(between), 0.0))
    return found


def carry_of(logs, place, target):
    ahead = jnp.zeros_like(logs[0])
    for k, log in enumerate(logs):
        ahead = ahead + jnp.where((place ^ k) < target, log, 0.0)
    return jnp.exp(ahead)


def up_kernel(stage, following, count, apart, *refs):
    taken = 2 * count if apart else count
    parts, outs = paired(refs[:taken], apart), refs[taken:]
    place, target = place_of(stage), place_of(following)
    width = outs[0].shape[1]
    chunk = min(256, width)
    order = list(range(1, len(outs))) + [0]
    for k in order:
        for at in range(0, width, chunk):
            start = at if len(outs) == 1 else (target ^ k) * width + at
            at_in = window(start, chunk)
            logs = [logs_of(part, at_in) for part in parts]
            scale = weights_of(logs, place, count)
            state = sum(w * state_of(part, at_in) for w, part in zip(scale, parts))
            outs[k][:STATE_SIZE, at : at + chunk] = state.astype(BF16)
            mine = sum(extra_of(part, at_in) for part in parts)
            total = jnp.concatenate(
                split(sum(logs), 3) + [jnp.zeros((5, chunk), F32)], axis=0
            )
            outs[k][STATE_SIZE:, at : at + chunk] = jnp.concatenate(
                [mine[:24], total], axis=0
            ).astype(BF16)


def top_kernel(stage, count, *refs):
    parts, outs, prompt_ref = paired(turned(refs[:count]), False), refs[count:-1], refs[-1]
    whole = slice(None)
    place = place_of(stage)
    width = prompt_ref.shape[1]
    logs = [logs_of(part, whole) for part in parts]
    states = [state_of(part, whole) for part in parts]
    final = sum(w * s for w, s in zip(weights_of(logs, place, count), states)).astype(BF16)
    prompt_ref[...] = final
    mine = sum(extra_of(part, whole) for part in parts)
    reads = mine[16:24, :STATE_SIZE].astype(BF16)
    gated = mine[0:8] + mine[8:16] * dot(reads, final)
    gated = jnp.concatenate(split(gated, 2), axis=0).astype(BF16)
    for k in list(range(1, len(outs))) + [0]:
        scale = weights_of(logs, place, place ^ k)
        outs[k][:STATE_SIZE, :] = sum(w * s for w, s in zip(scale, states)).astype(BF16)
        outs[k][STATE_SIZE:, :] = gated


def down_kernel(stage, above, above_count, count, apart, targets, handed, *refs):
    end = above_count + (2 * count if apart else count)
    pieces, outs = turned(refs[:above_count]), refs[end:]
    parts = paired(refs[above_count:end], apart)
    if handed:
        outs[-1][...] = outs[0][...]
        outs = outs[1:-1]
    place, source = place_of(stage), place_of(above)
    width = pieces[0].shape[1]
    chunk = min(256, width)
    for k, out_ref in zip(targets, outs):
        for piece in range(above_count):
            for at in range(0, width, chunk):
                start = at if above_count == 1 else (source ^ piece) * width + at
                at_out = window(start, chunk)
                block = pieces[piece][:, at : at + chunk]
                logs = [logs_of(part, at_out) for part in parts]
                state = carry_of(logs, place, place ^ k) * block[:STATE_SIZE].astype(F32)
                for w, part in zip(weights_of(logs, place, place ^ k), parts):
                    state = state + w * state_of(part, at_out)
                out_ref[:STATE_SIZE, at_out] = state.astype(BF16)
                out_ref[STATE_SIZE:, at_out] = block[STATE_SIZE:]


def intra_kernel(group, run_ref, runt_ref, stept_ref, skip_ref, x_ref, write_ref, read_ref, *refs):
    fetch = None
    out_ref = refs[0]
    if len(refs) > 1:
        source_ref, out_ref, held_ref, sem = refs
        fetch = pltpu.make_async_copy(source_ref, held_ref, sem)
        fetch.start()
    span, heads = run_ref.shape[1:]
    mid = span // 2
    states = slice(group * STATE_SIZE, (group + 1) * STATE_SIZE)
    scores = dot(read_ref[:, states], write_ref[:, states], ((1,), (1,)))
    row = lax.broadcasted_iota(jnp.int32, (mid, mid), 0)
    causal = row >= lax.broadcasted_iota(jnp.int32, (mid, mid), 1)
    running = run_ref[group]
    low, high = slice(0, mid), slice(mid, span)
    for pair in range(heads // 2):
        found = []
        for k in (2 * pair, 2 * pair + 1):
            h = group * heads + k
            x = x_ref[:, h * HEAD_DIM : (h + 1) * HEAD_DIM]
            t_run, j_run = running[:, k : k + 1], runt_ref[h : h + 1, :]
            step = stept_ref[h : h + 1, :]

            def mixed(rows, cols, masked):
                gap = t_run[rows] - j_run[:, cols]
                if masked:
                    gap = jnp.where(causal, gap, -jnp.inf)
                return (scores[rows, cols] * jnp.exp(gap) * step[:, cols]).astype(BF16)

            top = dot(mixed(low, low, True), x[low])
            bottom = dot(mixed(high, low, False), x[low]) + dot(mixed(high, high, True), x[high])
            found.append(jnp.concatenate([top, bottom], axis=0))
        at = slice(pair * 2 * HEAD_DIM, (pair + 1) * 2 * HEAD_DIM)
        lanes = slice((group * heads + 2 * pair) * HEAD_DIM, (group * heads + 2 * pair + 2) * HEAD_DIM)
        both = jnp.concatenate(found, axis=1)
        out_ref[:, at] = both + skip_ref[:, lanes] * x_ref[:, lanes].astype(F32)
    if fetch is not None:
        fetch.wait()


def intra(group, run, runt, stept, skip, x, write, read, after, wanted=()):
    span, per_group = run.shape[1:]
    wide = per_group * HEAD_DIM
    return call(
        functools.partial(intra_kernel, group),
        "intra",
        [shape((span, wide), F32)] + [shape(value.shape, value.dtype) for value in wanted],
        (run, runt, stept, skip, x, write, read, *map(in_hbm, wanted)),
        specs=[WHOLE] * 7 + [IN_HBM] * len(wanted),
        scratch=[pltpu.SemaphoreType.DMA] * len(wanted),
        after=after,
        flops=per_group * span * span * HEAD_DIM * 2,
        moved=wide * span * 6,
        exps=per_group * span * span * 3 // 4,
    )


def finish_kernel(stage, offset, reach_ref, read_ref, entering_ref, *refs):
    base_refs, (out_ref, token_ref, held_ref, sems) = refs[:-4], refs[-4:]
    if offset:
        base_refs = base_refs[:-1]
    token_ref[...] = jnp.zeros_like(token_ref)
    side = place_of(stage) ^ offset
    heads = reach_ref.shape[1] // 2
    half = held_ref.shape[1]
    wide = 2 * half // len(base_refs)
    chunk = half // sems.shape[0]
    copies = []
    for k, at in enumerate(range(0, half, chunk)):
        found = []
        for lane0 in (at, half + at):
            group = lane0 // wide
            found.append(
                (
                    read_ref[:, group * STATE_SIZE : (group + 1) * STATE_SIZE],
                    base_refs[group][:, lane0 % wide : lane0 % wide + chunk],
                )
            )
        reads, base = (jnp.where(side == 0, a, b) for a, b in zip(*found))
        lane0 = side * half + at
        inter = dot(reads, entering_ref[:STATE_SIZE, at : at + chunk])
        inter = inter * dot(reach_ref[...], head_mask(2 * heads, heads, chunk, lane0))
        held_ref[:, at : at + chunk] = (inter + base).astype(BF16)
        copies.append(
            pltpu.make_async_copy(
                held_ref.at[:, at : at + chunk], out_ref.at[:, window(lane0, chunk)], sems.at[k]
            )
        )
        copies[-1].start()
    for copy in copies:
        copy.wait()


def finish(stage, offset, reach, read, entering, bases, out, after):
    span, half = read.shape[0], entering.shape[1]
    chunk = min(512, half)
    args = [reach, read, entering, *bases]
    specs = [WHOLE] * len(args)
    if offset:
        args.append(out)
        specs.append(IN_HBM)
    return call(
        functools.partial(finish_kernel, stage, offset),
        "finish",
        [shape((span, 2 * half), BF16), shape((8, 128), F32)],
        args,
        specs=specs,
        out_specs=[IN_HBM, WHOLE],
        after=after,
        alias={len(args) - 1: 0} if offset else None,
        scratch=[pltpu.VMEM((span, half), BF16), pltpu.SemaphoreType.DMA((half // chunk,))],
        moved=1,
    )


def resident_kernel(state_ref, vread_ref, q1_ref, q2_ref, gain_ref, out_ref):
    groups = vread_ref.shape[1] // STATE_SIZE
    wide = state_ref.shape[0] // groups
    for g in range(groups):
        at = slice(g * wide, (g + 1) * wide)
        reads = vread_ref[:, g * STATE_SIZE : (g + 1) * STATE_SIZE]
        drawn = dot(reads, state_ref[at, :], ((1,), (1,)))
        gated = q1_ref[:, at] + q2_ref[:, at] * drawn
        out_ref[:, at] = normed(gated, gain_ref[:, at]).astype(BF16)


def normed(gated, gain):
    mean_square = jnp.mean(gated * gated, axis=1, keepdims=True)
    return gated * lax.rsqrt(mean_square + EPSILON) * gain


def resident_hidden(state, vread, q1, q2, gain, after):
    lanes = state.shape[0]
    return call(
        resident_kernel,
        "resident_hidden",
        [shape((DRAFTS, lanes), BF16)],
        (state, vread, q1, q2, gain),
        after=after,
        flops=2 * DRAFTS * lanes * STATE_SIZE,
    )[0]


def hand_on(value, after):
    def copy(value_ref, out_ref):
        out_ref[...] = value_ref[...]

    return call(copy, "hand_on", [shape(value.shape, value.dtype)], [value], after=after)[0]


def join_kernel(axis, *refs):
    out_ref = refs[-1]
    for k, ref in enumerate(refs[:-1]):
        size = ref.shape[axis]
        at = slice(k * size, (k + 1) * size)
        if axis == 0:
            out_ref[at, :] = ref[...]
        else:
            out_ref[:, at] = ref[...]


def join(parts, axis, after=()):
    dims = list(parts[0].shape)
    dims[axis] *= len(parts)
    return call(
        functools.partial(join_kernel, axis), "join", [shape(tuple(dims), parts[0].dtype)], parts, after=after, moved=1
    )[0]


def project_kernel(stages, head_count, *refs):
    owner_ref, own_rows, got_rows, own_ref, got_ref, gain_ref, weight_ref = refs[:7]
    outs = refs[7 : 7 + head_count]
    gated_ref, left_ref, total_ref = refs[7 + head_count :]
    here, head = lax.axis_index("seq"), lax.axis_index("head")
    place = place_of(stages[0])
    half = own_ref.shape[1]
    lanes = weight_ref.shape[0]
    wide = min(1024, lanes)
    rows = own_rows.shape[0]
    for k, ref in enumerate((own_ref, got_ref)):
        both = ref[STATE_SIZE:, :].astype(F32)
        gated_ref[:, window((place ^ k) * half, half)] = both[0:8] + both[8:16]
    left_ref[0:rows, :] = own_rows[...]
    left_ref[rows : 2 * rows, :] = got_rows[...]
    for lane0 in range(0, lanes, wide):
        at = slice(lane0, lane0 + wide)
        hidden = normed(gated_ref[:, at], gain_ref[:, at])
        hidden = jnp.concatenate([hidden, jnp.zeros_like(hidden)], axis=0)
        left_ref[2 * rows :, at] = hidden.astype(BF16)
    total_ref[...] = dot(left_ref[...], weight_ref[...])

    per_head = 2 * rows // DRAFTS // head_count
    offsets = [0]
    for factor, stride in reversed(stages):
        offsets = [a + k * stride for k in range(factor) for a in offsets]
    owner = owner_ref[...]
    tail = total_ref[2 * rows : 2 * rows + DRAFTS, :]
    for k in range(head_count):
        first = (head ^ k) * per_head
        for slot in range(per_head):
            at = slice(slot * DRAFTS, (slot + 1) * DRAFTS)
            offset = here ^ (first + slot)
            block = jnp.int32(0)
            for position, value in enumerate(offsets):
                block = jnp.where(offset == value, position, block)
            drawn = total_ref[window(block * DRAFTS, DRAFTS), :]
            drawn = jnp.where(owner == first + slot, tail, drawn)
            outs[k][at, :] = drawn.astype(outs[k].dtype)


def project(stages, owner, own_rows, got_rows, own, got, gain, weight, head_count, after):
    lanes, cols = weight.shape
    rows = 2 * own_rows.shape[0]
    return call(
        functools.partial(project_kernel, stages, head_count),
        "project",
        [shape((rows // head_count, cols), BF16 if k else F32) for k in range(head_count)],
        (owner, own_rows, got_rows, own, got, gain, weight),
        after=after,
        scratch=[
            pltpu.VMEM((DRAFTS, lanes), F32),
            pltpu.VMEM((rows + 16, lanes), BF16),
            pltpu.VMEM((rows + 16, cols), F32),
        ],
        moved=1,
    )


def states_kernel(stage, scattered, offset, *refs):
    owner_ref, resident_ref, prompt_ref, tail_ref, vwrite_ref = refs[:5]
    here = lax.axis_index("seq")
    side = place_of(stage) ^ offset
    if offset:
        other_ref, _, new_ref, slice_ref, turned_ref, held_ref, sems = refs[5:]
    else:
        share_refs, (new_ref, turned_ref, verify_ref, held_ref, sems) = refs[5:-5], refs[-5:]
        verify_ref[...] = sum(ref[...].astype(F32) for ref in share_refs).astype(BF16)
    half = prompt_ref.shape[1]
    wide = 2 * half // (vwrite_ref.shape[1] // STATE_SIZE)
    blocks = [0]
    for factor, stride in scattered:
        blocks = [a | (k * stride) for k in range(factor) for a in blocks]
    width = half // len(blocks)
    chunk = half // sems.shape[0]
    is_owner = owner_ref[0:1, :STATE_SIZE] == here
    row = lax.broadcasted_iota(jnp.int32, (32, STATE_SIZE), 0)
    ones = jnp.where((row >= 24) & (row < 27), 1.0, 0.0)
    copies = []
    for part in range(sems.shape[0]):
        rows = slice(part * chunk, (part + 1) * chunk)
        for lane in range(part * chunk, (part + 1) * chunk, width):
            spot, size, rest = 0, half, lane
            for factor, stride in scattered:
                size = size // factor
                spot |= rest // size * stride
                rest %= size
            apart = (spot ^ here) & sum((factor - 1) * stride for factor, stride in scattered)
            position = jnp.int32(0)
            for place, value in enumerate(blocks):
                position = jnp.where(apart == value, place, position)
            found = prompt_ref[:, window(position * width, width)]
            turned_ref[lane : lane + width, :] = found.astype(F32).T
        groups = [start // wide for start in (part * chunk, half + part * chunk)]
        low, high = (vwrite_ref[:, g * STATE_SIZE : (g + 1) * STATE_SIZE] for g in groups)
        writes = jnp.where(side == 0, low, high).astype(F32)
        writes = jnp.concatenate([writes, writes, writes, jnp.zeros_like(writes)], axis=0)
        right = jnp.concatenate([writes, ones], axis=1).astype(BF16)
        at = window(side * half + part * chunk, chunk)
        left = tail_ref[:, at].astype(F32).T.astype(BF16)
        both = dot(left, right)
        start = jnp.where(is_owner, turned_ref[rows, :], resident_ref[at, :].astype(F32))
        held_ref[rows, :] = (start * both[:, STATE_SIZE:] + both[:, :STATE_SIZE]).astype(BF16)
        copies.append(pltpu.make_async_copy(held_ref.at[rows, :], new_ref.at[at, :], sems.at[part]))
        copies[-1].start()
    if offset:
        per_slice = slice_ref.shape[1] // STATE_SIZE
        heads = slice_ref.shape[0] // 2
        for k in range(per_slice):
            row = pl.ds(here * per_slice + k, heads, stride=HEAD_DIM)
            got, own = turned_ref[row, :], other_ref[row, :]
            low, high = jnp.where(side == 0, got, own), jnp.where(side == 0, own, got)
            at = slice(k * STATE_SIZE, (k + 1) * STATE_SIZE)
            slice_ref[:, at] = jnp.concatenate([low, high], axis=0).astype(BF16)
    for copy in copies:
        copy.wait()


def states(stage, scattered, owner, resident, prompts, tail, vwrite, shares, seq_count):
    lanes = resident.shape[0]
    half = lanes // 2
    chunk = min(512, half)
    args = [owner, resident, prompts[0], tail, vwrite, *shares]
    scratch = [pltpu.VMEM((half, STATE_SIZE), BF16), pltpu.SemaphoreType.DMA((half // chunk,))]
    new, turned, verify = call(
        functools.partial(states_kernel, stage, scattered, 0),
        "states",
        [
            shape((lanes, STATE_SIZE), BF16),
            shape((half, STATE_SIZE), F32),
            shape(shares[0].shape, BF16),
        ],
        args,
        out_specs=[IN_HBM, WHOLE, WHOLE],
        scratch=scratch,
        flops=lanes * STATE_SIZE * 64,
        moved=lanes * STATE_SIZE * 3,
    )
    args = [owner, resident, prompts[1], tail, vwrite, turned, new]
    new, sliced = call(
        functools.partial(states_kernel, stage, scattered, 1),
        "states",
        [
            shape((lanes, STATE_SIZE), BF16),
            shape((lanes // HEAD_DIM, HEAD_DIM // seq_count * STATE_SIZE), BF16),
        ],
        args,
        specs=[WHOLE] * 6 + [IN_HBM],
        out_specs=[IN_HBM, WHOLE],
        alias={6: 0},
        scratch=[pltpu.VMEM((half, STATE_SIZE), F32)] + scratch,
        flops=lanes * STATE_SIZE * 64,
        moved=lanes * STATE_SIZE * 3,
    )
    return new, verify, sliced


def on_device(
    prefill_input,
    prefill_step,
    write_proj,
    read_proj,
    decay_rate,
    skip_gain,
    resident_state,
    owner_slot,
    draft_ids,
    accepted_len,
    draft_input,
    draft_gate,
    draft_write,
    draft_read,
    draft_step,
    norm_gain,
    out_weight,
):
    span, lanes = prefill_input.shape
    assert span == BLOCK_LEN
    heads = decay_rate.shape[0]
    groups = write_proj.shape[1] // STATE_SIZE
    per_group = heads // groups
    half = lanes // 2
    seq_count, head_count = lax.axis_size("seq"), lax.axis_size("head")
    stages = tree_stages(seq_count)
    core, line, last = stages
    slots = owner_slot.shape[0]
    assert core[0] == 2 and slots == seq_count
    rate, skip, gain = decay_rate[None], skip_gain[None], norm_gain[None]
    resident = resident_state.reshape(lanes, STATE_SIZE)

    inputs = [
        in_hbm(value)
        for value in (
            prefill_step.T, rate, owner_slot, draft_ids.T, accepted_len, write_proj, prefill_input,
            draft_input, draft_gate, draft_write, draft_read, draft_step, skip, rate, read_proj, resident,
            gain,
        )
    ]
    passed = 12
    opened = call(
        functools.partial(open_kernel, core, len(inputs), passed),
        "open_block",
        [
            shape((STATE_SIZE, half), BF16),
            shape((groups, span, per_group), F32),
            shape((heads, span), F32),
            shape((heads, span), F32),
            shape((span, 2 * heads), BF16),
            shape((span, 2 * heads), BF16),
            shape((DRAFTS, draft_input.shape[0]), F32),
            shape((DRAFTS, 128), jnp.int32),
            shape((DRAFTS, out_weight.shape[1]), jnp.int32),
        ]
        + [shape(value.shape, value.dtype) for value in inputs[-passed:]],
        inputs,
        specs=[IN_HBM] * len(inputs),
        scratch=[pltpu.SemaphoreType.DMA((len(inputs),))]
        + [
            (pltpu.SMEM if value.dtype == jnp.int32 else pltpu.VMEM)(value.shape, value.dtype)
            for value in inputs[:-passed]
        ],
        flops=span * lanes * STATE_SIZE * 2,
    )
    sent, run, runt, stept, reach, end, pick, kept, owner = opened[:9]
    writes, x, din, dgate, dwrite, dread, dstep, skip, rate, reads, resident, gain = opened[9:]
    received = swap(sent, "seq", core, 1)
    own_extra, sent_extra, skip_lanes, q1, q2, vread, vwrite, tail = call(
        functools.partial(draft_kernel, core),
        "draft_rows",
        [
            shape((EXTRA, half), BF16),
            shape((EXTRA, half), BF16),
            shape((1, lanes), F32),
            shape((DRAFTS, lanes), F32),
            shape((DRAFTS, lanes), F32),
            shape((DRAFTS, groups * STATE_SIZE), BF16),
            shape((DRAFTS, groups * STATE_SIZE), BF16),
            shape((32, lanes), BF16),
        ],
        (pick, kept, owner, runt, rate, skip, din, dgate, dwrite, dread, dstep),
        after=[sent],
        scratch=[pltpu.VMEM((EXTRA, lanes), BF16)],
        flops=DRAFTS * lanes * 100,
    )
    received_extra = swap(sent_extra, "seq", core, 1)
    (own,) = call(
        functools.partial(own_kernel, core),
        "own_message",
        [shape((STATE_SIZE, half), BF16)],
        (end, x, writes),
        after=[sent_extra],
        flops=span * lanes * STATE_SIZE,
    )
    core_parts = [own, own_extra, received, received_extra]
    hidden = resident_hidden(resident, vread, q1, q2, gain, [own])

    bases, fetched = [], []

    def fill(after):
        if len(bases) < groups:
            wanted = [] if bases else [out_weight]
            base, *found = intra(
                len(bases), run, runt, stept, skip_lanes, x, writes, reads, after, wanted
            )
            bases.append(base)
            fetched.extend(found)
        return bases[-1:]

    def exchange(parts, stage):
        got = {k: swap(parts[k], "seq", stage, k) for k in range(1, stage[0])}
        return [parts[0]] + [got[k] for k in range(1, stage[0])]

    line_width = half // line[0]
    split_last = line_width % (last[0] * 128) == 0
    last_width = line_width // last[0] if split_last else line_width
    outs = call(
        functools.partial(up_kernel, core, line, 2, True),
        "up_line",
        [shape((UP_ROWS, line_width), BF16)] * line[0],
        core_parts,
        after=[hidden],
        flops=half * UP_ROWS * 4,
    )
    line_parts = exchange(outs, line)
    hiddens = exchange([hand_on(hidden, [outs[-1]])] * last[0], last)
    filled = fill([outs[-1]])
    outs = call(
        functools.partial(up_kernel, line, last, line[0], False),
        "up_last",
        [shape((UP_ROWS, last_width), BF16)] * (last[0] if split_last else 1),
        line_parts,
        after=filled + hiddens[2:],
        flops=line_width * UP_ROWS * 4,
    )
    last_parts = exchange(outs if split_last else outs * last[0], last)
    filled = fill([outs[-1]])
    *outs, prompt = call(
        functools.partial(top_kernel, last, last[0]),
        "top",
        [shape((DOWN_ROWS, last_width), BF16)] * (last[0] if split_last else 1)
        + [shape((STATE_SIZE, last_width), BF16)],
        turned(last_parts),
        after=filled,
        flops=last_width * UP_ROWS * 16,
    )

    pieces = exchange(outs, last) if split_last else outs
    hidden = join(hiddens, 0, [outs[-1]])
    hiddens = exchange([hidden] * line[0], line)
    filled = fill([outs[-1]])
    prompts = exchange([prompt] * line[0], line)
    outs = call(
        functools.partial(down_kernel, line, last, len(pieces), line[0], False, range(line[0]), False),
        "down_line",
        [shape((DOWN_ROWS, line_width), BF16)] * line[0],
        [*turned(pieces), *line_parts],
        after=filled + prompts[1:] + hiddens[1:],
        flops=line_width * UP_ROWS * 8,
    )
    pieces = exchange(outs, line)
    filled = fill([outs[-1]])
    scattered = [line, last] if split_last else [line]
    hidden = join(hiddens, 0, [outs[-1]])
    prompt = join(prompts, 1, [outs[-1]])
    prompts = exchange([prompt] * last[0], last) if split_last else [prompt]
    def down_core(target, after):
        return call(
            functools.partial(down_kernel, core, line, line[0], 2, True, (target,), False),
            "down_core",
            [shape((DOWN_ROWS, half), BF16)],
            turned(pieces) + core_parts,
            after=after,
            moved=1,
        )[0]

    sent = down_core(1, filled + [prompts[k] for k in (1, last[0] - 1) if split_last])
    entering = [down_core(0, [sent]), swap(sent, "seq", core, 1)]
    while len(bases) < groups:
        fill([])

    prefill_out, token = finish(core, 0, reach, reads, entering[0], bases, None, entering[:1])
    shares = project(
        stages, owner, hidden, swap(hidden, "seq", core, 1), *entering, gain, fetched[0], head_count, [token]
    )
    prefill_out, token = finish(
        core, 1, reach, reads, entering[1], bases, prefill_out, [shares[0], token]
    )
    shares = [shares[0]] + [swap(shares[k], "head", (head_count, 1), k) for k in range(1, head_count)]

    prompt = join(prompts, 1, [token, *shares[1:]])
    prompts = exchange([prompt] * 2, core)
    new_state, verify_out, state_slice = states(
        core, scattered, owner, resident, prompts, tail, vwrite, shares, seq_count
    )
    return (
        prefill_out,
        new_state.reshape(1, heads, HEAD_DIM, STATE_SIZE),
        verify_out,
        state_slice,
    )


def solution(mesh):
    return jax.shard_map(
        on_device,
        mesh=mesh,
        in_specs=(
            P("seq", "head"),
            P("seq", "head"),
            P("seq", "head"),
            P("seq", "head"),
            P("head"),
            P("head"),
            P("seq", "head", None, None),
            P(),
            P(),
            P(),
            P("seq", "head"),
            P("seq", "head"),
            P("seq", "head"),
            P("seq", "head"),
            P("seq", "head"),
            P("head"),
            P("head", "seq"),
        ),
        out_specs=(
            P("seq", "head"),
            P("seq", "head", None, None),
            P("head", "seq"),
            P("head", "seq"),
        ),
        check_vma=False,
    )
```

```python
import functools

import jax
import jax.numpy as jnp
from jax import lax
from jax.experimental import pallas as pl
from jax.experimental.pallas import tpu as pltpu
from jax.sharding import PartitionSpec as P

HEAD_DIM = 64
STATE_SIZE = 128
BLOCK_LEN = 256
DRAFTS = 8
EPSILON = 1e-05
EXTRA = 32
UP_ROWS = STATE_SIZE + EXTRA
READ_AT = STATE_SIZE + 16
LOG_AT = STATE_SIZE + 24
DOWN_ROWS = STATE_SIZE + 16

F32 = jnp.float32
BF16 = jnp.bfloat16


def tree_stages(count):
    factors, rest = [], count
    if rest > 1:
        factors.append(2)
        rest //= 2
    inner = 1
    while inner * inner * 4 <= rest:
        inner *= 2
    factors += [inner, rest // inner]
    stages, stride = [], 1
    for factor in factors:
        stages.append((factor, stride))
        stride *= factor
    assert stride == count
    return stages


def swap(value, axis, stage, offset):
    count, stride = lax.axis_size(axis), stage[1]
    return lax.ppermute(value, axis, [(k, k ^ (offset * stride)) for k in range(count)])


def shift(value, axis, stage, step):
    count, (factor, stride) = lax.axis_size(axis), stage
    pairs = [
        (k, k + step * stride) for k in range(count) if 0 <= k // stride % factor + step < factor
    ]
    return lax.ppermute(value, axis, pairs)


def chain(value, stage):
    before, after = [], []
    up = down = value
    for _ in range(1, stage[0]):
        up, down = shift(up, "seq", stage, 1), shift(down, "seq", stage, -1)
        before.append(up)
        after.append(down)
    return before, after


def place_of(stage):
    factor, stride = stage
    return lax.rem(lax.div(lax.axis_index("seq"), stride), factor)


def dot(a, b, dims=((1,), (0,))):
    return lax.dot_general(a, b, (dims, ((), ())), preferred_element_type=F32)


def split(value, parts):
    found = []
    for _ in range(parts):
        part = value.astype(BF16).astype(F32)
        found.append(part)
        value = value - part
    return found


def head_mask(rows, heads, lanes, lane0):
    row = lax.broadcasted_iota(jnp.int32, (rows, lanes), 0) & (heads - 1)
    head = lax.shift_right_logical(lax.broadcasted_iota(jnp.int32, (rows, lanes), 1) + lane0, 6)
    return jnp.where(row == head, 1.0, 0.0).astype(BF16)


def window(start, size):
    return pl.ds(pl.multiple_of(start, size), size)


def ordered(kernel, count):
    return lambda *refs: kernel(*refs[count:])


ANYWHERE = pl.BlockSpec(memory_space=pl.ANY)
WHOLE = pl.BlockSpec(memory_space=pltpu.VMEM)
IN_HBM = pl.BlockSpec(memory_space=pltpu.HBM)


def call(
    kernel, name, outs, args, specs=None, out_specs=None, grid=(), after=(), scratch=(), alias=None,
    flops=0, exps=0, moved=None, vmem=32,
):
    if specs is None:
        specs = [WHOLE] * len(args)
    if out_specs is None:
        out_specs = [WHOLE] * len(outs)
    if moved is None:
        moved = sum(a.size * a.dtype.itemsize for a in (*args, *outs))
    first = len(after)
    return pl.pallas_call(
        ordered(kernel, first),
        name=name,
        grid=grid,
        out_shape=outs,
        in_specs=[ANYWHERE] * first + specs,
        out_specs=out_specs,
        scratch_shapes=list(scratch),
        input_output_aliases={first + k: v for k, v in (alias or {}).items()},
        compiler_params=pltpu.CompilerParams(vmem_limit_bytes=vmem * 1024 * 1024),
        cost_estimate=pl.CostEstimate(flops=flops, bytes_accessed=moved, transcendentals=exps),
    )(*after, *args)


def in_hbm(value):
    return pltpu.with_memory_space_constraint(value, pltpu.HBM)


def shape(dims, dtype):
    return jax.ShapeDtypeStruct(dims, dtype)


def open_kernel(stage, count, passed, *refs):
    sources, rest = refs[:count], refs[count:]
    outs, scratch = rest[: 9 + passed], rest[9 + passed :]
    outs, later = outs[:9], list(outs[9:])
    sent_ref, run_ref, runt_ref, stept_ref, reach_ref, end_ref, pick_ref, kept_out, owner_out = outs
    sems, held = scratch[0], [*scratch[1:], *later]
    fetches = [
        pltpu.make_async_copy(source, target, sems.at[k])
        for k, (source, target) in enumerate(zip(sources, held))
    ]
    for fetch in fetches:
        fetch.start()
    early = count - passed
    for fetch in fetches[:early]:
        fetch.wait()
    turned_ref, rate_ref, owner_ref, ids_ref, kept_ref, write_ref, x_ref = held[:7]
    heads, span = turned_ref.shape
    groups = write_ref.shape[1] // STATE_SIZE
    per_group = heads // groups
    here = lax.axis_index("seq")
    place = place_of(stage)

    step_rows = turned_ref[...]
    stept_ref[...] = step_rows
    pad = (-heads) % 128
    if pad:
        step_rows = jnp.concatenate([step_rows, jnp.zeros((pad, span), F32)], axis=0)
    step = step_rows.T[:, :heads]
    log_decay = -step * rate_ref[...]
    lower = lax.broadcasted_iota(jnp.int32, (span, span), 0) >= lax.broadcasted_iota(
        jnp.int32, (span, span), 1
    )
    lower = jnp.where(lower, 1.0, 0.0).astype(BF16)
    running = sum(dot(lower, part.astype(BF16)) for part in split(log_decay, 3))
    to_end = jnp.exp(running[span - 1 : span, :] - running) * step
    end_ref[...] = jnp.concatenate(split(to_end, 2), axis=1).astype(BF16)

    for fetch in fetches[early : early + 2]:
        fetch.wait()
    fill_message(place ^ 1, end_ref, x_ref, write_ref, sent_ref)

    wide_run = running
    if pad:
        wide_run = jnp.concatenate([running, jnp.zeros((span, pad), F32)], axis=1)
    runt_ref[...] = wide_run.T[:heads]
    for g in range(groups):
        run_ref[g] = running[:, g * per_group : (g + 1) * per_group]
    reach_ref[...] = jnp.concatenate(split(jnp.exp(running), 2), axis=1).astype(BF16)

    slots = owner_ref.shape[0]
    request = lax.fori_loop(
        0, slots, lambda r, found: jnp.where(owner_ref[r] == here, r, found), jnp.int32(0)
    )
    row = lax.broadcasted_iota(jnp.int32, pick_ref.shape, 0)
    col = lax.broadcasted_iota(jnp.int32, pick_ref.shape, 1)
    pick = jnp.zeros(pick_ref.shape, F32)
    for i in range(DRAFTS):
        pick = jnp.where((row == i) & (col == ids_ref[i, request]), 1.0, pick)
    pick_ref[...] = pick
    kept_out[...] = jnp.zeros(kept_out.shape, jnp.int32) + kept_ref[request]
    owner_out[...] = jnp.zeros(owner_out.shape, jnp.int32) + owner_ref[0]
    for fetch in fetches[early + 2 :]:
        fetch.wait()


def draft_kernel(
    stage,
    pick_ref,
    kept_ref,
    owner_ref,
    runt_ref,
    rate_ref,
    skip_ref,
    din_ref,
    dgate_ref,
    dwrite_ref,
    dread_ref,
    dstep_ref,
    own_ref,
    sent_ref,
    skip_out,
    q1_ref,
    q2_ref,
    vread_ref,
    vwrite_ref,
    tail_ref,
    extra_ref,
):
    heads, span = runt_ref.shape
    lanes = din_ref.shape[1]
    groups = dwrite_ref.shape[1] // STATE_SIZE
    wide = lanes // groups
    here = lax.axis_index("seq")
    place = place_of(stage)
    pick = pick_ref[...].astype(BF16)
    vin = dot(pick, din_ref[...])
    vgate = dot(pick, dgate_ref[...])
    vwrite = dot(pick, dwrite_ref[...]).astype(BF16)
    vread = dot(pick, dread_ref[...]).astype(BF16)
    vwrite_ref[...] = vwrite
    vread_ref[...] = vread
    vstep = sum(dot(pick, part.astype(BF16)) for part in split(dstep_ref[...], 3))
    vlog = -vstep * rate_ref[...]
    index = lax.broadcasted_iota(jnp.int32, (DRAFTS, heads), 0)
    kept_heads = kept_ref[:, :1]
    acc = jnp.zeros((1, heads), F32)
    vrun = jnp.zeros((DRAFTS, heads), F32)
    reach = jnp.zeros((1, heads), F32)
    for i in range(DRAFTS):
        acc = acc + vlog[i : i + 1]
        vrun = jnp.where(index == i, acc, vrun)
        reach = jnp.where(i < kept_heads[0:1], acc, reach)
    total = runt_ref[:, span - 128 :]
    if heads < 128:
        total = jnp.concatenate([total, jnp.zeros((128 - heads, 128), F32)], axis=0)
    total = total.T[127:128, :heads]
    others = jnp.where(index == 0, total, jnp.where(index == 1, skip_ref[...], reach))
    stacked = split(jnp.concatenate([vrun, vstep, others], axis=0), 3)
    stacked = jnp.concatenate(stacked, axis=0).astype(BF16)
    row = lax.broadcasted_iota(jnp.int32, (DRAFTS, wide), 0)
    kept = kept_ref[:, :1]
    is_owner = owner_ref[0:1, :1] == here
    for g in range(groups):
        at = slice(g * wide, (g + 1) * wide)
        spread = dot(stacked, head_mask(heads, heads, wide, g * wide))
        spread = spread[0:24] + spread[24:48] + spread[48:72]
        vrun_l, vstep_l = spread[0:8], spread[8:16]
        total_l, skip_l, reach_l = spread[16:17], spread[17:18], spread[18:19]
        skip_out[:, at] = skip_l
        vin_g = vin[:, at]
        vr = vread[:, g * STATE_SIZE : (g + 1) * STATE_SIZE]
        vw = vwrite[:, g * STATE_SIZE : (g + 1) * STATE_SIZE]
        scores = dot(vr, vw, ((1,), (1,)))
        direct = skip_l * vin_g
        for j in range(DRAFTS):
            decay = jnp.exp(jnp.where(row >= j, vrun_l - vrun_l[j : j + 1], -jnp.inf))
            direct = direct + decay * scores[:, j : j + 1] * (vstep_l[j : j + 1] * vin_g[j : j + 1])
        gate = vgate[:, at]
        gate = gate / (1.0 + jnp.exp(-gate))
        q1 = direct * gate
        q2 = jnp.exp(vrun_l) * gate
        q1_ref[:, at] = q1
        q2_ref[:, at] = q2
        live = jnp.exp(jnp.where(row < kept, reach_l - vrun_l, -jnp.inf)) * vstep_l * vin_g
        keep_l = jnp.concatenate(
            split(jnp.exp(reach_l), 3) + [jnp.zeros((5, wide), F32)], axis=0
        )
        tail_ref[:, at] = jnp.concatenate(split(live, 3) + [keep_l], axis=0).astype(BF16)
        read_l = jnp.concatenate([vr.astype(F32)] * (wide // STATE_SIZE), axis=1)
        mine = jnp.concatenate([q1, q2, read_l], axis=0)
        mine = jnp.where(is_owner, mine, 0.0)
        logs = jnp.concatenate(split(total_l, 3) + [jnp.zeros((5, wide), F32)], axis=0)
        extra_ref[:, at] = jnp.concatenate([mine, logs], axis=0).astype(BF16)
    half = lanes // 2
    own_ref[...] = extra_ref[:, window(place * half, half)]
    sent_ref[...] = extra_ref[:, window((place ^ 1) * half, half)]


def fill_message(side, end_ref, x_ref, write_ref, out_ref):
    heads = end_ref.shape[1] // 2
    half = out_ref.shape[1]
    wide = 2 * half // (write_ref.shape[1] // STATE_SIZE)
    chunk = min(wide, half)
    start = side * half
    for at in range(0, half, chunk):
        lane0 = start + at
        group = lax.div(lane0, wide)
        scale = dot(end_ref[...], head_mask(2 * heads, heads, chunk, lane0))
        weighted = (x_ref[:, window(lane0, chunk)].astype(F32) * scale).astype(BF16)
        writes = write_ref[:, window(group * STATE_SIZE, STATE_SIZE)]
        writes = writes.astype(F32).T.astype(BF16)
        out_ref[:, at : at + chunk] = dot(writes, weighted).astype(BF16)


def own_kernel(stage, end_ref, x_ref, write_ref, out_ref):
    fill_message(place_of(stage), end_ref, x_ref, write_ref, out_ref)


def state_of(part, at):
    return part[0][:STATE_SIZE, at].astype(F32)


def extra_of(part, at):
    return (part[1][:, at] if part[2] else part[0][STATE_SIZE:UP_ROWS, at]).astype(F32)


def logs_of(part, at):
    found = extra_of(part, at)[LOG_AT - STATE_SIZE :]
    return found[0:1] + found[1:2] + found[2:3]


def turned(parts):
    return [parts[0], *parts[:0:-1]]


def paired(refs, apart):
    if apart:
        return [(refs[k], refs[k + 1], True) for k in range(0, len(refs), 2)]
    return [(ref, None, False) for ref in refs]


def weights_of(logs, place, target):
    spots = [place ^ k for k in range(len(logs))]
    found = []
    for k, spot in enumerate(spots):
        between = jnp.zeros_like(logs[0])
        for other, log in zip(spots, logs):
            if other is not spot:
                between = between + jnp.where((spot < other) & (other < target), log, 0.0)
        found.append(jnp.where(spot < target, jnp.exp(between), 0.0))
    return found


def carry_of(logs, place, target):
    ahead = jnp.zeros_like(logs[0])
    for k, log in enumerate(logs):
        ahead = ahead + jnp.where((place ^ k) < target, log, 0.0)
    return jnp.exp(ahead)


def up_kernel(stage, following, count, apart, *refs):
    taken = 2 * count if apart else count
    parts, outs = paired(refs[:taken], apart), refs[taken:]
    place, target = place_of(stage), place_of(following)
    width = outs[0].shape[1]
    chunk = min(256, width)
    order = list(range(1, len(outs))) + [0]
    for k in order:
        for at in range(0, width, chunk):
            start = at if len(outs) == 1 else (target ^ k) * width + at
            at_in = window(start, chunk)
            logs = [logs_of(part, at_in) for part in parts]
            scale = weights_of(logs, place, count)
            state = sum(w * state_of(part, at_in) for w, part in zip(scale, parts))
            outs[k][:STATE_SIZE, at : at + chunk] = state.astype(BF16)
            mine = sum(extra_of(part, at_in) for part in parts)
            total = jnp.concatenate(
                split(sum(logs), 3) + [jnp.zeros((5, chunk), F32)], axis=0
            )
            outs[k][STATE_SIZE:, at : at + chunk] = jnp.concatenate(
                [mine[:24], total], axis=0
            ).astype(BF16)


def top_kernel(stage, count, *refs):
    parts, outs, prompt_ref = paired(turned(refs[:count]), False), refs[count:-1], refs[-1]
    whole = slice(None)
    place = place_of(stage)
    width = prompt_ref.shape[1]
    logs = [logs_of(part, whole) for part in parts]
    states = [state_of(part, whole) for part in parts]
    final = sum(w * s for w, s in zip(weights_of(logs, place, count), states)).astype(BF16)
    prompt_ref[...] = final
    mine = sum(extra_of(part, whole) for part in parts)
    reads = mine[16:24, :STATE_SIZE].astype(BF16)
    gated = mine[0:8] + mine[8:16] * dot(reads, final)
    gated = jnp.concatenate(split(gated, 2), axis=0).astype(BF16)
    for k in list(range(1, len(outs))) + [0]:
        scale = weights_of(logs, place, place ^ k)
        outs[k][:STATE_SIZE, :] = sum(w * s for w, s in zip(scale, states)).astype(BF16)
        outs[k][STATE_SIZE:, :] = gated


def down_kernel(stage, above, above_count, count, apart, targets, handed, *refs):
    end = above_count + (2 * count if apart else count)
    pieces, outs = turned(refs[:above_count]), refs[end:]
    parts = paired(refs[above_count:end], apart)
    if handed:
        outs[-1][...] = outs[0][...]
        outs = outs[1:-1]
    place, source = place_of(stage), place_of(above)
    width = pieces[0].shape[1]
    chunk = min(256, width)
    gated_ref = outs[1] if apart and len(outs) > 1 else None
    for k, out_ref in zip(targets, outs):
        for piece in range(above_count):
            for at in range(0, width, chunk):
                start = at if above_count == 1 else (source ^ piece) * width + at
                at_out = window(start, chunk)
                block = pieces[piece][:, at : at + chunk]
                logs = [logs_of(part, at_out) for part in parts]
                state = carry_of(logs, place, place ^ k) * block[:STATE_SIZE].astype(F32)
                for w, part in zip(weights_of(logs, place, place ^ k), parts):
                    state = state + w * state_of(part, at_out)
                out_ref[:STATE_SIZE, at_out] = state.astype(BF16)
                if gated_ref is not None:
                    gated_ref[:, at_out] = block[STATE_SIZE:]
                elif out_ref.shape[0] > STATE_SIZE:
                    out_ref[STATE_SIZE:, at_out] = block[STATE_SIZE:]


def intra_kernel(group, run_ref, runt_ref, stept_ref, skip_ref, x_ref, write_ref, read_ref, *refs):
    fetch = None
    out_ref = refs[0]
    if len(refs) > 1:
        source_ref, out_ref, held_ref, sem = refs
        wanted = held_ref.shape[0]
        fetch = pltpu.make_async_copy(
            source_ref.at[group * wanted : (group + 1) * wanted, :], held_ref, sem
        )
        fetch.start()
    span, heads = run_ref.shape[1:]
    mid = span // 2
    states = slice(group * STATE_SIZE, (group + 1) * STATE_SIZE)
    scores = dot(read_ref[:, states], write_ref[:, states], ((1,), (1,)))
    row = lax.broadcasted_iota(jnp.int32, (mid, mid), 0)
    causal = row >= lax.broadcasted_iota(jnp.int32, (mid, mid), 1)
    running = run_ref[group]
    low, high = slice(0, mid), slice(mid, span)
    for pair in range(heads // 2):
        found = []
        for k in (2 * pair, 2 * pair + 1):
            h = group * heads + k
            x = x_ref[:, h * HEAD_DIM : (h + 1) * HEAD_DIM]
            t_run, j_run = running[:, k : k + 1], runt_ref[h : h + 1, :]
            step = stept_ref[h : h + 1, :]

            def mixed(rows, cols, masked):
                gap = t_run[rows] - j_run[:, cols]
                if masked:
                    gap = jnp.where(causal, gap, -jnp.inf)
                return (scores[rows, cols] * jnp.exp(gap) * step[:, cols]).astype(BF16)

            top = dot(mixed(low, low, True), x[low])
            bottom = dot(mixed(high, low, False), x[low]) + dot(mixed(high, high, True), x[high])
            found.append(jnp.concatenate([top, bottom], axis=0))
        at = slice(pair * 2 * HEAD_DIM, (pair + 1) * 2 * HEAD_DIM)
        lanes = slice((group * heads + 2 * pair) * HEAD_DIM, (group * heads + 2 * pair + 2) * HEAD_DIM)
        both = jnp.concatenate(found, axis=1)
        out_ref[:, at] = both + skip_ref[:, lanes] * x_ref[:, lanes].astype(F32)
    if fetch is not None:
        fetch.wait()


def intra(group, run, runt, stept, skip, x, write, read, weight, after):
    span, per_group = run.shape[1:]
    wide = per_group * HEAD_DIM
    return call(
        functools.partial(intra_kernel, group),
        "intra",
        [shape((span, wide), F32), shape((wide, weight.shape[1]), weight.dtype)],
        (run, runt, stept, skip, x, write, read, in_hbm(weight)),
        specs=[WHOLE] * 7 + [IN_HBM],
        scratch=[pltpu.SemaphoreType.DMA],
        after=after,
        flops=per_group * span * span * HEAD_DIM * 2,
        moved=wide * span * 6,
        exps=per_group * span * span * 3 // 4,
    )


def finish_kernel(stage, reach_ref, read_ref, own_ref, got_ref, *refs):
    base_refs, (out_ref, token_ref, held_ref, sems) = refs[:-4], refs[-4:]
    token_ref[...] = jnp.zeros_like(token_ref)
    place = place_of(stage)
    heads = reach_ref.shape[1] // 2
    lanes = held_ref.shape[1]
    wide = lanes // len(base_refs)
    half = lanes // 2
    chunk = lanes // sems.shape[0]
    copies = []
    for k, lane0 in enumerate(range(0, lanes, chunk)):
        group, at = lane0 // wide, lane0 % half
        at_in, at_out = slice(at, at + chunk), slice(lane0, lane0 + chunk)
        entering = jnp.where(place == lane0 // half, own_ref[:, at_in], got_ref[:, at_in])
        inter = dot(read_ref[:, group * STATE_SIZE : (group + 1) * STATE_SIZE], entering)
        inter = inter * dot(reach_ref[...], head_mask(2 * heads, heads, chunk, lane0))
        base = base_refs[group][:, lane0 % wide : lane0 % wide + chunk]
        held_ref[:, at_out] = (inter + base).astype(BF16)
        copies.append(
            pltpu.make_async_copy(held_ref.at[:, at_out], out_ref.at[:, at_out], sems.at[k])
        )
        copies[-1].start()
    for copy in copies:
        copy.wait()


def finish(stage, reach, read, own, got, bases):
    span = read.shape[0]
    lanes = 2 * own.shape[1]
    chunk = min(512, own.shape[1])
    return call(
        functools.partial(finish_kernel, stage),
        "finish",
        [shape((span, lanes), BF16), shape((8, 128), F32)],
        (reach, read, own, got, *bases),
        out_specs=[IN_HBM, WHOLE],
        scratch=[pltpu.VMEM((span, lanes), BF16), pltpu.SemaphoreType.DMA((lanes // chunk,))],
        moved=1,
    )


def resident_kernel(state_ref, vread_ref, q1_ref, q2_ref, gain_ref, out_ref):
    groups = vread_ref.shape[1] // STATE_SIZE
    wide = state_ref.shape[0] // groups
    for g in range(groups):
        at = slice(g * wide, (g + 1) * wide)
        reads = vread_ref[:, g * STATE_SIZE : (g + 1) * STATE_SIZE]
        drawn = dot(reads, state_ref[at, :], ((1,), (1,)))
        gated = q1_ref[:, at] + q2_ref[:, at] * drawn
        out_ref[:, at] = normed(gated, gain_ref[:, at]).astype(BF16)


def normed(gated, gain):
    mean_square = jnp.mean(gated * gated, axis=1, keepdims=True)
    return gated * lax.rsqrt(mean_square + EPSILON) * gain


def resident_hidden(state, vread, q1, q2, gain, after):
    lanes = state.shape[0]
    return call(
        resident_kernel,
        "resident_hidden",
        [shape((DRAFTS, lanes), BF16)],
        (state, vread, q1, q2, gain),
        after=after,
        flops=2 * DRAFTS * lanes * STATE_SIZE,
    )[0]


def hand_on(value, after):
    def copy(value_ref, out_ref):
        out_ref[...] = value_ref[...]

    return call(copy, "hand_on", [shape(value.shape, value.dtype)], [value], after=after)[0]


def line_up_kernel(stage, axis, *refs):
    refs, out_ref = refs[:-1], refs[-1]
    place = place_of(stage)
    size = refs[0].shape[1]
    others = (len(refs) - 1) // 2

    def put(ref, spot):
        if axis == 0:
            out_ref[spot] = ref[...]
        else:
            out_ref[:, window(spot * size, size)] = ref[...]

    put(refs[0], place)
    for k in range(1, others + 1):
        pl.when(place - k >= 0)(functools.partial(put, refs[k], place - k))
        pl.when(place + k < stage[0])(functools.partial(put, refs[others + k], place + k))


def line_up(stage, axis, own, chained, after=()):
    if axis == 0:
        dims = (stage[0], *own.shape)
    else:
        dims = (own.shape[0], stage[0] * own.shape[1])
    return call(
        functools.partial(line_up_kernel, stage, axis),
        "line_up",
        [shape(dims, own.dtype)],
        (own, *chained[0], *chained[1]),
        after=after,
        moved=1,
    )[0]


def stack_kernel(*refs):
    for k, ref in enumerate(refs[:-1]):
        refs[-1][k] = ref[...]


def stack(parts, after=()):
    dims = (len(parts), *parts[0].shape)
    return call(stack_kernel, "stack", [shape(dims, parts[0].dtype)], parts, after=after, moved=1)[0]


def join_kernel(axis, *refs):
    out_ref = refs[-1]
    for k, ref in enumerate(refs[:-1]):
        size = ref.shape[axis]
        at = slice(k * size, (k + 1) * size)
        if axis == 0:
            out_ref[at, :] = ref[...]
        else:
            out_ref[:, at] = ref[...]


def join(parts, axis, after=()):
    dims = list(parts[0].shape)
    dims[axis] *= len(parts)
    return call(
        functools.partial(join_kernel, axis), "join", [shape(tuple(dims), parts[0].dtype)], parts, after=after, moved=1
    )[0]


def project_kernel(stages, head_count, pieces, *refs):
    owner_ref, own_rows, got_rows, own_ref, got_ref, gain_ref = refs[:6]
    weight_refs, refs = refs[6 : 6 + pieces], refs[6 + pieces :]
    outs, (gated_ref, left_ref, total_ref) = refs[:head_count], refs[head_count:]
    head = lax.axis_index("head")
    core, line, last = stages
    place = place_of(core)
    half = own_ref.shape[1]
    lanes = 2 * half
    wide = lanes // pieces
    for k, ref in enumerate((own_ref, got_ref)):
        both = ref[...].astype(F32)
        gated_ref[:, window((place ^ k) * half, half)] = both[0:8] + both[8:16]
    row = 0
    for ref in (own_rows, got_rows):
        for k in range(line[0]):
            for z in range(last[0]):
                left_ref[row : row + DRAFTS, :] = ref[k, z]
                row += DRAFTS
    norm = min(1024, lanes)
    for lane0 in range(0, lanes, norm):
        at = slice(lane0, lane0 + norm)
        hidden = normed(gated_ref[:, at], gain_ref[:, at])
        hidden = jnp.concatenate([hidden, jnp.zeros_like(hidden)], axis=0)
        left_ref[row:, at] = hidden.astype(BF16)
    total_ref[...] = sum(
        dot(left_ref[:, k * wide : (k + 1) * wide], ref[...]) for k, ref in enumerate(weight_refs)
    )

    per_head = row // DRAFTS // head_count
    owner = owner_ref[...]
    tail = total_ref[row : row + DRAFTS, :]
    for k in list(range(1, head_count)) + [0]:
        first = (head ^ k) * per_head
        for slot in range(per_head):
            at = slice(slot * DRAFTS, (slot + 1) * DRAFTS)
            spot = first + slot
            block = (lax.rem(spot, 2) ^ place) * line[0]
            block = block + (lax.rem(lax.div(spot, line[1]), line[0]) ^ place_of(line))
            block = block * last[0] + lax.div(spot, last[1])
            drawn = total_ref[window(block * DRAFTS, DRAFTS), :]
            drawn = jnp.where(owner == spot, tail, drawn)
            outs[k][at, :] = drawn.astype(outs[k].dtype)


def project(stages, owner, own_rows, got_rows, own, got, gain, weights, head_count):
    lanes, cols = gain.shape[1], weights[0].shape[1]
    rows = 2 * own_rows.size // lanes
    return call(
        functools.partial(project_kernel, stages, head_count, len(weights)),
        "project",
        [shape((rows // head_count, cols), BF16 if k else F32) for k in range(head_count)],
        (owner, own_rows, got_rows, own, got, gain, *weights),
        scratch=[
            pltpu.VMEM((DRAFTS, lanes), F32),
            pltpu.VMEM((rows + 16, lanes), BF16),
            pltpu.VMEM((rows + 16, cols), F32),
        ],
        moved=1,
    )


def states_kernel(stage, scattered, offset, *refs):
    owner_ref, resident_ref, prompt_ref, tail_ref, vwrite_ref = refs[:5]
    here = lax.axis_index("seq")
    side = place_of(stage) ^ offset
    if offset:
        other_ref, _, new_ref, slice_ref, turned_ref, held_ref, sems = refs[5:]
    else:
        share_refs, (new_ref, turned_ref, verify_ref, held_ref, sems) = refs[5:-5], refs[-5:]
        verify_ref[...] = sum(ref[...].astype(F32) for ref in share_refs).astype(BF16)
    half = prompt_ref.shape[1]
    wide = 2 * half // (vwrite_ref.shape[1] // STATE_SIZE)
    width = half
    for factor, _ in scattered:
        width //= factor
    chunk = half // sems.shape[0]
    is_owner = owner_ref[0:1, :STATE_SIZE] == here
    row = lax.broadcasted_iota(jnp.int32, (32, STATE_SIZE), 0)
    ones = jnp.where((row >= 24) & (row < 27), 1.0, 0.0)
    copies = []
    for step in range(sems.shape[0]):
        rows = slice(step * chunk, (step + 1) * chunk)
        for lane in range(step * chunk, (step + 1) * chunk, width):
            line = scattered[0]
            part = half // line[0]
            position = (lane // part) ^ place_of(line)
            if len(scattered) > 1:
                position = lane % part // width * line[0] + position
            found = prompt_ref[:, window(position * width, width)]
            turned_ref[lane : lane + width, :] = found.astype(F32).T
        groups = [start // wide for start in (step * chunk, half + step * chunk)]
        low, high = (vwrite_ref[:, g * STATE_SIZE : (g + 1) * STATE_SIZE] for g in groups)
        writes = jnp.where(side == 0, low, high).astype(F32)
        writes = jnp.concatenate([writes, writes, writes, jnp.zeros_like(writes)], axis=0)
        right = jnp.concatenate([writes, ones], axis=1).astype(BF16)
        at = window(side * half + step * chunk, chunk)
        left = tail_ref[:, at].astype(F32).T.astype(BF16)
        both = dot(left, right)
        start = jnp.where(is_owner, turned_ref[rows, :], resident_ref[at, :].astype(F32))
        held_ref[rows, :] = (start * both[:, STATE_SIZE:] + both[:, :STATE_SIZE]).astype(BF16)
        copies.append(pltpu.make_async_copy(held_ref.at[rows, :], new_ref.at[at, :], sems.at[step]))
        copies[-1].start()
    if offset:
        per_slice = slice_ref.shape[1] // STATE_SIZE
        heads = slice_ref.shape[0] // 2
        for k in range(per_slice):
            row = pl.ds(here * per_slice + k, heads, stride=HEAD_DIM)
            got, own = turned_ref[row, :], other_ref[row, :]
            low, high = jnp.where(side == 0, got, own), jnp.where(side == 0, own, got)
            at = slice(k * STATE_SIZE, (k + 1) * STATE_SIZE)
            slice_ref[:, at] = jnp.concatenate([low, high], axis=0).astype(BF16)
    for copy in copies:
        copy.wait()


def states(stage, scattered, owner, resident, prompts, tail, vwrite, shares, seq_count):
    lanes = resident.shape[0]
    half = lanes // 2
    chunk = min(512, half)
    args = [owner, resident, prompts[0], tail, vwrite, *shares]
    scratch = [pltpu.VMEM((half, STATE_SIZE), BF16), pltpu.SemaphoreType.DMA((half // chunk,))]
    new, turned, verify = call(
        functools.partial(states_kernel, stage, scattered, 0),
        "states",
        [
            shape((lanes, STATE_SIZE), BF16),
            shape((half, STATE_SIZE), F32),
            shape(shares[0].shape, BF16),
        ],
        args,
        out_specs=[IN_HBM, WHOLE, WHOLE],
        scratch=scratch,
        flops=lanes * STATE_SIZE * 64,
        moved=lanes * STATE_SIZE * 3,
    )
    args = [owner, resident, prompts[1], tail, vwrite, turned, new]
    new, sliced = call(
        functools.partial(states_kernel, stage, scattered, 1),
        "states",
        [
            shape((lanes, STATE_SIZE), BF16),
            shape((lanes // HEAD_DIM, HEAD_DIM // seq_count * STATE_SIZE), BF16),
        ],
        args,
        specs=[WHOLE] * 6 + [IN_HBM],
        out_specs=[IN_HBM, WHOLE],
        alias={6: 0},
        scratch=[pltpu.VMEM((half, STATE_SIZE), F32)] + scratch,
        flops=lanes * STATE_SIZE * 64,
        moved=lanes * STATE_SIZE * 3,
    )
    return new, verify, sliced


def on_device(
    prefill_input,
    prefill_step,
    write_proj,
    read_proj,
    decay_rate,
    skip_gain,
    resident_state,
    owner_slot,
    draft_ids,
    accepted_len,
    draft_input,
    draft_gate,
    draft_write,
    draft_read,
    draft_step,
    norm_gain,
    out_weight,
):
    span, lanes = prefill_input.shape
    assert span == BLOCK_LEN
    heads = decay_rate.shape[0]
    groups = write_proj.shape[1] // STATE_SIZE
    per_group = heads // groups
    half = lanes // 2
    seq_count, head_count = lax.axis_size("seq"), lax.axis_size("head")
    stages = tree_stages(seq_count)
    core, line, last = stages
    slots = owner_slot.shape[0]
    assert core[0] == 2 and slots == seq_count
    rate, skip, gain = decay_rate[None], skip_gain[None], norm_gain[None]
    resident = resident_state.reshape(lanes, STATE_SIZE)

    inputs = [
        in_hbm(value)
        for value in (
            prefill_step.T, rate, owner_slot, draft_ids.T, accepted_len, write_proj, prefill_input,
            draft_input, draft_gate, draft_write, draft_read, draft_step, skip, rate, read_proj, resident,
            gain,
        )
    ]
    passed = 12
    opened = call(
        functools.partial(open_kernel, core, len(inputs), passed),
        "open_block",
        [
            shape((STATE_SIZE, half), BF16),
            shape((groups, span, per_group), F32),
            shape((heads, span), F32),
            shape((heads, span), F32),
            shape((span, 2 * heads), BF16),
            shape((span, 2 * heads), BF16),
            shape((DRAFTS, draft_input.shape[0]), F32),
            shape((DRAFTS, 128), jnp.int32),
            shape((DRAFTS, out_weight.shape[1]), jnp.int32),
        ]
        + [shape(value.shape, value.dtype) for value in inputs[-passed:]],
        inputs,
        specs=[IN_HBM] * len(inputs),
        scratch=[pltpu.SemaphoreType.DMA((len(inputs),))]
        + [
            (pltpu.SMEM if value.dtype == jnp.int32 else pltpu.VMEM)(value.shape, value.dtype)
            for value in inputs[:-passed]
        ],
        flops=span * lanes * STATE_SIZE * 2,
    )
    sent, run, runt, stept, reach, end, pick, kept, owner = opened[:9]
    writes, x, din, dgate, dwrite, dread, dstep, skip, rate, reads, resident, gain = opened[9:]
    received = swap(sent, "seq", core, 1)
    own_extra, sent_extra, skip_lanes, q1, q2, vread, vwrite, tail = call(
        functools.partial(draft_kernel, core),
        "draft_rows",
        [
            shape((EXTRA, half), BF16),
            shape((EXTRA, half), BF16),
            shape((1, lanes), F32),
            shape((DRAFTS, lanes), F32),
            shape((DRAFTS, lanes), F32),
            shape((DRAFTS, groups * STATE_SIZE), BF16),
            shape((DRAFTS, groups * STATE_SIZE), BF16),
            shape((32, lanes), BF16),
        ],
        (pick, kept, owner, runt, rate, skip, din, dgate, dwrite, dread, dstep),
        after=[sent],
        scratch=[pltpu.VMEM((EXTRA, lanes), BF16)],
        flops=DRAFTS * lanes * 100,
    )
    received_extra = swap(sent_extra, "seq", core, 1)
    (own,) = call(
        functools.partial(own_kernel, core),
        "own_message",
        [shape((STATE_SIZE, half), BF16)],
        (end, x, writes),
        after=[sent_extra],
        flops=span * lanes * STATE_SIZE,
    )
    core_parts = [own, own_extra, received, received_extra]
    hidden = resident_hidden(resident, vread, q1, q2, gain, [own])

    bases, fetched = [], []

    def fill(after):
        if len(bases) < groups:
            base, weight = intra(
                len(bases), run, runt, stept, skip_lanes, x, writes, reads, out_weight, after
            )
            bases.append(base)
            fetched.append(weight)
        return bases[-1:]

    def exchange(parts, stage):
        got = {k: swap(parts[k], "seq", stage, k) for k in range(1, stage[0])}
        return [parts[0]] + [got[k] for k in range(1, stage[0])]

    line_width = half // line[0]
    split_last = line_width % (last[0] * 128) == 0
    last_width = line_width // last[0] if split_last else line_width
    outs = call(
        functools.partial(up_kernel, core, line, 2, True),
        "up_line",
        [shape((UP_ROWS, line_width), BF16)] * line[0],
        core_parts,
        after=[hidden],
        flops=half * UP_ROWS * 4,
    )
    line_parts = exchange(outs, line)
    hidden = hand_on(hidden, [outs[-1]])
    hiddens = chain(hidden, last)
    filled = fill([outs[-1]])
    arrived = [side[k] for side in hiddens for k in range(len(side) - 1)]
    outs = call(
        functools.partial(up_kernel, line, last, line[0], False),
        "up_last",
        [shape((UP_ROWS, last_width), BF16)] * (last[0] if split_last else 1),
        line_parts,
        after=filled + arrived,
        flops=line_width * UP_ROWS * 4,
    )
    last_parts = exchange(outs if split_last else outs * last[0], last)
    filled = fill([outs[-1]])
    *outs, prompt = call(
        functools.partial(top_kernel, last, last[0]),
        "top",
        [shape((DOWN_ROWS, last_width), BF16)] * (last[0] if split_last else 1)
        + [shape((STATE_SIZE, last_width), BF16)],
        turned(last_parts),
        after=filled,
        flops=last_width * UP_ROWS * 16,
    )

    pieces = exchange(outs, last) if split_last else outs
    hidden = line_up(last, 0, hidden, hiddens, [outs[-1]])
    hiddens = exchange([hidden] * line[0], line)
    filled = fill([outs[-1]])
    prompts = exchange([prompt] * line[0], line)
    outs = call(
        functools.partial(down_kernel, line, last, len(pieces), line[0], False, range(line[0]), False),
        "down_line",
        [shape((DOWN_ROWS, line_width), BF16)] * line[0],
        [*turned(pieces), *line_parts],
        after=filled + prompts[1:] + hiddens[1:],
        flops=line_width * UP_ROWS * 8,
    )
    pieces = exchange(outs, line)
    hidden = stack(hiddens, [outs[-1]])
    hiddens = [hidden, swap(hidden, "seq", core, 1)]
    scattered = [line, last] if split_last else [line]
    prompt = join(prompts, 1, [outs[-1]])
    filled = fill([outs[-1]]) + hiddens[1:]
    if split_last:
        prompts = chain(prompt, last)
        filled += [side[k] for side in prompts for k in range(len(side) - 1)]

    def down_core(target, after):
        return call(
            functools.partial(down_kernel, core, line, line[0], 2, True, (target,), False),
            "down_core",
            [shape((STATE_SIZE, half), BF16)] + [shape((16, half), BF16)] * target,
            turned(pieces) + core_parts,
            after=after,
            moved=1,
        )

    sent, gated = down_core(1, filled)
    received_gated, received = swap(gated, "seq", core, 1), swap(sent, "seq", core, 1)
    while len(bases) < groups:
        fill([])

    shares = project(stages, owner, *hiddens, gated, received_gated, gain, fetched, head_count)
    (entering,) = down_core(0, shares[:1])
    prefill_out, token = finish(core, reach, reads, entering, received, bases)
    shares = [shares[0]] + [swap(shares[k], "head", (head_count, 1), k) for k in range(1, head_count)]

    if split_last:
        prompt = line_up(last, 1, prompt, prompts, [token, *shares[1:]])
    prompts = exchange([prompt] * 2, core)
    new_state, verify_out, state_slice = states(
        core, scattered, owner, resident, prompts, tail, vwrite, shares, seq_count
    )
    return (
        prefill_out,
        new_state.reshape(1, heads, HEAD_DIM, STATE_SIZE),
        verify_out,
        state_slice,
    )


def solution(mesh):
    return jax.shard_map(
        on_device,
        mesh=mesh,
        in_specs=(
            P("seq", "head"),
            P("seq", "head"),
            P("seq", "head"),
            P("seq", "head"),
            P("head"),
            P("head"),
            P("seq", "head", None, None),
            P(),
            P(),
            P(),
            P("seq", "head"),
            P("seq", "head"),
            P("seq", "head"),
            P("seq", "head"),
            P("seq", "head"),
            P("head"),
            P("head", "seq"),
        ),
        out_specs=(
            P("seq", "head"),
            P("seq", "head", None, None),
            P("head", "seq"),
            P("head", "seq"),
        ),
        check_vma=False,
    )
```

```python
import functools

import jax
import jax.numpy as jnp
from jax import lax
from jax.experimental import pallas as pl
from jax.experimental.pallas import tpu as pltpu
from jax.sharding import PartitionSpec as P

HEAD_DIM = 64
STATE_SIZE = 128
BLOCK_LEN = 256
DRAFTS = 8
EPSILON = 1e-05
EXTRA = 32
UP_ROWS = STATE_SIZE + EXTRA
READ_AT = STATE_SIZE + 16
LOG_AT = STATE_SIZE + 24
DOWN_ROWS = STATE_SIZE + 16

F32 = jnp.float32
BF16 = jnp.bfloat16


def tree_stages(count):
    factors, rest = [], count
    if rest > 1:
        factors.append(2)
        rest //= 2
    inner = 1
    while inner * inner * 4 <= rest:
        inner *= 2
    factors += [inner, rest // inner]
    stages, stride = [], 1
    for factor in factors:
        stages.append((factor, stride))
        stride *= factor
    assert stride == count
    return stages


def swap(value, axis, stage, offset):
    count, stride = lax.axis_size(axis), stage[1]
    return lax.ppermute(value, axis, [(k, k ^ (offset * stride)) for k in range(count)])


def place_of(stage):
    factor, stride = stage
    return lax.rem(lax.div(lax.axis_index("seq"), stride), factor)


def dot(a, b, dims=((1,), (0,))):
    return lax.dot_general(a, b, (dims, ((), ())), preferred_element_type=F32)


def split(value, parts):
    found = []
    for _ in range(parts):
        part = value.astype(BF16).astype(F32)
        found.append(part)
        value = value - part
    return found


def head_mask(rows, heads, lanes, lane0):
    row = lax.broadcasted_iota(jnp.int32, (rows, lanes), 0) & (heads - 1)
    head = lax.shift_right_logical(lax.broadcasted_iota(jnp.int32, (rows, lanes), 1) + lane0, 6)
    return jnp.where(row == head, 1.0, 0.0).astype(BF16)


def window(start, size):
    return pl.ds(pl.multiple_of(start, size), size)


def ordered(kernel, count):
    return lambda *refs: kernel(*refs[count:])


ANYWHERE = pl.BlockSpec(memory_space=pl.ANY)
WHOLE = pl.BlockSpec(memory_space=pltpu.VMEM)
IN_HBM = pl.BlockSpec(memory_space=pltpu.HBM)


def call(
    kernel, name, outs, args, specs=None, out_specs=None, grid=(), after=(), scratch=(), alias=None,
    flops=0, exps=0, moved=None, vmem=32,
):
    if specs is None:
        specs = [WHOLE] * len(args)
    if out_specs is None:
        out_specs = [WHOLE] * len(outs)
    if moved is None:
        moved = sum(a.size * a.dtype.itemsize for a in (*args, *outs))
    first = len(after)
    return pl.pallas_call(
        ordered(kernel, first),
        name=name,
        grid=grid,
        out_shape=outs,
        in_specs=[ANYWHERE] * first + specs,
        out_specs=out_specs,
        scratch_shapes=list(scratch),
        input_output_aliases={first + k: v for k, v in (alias or {}).items()},
        compiler_params=pltpu.CompilerParams(vmem_limit_bytes=vmem * 1024 * 1024),
        cost_estimate=pl.CostEstimate(flops=flops, bytes_accessed=moved, transcendentals=exps),
    )(*after, *args)


def in_hbm(value):
    return pltpu.with_memory_space_constraint(value, pltpu.HBM)


def shape(dims, dtype):
    return jax.ShapeDtypeStruct(dims, dtype)


def open_kernel(stage, count, passed, *refs):
    sources, rest = refs[:count], refs[count:]
    outs, scratch = rest[: 9 + passed], rest[9 + passed :]
    outs, later = outs[:9], list(outs[9:])
    sent_ref, run_ref, runt_ref, stept_ref, reach_ref, end_ref, pick_ref, kept_out, owner_out = outs
    sems, held = scratch[0], [*scratch[1:], *later]
    fetches = [
        pltpu.make_async_copy(source, target, sems.at[k])
        for k, (source, target) in enumerate(zip(sources, held))
    ]
    for fetch in fetches:
        fetch.start()
    early = count - passed
    for fetch in fetches[:early]:
        fetch.wait()
    turned_ref, rate_ref, owner_ref, ids_ref, kept_ref, write_ref, x_ref = held[:7]
    heads, span = turned_ref.shape
    groups = write_ref.shape[1] // STATE_SIZE
    per_group = heads // groups
    here = lax.axis_index("seq")
    place = place_of(stage)

    step_rows = turned_ref[...]
    stept_ref[...] = step_rows
    pad = (-heads) % 128
    if pad:
        step_rows = jnp.concatenate([step_rows, jnp.zeros((pad, span), F32)], axis=0)
    step = step_rows.T[:, :heads]
    log_decay = -step * rate_ref[...]
    lower = lax.broadcasted_iota(jnp.int32, (span, span), 0) >= lax.broadcasted_iota(
        jnp.int32, (span, span), 1
    )
    lower = jnp.where(lower, 1.0, 0.0).astype(BF16)
    running = sum(dot(lower, part.astype(BF16)) for part in split(log_decay, 3))
    to_end = jnp.exp(running[span - 1 : span, :] - running) * step
    end_ref[...] = jnp.concatenate(split(to_end, 2), axis=1).astype(BF16)

    for fetch in fetches[early : early + 2]:
        fetch.wait()
    fill_message(place ^ 1, end_ref, x_ref, write_ref, sent_ref)

    wide_run = running
    if pad:
        wide_run = jnp.concatenate([running, jnp.zeros((span, pad), F32)], axis=1)
    runt_ref[...] = wide_run.T[:heads]
    for g in range(groups):
        run_ref[g] = running[:, g * per_group : (g + 1) * per_group]
    reach_ref[...] = jnp.concatenate(split(jnp.exp(running), 2), axis=1).astype(BF16)

    slots = owner_ref.shape[0]
    request = lax.fori_loop(
        0, slots, lambda r, found: jnp.where(owner_ref[r] == here, r, found), jnp.int32(0)
    )
    row = lax.broadcasted_iota(jnp.int32, pick_ref.shape, 0)
    col = lax.broadcasted_iota(jnp.int32, pick_ref.shape, 1)
    pick = jnp.zeros(pick_ref.shape, F32)
    for i in range(DRAFTS):
        pick = jnp.where((row == i) & (col == ids_ref[i, request]), 1.0, pick)
    pick_ref[...] = pick
    kept_out[...] = jnp.zeros(kept_out.shape, jnp.int32) + kept_ref[request]
    owner_out[...] = jnp.zeros(owner_out.shape, jnp.int32) + owner_ref[0]
    for fetch in fetches[early + 2 :]:
        fetch.wait()


def draft_kernel(
    stage,
    pick_ref,
    kept_ref,
    owner_ref,
    runt_ref,
    rate_ref,
    skip_ref,
    din_ref,
    dgate_ref,
    dwrite_ref,
    dread_ref,
    dstep_ref,
    own_ref,
    sent_ref,
    skip_out,
    q1_ref,
    q2_ref,
    vread_ref,
    vwrite_ref,
    tail_ref,
    extra_ref,
):
    heads, span = runt_ref.shape
    lanes = din_ref.shape[1]
    groups = dwrite_ref.shape[1] // STATE_SIZE
    wide = lanes // groups
    here = lax.axis_index("seq")
    place = place_of(stage)
    pick = pick_ref[...].astype(BF16)
    vin = dot(pick, din_ref[...])
    vgate = dot(pick, dgate_ref[...])
    vwrite = dot(pick, dwrite_ref[...]).astype(BF16)
    vread = dot(pick, dread_ref[...]).astype(BF16)
    vwrite_ref[...] = vwrite
    vread_ref[...] = vread
    vstep = sum(dot(pick, part.astype(BF16)) for part in split(dstep_ref[...], 3))
    vlog = -vstep * rate_ref[...]
    index = lax.broadcasted_iota(jnp.int32, (DRAFTS, heads), 0)
    kept_heads = kept_ref[:, :1]
    acc = jnp.zeros((1, heads), F32)
    vrun = jnp.zeros((DRAFTS, heads), F32)
    reach = jnp.zeros((1, heads), F32)
    for i in range(DRAFTS):
        acc = acc + vlog[i : i + 1]
        vrun = jnp.where(index == i, acc, vrun)
        reach = jnp.where(i < kept_heads[0:1], acc, reach)
    total = runt_ref[:, span - 128 :]
    if heads < 128:
        total = jnp.concatenate([total, jnp.zeros((128 - heads, 128), F32)], axis=0)
    total = total.T[127:128, :heads]
    others = jnp.where(index == 0, total, jnp.where(index == 1, skip_ref[...], reach))
    stacked = split(jnp.concatenate([vrun, vstep, others], axis=0), 3)
    stacked = jnp.concatenate(stacked, axis=0).astype(BF16)
    row = lax.broadcasted_iota(jnp.int32, (DRAFTS, wide), 0)
    kept = kept_ref[:, :1]
    is_owner = owner_ref[0:1, :1] == here
    for g in range(groups):
        at = slice(g * wide, (g + 1) * wide)
        spread = dot(stacked, head_mask(heads, heads, wide, g * wide))
        spread = spread[0:24] + spread[24:48] + spread[48:72]
        vrun_l, vstep_l = spread[0:8], spread[8:16]
        total_l, skip_l, reach_l = spread[16:17], spread[17:18], spread[18:19]
        skip_out[:, at] = skip_l
        vin_g = vin[:, at]
        vr = vread[:, g * STATE_SIZE : (g + 1) * STATE_SIZE]
        vw = vwrite[:, g * STATE_SIZE : (g + 1) * STATE_SIZE]
        scores = dot(vr, vw, ((1,), (1,)))
        direct = skip_l * vin_g
        for j in range(DRAFTS):
            decay = jnp.exp(jnp.where(row >= j, vrun_l - vrun_l[j : j + 1], -jnp.inf))
            direct = direct + decay * scores[:, j : j + 1] * (vstep_l[j : j + 1] * vin_g[j : j + 1])
        gate = vgate[:, at]
        gate = gate / (1.0 + jnp.exp(-gate))
        q1 = direct * gate
        q2 = jnp.exp(vrun_l) * gate
        q1_ref[:, at] = q1
        q2_ref[:, at] = q2
        live = jnp.exp(jnp.where(row < kept, reach_l - vrun_l, -jnp.inf)) * vstep_l * vin_g
        keep_l = jnp.concatenate(
            split(jnp.exp(reach_l), 3) + [jnp.zeros((5, wide), F32)], axis=0
        )
        tail_ref[:, at] = jnp.concatenate(split(live, 3) + [keep_l], axis=0).astype(BF16)
        read_l = jnp.concatenate([vr.astype(F32)] * (wide // STATE_SIZE), axis=1)
        mine = jnp.concatenate([q1, q2, read_l], axis=0)
        mine = jnp.where(is_owner, mine, 0.0)
        logs = jnp.concatenate(split(total_l, 3) + [jnp.zeros((5, wide), F32)], axis=0)
        extra_ref[:, at] = jnp.concatenate([mine, logs], axis=0).astype(BF16)
    half = lanes // 2
    own_ref[...] = extra_ref[:, window(place * half, half)]
    sent_ref[...] = extra_ref[:, window((place ^ 1) * half, half)]


def fill_message(side, end_ref, x_ref, write_ref, out_ref):
    heads = end_ref.shape[1] // 2
    half = out_ref.shape[1]
    wide = 2 * half // (write_ref.shape[1] // STATE_SIZE)
    chunk = min(wide, half)
    start = side * half
    for at in range(0, half, chunk):
        lane0 = start + at
        group = lax.div(lane0, wide)
        scale = dot(end_ref[...], head_mask(2 * heads, heads, chunk, lane0))
        weighted = (x_ref[:, window(lane0, chunk)].astype(F32) * scale).astype(BF16)
        writes = write_ref[:, window(group * STATE_SIZE, STATE_SIZE)]
        writes = writes.astype(F32).T.astype(BF16)
        out_ref[:, at : at + chunk] = dot(writes, weighted).astype(BF16)


def own_kernel(stage, end_ref, x_ref, write_ref, out_ref):
    fill_message(place_of(stage), end_ref, x_ref, write_ref, out_ref)


def state_of(part, at):
    return part[0][:STATE_SIZE, at].astype(F32)


def extra_of(part, at):
    return (part[1][:, at] if part[2] else part[0][STATE_SIZE:UP_ROWS, at]).astype(F32)


def logs_of(part, at):
    found = extra_of(part, at)[LOG_AT - STATE_SIZE :]
    return found[0:1] + found[1:2] + found[2:3]


def turned(parts):
    return [parts[0], *parts[:0:-1]]


def paired(refs, apart):
    if apart:
        return [(refs[k], refs[k + 1], True) for k in range(0, len(refs), 2)]
    return [(ref, None, False) for ref in refs]


def weights_of(logs, place, target):
    spots = [place ^ k for k in range(len(logs))]
    found = []
    for k, spot in enumerate(spots):
        between = jnp.zeros_like(logs[0])
        for other, log in zip(spots, logs):
            if other is not spot:
                between = between + jnp.where((spot < other) & (other < target), log, 0.0)
        found.append(jnp.where(spot < target, jnp.exp(between), 0.0))
    return found


def carry_of(logs, place, target):
    ahead = jnp.zeros_like(logs[0])
    for k, log in enumerate(logs):
        ahead = ahead + jnp.where((place ^ k) < target, log, 0.0)
    return jnp.exp(ahead)


def up_kernel(stage, following, count, apart, *refs):
    taken = 2 * count if apart else count
    parts, outs = paired(refs[:taken], apart), refs[taken:]
    place, target = place_of(stage), place_of(following)
    width = outs[0].shape[1]
    chunk = min(256, width)
    order = list(range(1, len(outs))) + [0]
    for k in order:
        for at in range(0, width, chunk):
            start = at if len(outs) == 1 else (target ^ k) * width + at
            at_in = window(start, chunk)
            logs = [logs_of(part, at_in) for part in parts]
            scale = weights_of(logs, place, count)
            state = sum(w * state_of(part, at_in) for w, part in zip(scale, parts))
            outs[k][:STATE_SIZE, at : at + chunk] = state.astype(BF16)
            mine = sum(extra_of(part, at_in) for part in parts)
            total = jnp.concatenate(
                split(sum(logs), 3) + [jnp.zeros((5, chunk), F32)], axis=0
            )
            outs[k][STATE_SIZE:, at : at + chunk] = jnp.concatenate(
                [mine[:24], total], axis=0
            ).astype(BF16)


def top_kernel(stage, count, *refs):
    parts, outs, prompt_ref = paired(turned(refs[:count]), False), refs[count:-1], refs[-1]
    whole = slice(None)
    place = place_of(stage)
    width = prompt_ref.shape[1]
    logs = [logs_of(part, whole) for part in parts]
    states = [state_of(part, whole) for part in parts]
    final = sum(w * s for w, s in zip(weights_of(logs, place, count), states)).astype(BF16)
    prompt_ref[...] = final
    mine = sum(extra_of(part, whole) for part in parts)
    reads = mine[16:24, :STATE_SIZE].astype(BF16)
    gated = mine[0:8] + mine[8:16] * dot(reads, final)
    gated = jnp.concatenate(split(gated, 2), axis=0).astype(BF16)
    for k in list(range(1, len(outs))) + [0]:
        scale = weights_of(logs, place, place ^ k)
        outs[k][:STATE_SIZE, :] = sum(w * s for w, s in zip(scale, states)).astype(BF16)
        outs[k][STATE_SIZE:, :] = gated


def down_kernel(stage, above, above_count, count, apart, targets, handed, *refs):
    end = above_count + (2 * count if apart else count)
    pieces, outs = turned(refs[:above_count]), refs[end:]
    parts = paired(refs[above_count:end], apart)
    if handed:
        outs[-1][...] = outs[0][...]
        outs = outs[1:-1]
    place, source = place_of(stage), place_of(above)
    width = pieces[0].shape[1]
    chunk = min(256, width)
    gated_ref = outs[1] if apart and len(outs) > 1 else None
    for k, out_ref in zip(targets, outs):
        for piece in range(above_count):
            for at in range(0, width, chunk):
                start = at if above_count == 1 else (source ^ piece) * width + at
                at_out = window(start, chunk)
                block = pieces[piece][:, at : at + chunk]
                logs = [logs_of(part, at_out) for part in parts]
                state = carry_of(logs, place, place ^ k) * block[:STATE_SIZE].astype(F32)
                for w, part in zip(weights_of(logs, place, place ^ k), parts):
                    state = state + w * state_of(part, at_out)
                out_ref[:STATE_SIZE, at_out] = state.astype(BF16)
                if gated_ref is not None:
                    gated_ref[:, at_out] = block[STATE_SIZE:]
                elif out_ref.shape[0] > STATE_SIZE:
                    out_ref[STATE_SIZE:, at_out] = block[STATE_SIZE:]


def intra_kernel(group, run_ref, runt_ref, stept_ref, skip_ref, x_ref, write_ref, read_ref, *refs):
    fetch = None
    out_ref = refs[0]
    if len(refs) > 1:
        source_ref, out_ref, held_ref, sem = refs
        fetch = pltpu.make_async_copy(source_ref, held_ref, sem)
        fetch.start()
    span, heads = run_ref.shape[1:]
    mid = span // 2
    states = slice(group * STATE_SIZE, (group + 1) * STATE_SIZE)
    scores = dot(read_ref[:, states], write_ref[:, states], ((1,), (1,)))
    row = lax.broadcasted_iota(jnp.int32, (mid, mid), 0)
    causal = row >= lax.broadcasted_iota(jnp.int32, (mid, mid), 1)
    running = run_ref[group]
    low, high = slice(0, mid), slice(mid, span)
    for pair in range(heads // 2):
        found = []
        for k in (2 * pair, 2 * pair + 1):
            h = group * heads + k
            x = x_ref[:, h * HEAD_DIM : (h + 1) * HEAD_DIM]
            t_run, j_run = running[:, k : k + 1], runt_ref[h : h + 1, :]
            step = stept_ref[h : h + 1, :]

            def mixed(rows, cols, masked):
                gap = t_run[rows] - j_run[:, cols]
                if masked:
                    gap = jnp.where(causal, gap, -jnp.inf)
                return (scores[rows, cols] * jnp.exp(gap) * step[:, cols]).astype(BF16)

            top = dot(mixed(low, low, True), x[low])
            bottom = dot(mixed(high, low, False), x[low]) + dot(mixed(high, high, True), x[high])
            found.append(jnp.concatenate([top, bottom], axis=0))
        at = slice(pair * 2 * HEAD_DIM, (pair + 1) * 2 * HEAD_DIM)
        lanes = slice((group * heads + 2 * pair) * HEAD_DIM, (group * heads + 2 * pair + 2) * HEAD_DIM)
        both = jnp.concatenate(found, axis=1)
        out_ref[:, at] = both + skip_ref[:, lanes] * x_ref[:, lanes].astype(F32)
    if fetch is not None:
        fetch.wait()


def intra(group, run, runt, stept, skip, x, write, read, after, wanted=()):
    span, per_group = run.shape[1:]
    wide = per_group * HEAD_DIM
    return call(
        functools.partial(intra_kernel, group),
        "intra",
        [shape((span, wide), F32)] + [shape(value.shape, value.dtype) for value in wanted],
        (run, runt, stept, skip, x, write, read, *map(in_hbm, wanted)),
        specs=[WHOLE] * 7 + [IN_HBM] * len(wanted),
        scratch=[pltpu.SemaphoreType.DMA] * len(wanted),
        after=after,
        flops=per_group * span * span * HEAD_DIM * 2,
        moved=wide * span * 6,
        exps=per_group * span * span * 3 // 4,
    )


def finish_kernel(stage, reach_ref, read_ref, own_ref, got_ref, *refs):
    base_refs, (out_ref, token_ref, held_ref, sems) = refs[:-4], refs[-4:]
    token_ref[...] = jnp.zeros_like(token_ref)
    place = place_of(stage)
    heads = reach_ref.shape[1] // 2
    lanes = held_ref.shape[1]
    wide = lanes // len(base_refs)
    half = lanes // 2
    chunk = lanes // sems.shape[0]
    copies = []
    for k, lane0 in enumerate(range(0, lanes, chunk)):
        group, at = lane0 // wide, lane0 % half
        at_in, at_out = slice(at, at + chunk), slice(lane0, lane0 + chunk)
        entering = jnp.where(place == lane0 // half, own_ref[:, at_in], got_ref[:, at_in])
        inter = dot(read_ref[:, group * STATE_SIZE : (group + 1) * STATE_SIZE], entering)
        inter = inter * dot(reach_ref[...], head_mask(2 * heads, heads, chunk, lane0))
        base = base_refs[group][:, lane0 % wide : lane0 % wide + chunk]
        held_ref[:, at_out] = (inter + base).astype(BF16)
        copies.append(
            pltpu.make_async_copy(held_ref.at[:, at_out], out_ref.at[:, at_out], sems.at[k])
        )
        copies[-1].start()
    for copy in copies:
        copy.wait()


def finish(stage, reach, read, own, got, bases):
    span = read.shape[0]
    lanes = 2 * own.shape[1]
    chunk = min(512, own.shape[1])
    return call(
        functools.partial(finish_kernel, stage),
        "finish",
        [shape((span, lanes), BF16), shape((8, 128), F32)],
        (reach, read, own, got, *bases),
        out_specs=[IN_HBM, WHOLE],
        scratch=[pltpu.VMEM((span, lanes), BF16), pltpu.SemaphoreType.DMA((lanes // chunk,))],
        moved=1,
    )


def resident_kernel(state_ref, vread_ref, q1_ref, q2_ref, gain_ref, out_ref):
    groups = vread_ref.shape[1] // STATE_SIZE
    wide = state_ref.shape[0] // groups
    for g in range(groups):
        at = slice(g * wide, (g + 1) * wide)
        reads = vread_ref[:, g * STATE_SIZE : (g + 1) * STATE_SIZE]
        drawn = dot(reads, state_ref[at, :], ((1,), (1,)))
        gated = q1_ref[:, at] + q2_ref[:, at] * drawn
        out_ref[:, at] = normed(gated, gain_ref[:, at]).astype(BF16)


def normed(gated, gain):
    mean_square = jnp.mean(gated * gated, axis=1, keepdims=True)
    return gated * lax.rsqrt(mean_square + EPSILON) * gain


def resident_hidden(state, vread, q1, q2, gain, after):
    lanes = state.shape[0]
    return call(
        resident_kernel,
        "resident_hidden",
        [shape((DRAFTS, lanes), BF16)],
        (state, vread, q1, q2, gain),
        after=after,
        flops=2 * DRAFTS * lanes * STATE_SIZE,
    )[0]


def hand_on(value, after):
    def copy(value_ref, out_ref):
        out_ref[...] = value_ref[...]

    return call(copy, "hand_on", [shape(value.shape, value.dtype)], [value], after=after)[0]


def join_kernel(axis, *refs):
    out_ref = refs[-1]
    for k, ref in enumerate(refs[:-1]):
        size = ref.shape[axis]
        at = slice(k * size, (k + 1) * size)
        if axis == 0:
            out_ref[at, :] = ref[...]
        else:
            out_ref[:, at] = ref[...]


def join(parts, axis, after=()):
    dims = list(parts[0].shape)
    dims[axis] *= len(parts)
    return call(
        functools.partial(join_kernel, axis), "join", [shape(tuple(dims), parts[0].dtype)], parts, after=after, moved=1
    )[0]


def project_kernel(stages, head_count, *refs):
    owner_ref, own_rows, got_rows, own_ref, got_ref, gain_ref, weight_ref = refs[:7]
    outs = refs[7 : 7 + head_count]
    gated_ref, left_ref, total_ref = refs[7 + head_count :]
    here, head = lax.axis_index("seq"), lax.axis_index("head")
    place = place_of(stages[0])
    half = own_ref.shape[1]
    lanes = weight_ref.shape[0]
    wide = min(1024, lanes)
    rows = own_rows.shape[0]
    for k, ref in enumerate((own_ref, got_ref)):
        both = ref[...].astype(F32)
        gated_ref[:, window((place ^ k) * half, half)] = both[0:8] + both[8:16]
    left_ref[0:rows, :] = own_rows[...]
    left_ref[rows : 2 * rows, :] = got_rows[...]
    for lane0 in range(0, lanes, wide):
        at = slice(lane0, lane0 + wide)
        hidden = normed(gated_ref[:, at], gain_ref[:, at])
        hidden = jnp.concatenate([hidden, jnp.zeros_like(hidden)], axis=0)
        left_ref[2 * rows :, at] = hidden.astype(BF16)
    total_ref[...] = dot(left_ref[...], weight_ref[...])

    per_head = 2 * rows // DRAFTS // head_count
    offsets = [0]
    for factor, stride in reversed(stages):
        offsets = [a + k * stride for k in range(factor) for a in offsets]
    owner = owner_ref[...]
    tail = total_ref[2 * rows : 2 * rows + DRAFTS, :]
    for k in list(range(1, head_count)) + [0]:
        first = (head ^ k) * per_head
        for slot in range(per_head):
            at = slice(slot * DRAFTS, (slot + 1) * DRAFTS)
            offset = here ^ (first + slot)
            block = jnp.int32(0)
            for position, value in enumerate(offsets):
                block = jnp.where(offset == value, position, block)
            drawn = total_ref[window(block * DRAFTS, DRAFTS), :]
            drawn = jnp.where(owner == first + slot, tail, drawn)
            outs[k][at, :] = drawn.astype(outs[k].dtype)


def project(stages, owner, own_rows, got_rows, own, got, gain, weight, head_count):
    lanes, cols = weight.shape
    rows = 2 * own_rows.shape[0]
    return call(
        functools.partial(project_kernel, stages, head_count),
        "project",
        [shape((rows // head_count, cols), BF16 if k else F32) for k in range(head_count)],
        (owner, own_rows, got_rows, own, got, gain, weight),
        scratch=[
            pltpu.VMEM((DRAFTS, lanes), F32),
            pltpu.VMEM((rows + 16, lanes), BF16),
            pltpu.VMEM((rows + 16, cols), F32),
        ],
        moved=1,
    )


def states_kernel(stages, scattered, pieces, *refs):
    owner_ref, resident_ref, tail_ref, vwrite_ref = refs[:4]
    prompt_refs, refs = refs[4 : 4 + pieces], refs[4 + pieces :]
    share_refs, (new_ref, slice_ref, verify_ref, turned_ref, held_ref, sems) = refs[:-6], refs[-6:]
    here = lax.axis_index("seq")
    verify_ref[...] = sum(ref[...].astype(F32) for ref in share_refs).astype(BF16)
    core, line, last = stages
    lanes = resident_ref.shape[0]
    wide = lanes // (vwrite_ref.shape[1] // STATE_SIZE)
    part = lanes // pieces
    width = part // (last[0] if len(scattered) > 1 else 1)
    chunk = lanes // sems.shape[0]
    is_owner = owner_ref[0:1, :STATE_SIZE] == here
    row = lax.broadcasted_iota(jnp.int32, (32, STATE_SIZE), 0)
    ones = jnp.where((row >= 24) & (row < 27), 1.0, 0.0)
    copies = []
    for step in range(sems.shape[0]):
        rows = slice(step * chunk, (step + 1) * chunk)
        for lane in range(step * chunk, (step + 1) * chunk, width):
            spot = lane // part
            piece = (spot // line[0] ^ place_of(core)) * line[0] + (spot % line[0] ^ place_of(line))
            position = jnp.int32(0)
            if len(scattered) > 1:
                position = lane % part // width ^ place_of(last)
            at = window(position * width, width)
            found = prompt_refs[0][:, at]
            for k in range(1, pieces):
                found = jnp.where(piece == k, prompt_refs[k][:, at], found)
            turned_ref[lane : lane + width, :] = found.astype(F32).T
        group = step * chunk // wide
        writes = vwrite_ref[:, group * STATE_SIZE : (group + 1) * STATE_SIZE].astype(F32)
        writes = jnp.concatenate([writes, writes, writes, jnp.zeros_like(writes)], axis=0)
        right = jnp.concatenate([writes, ones], axis=1).astype(BF16)
        left = tail_ref[:, rows].astype(F32).T.astype(BF16)
        both = dot(left, right)
        start = jnp.where(is_owner, turned_ref[rows, :], resident_ref[rows, :].astype(F32))
        held_ref[rows, :] = (start * both[:, STATE_SIZE:] + both[:, :STATE_SIZE]).astype(BF16)
        copies.append(pltpu.make_async_copy(held_ref.at[rows, :], new_ref.at[rows, :], sems.at[step]))
        copies[-1].start()
    per_slice = slice_ref.shape[1] // STATE_SIZE
    heads = slice_ref.shape[0]
    for k in range(per_slice):
        picked = turned_ref[pl.ds(here * per_slice + k, heads, stride=HEAD_DIM), :]
        slice_ref[:, k * STATE_SIZE : (k + 1) * STATE_SIZE] = picked.astype(BF16)
    for copy in copies:
        copy.wait()


def states(stages, scattered, owner, resident, prompts, tail, vwrite, shares, seq_count):
    lanes = resident.shape[0]
    chunk = min(512, lanes // 2)
    return call(
        functools.partial(states_kernel, stages, scattered, len(prompts)),
        "states",
        [
            shape((lanes, STATE_SIZE), BF16),
            shape((lanes // HEAD_DIM, HEAD_DIM // seq_count * STATE_SIZE), BF16),
            shape(shares[0].shape, BF16),
        ],
        (owner, resident, tail, vwrite, *prompts, *shares),
        out_specs=[IN_HBM, WHOLE, WHOLE],
        scratch=[
            pltpu.VMEM((lanes, STATE_SIZE), F32),
            pltpu.VMEM((lanes, STATE_SIZE), BF16),
            pltpu.SemaphoreType.DMA((lanes // chunk,)),
        ],
        flops=2 * lanes * STATE_SIZE * 64,
    )


def on_device(
    prefill_input,
    prefill_step,
    write_proj,
    read_proj,
    decay_rate,
    skip_gain,
    resident_state,
    owner_slot,
    draft_ids,
    accepted_len,
    draft_input,
    draft_gate,
    draft_write,
    draft_read,
    draft_step,
    norm_gain,
    out_weight,
):
    span, lanes = prefill_input.shape
    assert span == BLOCK_LEN
    heads = decay_rate.shape[0]
    groups = write_proj.shape[1] // STATE_SIZE
    per_group = heads // groups
    half = lanes // 2
    seq_count, head_count = lax.axis_size("seq"), lax.axis_size("head")
    stages = tree_stages(seq_count)
    core, line, last = stages
    slots = owner_slot.shape[0]
    assert core[0] == 2 and slots == seq_count
    rate, skip, gain = decay_rate[None], skip_gain[None], norm_gain[None]
    resident = resident_state.reshape(lanes, STATE_SIZE)

    inputs = [
        in_hbm(value)
        for value in (
            prefill_step.T, rate, owner_slot, draft_ids.T, accepted_len, write_proj, prefill_input,
            draft_input, draft_gate, draft_write, draft_read, draft_step, skip, rate, read_proj, resident,
            gain,
        )
    ]
    passed = 12
    opened = call(
        functools.partial(open_kernel, core, len(inputs), passed),
        "open_block",
        [
            shape((STATE_SIZE, half), BF16),
            shape((groups, span, per_group), F32),
            shape((heads, span), F32),
            shape((heads, span), F32),
            shape((span, 2 * heads), BF16),
            shape((span, 2 * heads), BF16),
            shape((DRAFTS, draft_input.shape[0]), F32),
            shape((DRAFTS, 128), jnp.int32),
            shape((DRAFTS, out_weight.shape[1]), jnp.int32),
        ]
        + [shape(value.shape, value.dtype) for value in inputs[-passed:]],
        inputs,
        specs=[IN_HBM] * len(inputs),
        scratch=[pltpu.SemaphoreType.DMA((len(inputs),))]
        + [
            (pltpu.SMEM if value.dtype == jnp.int32 else pltpu.VMEM)(value.shape, value.dtype)
            for value in inputs[:-passed]
        ],
        flops=span * lanes * STATE_SIZE * 2,
    )
    sent, run, runt, stept, reach, end, pick, kept, owner = opened[:9]
    writes, x, din, dgate, dwrite, dread, dstep, skip, rate, reads, resident, gain = opened[9:]
    received = swap(sent, "seq", core, 1)
    own_extra, sent_extra, skip_lanes, q1, q2, vread, vwrite, tail = call(
        functools.partial(draft_kernel, core),
        "draft_rows",
        [
            shape((EXTRA, half), BF16),
            shape((EXTRA, half), BF16),
            shape((1, lanes), F32),
            shape((DRAFTS, lanes), F32),
            shape((DRAFTS, lanes), F32),
            shape((DRAFTS, groups * STATE_SIZE), BF16),
            shape((DRAFTS, groups * STATE_SIZE), BF16),
            shape((32, lanes), BF16),
        ],
        (pick, kept, owner, runt, rate, skip, din, dgate, dwrite, dread, dstep),
        after=[sent],
        scratch=[pltpu.VMEM((EXTRA, lanes), BF16)],
        flops=DRAFTS * lanes * 100,
    )
    received_extra = swap(sent_extra, "seq", core, 1)
    (own,) = call(
        functools.partial(own_kernel, core),
        "own_message",
        [shape((STATE_SIZE, half), BF16)],
        (end, x, writes),
        after=[sent_extra],
        flops=span * lanes * STATE_SIZE,
    )
    core_parts = [own, own_extra, received, received_extra]
    hidden = resident_hidden(resident, vread, q1, q2, gain, [own])

    bases, fetched = [], []

    def fill(after):
        if len(bases) < groups:
            wanted = [] if bases else [out_weight]
            base, *found = intra(
                len(bases), run, runt, stept, skip_lanes, x, writes, reads, after, wanted
            )
            bases.append(base)
            fetched.extend(found)
        return bases[-1:]

    def exchange(parts, stage):
        got = {k: swap(parts[k], "seq", stage, k) for k in range(1, stage[0])}
        return [parts[0]] + [got[k] for k in range(1, stage[0])]

    line_width = half // line[0]
    split_last = line_width % (last[0] * 128) == 0
    last_width = line_width // last[0] if split_last else line_width
    outs = call(
        functools.partial(up_kernel, core, line, 2, True),
        "up_line",
        [shape((UP_ROWS, line_width), BF16)] * line[0],
        core_parts,
        after=[hidden],
        flops=half * UP_ROWS * 4,
    )
    line_parts = exchange(outs, line)
    hiddens = exchange([hand_on(hidden, [outs[-1]])] * last[0], last)
    filled = fill([outs[-1]])
    outs = call(
        functools.partial(up_kernel, line, last, line[0], False),
        "up_last",
        [shape((UP_ROWS, last_width), BF16)] * (last[0] if split_last else 1),
        line_parts,
        after=filled + hiddens[2:],
        flops=line_width * UP_ROWS * 4,
    )
    last_parts = exchange(outs if split_last else outs * last[0], last)
    filled = fill([outs[-1]])
    *outs, prompt = call(
        functools.partial(top_kernel, last, last[0]),
        "top",
        [shape((DOWN_ROWS, last_width), BF16)] * (last[0] if split_last else 1)
        + [shape((STATE_SIZE, last_width), BF16)],
        turned(last_parts),
        after=filled,
        flops=last_width * UP_ROWS * 16,
    )

    pieces = exchange(outs, last) if split_last else outs
    hidden = join(hiddens, 0, [outs[-1]])
    hiddens = exchange([hidden] * line[0], line)
    filled = fill([outs[-1]])
    outs = call(
        functools.partial(down_kernel, line, last, len(pieces), line[0], False, range(line[0]), False),
        "down_line",
        [shape((DOWN_ROWS, line_width), BF16)] * line[0],
        [*turned(pieces), *line_parts],
        after=filled + hiddens[1:],
        flops=line_width * UP_ROWS * 8,
    )
    pieces = exchange(outs, line)
    hidden = join(hiddens, 0, [outs[-1]])
    hiddens = [hidden, swap(hidden, "seq", core, 1)]
    filled = fill([outs[-1]]) + hiddens[1:]
    scattered = [line, last] if split_last else [line]
    if split_last:
        prompt = hand_on(prompt, [outs[-1]])
        prompt = join(exchange([prompt] * last[0], last), 1)
        filled.append(prompt)

    def down_core(target, after):
        return call(
            functools.partial(down_kernel, core, line, line[0], 2, True, (target,), False),
            "down_core",
            [shape((STATE_SIZE, half), BF16)] + [shape((16, half), BF16)] * target,
            turned(pieces) + core_parts,
            after=after,
            moved=1,
        )

    sent, gated = down_core(1, filled)
    received_gated, received = swap(gated, "seq", core, 1), swap(sent, "seq", core, 1)
    while len(bases) < groups:
        fill([])

    shares = project(
        stages, owner, *hiddens, gated, received_gated, gain, fetched[0], head_count
    )
    (entering,) = down_core(0, shares[:1])
    prefill_out, token = finish(core, reach, reads, entering, received, bases)
    shares = [shares[0]] + [swap(shares[k], "head", (head_count, 1), k) for k in range(1, head_count)]

    prompts = exchange([prompt] * line[0], line)
    first = swap(hand_on(prompt, shares[:1]), "seq", core, 1)
    late = [hand_on(piece, [token, *shares[1:]]) for piece in prompts[1:]]
    prompts += [first] + [swap(piece, "seq", core, 1) for piece in late]
    new_state, state_slice, verify_out = states(
        stages, scattered, owner, resident, prompts, tail, vwrite, shares, seq_count
    )
    return (
        prefill_out,
        new_state.reshape(1, heads, HEAD_DIM, STATE_SIZE),
        verify_out,
        state_slice,
    )


def solution(mesh):
    return jax.shard_map(
        on_device,
        mesh=mesh,
        in_specs=(
            P("seq", "head"),
            P("seq", "head"),
            P("seq", "head"),
            P("seq", "head"),
            P("head"),
            P("head"),
            P("seq", "head", None, None),
            P(),
            P(),
            P(),
            P("seq", "head"),
            P("seq", "head"),
            P("seq", "head"),
            P("seq", "head"),
            P("seq", "head"),
            P("head"),
            P("head", "seq"),
        ),
        out_specs=(
            P("seq", "head"),
            P("seq", "head", None, None),
            P("head", "seq"),
            P("head", "seq"),
        ),
        check_vma=False,
    )
```

```python
import functools

import jax
import jax.numpy as jnp
from jax import lax
from jax.experimental import pallas as pl
from jax.experimental.pallas import tpu as pltpu
from jax.sharding import PartitionSpec as P

HEAD_DIM = 64
STATE_SIZE = 128
BLOCK_LEN = 256
DRAFTS = 8
EPSILON = 1e-05
EXTRA = 32
UP_ROWS = STATE_SIZE + EXTRA
READ_AT = STATE_SIZE + 16
LOG_AT = STATE_SIZE + 24
DOWN_ROWS = STATE_SIZE + 8

F32 = jnp.float32
BF16 = jnp.bfloat16


def tree_stages(count):
    factors, rest = [], count
    if rest > 1:
        factors.append(2)
        rest //= 2
    inner = 1
    while inner * inner * 4 <= rest:
        inner *= 2
    factors += [inner, rest // inner]
    stages, stride = [], 1
    for factor in factors:
        stages.append((factor, stride))
        stride *= factor
    assert stride == count
    return stages


def swap(value, axis, stage, offset):
    count, stride = lax.axis_size(axis), stage[1]
    return lax.ppermute(value, axis, [(k, k ^ (offset * stride)) for k in range(count)])


def place_of(stage):
    factor, stride = stage
    return lax.rem(lax.div(lax.axis_index("seq"), stride), factor)


def dot(a, b, dims=((1,), (0,))):
    return lax.dot_general(a, b, (dims, ((), ())), preferred_element_type=F32)


def split(value, parts):
    found = []
    for _ in range(parts):
        part = value.astype(BF16).astype(F32)
        found.append(part)
        value = value - part
    return found


def head_mask(rows, heads, lanes, lane0):
    row = lax.broadcasted_iota(jnp.int32, (rows, lanes), 0) & (heads - 1)
    head = lax.shift_right_logical(lax.broadcasted_iota(jnp.int32, (rows, lanes), 1) + lane0, 6)
    return jnp.where(row == head, 1.0, 0.0).astype(BF16)


def window(start, size):
    return pl.ds(pl.multiple_of(start, size), size)


def ordered(kernel, count):
    return lambda *refs: kernel(*refs[count:])


ANYWHERE = pl.BlockSpec(memory_space=pl.ANY)
WHOLE = pl.BlockSpec(memory_space=pltpu.VMEM)
IN_HBM = pl.BlockSpec(memory_space=pltpu.HBM)


def call(
    kernel, name, outs, args, specs=None, out_specs=None, grid=(), after=(), scratch=(), alias=None,
    flops=0, exps=0, moved=None, vmem=32,
):
    if specs is None:
        specs = [WHOLE] * len(args)
    if out_specs is None:
        out_specs = [WHOLE] * len(outs)
    if moved is None:
        moved = sum(a.size * a.dtype.itemsize for a in (*args, *outs))
    first = len(after)
    return pl.pallas_call(
        ordered(kernel, first),
        name=name,
        grid=grid,
        out_shape=outs,
        in_specs=[ANYWHERE] * first + specs,
        out_specs=out_specs,
        scratch_shapes=list(scratch),
        input_output_aliases={first + k: v for k, v in (alias or {}).items()},
        compiler_params=pltpu.CompilerParams(vmem_limit_bytes=vmem * 1024 * 1024),
        cost_estimate=pl.CostEstimate(flops=flops, bytes_accessed=moved, transcendentals=exps),
    )(*after, *args)


def in_hbm(value):
    return pltpu.with_memory_space_constraint(value, pltpu.HBM)


def shape(dims, dtype):
    return jax.ShapeDtypeStruct(dims, dtype)


def open_kernel(stage, count, passed, *refs):
    sources, rest = refs[:count], refs[count:]
    outs, scratch = rest[: 9 + passed], rest[9 + passed :]
    outs, later = outs[:9], list(outs[9:])
    sent_ref, run_ref, runt_ref, stept_ref, reach_ref, end_ref, pick_ref, kept_out, owner_out = outs
    sems, held = scratch[0], [*scratch[1:], *later]
    here = lax.axis_index("seq")
    place = place_of(stage)
    early = count - passed
    half = sent_ref.shape[1]

    def fetch(k, at=None):
        if at is None:
            return pltpu.make_async_copy(sources[k], held[k], sems.at[k])
        sem = sems.at[k if at == 1 else count]
        lanes = window((place ^ at) * half, half)
        return pltpu.make_async_copy(sources[k].at[:, lanes], held[k].at[:, lanes], sem)

    first = [fetch(k) for k in range(early + 1)] + [fetch(early + 1, 1)]
    rest = [fetch(early + 1, 0)] + [fetch(k) for k in range(early + 2, count)]
    for copy in first:
        copy.start()
    for copy in first[:early]:
        copy.wait()
    for copy in rest:
        copy.start()
    turned_ref, rate_ref, owner_ref, ids_ref, kept_ref, write_ref, x_ref = held[:7]
    heads, span = turned_ref.shape
    groups = write_ref.shape[1] // STATE_SIZE
    per_group = heads // groups

    step_rows = turned_ref[...]
    stept_ref[...] = step_rows
    pad = (-heads) % 128
    if pad:
        step_rows = jnp.concatenate([step_rows, jnp.zeros((pad, span), F32)], axis=0)
    step = step_rows.T[:, :heads]
    log_decay = -step * rate_ref[...]
    lower = lax.broadcasted_iota(jnp.int32, (span, span), 0) >= lax.broadcasted_iota(
        jnp.int32, (span, span), 1
    )
    lower = jnp.where(lower, 1.0, 0.0).astype(BF16)
    running = sum(dot(lower, part.astype(BF16)) for part in split(log_decay, 3))
    to_end = jnp.exp(running[span - 1 : span, :] - running) * step
    end_ref[...] = jnp.concatenate(split(to_end, 2), axis=1).astype(BF16)

    for copy in first[early:]:
        copy.wait()
    fill_message(place ^ 1, end_ref, x_ref, write_ref, sent_ref)

    wide_run = running
    if pad:
        wide_run = jnp.concatenate([running, jnp.zeros((span, pad), F32)], axis=1)
    runt_ref[...] = wide_run.T[:heads]
    for g in range(groups):
        run_ref[g] = running[:, g * per_group : (g + 1) * per_group]
    reach_ref[...] = jnp.concatenate(split(jnp.exp(running), 2), axis=1).astype(BF16)

    slots = owner_ref.shape[0]
    request = lax.fori_loop(
        0, slots, lambda r, found: jnp.where(owner_ref[r] == here, r, found), jnp.int32(0)
    )
    row = lax.broadcasted_iota(jnp.int32, pick_ref.shape, 0)
    col = lax.broadcasted_iota(jnp.int32, pick_ref.shape, 1)
    pick = jnp.zeros(pick_ref.shape, F32)
    for i in range(DRAFTS):
        pick = jnp.where((row == i) & (col == ids_ref[i, request]), 1.0, pick)
    pick_ref[...] = pick
    kept_out[...] = jnp.zeros(kept_out.shape, jnp.int32) + kept_ref[request]
    owner_out[...] = jnp.zeros(owner_out.shape, jnp.int32) + owner_ref[0]
    for copy in rest:
        copy.wait()


def draft_kernel(
    stage,
    pick_ref,
    kept_ref,
    owner_ref,
    runt_ref,
    rate_ref,
    skip_ref,
    din_ref,
    dgate_ref,
    dwrite_ref,
    dread_ref,
    dstep_ref,
    own_ref,
    sent_ref,
    skip_out,
    q1_ref,
    q2_ref,
    vread_ref,
    vwrite_ref,
    tail_ref,
    extra_ref,
):
    heads, span = runt_ref.shape
    lanes = din_ref.shape[1]
    groups = dwrite_ref.shape[1] // STATE_SIZE
    wide = lanes // groups
    here = lax.axis_index("seq")
    place = place_of(stage)
    pick = pick_ref[...].astype(BF16)
    vin = dot(pick, din_ref[...])
    vgate = dot(pick, dgate_ref[...])
    vwrite = dot(pick, dwrite_ref[...]).astype(BF16)
    vread = dot(pick, dread_ref[...]).astype(BF16)
    vwrite_ref[...] = vwrite
    vread_ref[...] = vread
    vstep = sum(dot(pick, part.astype(BF16)) for part in split(dstep_ref[...], 3))
    vlog = -vstep * rate_ref[...]
    index = lax.broadcasted_iota(jnp.int32, (DRAFTS, heads), 0)
    kept_heads = kept_ref[:, :1]
    acc = jnp.zeros((1, heads), F32)
    vrun = jnp.zeros((DRAFTS, heads), F32)
    reach = jnp.zeros((1, heads), F32)
    for i in range(DRAFTS):
        acc = acc + vlog[i : i + 1]
        vrun = jnp.where(index == i, acc, vrun)
        reach = jnp.where(i < kept_heads[0:1], acc, reach)
    total = runt_ref[:, span - 128 :]
    if heads < 128:
        total = jnp.concatenate([total, jnp.zeros((128 - heads, 128), F32)], axis=0)
    total = total.T[127:128, :heads]
    others = jnp.where(index == 0, total, jnp.where(index == 1, skip_ref[...], reach))
    stacked = split(jnp.concatenate([vrun, vstep, others], axis=0), 3)
    stacked = jnp.concatenate(stacked, axis=0).astype(BF16)
    row = lax.broadcasted_iota(jnp.int32, (DRAFTS, wide), 0)
    kept = kept_ref[:, :1]
    is_owner = owner_ref[0:1, :1] == here
    for g in range(groups):
        at = slice(g * wide, (g + 1) * wide)
        spread = dot(stacked, head_mask(heads, heads, wide, g * wide))
        spread = spread[0:24] + spread[24:48] + spread[48:72]
        vrun_l, vstep_l = spread[0:8], spread[8:16]
        total_l, skip_l, reach_l = spread[16:17], spread[17:18], spread[18:19]
        skip_out[:, at] = skip_l
        vin_g = vin[:, at]
        vr = vread[:, g * STATE_SIZE : (g + 1) * STATE_SIZE]
        vw = vwrite[:, g * STATE_SIZE : (g + 1) * STATE_SIZE]
        scores = dot(vr, vw, ((1,), (1,)))
        direct = skip_l * vin_g
        for j in range(DRAFTS):
            decay = jnp.exp(jnp.where(row >= j, vrun_l - vrun_l[j : j + 1], -jnp.inf))
            direct = direct + decay * scores[:, j : j + 1] * (vstep_l[j : j + 1] * vin_g[j : j + 1])
        gate = vgate[:, at]
        gate = gate / (1.0 + jnp.exp(-gate))
        q1 = direct * gate
        q2 = jnp.exp(vrun_l) * gate
        q1_ref[:, at] = q1
        q2_ref[:, at] = q2
        live = jnp.exp(jnp.where(row < kept, reach_l - vrun_l, -jnp.inf)) * vstep_l * vin_g
        keep_l = jnp.concatenate(
            split(jnp.exp(reach_l), 3) + [jnp.zeros((5, wide), F32)], axis=0
        )
        tail_ref[:, at] = jnp.concatenate(split(live, 3) + [keep_l], axis=0).astype(BF16)
        read_l = jnp.concatenate([vr.astype(F32)] * (wide // STATE_SIZE), axis=1)
        mine = jnp.concatenate([q1, q2, read_l], axis=0)
        mine = jnp.where(is_owner, mine, 0.0)
        logs = jnp.concatenate(split(total_l, 3) + [jnp.zeros((5, wide), F32)], axis=0)
        extra_ref[:, at] = jnp.concatenate([mine, logs], axis=0).astype(BF16)
    half = lanes // 2
    own_ref[...] = extra_ref[:, window(place * half, half)]
    sent_ref[...] = extra_ref[:, window((place ^ 1) * half, half)]


def fill_message(side, end_ref, x_ref, write_ref, out_ref):
    heads = end_ref.shape[1] // 2
    half = out_ref.shape[1]
    wide = 2 * half // (write_ref.shape[1] // STATE_SIZE)
    chunk = min(wide, half)
    start = side * half
    for at in range(0, half, chunk):
        lane0 = start + at
        group = lax.div(lane0, wide)
        scale = dot(end_ref[...], head_mask(2 * heads, heads, chunk, lane0))
        weighted = (x_ref[:, window(lane0, chunk)].astype(F32) * scale).astype(BF16)
        writes = write_ref[:, window(group * STATE_SIZE, STATE_SIZE)]
        writes = writes.astype(F32).T.astype(BF16)
        out_ref[:, at : at + chunk] = dot(writes, weighted).astype(BF16)


def own_kernel(stage, end_ref, x_ref, write_ref, out_ref):
    fill_message(place_of(stage), end_ref, x_ref, write_ref, out_ref)


def state_of(part, at):
    return part[0][:STATE_SIZE, at].astype(F32)


def extra_of(part, at):
    return (part[1][:, at] if part[2] else part[0][STATE_SIZE:UP_ROWS, at]).astype(F32)


def logs_of(part, at):
    found = extra_of(part, at)[LOG_AT - STATE_SIZE :]
    return found[0:1] + found[1:2] + found[2:3]


def turned(parts):
    return [parts[0], *parts[:0:-1]]


def paired(refs, apart):
    if apart:
        return [(refs[k], refs[k + 1], True) for k in range(0, len(refs), 2)]
    return [(ref, None, False) for ref in refs]


def weights_of(logs, place, target):
    spots = [place ^ k for k in range(len(logs))]
    found = []
    for k, spot in enumerate(spots):
        between = jnp.zeros_like(logs[0])
        for other, log in zip(spots, logs):
            if other is not spot:
                between = between + jnp.where((spot < other) & (other < target), log, 0.0)
        found.append(jnp.where(spot < target, jnp.exp(between), 0.0))
    return found


def carry_of(logs, place, target):
    ahead = jnp.zeros_like(logs[0])
    for k, log in enumerate(logs):
        ahead = ahead + jnp.where((place ^ k) < target, log, 0.0)
    return jnp.exp(ahead)


def up_kernel(stage, following, count, apart, *refs):
    taken = 2 * count if apart else count
    parts, outs = paired(refs[:taken], apart), refs[taken:]
    place, target = place_of(stage), place_of(following)
    width = outs[0].shape[1]
    chunk = min(256, width)
    order = list(range(1, len(outs))) + [0]
    for k in order:
        for at in range(0, width, chunk):
            start = at if len(outs) == 1 else (target ^ k) * width + at
            at_in = window(start, chunk)
            logs = [logs_of(part, at_in) for part in parts]
            scale = weights_of(logs, place, count)
            state = sum(w * state_of(part, at_in) for w, part in zip(scale, parts))
            outs[k][:STATE_SIZE, at : at + chunk] = state.astype(BF16)
            mine = sum(extra_of(part, at_in) for part in parts)
            total = jnp.concatenate(
                split(sum(logs), 3) + [jnp.zeros((5, chunk), F32)], axis=0
            )
            outs[k][STATE_SIZE:, at : at + chunk] = jnp.concatenate(
                [mine[:24], total], axis=0
            ).astype(BF16)


def top_kernel(stage, count, *refs):
    parts, outs, prompt_ref = paired(turned(refs[:count]), False), refs[count:-1], refs[-1]
    whole = slice(None)
    place = place_of(stage)
    width = prompt_ref.shape[1]
    logs = [logs_of(part, whole) for part in parts]
    states = [state_of(part, whole) for part in parts]
    final = sum(w * s for w, s in zip(weights_of(logs, place, count), states)).astype(BF16)
    prompt_ref[...] = final
    mine = sum(extra_of(part, whole) for part in parts)
    reads = mine[16:24, :STATE_SIZE].astype(BF16)
    gated = mine[0:8] + mine[8:16] * dot(reads, final)
    gated = gated.astype(BF16)
    for k in list(range(1, len(outs))) + [0]:
        scale = weights_of(logs, place, place ^ k)
        outs[k][:STATE_SIZE, :] = sum(w * s for w, s in zip(scale, states)).astype(BF16)
        outs[k][STATE_SIZE:, :] = gated


def down_kernel(stage, above, above_count, count, apart, targets, handed, *refs):
    end = above_count + (2 * count if apart else count)
    pieces, outs = turned(refs[:above_count]), refs[end:]
    parts = paired(refs[above_count:end], apart)
    if handed:
        outs[-1][...] = outs[0][...]
        outs = outs[1:-1]
    place, source = place_of(stage), place_of(above)
    width = pieces[0].shape[1]
    chunk = min(256, width)
    gated_ref = outs[1] if apart and len(outs) > 1 else None
    for k, out_ref in zip(targets, outs):
        for piece in range(above_count):
            for at in range(0, width, chunk):
                start = at if above_count == 1 else (source ^ piece) * width + at
                at_out = window(start, chunk)
                block = pieces[piece][:, at : at + chunk]
                logs = [logs_of(part, at_out) for part in parts]
                state = carry_of(logs, place, place ^ k) * block[:STATE_SIZE].astype(F32)
                for w, part in zip(weights_of(logs, place, place ^ k), parts):
                    state = state + w * state_of(part, at_out)
                out_ref[:STATE_SIZE, at_out] = state.astype(BF16)
                if gated_ref is not None:
                    gated_ref[:, at_out] = block[STATE_SIZE:]
                elif out_ref.shape[0] > STATE_SIZE:
                    out_ref[STATE_SIZE:, at_out] = block[STATE_SIZE:]


def intra_kernel(group, run_ref, runt_ref, stept_ref, skip_ref, x_ref, write_ref, read_ref, *refs):
    fetch = None
    out_ref = refs[0]
    if len(refs) > 1:
        source_ref, out_ref, held_ref, sem = refs
        fetch = pltpu.make_async_copy(source_ref, held_ref, sem)
        fetch.start()
    span, heads = run_ref.shape[1:]
    mid = span // 2
    states = slice(group * STATE_SIZE, (group + 1) * STATE_SIZE)
    scores = dot(read_ref[:, states], write_ref[:, states], ((1,), (1,)))
    row = lax.broadcasted_iota(jnp.int32, (mid, mid), 0)
    causal = row >= lax.broadcasted_iota(jnp.int32, (mid, mid), 1)
    running = run_ref[group]
    low, high = slice(0, mid), slice(mid, span)
    for pair in range(heads // 2):
        found = []
        for k in (2 * pair, 2 * pair + 1):
            h = group * heads + k
            x = x_ref[:, h * HEAD_DIM : (h + 1) * HEAD_DIM]
            t_run, j_run = running[:, k : k + 1], runt_ref[h : h + 1, :]
            step = stept_ref[h : h + 1, :]

            def mixed(rows, cols, masked):
                gap = t_run[rows] - j_run[:, cols]
                if masked:
                    gap = jnp.where(causal, gap, -jnp.inf)
                return (scores[rows, cols] * jnp.exp(gap) * step[:, cols]).astype(BF16)

            top = dot(mixed(low, low, True), x[low])
            bottom = dot(mixed(high, low, False), x[low]) + dot(mixed(high, high, True), x[high])
            found.append(jnp.concatenate([top, bottom], axis=0))
        at = slice(pair * 2 * HEAD_DIM, (pair + 1) * 2 * HEAD_DIM)
        lanes = slice((group * heads + 2 * pair) * HEAD_DIM, (group * heads + 2 * pair + 2) * HEAD_DIM)
        both = jnp.concatenate(found, axis=1)
        out_ref[:, at] = both + skip_ref[:, lanes] * x_ref[:, lanes].astype(F32)
    if fetch is not None:
        fetch.wait()


def intra(group, run, runt, stept, skip, x, write, read, after, wanted=()):
    span, per_group = run.shape[1:]
    wide = per_group * HEAD_DIM
    return call(
        functools.partial(intra_kernel, group),
        "intra",
        [shape((span, wide), F32)] + [shape(value.shape, value.dtype) for value in wanted],
        (run, runt, stept, skip, x, write, read, *map(in_hbm, wanted)),
        specs=[WHOLE] * 7 + [IN_HBM] * len(wanted),
        scratch=[pltpu.SemaphoreType.DMA] * len(wanted),
        after=after,
        flops=per_group * span * span * HEAD_DIM * 2,
        moved=wide * span * 6,
        exps=per_group * span * span * 3 // 4,
    )


def finish_kernel(stage, reach_ref, read_ref, own_ref, got_ref, *refs):
    base_refs, (out_ref, token_ref, held_ref, sems) = refs[:-4], refs[-4:]
    token_ref[...] = jnp.zeros_like(token_ref)
    place = place_of(stage)
    heads = reach_ref.shape[1] // 2
    lanes = held_ref.shape[1]
    wide = lanes // len(base_refs)
    half = lanes // 2
    chunk = lanes // sems.shape[0]
    copies = []
    for k, lane0 in enumerate(range(0, lanes, chunk)):
        group, at = lane0 // wide, lane0 % half
        at_in, at_out = slice(at, at + chunk), slice(lane0, lane0 + chunk)
        entering = jnp.where(place == lane0 // half, own_ref[:, at_in], got_ref[:, at_in])
        inter = dot(read_ref[:, group * STATE_SIZE : (group + 1) * STATE_SIZE], entering)
        inter = inter * dot(reach_ref[...], head_mask(2 * heads, heads, chunk, lane0))
        base = base_refs[group][:, lane0 % wide : lane0 % wide + chunk]
        held_ref[:, at_out] = (inter + base).astype(BF16)
        copies.append(
            pltpu.make_async_copy(held_ref.at[:, at_out], out_ref.at[:, at_out], sems.at[k])
        )
        copies[-1].start()
    for copy in copies:
        copy.wait()


def finish(stage, reach, read, own, got, bases):
    span = read.shape[0]
    lanes = 2 * own.shape[1]
    chunk = min(512, own.shape[1])
    return call(
        functools.partial(finish_kernel, stage),
        "finish",
        [shape((span, lanes), BF16), shape((8, 128), F32)],
        (reach, read, own, got, *bases),
        out_specs=[IN_HBM, WHOLE],
        scratch=[pltpu.VMEM((span, lanes), BF16), pltpu.SemaphoreType.DMA((lanes // chunk,))],
        moved=1,
    )


def resident_kernel(state_ref, vread_ref, q1_ref, q2_ref, gain_ref, out_ref):
    groups = vread_ref.shape[1] // STATE_SIZE
    wide = state_ref.shape[0] // groups
    for g in range(groups):
        at = slice(g * wide, (g + 1) * wide)
        reads = vread_ref[:, g * STATE_SIZE : (g + 1) * STATE_SIZE]
        drawn = dot(reads, state_ref[at, :], ((1,), (1,)))
        gated = q1_ref[:, at] + q2_ref[:, at] * drawn
        out_ref[:, at] = normed(gated, gain_ref[:, at]).astype(BF16)


def normed(gated, gain):
    mean_square = jnp.mean(gated * gated, axis=1, keepdims=True)
    return gated * lax.rsqrt(mean_square + EPSILON) * gain


def resident_hidden(state, vread, q1, q2, gain, after):
    lanes = state.shape[0]
    return call(
        resident_kernel,
        "resident_hidden",
        [shape((DRAFTS, lanes), BF16)],
        (state, vread, q1, q2, gain),
        after=after,
        flops=2 * DRAFTS * lanes * STATE_SIZE,
    )[0]


def hand_on(value, after):
    def copy(value_ref, out_ref):
        out_ref[...] = value_ref[...]

    return call(copy, "hand_on", [shape(value.shape, value.dtype)], [value], after=after)[0]


def gather_in(values):
    def copy(*refs):
        for k in range(len(values)):
            refs[len(values) + k][...] = refs[k][...]

    return call(
        copy, "gather_in", [shape(v.shape, v.dtype) for v in values], values, flops=10**10, moved=1
    )


def join_kernel(axis, *refs):
    out_ref = refs[-1]
    for k, ref in enumerate(refs[:-1]):
        size = ref.shape[axis]
        at = slice(k * size, (k + 1) * size)
        if axis == 0:
            out_ref[at, :] = ref[...]
        else:
            out_ref[:, at] = ref[...]


def join(parts, axis, after=()):
    dims = list(parts[0].shape)
    dims[axis] *= len(parts)
    return call(
        functools.partial(join_kernel, axis), "join", [shape(tuple(dims), parts[0].dtype)], parts, after=after, moved=1
    )[0]


def project_kernel(stages, head_count, *refs):
    owner_ref, own_rows, got_rows, own_ref, got_ref, gain_ref, weight_ref = refs[:7]
    outs = refs[7 : 7 + head_count]
    gated_ref, left_ref, total_ref = refs[7 + head_count :]
    here, head = lax.axis_index("seq"), lax.axis_index("head")
    place = place_of(stages[0])
    half = own_ref.shape[1]
    lanes = weight_ref.shape[0]
    wide = min(1024, lanes)
    rows = own_rows.shape[0]
    for k, ref in enumerate((own_ref, got_ref)):
        gated_ref[:, window((place ^ k) * half, half)] = ref[...].astype(F32)
    left_ref[0:rows, :] = own_rows[...]
    left_ref[rows : 2 * rows, :] = got_rows[...]
    for lane0 in range(0, lanes, wide):
        at = slice(lane0, lane0 + wide)
        hidden = normed(gated_ref[:, at], gain_ref[:, at])
        hidden = jnp.concatenate([hidden, jnp.zeros_like(hidden)], axis=0)
        left_ref[2 * rows :, at] = hidden.astype(BF16)
    total_ref[...] = dot(left_ref[...], weight_ref[...])

    per_head = 2 * rows // DRAFTS // head_count
    offsets = [0]
    for factor, stride in reversed(stages):
        offsets = [a + k * stride for k in range(factor) for a in offsets]
    owner = owner_ref[...]
    tail = total_ref[2 * rows : 2 * rows + DRAFTS, :]
    for k in list(range(1, head_count)) + [0]:
        first = (head ^ k) * per_head
        for slot in range(per_head):
            at = slice(slot * DRAFTS, (slot + 1) * DRAFTS)
            offset = here ^ (first + slot)
            block = jnp.int32(0)
            for position, value in enumerate(offsets):
                block = jnp.where(offset == value, position, block)
            drawn = total_ref[window(block * DRAFTS, DRAFTS), :]
            drawn = jnp.where(owner == first + slot, tail, drawn)
            outs[k][at, :] = drawn.astype(outs[k].dtype)


def project(stages, owner, own_rows, got_rows, own, got, gain, weight, head_count):
    lanes, cols = weight.shape
    rows = 2 * own_rows.shape[0]
    return call(
        functools.partial(project_kernel, stages, head_count),
        "project",
        [shape((rows // head_count, cols), BF16 if k else F32) for k in range(head_count)],
        (owner, own_rows, got_rows, own, got, gain, weight),
        scratch=[
            pltpu.VMEM((DRAFTS, lanes), F32),
            pltpu.VMEM((rows + 16, lanes), BF16),
            pltpu.VMEM((rows + 16, cols), F32),
        ],
        moved=1,
    )


def prepare_kernel(owner_ref, resident_ref, tail_ref, vwrite_ref, base_ref, factor_ref):
    here = lax.axis_index("seq")
    lanes = resident_ref.shape[0]
    wide = lanes // (vwrite_ref.shape[1] // STATE_SIZE)
    chunk = min(512, wide)
    is_owner = owner_ref[0:1, :STATE_SIZE] == here
    row = lax.broadcasted_iota(jnp.int32, (32, STATE_SIZE), 0)
    ones = jnp.where((row >= 24) & (row < 27), 1.0, 0.0)
    for start in range(0, lanes, chunk):
        rows, group = slice(start, start + chunk), start // wide
        writes = vwrite_ref[:, group * STATE_SIZE : (group + 1) * STATE_SIZE].astype(F32)
        writes = jnp.concatenate([writes, writes, writes, jnp.zeros_like(writes)], axis=0)
        right = jnp.concatenate([writes, ones], axis=1).astype(BF16)
        left = tail_ref[:, rows].astype(F32).T.astype(BF16)
        both = dot(left, right)
        added, decay = both[:, :STATE_SIZE], both[:, STATE_SIZE:]
        kept = decay * resident_ref[rows, :].astype(F32)
        base_ref[rows, :] = added + jnp.where(is_owner, 0.0, kept)
        factor_ref[rows, :] = jnp.where(is_owner, decay, 0.0)


def prepare(owner, resident, tail, vwrite, after):
    return call(
        prepare_kernel,
        "prepare_states",
        [shape(resident.shape, F32)] * 2,
        (owner, resident, tail, vwrite),
        after=after,
        moved=1,
    )


def states_kernel(stages, scattered, pieces, *refs):
    base_ref, factor_ref = refs[:2]
    prompt_refs, refs = refs[2 : 2 + pieces], refs[2 + pieces :]
    share_refs, (new_ref, slice_ref, verify_ref, turned_ref, held_ref, sems) = refs[:-6], refs[-6:]
    here = lax.axis_index("seq")
    verify_ref[...] = sum(ref[...].astype(F32) for ref in share_refs).astype(BF16)
    core, line, last = stages
    lanes = base_ref.shape[0]
    part = lanes // pieces
    width = part // (last[0] if len(scattered) > 1 else 1)
    chunk = lanes // sems.shape[0]
    copies = []
    for step in range(sems.shape[0]):
        rows = slice(step * chunk, (step + 1) * chunk)
        for lane in range(step * chunk, (step + 1) * chunk, width):
            spot = lane // part
            piece = (spot // line[0] ^ place_of(core)) * line[0] + (spot % line[0] ^ place_of(line))
            position = jnp.int32(0)
            if len(scattered) > 1:
                position = lane % part // width ^ place_of(last)
            at = window(position * width, width)
            found = prompt_refs[0][:, at]
            for k in range(1, pieces):
                found = jnp.where(piece == k, prompt_refs[k][:, at], found)
            turned_ref[lane : lane + width, :] = found.astype(F32).T
        new = factor_ref[rows, :] * turned_ref[rows, :] + base_ref[rows, :]
        held_ref[rows, :] = new.astype(BF16)
        copies.append(pltpu.make_async_copy(held_ref.at[rows, :], new_ref.at[rows, :], sems.at[step]))
        copies[-1].start()
    per_slice = slice_ref.shape[1] // STATE_SIZE
    heads = slice_ref.shape[0]
    for k in range(per_slice):
        picked = turned_ref[pl.ds(here * per_slice + k, heads, stride=HEAD_DIM), :]
        slice_ref[:, k * STATE_SIZE : (k + 1) * STATE_SIZE] = picked.astype(BF16)
    for copy in copies:
        copy.wait()


def states(stages, scattered, prepared, prompts, shares, seq_count):
    lanes = prepared[0].shape[0]
    chunk = min(512, lanes // 2)
    return call(
        functools.partial(states_kernel, stages, scattered, len(prompts)),
        "states",
        [
            shape((lanes, STATE_SIZE), BF16),
            shape((lanes // HEAD_DIM, HEAD_DIM // seq_count * STATE_SIZE), BF16),
            shape(shares[0].shape, BF16),
        ],
        (*prepared, *prompts, *shares),
        out_specs=[IN_HBM, WHOLE, WHOLE],
        scratch=[
            pltpu.VMEM((lanes, STATE_SIZE), F32),
            pltpu.VMEM((lanes, STATE_SIZE), BF16),
            pltpu.SemaphoreType.DMA((lanes // chunk,)),
        ],
        flops=2 * lanes * STATE_SIZE * 64,
    )


def on_device(
    prefill_input,
    prefill_step,
    write_proj,
    read_proj,
    decay_rate,
    skip_gain,
    resident_state,
    owner_slot,
    draft_ids,
    accepted_len,
    draft_input,
    draft_gate,
    draft_write,
    draft_read,
    draft_step,
    norm_gain,
    out_weight,
):
    span, lanes = prefill_input.shape
    assert span == BLOCK_LEN
    heads = decay_rate.shape[0]
    groups = write_proj.shape[1] // STATE_SIZE
    per_group = heads // groups
    half = lanes // 2
    seq_count, head_count = lax.axis_size("seq"), lax.axis_size("head")
    stages = tree_stages(seq_count)
    core, line, last = stages
    slots = owner_slot.shape[0]
    assert core[0] == 2 and slots == seq_count
    rate, skip, gain = decay_rate[None], skip_gain[None], norm_gain[None]
    resident = resident_state.reshape(lanes, STATE_SIZE)

    inputs = [
        in_hbm(value)
        for value in (
            prefill_step.T, rate, owner_slot, draft_ids.T, accepted_len, write_proj, prefill_input,
            draft_input, draft_gate, draft_write, draft_read, draft_step, skip, rate, read_proj, resident,
            gain,
        )
    ]
    passed = 12
    opened = call(
        functools.partial(open_kernel, core, len(inputs), passed),
        "open_block",
        [
            shape((STATE_SIZE, half), BF16),
            shape((groups, span, per_group), F32),
            shape((heads, span), F32),
            shape((heads, span), F32),
            shape((span, 2 * heads), BF16),
            shape((span, 2 * heads), BF16),
            shape((DRAFTS, draft_input.shape[0]), F32),
            shape((DRAFTS, 128), jnp.int32),
            shape((DRAFTS, out_weight.shape[1]), jnp.int32),
        ]
        + [shape(value.shape, value.dtype) for value in inputs[-passed:]],
        inputs,
        specs=[IN_HBM] * len(inputs),
        scratch=[pltpu.SemaphoreType.DMA((len(inputs) + 1,))]
        + [
            (pltpu.SMEM if value.dtype == jnp.int32 else pltpu.VMEM)(value.shape, value.dtype)
            for value in inputs[:-passed]
        ],
        flops=span * lanes * STATE_SIZE * 2,
    )
    sent, run, runt, stept, reach, end, pick, kept, owner = opened[:9]
    writes, x, din, dgate, dwrite, dread, dstep, skip, rate, reads, resident, gain = opened[9:]
    received = swap(sent, "seq", core, 1)
    own_extra, sent_extra, skip_lanes, q1, q2, vread, vwrite, tail = call(
        functools.partial(draft_kernel, core),
        "draft_rows",
        [
            shape((EXTRA, half), BF16),
            shape((EXTRA, half), BF16),
            shape((1, lanes), F32),
            shape((DRAFTS, lanes), F32),
            shape((DRAFTS, lanes), F32),
            shape((DRAFTS, groups * STATE_SIZE), BF16),
            shape((DRAFTS, groups * STATE_SIZE), BF16),
            shape((32, lanes), BF16),
        ],
        (pick, kept, owner, runt, rate, skip, din, dgate, dwrite, dread, dstep),
        after=[sent],
        scratch=[pltpu.VMEM((EXTRA, lanes), BF16)],
        flops=DRAFTS * lanes * 100,
    )
    received_extra = swap(sent_extra, "seq", core, 1)
    (own,) = call(
        functools.partial(own_kernel, core),
        "own_message",
        [shape((STATE_SIZE, half), BF16)],
        (end, x, writes),
        after=[sent_extra],
        flops=span * lanes * STATE_SIZE,
    )
    core_parts = [own, own_extra, received, received_extra]

    bases, fetched = [], []

    def fill(after):
        if len(bases) < groups:
            wanted = [] if bases else [out_weight]
            base, *found = intra(
                len(bases), run, runt, stept, skip_lanes, x, writes, reads, after, wanted
            )
            bases.append(base)
            fetched.extend(found)
        return bases[-1:]

    def exchange(parts, stage):
        got = {k: swap(parts[k], "seq", stage, k) for k in range(1, stage[0])}
        return [parts[0]] + [got[k] for k in range(1, stage[0])]

    line_width = half // line[0]
    split_last = line_width % (last[0] * 128) == 0
    last_width = line_width // last[0] if split_last else line_width
    outs = call(
        functools.partial(up_kernel, core, line, 2, True),
        "up_line",
        [shape((UP_ROWS, line_width), BF16)] * line[0],
        core_parts,
        flops=half * UP_ROWS * 4,
    )
    line_parts = exchange(outs, line)
    hidden = resident_hidden(resident, vread, q1, q2, gain, [outs[-1]])
    hiddens = exchange([hidden] * last[0], last)
    filled = fill([outs[-1]])
    outs = call(
        functools.partial(up_kernel, line, last, line[0], False),
        "up_last",
        [shape((UP_ROWS, last_width), BF16)] * (last[0] if split_last else 1),
        line_parts,
        after=filled + hiddens[2:],
        flops=line_width * UP_ROWS * 4,
    )
    last_parts = exchange(outs if split_last else outs * last[0], last)
    filled = fill([outs[-1]])
    *outs, prompt = call(
        functools.partial(top_kernel, last, last[0]),
        "top",
        [shape((DOWN_ROWS, last_width), BF16)] * (last[0] if split_last else 1)
        + [shape((STATE_SIZE, last_width), BF16)],
        turned(last_parts),
        after=filled,
        flops=last_width * UP_ROWS * 16,
    )

    pieces = exchange(outs, last) if split_last else outs
    if split_last:
        pieces = pieces[:1] + list(gather_in(pieces[:0:-1]))[::-1]
    hidden = join(hiddens, 0, [outs[-1]])
    hiddens = exchange([hidden] * line[0], line)
    filled = fill([outs[-1]])
    outs = call(
        functools.partial(down_kernel, line, last, len(pieces), line[0], False, range(line[0]), False),
        "down_line",
        [shape((DOWN_ROWS, line_width), BF16)] * line[0],
        [*turned(pieces), *line_parts],
        after=filled + hiddens[1:],
        flops=line_width * UP_ROWS * 8,
    )
    pieces = exchange(outs, line)
    hidden = join(hiddens, 0, [outs[-1]])
    hiddens = [hidden, swap(hidden, "seq", core, 1)]
    filled = fill([outs[-1]])
    prepared = prepare(owner, resident, tail, vwrite, filled)
    filled = [*prepared, *hiddens[1:]]
    scattered = [line, last] if split_last else [line]
    if split_last:
        prompt = hand_on(prompt, [outs[-1]])
        prompt = join(exchange([prompt] * last[0], last), 1)
        filled.append(prompt)

    def down_core(target, after):
        return call(
            functools.partial(down_kernel, core, line, line[0], 2, True, (target,), False),
            "down_core",
            [shape((STATE_SIZE, half), BF16)] + [shape((DRAFTS, half), BF16)] * target,
            turned(pieces) + core_parts,
            after=after,
            moved=1,
        )

    sent, gated = down_core(1, filled)
    received_gated, received = swap(gated, "seq", core, 1), swap(sent, "seq", core, 1)
    while len(bases) < groups:
        fill([])

    shares = project(
        stages, owner, *hiddens, gated, received_gated, gain, fetched[0], head_count
    )
    (entering,) = down_core(0, shares[:1])
    prefill_out, token = finish(core, reach, reads, entering, received, bases)
    shares = [shares[0]] + [swap(shares[k], "head", (head_count, 1), k) for k in range(1, head_count)]

    prompts = exchange([prompt] * line[0], line)
    first = swap(hand_on(prompt, shares[:1]), "seq", core, 1)
    late = [hand_on(piece, [token, *shares[1:]]) for piece in prompts[1:]]
    prompts += [first] + [swap(piece, "seq", core, 1) for piece in late]
    new_state, state_slice, verify_out = states(
        stages, scattered, prepared, prompts, shares, seq_count
    )
    return (
        prefill_out,
        new_state.reshape(1, heads, HEAD_DIM, STATE_SIZE),
        verify_out,
        state_slice,
    )


def solution(mesh):
    return jax.shard_map(
        on_device,
        mesh=mesh,
        in_specs=(
            P("seq", "head"),
            P("seq", "head"),
            P("seq", "head"),
            P("seq", "head"),
            P("head"),
            P("head"),
            P("seq", "head", None, None),
            P(),
            P(),
            P(),
            P("seq", "head"),
            P("seq", "head"),
            P("seq", "head"),
            P("seq", "head"),
            P("seq", "head"),
            P("head"),
            P("head", "seq"),
        ),
        out_specs=(
            P("seq", "head"),
            P("seq", "head", None, None),
            P("head", "seq"),
            P("head", "seq"),
        ),
        check_vma=False,
    )
```

```python
import functools

import jax
import jax.numpy as jnp
from jax import lax
from jax.experimental import pallas as pl
from jax.experimental.pallas import tpu as pltpu
from jax.sharding import PartitionSpec as P

HEAD_DIM = 64
STATE_SIZE = 128
BLOCK_LEN = 256
DRAFTS = 8
EPSILON = 1e-05
EXTRA = 32
UP_ROWS = STATE_SIZE + EXTRA
READ_AT = STATE_SIZE + 16
LOG_AT = STATE_SIZE + 24
DOWN_ROWS = STATE_SIZE + 8

F32 = jnp.float32
BF16 = jnp.bfloat16


def tree_stages(count):
    factors, rest = [], count
    if rest > 1:
        factors.append(2)
        rest //= 2
    inner = 1
    while inner * inner * 4 <= rest:
        inner *= 2
    factors += [inner, rest // inner]
    stages, stride = [], 1
    for factor in factors:
        stages.append((factor, stride))
        stride *= factor
    assert stride == count
    return stages


def swap(value, axis, stage, offset):
    count, stride = lax.axis_size(axis), stage[1]
    return lax.ppermute(value, axis, [(k, k ^ (offset * stride)) for k in range(count)])


def place_of(stage):
    factor, stride = stage
    return lax.rem(lax.div(lax.axis_index("seq"), stride), factor)


def dot(a, b, dims=((1,), (0,))):
    return lax.dot_general(a, b, (dims, ((), ())), preferred_element_type=F32)


def split(value, parts):
    found = []
    for _ in range(parts):
        part = value.astype(BF16).astype(F32)
        found.append(part)
        value = value - part
    return found


def head_mask(rows, heads, lanes, lane0):
    row = lax.broadcasted_iota(jnp.int32, (rows, lanes), 0) & (heads - 1)
    head = lax.shift_right_logical(lax.broadcasted_iota(jnp.int32, (rows, lanes), 1) + lane0, 6)
    return jnp.where(row == head, 1.0, 0.0).astype(BF16)


def window(start, size):
    return pl.ds(pl.multiple_of(start, size), size)


def ordered(kernel, count):
    return lambda *refs: kernel(*refs[count:])


ANYWHERE = pl.BlockSpec(memory_space=pl.ANY)
WHOLE = pl.BlockSpec(memory_space=pltpu.VMEM)
IN_HBM = pl.BlockSpec(memory_space=pltpu.HBM)


def call(
    kernel, name, outs, args, specs=None, out_specs=None, grid=(), after=(), scratch=(), alias=None,
    flops=0, exps=0, moved=None, vmem=32,
):
    if specs is None:
        specs = [WHOLE] * len(args)
    if out_specs is None:
        out_specs = [WHOLE] * len(outs)
    if moved is None:
        moved = sum(a.size * a.dtype.itemsize for a in (*args, *outs))
    first = len(after)
    return pl.pallas_call(
        ordered(kernel, first),
        name=name,
        grid=grid,
        out_shape=outs,
        in_specs=[ANYWHERE] * first + specs,
        out_specs=out_specs,
        scratch_shapes=list(scratch),
        input_output_aliases={first + k: v for k, v in (alias or {}).items()},
        compiler_params=pltpu.CompilerParams(vmem_limit_bytes=vmem * 1024 * 1024),
        cost_estimate=pl.CostEstimate(flops=flops, bytes_accessed=moved, transcendentals=exps),
    )(*after, *args)


def in_hbm(value):
    return pltpu.with_memory_space_constraint(value, pltpu.HBM)


def shape(dims, dtype):
    return jax.ShapeDtypeStruct(dims, dtype)


def open_kernel(stage, count, passed, *refs):
    sources, rest = refs[:count], refs[count:]
    outs, scratch = rest[: 9 + passed], rest[9 + passed :]
    outs, later = outs[:9], list(outs[9:])
    sent_ref, run_ref, runt_ref, stept_ref, reach_ref, end_ref, pick_ref, kept_out, owner_out = outs
    sems, held = scratch[0], [*scratch[1:], *later]
    here = lax.axis_index("seq")
    place = place_of(stage)
    early = count - passed
    half = sent_ref.shape[1]

    def fetch(k, at=None):
        if at is None:
            return pltpu.make_async_copy(sources[k], held[k], sems.at[k])
        sem = sems.at[k if at == 1 else count]
        lanes = window((place ^ at) * half, half)
        return pltpu.make_async_copy(sources[k].at[:, lanes], held[k].at[:, lanes], sem)

    first = [fetch(k) for k in range(early + 1)] + [fetch(early + 1, 1)]
    rest = [fetch(early + 1, 0)] + [fetch(k) for k in range(early + 2, count)]
    for copy in first:
        copy.start()
    for copy in first[:early]:
        copy.wait()
    for copy in rest:
        copy.start()
    turned_ref, rate_ref, owner_ref, ids_ref, kept_ref, write_ref, x_ref = held[:7]
    heads, span = turned_ref.shape
    groups = write_ref.shape[1] // STATE_SIZE
    per_group = heads // groups

    step_rows = turned_ref[...]
    stept_ref[...] = step_rows
    pad = (-heads) % 128
    if pad:
        step_rows = jnp.concatenate([step_rows, jnp.zeros((pad, span), F32)], axis=0)
    step = step_rows.T[:, :heads]
    log_decay = -step * rate_ref[...]
    lower = lax.broadcasted_iota(jnp.int32, (span, span), 0) >= lax.broadcasted_iota(
        jnp.int32, (span, span), 1
    )
    lower = jnp.where(lower, 1.0, 0.0).astype(BF16)
    running = sum(dot(lower, part.astype(BF16)) for part in split(log_decay, 3))
    to_end = jnp.exp(running[span - 1 : span, :] - running) * step
    end_ref[...] = jnp.concatenate(split(to_end, 2), axis=1).astype(BF16)

    for copy in first[early:]:
        copy.wait()
    fill_message(place ^ 1, end_ref, x_ref, write_ref, sent_ref)

    wide_run = running
    if pad:
        wide_run = jnp.concatenate([running, jnp.zeros((span, pad), F32)], axis=1)
    runt_ref[...] = wide_run.T[:heads]
    for g in range(groups):
        run_ref[g] = running[:, g * per_group : (g + 1) * per_group]
    reach_ref[...] = jnp.concatenate(split(jnp.exp(running), 2), axis=1).astype(BF16)

    slots = owner_ref.shape[0]
    request = lax.fori_loop(
        0, slots, lambda r, found: jnp.where(owner_ref[r] == here, r, found), jnp.int32(0)
    )
    row = lax.broadcasted_iota(jnp.int32, pick_ref.shape, 0)
    col = lax.broadcasted_iota(jnp.int32, pick_ref.shape, 1)
    pick = jnp.zeros(pick_ref.shape, F32)
    for i in range(DRAFTS):
        pick = jnp.where((row == i) & (col == ids_ref[i, request]), 1.0, pick)
    pick_ref[...] = pick
    kept_out[...] = jnp.zeros(kept_out.shape, jnp.int32) + kept_ref[request]
    owner_out[...] = jnp.zeros(owner_out.shape, jnp.int32) + owner_ref[0]
    for copy in rest:
        copy.wait()


def draft_kernel(
    stage,
    pick_ref,
    kept_ref,
    owner_ref,
    runt_ref,
    rate_ref,
    skip_ref,
    din_ref,
    dgate_ref,
    dwrite_ref,
    dread_ref,
    dstep_ref,
    own_ref,
    sent_ref,
    skip_out,
    q1_ref,
    q2_ref,
    vread_ref,
    vwrite_ref,
    tail_ref,
    extra_ref,
):
    heads, span = runt_ref.shape
    lanes = din_ref.shape[1]
    groups = dwrite_ref.shape[1] // STATE_SIZE
    wide = lanes // groups
    here = lax.axis_index("seq")
    place = place_of(stage)
    pick = pick_ref[...].astype(BF16)
    vin = dot(pick, din_ref[...])
    vgate = dot(pick, dgate_ref[...])
    vwrite = dot(pick, dwrite_ref[...]).astype(BF16)
    vread = dot(pick, dread_ref[...]).astype(BF16)
    vwrite_ref[...] = vwrite
    vread_ref[...] = vread
    vstep = sum(dot(pick, part.astype(BF16)) for part in split(dstep_ref[...], 3))
    vlog = -vstep * rate_ref[...]
    index = lax.broadcasted_iota(jnp.int32, (DRAFTS, heads), 0)
    kept_heads = kept_ref[:, :1]
    acc = jnp.zeros((1, heads), F32)
    vrun = jnp.zeros((DRAFTS, heads), F32)
    reach = jnp.zeros((1, heads), F32)
    for i in range(DRAFTS):
        acc = acc + vlog[i : i + 1]
        vrun = jnp.where(index == i, acc, vrun)
        reach = jnp.where(i < kept_heads[0:1], acc, reach)
    total = runt_ref[:, span - 128 :]
    if heads < 128:
        total = jnp.concatenate([total, jnp.zeros((128 - heads, 128), F32)], axis=0)
    total = total.T[127:128, :heads]
    others = jnp.where(index == 0, total, jnp.where(index == 1, skip_ref[...], reach))
    stacked = split(jnp.concatenate([vrun, vstep, others], axis=0), 3)
    stacked = jnp.concatenate(stacked, axis=0).astype(BF16)
    row = lax.broadcasted_iota(jnp.int32, (DRAFTS, wide), 0)
    kept = kept_ref[:, :1]
    is_owner = owner_ref[0:1, :1] == here
    for g in range(groups):
        at = slice(g * wide, (g + 1) * wide)
        spread = dot(stacked, head_mask(heads, heads, wide, g * wide))
        spread = spread[0:24] + spread[24:48] + spread[48:72]
        vrun_l, vstep_l = spread[0:8], spread[8:16]
        total_l, skip_l, reach_l = spread[16:17], spread[17:18], spread[18:19]
        skip_out[:, at] = skip_l
        vin_g = vin[:, at]
        vr = vread[:, g * STATE_SIZE : (g + 1) * STATE_SIZE]
        vw = vwrite[:, g * STATE_SIZE : (g + 1) * STATE_SIZE]
        scores = dot(vr, vw, ((1,), (1,)))
        direct = skip_l * vin_g
        for j in range(DRAFTS):
            decay = jnp.exp(jnp.where(row >= j, vrun_l - vrun_l[j : j + 1], -jnp.inf))
            direct = direct + decay * scores[:, j : j + 1] * (vstep_l[j : j + 1] * vin_g[j : j + 1])
        gate = vgate[:, at]
        gate = gate / (1.0 + jnp.exp(-gate))
        q1 = direct * gate
        q2 = jnp.exp(vrun_l) * gate
        q1_ref[:, at] = q1
        q2_ref[:, at] = q2
        live = jnp.exp(jnp.where(row < kept, reach_l - vrun_l, -jnp.inf)) * vstep_l * vin_g
        keep_l = jnp.concatenate(
            split(jnp.exp(reach_l), 3) + [jnp.zeros((5, wide), F32)], axis=0
        )
        tail_ref[:, at] = jnp.concatenate(split(live, 3) + [keep_l], axis=0).astype(BF16)
        read_l = jnp.concatenate([vr.astype(F32)] * (wide // STATE_SIZE), axis=1)
        mine = jnp.concatenate([q1, q2, read_l], axis=0)
        mine = jnp.where(is_owner, mine, 0.0)
        logs = jnp.concatenate(split(total_l, 3) + [jnp.zeros((5, wide), F32)], axis=0)
        extra_ref[:, at] = jnp.concatenate([mine, logs], axis=0).astype(BF16)
    half = lanes // 2
    own_ref[...] = extra_ref[:, window(place * half, half)]
    sent_ref[...] = extra_ref[:, window((place ^ 1) * half, half)]


def fill_message(side, end_ref, x_ref, write_ref, out_ref):
    heads = end_ref.shape[1] // 2
    half = out_ref.shape[1]
    wide = 2 * half // (write_ref.shape[1] // STATE_SIZE)
    chunk = min(wide, half)
    start = side * half
    for at in range(0, half, chunk):
        lane0 = start + at
        group = lax.div(lane0, wide)
        scale = dot(end_ref[...], head_mask(2 * heads, heads, chunk, lane0))
        weighted = (x_ref[:, window(lane0, chunk)].astype(F32) * scale).astype(BF16)
        writes = write_ref[:, window(group * STATE_SIZE, STATE_SIZE)]
        writes = writes.astype(F32).T.astype(BF16)
        out_ref[:, at : at + chunk] = dot(writes, weighted).astype(BF16)


def own_kernel(stage, end_ref, x_ref, write_ref, out_ref):
    fill_message(place_of(stage), end_ref, x_ref, write_ref, out_ref)


def state_of(part, at):
    return part[0][:STATE_SIZE, at].astype(F32)


def extra_of(part, at):
    return (part[1][:, at] if part[2] else part[0][STATE_SIZE:UP_ROWS, at]).astype(F32)


def logs_of(part, at):
    found = extra_of(part, at)[LOG_AT - STATE_SIZE :]
    return found[0:1] + found[1:2] + found[2:3]


def turned(parts):
    return [parts[0], *parts[:0:-1]]


def paired(refs, apart):
    if apart:
        return [(refs[k], refs[k + 1], True) for k in range(0, len(refs), 2)]
    return [(ref, None, False) for ref in refs]


def weights_of(logs, place, target):
    spots = [place ^ k for k in range(len(logs))]
    found = []
    for k, spot in enumerate(spots):
        between = jnp.zeros_like(logs[0])
        for other, log in zip(spots, logs):
            if other is not spot:
                between = between + jnp.where((spot < other) & (other < target), log, 0.0)
        found.append(jnp.where(spot < target, jnp.exp(between), 0.0))
    return found


def carry_of(logs, place, target):
    ahead = jnp.zeros_like(logs[0])
    for k, log in enumerate(logs):
        ahead = ahead + jnp.where((place ^ k) < target, log, 0.0)
    return jnp.exp(ahead)


def up_kernel(stage, following, count, apart, *refs):
    taken = 2 * count if apart else count
    parts, outs = paired(refs[:taken], apart), refs[taken:]
    place, target = place_of(stage), place_of(following)
    width = outs[0].shape[1]
    chunk = min(256, width)
    order = list(range(1, len(outs))) + [0]
    for k in order:
        for at in range(0, width, chunk):
            start = at if len(outs) == 1 else (target ^ k) * width + at
            at_in = window(start, chunk)
            logs = [logs_of(part, at_in) for part in parts]
            scale = weights_of(logs, place, count)
            state = sum(w * state_of(part, at_in) for w, part in zip(scale, parts))
            outs[k][:STATE_SIZE, at : at + chunk] = state.astype(BF16)
            mine = sum(extra_of(part, at_in) for part in parts)
            total = jnp.concatenate(
                split(sum(logs), 3) + [jnp.zeros((5, chunk), F32)], axis=0
            )
            outs[k][STATE_SIZE:, at : at + chunk] = jnp.concatenate(
                [mine[:24], total], axis=0
            ).astype(BF16)


def top_kernel(stage, count, *refs):
    parts, outs, prompt_ref = paired(turned(refs[:count]), False), refs[count:-1], refs[-1]
    whole = slice(None)
    place = place_of(stage)
    width = prompt_ref.shape[1]
    logs = [logs_of(part, whole) for part in parts]
    states = [state_of(part, whole) for part in parts]
    final = sum(w * s for w, s in zip(weights_of(logs, place, count), states)).astype(BF16)
    prompt_ref[...] = final
    mine = sum(extra_of(part, whole) for part in parts)
    reads = mine[16:24, :STATE_SIZE].astype(BF16)
    gated = mine[0:8] + mine[8:16] * dot(reads, final)
    gated = gated.astype(BF16)
    for k in list(range(1, len(outs))) + [0]:
        scale = weights_of(logs, place, place ^ k)
        outs[k][:STATE_SIZE, :] = sum(w * s for w, s in zip(scale, states)).astype(BF16)
        outs[k][STATE_SIZE:, :] = gated


def down_kernel(stage, above, above_count, count, apart, targets, handed, *refs):
    end = above_count + (2 * count if apart else count)
    pieces, outs = turned(refs[:above_count]), refs[end:]
    parts = paired(refs[above_count:end], apart)
    if handed:
        outs[-1][...] = outs[0][...]
        outs = outs[1:-1]
    place, source = place_of(stage), place_of(above)
    width = pieces[0].shape[1]
    chunk = min(256, width)
    gated_ref = outs[1] if apart and len(outs) > 1 else None
    for k, out_ref in zip(targets, outs):
        for piece in range(above_count):
            for at in range(0, width, chunk):
                start = at if above_count == 1 else (source ^ piece) * width + at
                at_out = window(start, chunk)
                block = pieces[piece][:, at : at + chunk]
                logs = [logs_of(part, at_out) for part in parts]
                state = carry_of(logs, place, place ^ k) * block[:STATE_SIZE].astype(F32)
                for w, part in zip(weights_of(logs, place, place ^ k), parts):
                    state = state + w * state_of(part, at_out)
                out_ref[:STATE_SIZE, at_out] = state.astype(BF16)
                if gated_ref is not None:
                    gated_ref[:, at_out] = block[STATE_SIZE:]
                elif out_ref.shape[0] > STATE_SIZE:
                    out_ref[STATE_SIZE:, at_out] = block[STATE_SIZE:]


def intra_kernel(group, run_ref, runt_ref, stept_ref, skip_ref, x_ref, write_ref, read_ref, *refs):
    fetch = None
    out_ref = refs[0]
    if len(refs) > 1:
        source_ref, out_ref, held_ref, sem = refs
        fetch = pltpu.make_async_copy(source_ref, held_ref, sem)
        fetch.start()
    span, heads = run_ref.shape[1:]
    mid = span // 2
    states = slice(group * STATE_SIZE, (group + 1) * STATE_SIZE)
    scores = dot(read_ref[:, states], write_ref[:, states], ((1,), (1,)))
    row = lax.broadcasted_iota(jnp.int32, (mid, mid), 0)
    causal = row >= lax.broadcasted_iota(jnp.int32, (mid, mid), 1)
    running = run_ref[group]
    low, high = slice(0, mid), slice(mid, span)
    for pair in range(heads // 2):
        found = []
        for k in (2 * pair, 2 * pair + 1):
            h = group * heads + k
            x = x_ref[:, h * HEAD_DIM : (h + 1) * HEAD_DIM]
            t_run, j_run = running[:, k : k + 1], runt_ref[h : h + 1, :]
            step = stept_ref[h : h + 1, :]

            def mixed(rows, cols, masked):
                gap = t_run[rows] - j_run[:, cols]
                if masked:
                    gap = jnp.where(causal, gap, -jnp.inf)
                return (scores[rows, cols] * jnp.exp(gap) * step[:, cols]).astype(BF16)

            top = dot(mixed(low, low, True), x[low])
            bottom = dot(mixed(high, low, False), x[low]) + dot(mixed(high, high, True), x[high])
            found.append(jnp.concatenate([top, bottom], axis=0))
        at = slice(pair * 2 * HEAD_DIM, (pair + 1) * 2 * HEAD_DIM)
        lanes = slice((group * heads + 2 * pair) * HEAD_DIM, (group * heads + 2 * pair + 2) * HEAD_DIM)
        both = jnp.concatenate(found, axis=1)
        out_ref[:, at] = both + skip_ref[:, lanes] * x_ref[:, lanes].astype(F32)
    if fetch is not None:
        fetch.wait()


def intra(group, run, runt, stept, skip, x, write, read, after, wanted=()):
    span, per_group = run.shape[1:]
    wide = per_group * HEAD_DIM
    return call(
        functools.partial(intra_kernel, group),
        "intra",
        [shape((span, wide), F32)] + [shape(value.shape, value.dtype) for value in wanted],
        (run, runt, stept, skip, x, write, read, *map(in_hbm, wanted)),
        specs=[WHOLE] * 7 + [IN_HBM] * len(wanted),
        scratch=[pltpu.SemaphoreType.DMA] * len(wanted),
        after=after,
        flops=per_group * span * span * HEAD_DIM * 2,
        moved=wide * span * 6,
        exps=per_group * span * span * 3 // 4,
    )


def finish_kernel(stage, reach_ref, read_ref, own_ref, got_ref, *refs):
    base_refs, (out_ref, token_ref, held_ref, sems) = refs[:-4], refs[-4:]
    token_ref[...] = jnp.zeros_like(token_ref)
    place = place_of(stage)
    heads = reach_ref.shape[1] // 2
    lanes = held_ref.shape[1]
    wide = lanes // len(base_refs)
    half = lanes // 2
    chunk = lanes // sems.shape[0]
    copies = []
    for k, lane0 in enumerate(range(0, lanes, chunk)):
        group, at = lane0 // wide, lane0 % half
        at_in, at_out = slice(at, at + chunk), slice(lane0, lane0 + chunk)
        entering = jnp.where(place == lane0 // half, own_ref[:, at_in], got_ref[:, at_in])
        inter = dot(read_ref[:, group * STATE_SIZE : (group + 1) * STATE_SIZE], entering)
        inter = inter * dot(reach_ref[...], head_mask(2 * heads, heads, chunk, lane0))
        base = base_refs[group][:, lane0 % wide : lane0 % wide + chunk]
        held_ref[:, at_out] = (inter + base).astype(BF16)
        copies.append(
            pltpu.make_async_copy(held_ref.at[:, at_out], out_ref.at[:, at_out], sems.at[k])
        )
        copies[-1].start()
    for copy in copies:
        copy.wait()


def finish(stage, reach, read, own, got, bases):
    span = read.shape[0]
    lanes = 2 * own.shape[1]
    chunk = min(512, own.shape[1])
    return call(
        functools.partial(finish_kernel, stage),
        "finish",
        [shape((span, lanes), BF16), shape((8, 128), F32)],
        (reach, read, own, got, *bases),
        out_specs=[IN_HBM, WHOLE],
        scratch=[pltpu.VMEM((span, lanes), BF16), pltpu.SemaphoreType.DMA((lanes // chunk,))],
        moved=1,
    )


def resident_kernel(state_ref, vread_ref, q1_ref, q2_ref, gain_ref, out_ref):
    groups = vread_ref.shape[1] // STATE_SIZE
    wide = state_ref.shape[0] // groups
    for g in range(groups):
        at = slice(g * wide, (g + 1) * wide)
        reads = vread_ref[:, g * STATE_SIZE : (g + 1) * STATE_SIZE]
        drawn = dot(reads, state_ref[at, :], ((1,), (1,)))
        gated = q1_ref[:, at] + q2_ref[:, at] * drawn
        out_ref[:, at] = normed(gated, gain_ref[:, at]).astype(BF16)


def normed(gated, gain):
    mean_square = jnp.mean(gated * gated, axis=1, keepdims=True)
    return gated * lax.rsqrt(mean_square + EPSILON) * gain


def resident_hidden(state, vread, q1, q2, gain, after):
    lanes = state.shape[0]
    return call(
        resident_kernel,
        "resident_hidden",
        [shape((DRAFTS, lanes), BF16)],
        (state, vread, q1, q2, gain),
        after=after,
        flops=2 * DRAFTS * lanes * STATE_SIZE,
    )[0]


def hand_on(value, after):
    def copy(value_ref, out_ref):
        out_ref[...] = value_ref[...]

    return call(copy, "hand_on", [shape(value.shape, value.dtype)], [value], after=after)[0]


def gather_in(values, after=()):
    def copy(*refs):
        for k in range(len(values)):
            refs[len(values) + k][...] = refs[k][...]

    return call(
        copy, "gather_in", [shape(v.shape, v.dtype) for v in values], values, after=after,
        flops=10**10, moved=1,
    )


def join_kernel(axis, *refs):
    out_ref = refs[-1]
    for k, ref in enumerate(refs[:-1]):
        size = ref.shape[axis]
        at = slice(k * size, (k + 1) * size)
        if axis == 0:
            out_ref[at, :] = ref[...]
        else:
            out_ref[:, at] = ref[...]


def join(parts, axis, after=()):
    dims = list(parts[0].shape)
    dims[axis] *= len(parts)
    return call(
        functools.partial(join_kernel, axis), "join", [shape(tuple(dims), parts[0].dtype)], parts, after=after, moved=1
    )[0]


def project_kernel(stages, head_count, *refs):
    owner_ref, own_rows, got_rows, own_ref, got_ref, gain_ref, weight_ref = refs[:7]
    outs = refs[7 : 7 + head_count]
    gated_ref, left_ref, total_ref = refs[7 + head_count :]
    here, head = lax.axis_index("seq"), lax.axis_index("head")
    place = place_of(stages[0])
    half = own_ref.shape[1]
    lanes = weight_ref.shape[0]
    wide = min(1024, lanes)
    rows = own_rows.shape[0]
    for k, ref in enumerate((own_ref, got_ref)):
        gated_ref[:, window((place ^ k) * half, half)] = ref[...].astype(F32)
    left_ref[0:rows, :] = own_rows[...]
    left_ref[rows : 2 * rows, :] = got_rows[...]
    for lane0 in range(0, lanes, wide):
        at = slice(lane0, lane0 + wide)
        hidden = normed(gated_ref[:, at], gain_ref[:, at])
        hidden = jnp.concatenate([hidden, jnp.zeros_like(hidden)], axis=0)
        left_ref[2 * rows :, at] = hidden.astype(BF16)
    total_ref[...] = dot(left_ref[...], weight_ref[...])

    per_head = 2 * rows // DRAFTS // head_count
    offsets = [0]
    for factor, stride in reversed(stages):
        offsets = [a + k * stride for k in range(factor) for a in offsets]
    owner = owner_ref[...]
    tail = total_ref[2 * rows : 2 * rows + DRAFTS, :]
    for k in list(range(1, head_count)) + [0]:
        first = (head ^ k) * per_head
        for slot in range(per_head):
            at = slice(slot * DRAFTS, (slot + 1) * DRAFTS)
            offset = here ^ (first + slot)
            block = jnp.int32(0)
            for position, value in enumerate(offsets):
                block = jnp.where(offset == value, position, block)
            drawn = total_ref[window(block * DRAFTS, DRAFTS), :]
            drawn = jnp.where(owner == first + slot, tail, drawn)
            outs[k][at, :] = drawn.astype(outs[k].dtype)


def project(stages, owner, own_rows, got_rows, own, got, gain, weight, head_count):
    lanes, cols = weight.shape
    rows = 2 * own_rows.shape[0]
    return call(
        functools.partial(project_kernel, stages, head_count),
        "project",
        [shape((rows // head_count, cols), BF16 if k else F32) for k in range(head_count)],
        (owner, own_rows, got_rows, own, got, gain, weight),
        scratch=[
            pltpu.VMEM((DRAFTS, lanes), F32),
            pltpu.VMEM((rows + 16, lanes), BF16),
            pltpu.VMEM((rows + 16, cols), F32),
        ],
        moved=1,
    )


def prepare_kernel(owner_ref, resident_ref, tail_ref, vwrite_ref, base_ref, factor_ref):
    here = lax.axis_index("seq")
    lanes = resident_ref.shape[0]
    wide = lanes // (vwrite_ref.shape[1] // STATE_SIZE)
    chunk = min(512, wide)
    is_owner = owner_ref[0:1, :STATE_SIZE] == here
    row = lax.broadcasted_iota(jnp.int32, (32, STATE_SIZE), 0)
    ones = jnp.where((row >= 24) & (row < 27), 1.0, 0.0)
    for start in range(0, lanes, chunk):
        rows, group = slice(start, start + chunk), start // wide
        writes = vwrite_ref[:, group * STATE_SIZE : (group + 1) * STATE_SIZE].astype(F32)
        writes = jnp.concatenate([writes, writes, writes, jnp.zeros_like(writes)], axis=0)
        right = jnp.concatenate([writes, ones], axis=1).astype(BF16)
        left = tail_ref[:, rows].astype(F32).T.astype(BF16)
        both = dot(left, right)
        added, decay = both[:, :STATE_SIZE], both[:, STATE_SIZE:]
        kept = decay * resident_ref[rows, :].astype(F32)
        base_ref[rows, :] = added + jnp.where(is_owner, 0.0, kept)
        factor_ref[rows, :] = jnp.where(is_owner, decay, 0.0)


def prepare(owner, resident, tail, vwrite, after):
    return call(
        prepare_kernel,
        "prepare_states",
        [shape(resident.shape, F32)] * 2,
        (owner, resident, tail, vwrite),
        after=after,
        moved=1,
    )


def states_kernel(stages, scattered, pieces, *refs):
    base_ref, factor_ref = refs[:2]
    prompt_refs, refs = refs[2 : 2 + pieces], refs[2 + pieces :]
    share_refs, (new_ref, slice_ref, verify_ref, turned_ref, held_ref, sems) = refs[:-6], refs[-6:]
    here = lax.axis_index("seq")
    verify_ref[...] = sum(ref[...].astype(F32) for ref in share_refs).astype(BF16)
    core, line, last = stages
    lanes = base_ref.shape[0]
    part = lanes // pieces
    width = part // (last[0] if len(scattered) > 1 else 1)
    chunk = lanes // sems.shape[0]
    copies = []
    for step in range(sems.shape[0]):
        rows = slice(step * chunk, (step + 1) * chunk)
        for lane in range(step * chunk, (step + 1) * chunk, width):
            spot = lane // part
            piece = (spot // line[0] ^ place_of(core)) * line[0] + (spot % line[0] ^ place_of(line))
            position = jnp.int32(0)
            if len(scattered) > 1:
                apart = lane % part // width ^ place_of(last)
                position = jnp.where(apart == 0, 0, last[0] - apart)
            at = window(position * width, width)
            found = prompt_refs[0][:, at]
            for k in range(1, pieces):
                found = jnp.where(piece == k, prompt_refs[k][:, at], found)
            turned_ref[lane : lane + width, :] = found.astype(F32).T
        new = factor_ref[rows, :] * turned_ref[rows, :] + base_ref[rows, :]
        held_ref[rows, :] = new.astype(BF16)
        copies.append(pltpu.make_async_copy(held_ref.at[rows, :], new_ref.at[rows, :], sems.at[step]))
        copies[-1].start()
    per_slice = slice_ref.shape[1] // STATE_SIZE
    heads = slice_ref.shape[0]
    for k in range(per_slice):
        picked = turned_ref[pl.ds(here * per_slice + k, heads, stride=HEAD_DIM), :]
        slice_ref[:, k * STATE_SIZE : (k + 1) * STATE_SIZE] = picked.astype(BF16)
    for copy in copies:
        copy.wait()


def states(stages, scattered, prepared, prompts, shares, seq_count):
    lanes = prepared[0].shape[0]
    chunk = min(512, lanes // 2)
    return call(
        functools.partial(states_kernel, stages, scattered, len(prompts)),
        "states",
        [
            shape((lanes, STATE_SIZE), BF16),
            shape((lanes // HEAD_DIM, HEAD_DIM // seq_count * STATE_SIZE), BF16),
            shape(shares[0].shape, BF16),
        ],
        (*prepared, *prompts, *shares),
        out_specs=[IN_HBM, WHOLE, WHOLE],
        scratch=[
            pltpu.VMEM((lanes, STATE_SIZE), F32),
            pltpu.VMEM((lanes, STATE_SIZE), BF16),
            pltpu.SemaphoreType.DMA((lanes // chunk,)),
        ],
        flops=2 * lanes * STATE_SIZE * 64,
    )


def on_device(
    prefill_input,
    prefill_step,
    write_proj,
    read_proj,
    decay_rate,
    skip_gain,
    resident_state,
    owner_slot,
    draft_ids,
    accepted_len,
    draft_input,
    draft_gate,
    draft_write,
    draft_read,
    draft_step,
    norm_gain,
    out_weight,
):
    span, lanes = prefill_input.shape
    assert span == BLOCK_LEN
    heads = decay_rate.shape[0]
    groups = write_proj.shape[1] // STATE_SIZE
    per_group = heads // groups
    half = lanes // 2
    seq_count, head_count = lax.axis_size("seq"), lax.axis_size("head")
    stages = tree_stages(seq_count)
    core, line, last = stages
    slots = owner_slot.shape[0]
    assert core[0] == 2 and slots == seq_count
    rate, skip, gain = decay_rate[None], skip_gain[None], norm_gain[None]
    resident = resident_state.reshape(lanes, STATE_SIZE)

    inputs = [
        in_hbm(value)
        for value in (
            prefill_step.T, rate, owner_slot, draft_ids.T, accepted_len, write_proj, prefill_input,
            draft_input, draft_gate, draft_write, draft_read, draft_step, skip, rate, read_proj, resident,
            gain,
        )
    ]
    passed = 12
    opened = call(
        functools.partial(open_kernel, core, len(inputs), passed),
        "open_block",
        [
            shape((STATE_SIZE, half), BF16),
            shape((groups, span, per_group), F32),
            shape((heads, span), F32),
            shape((heads, span), F32),
            shape((span, 2 * heads), BF16),
            shape((span, 2 * heads), BF16),
            shape((DRAFTS, draft_input.shape[0]), F32),
            shape((DRAFTS, 128), jnp.int32),
            shape((DRAFTS, out_weight.shape[1]), jnp.int32),
        ]
        + [shape(value.shape, value.dtype) for value in inputs[-passed:]],
        inputs,
        specs=[IN_HBM] * len(inputs),
        scratch=[pltpu.SemaphoreType.DMA((len(inputs) + 1,))]
        + [
            (pltpu.SMEM if value.dtype == jnp.int32 else pltpu.VMEM)(value.shape, value.dtype)
            for value in inputs[:-passed]
        ],
        flops=span * lanes * STATE_SIZE * 2,
    )
    sent, run, runt, stept, reach, end, pick, kept, owner = opened[:9]
    writes, x, din, dgate, dwrite, dread, dstep, skip, rate, reads, resident, gain = opened[9:]
    received = swap(sent, "seq", core, 1)
    own_extra, sent_extra, skip_lanes, q1, q2, vread, vwrite, tail = call(
        functools.partial(draft_kernel, core),
        "draft_rows",
        [
            shape((EXTRA, half), BF16),
            shape((EXTRA, half), BF16),
            shape((1, lanes), F32),
            shape((DRAFTS, lanes), F32),
            shape((DRAFTS, lanes), F32),
            shape((DRAFTS, groups * STATE_SIZE), BF16),
            shape((DRAFTS, groups * STATE_SIZE), BF16),
            shape((32, lanes), BF16),
        ],
        (pick, kept, owner, runt, rate, skip, din, dgate, dwrite, dread, dstep),
        after=[sent],
        scratch=[pltpu.VMEM((EXTRA, lanes), BF16)],
        flops=DRAFTS * lanes * 100,
    )
    received_extra = swap(sent_extra, "seq", core, 1)
    (own,) = call(
        functools.partial(own_kernel, core),
        "own_message",
        [shape((STATE_SIZE, half), BF16)],
        (end, x, writes),
        after=[sent_extra],
        flops=span * lanes * STATE_SIZE,
    )
    core_parts = [own, own_extra, received, received_extra]

    bases, fetched = [], []

    def fill(after):
        if len(bases) < groups:
            wanted = [out_weight] if len(bases) == min(1, groups - 1) else []
            base, *found = intra(
                len(bases), run, runt, stept, skip_lanes, x, writes, reads, after, wanted
            )
            bases.append(base)
            fetched.extend(found)
        return bases[-1:]

    def exchange(parts, stage):
        got = {k: swap(parts[k], "seq", stage, k) for k in range(1, stage[0])}
        return [parts[0]] + [got[k] for k in range(1, stage[0])]

    line_width = half // line[0]
    split_last = line_width % (last[0] * 128) == 0
    last_width = line_width // last[0] if split_last else line_width
    outs = call(
        functools.partial(up_kernel, core, line, 2, True),
        "up_line",
        [shape((UP_ROWS, line_width), BF16)] * line[0],
        core_parts,
        flops=half * UP_ROWS * 4,
    )
    line_parts = exchange(outs, line)
    hidden = resident_hidden(resident, vread, q1, q2, gain, [outs[-1]])
    hiddens = exchange([hidden] * last[0], last)
    filled = fill([outs[-1]])
    outs = call(
        functools.partial(up_kernel, line, last, line[0], False),
        "up_last",
        [shape((UP_ROWS, last_width), BF16)] * (last[0] if split_last else 1),
        line_parts,
        after=filled + hiddens[:0:-1],
        flops=line_width * UP_ROWS * 4,
    )
    last_parts = exchange(outs if split_last else outs * last[0], last)
    hidden = join(hiddens, 0, [outs[-1]])
    hiddens = exchange([hidden] * line[0], line)
    filled = fill([outs[-1]])
    last_parts = last_parts[:1] + list(gather_in(last_parts[:0:-1], filled))[::-1]
    *outs, prompt = call(
        functools.partial(top_kernel, last, last[0]),
        "top",
        [shape((DOWN_ROWS, last_width), BF16)] * (last[0] if split_last else 1)
        + [shape((STATE_SIZE, last_width), BF16)],
        turned(last_parts),
        after=filled,
        flops=last_width * UP_ROWS * 16,
    )

    pieces = exchange(outs, last) if split_last else outs
    hidden = join(hiddens, 0, [outs[-1]])
    filled = fill([outs[-1], hidden])
    if split_last:
        pieces = pieces[:1] + list(gather_in(pieces[:0:-1], filled))[::-1]
    outs = call(
        functools.partial(down_kernel, line, last, len(pieces), line[0], False, range(line[0]), False),
        "down_line",
        [shape((DOWN_ROWS, line_width), BF16)] * line[0],
        [*turned(pieces), *line_parts],
        after=filled,
        flops=line_width * UP_ROWS * 8,
    )
    pieces = exchange(outs, line)
    hiddens = [hidden, swap(hidden, "seq", core, 1)]
    filled = fill([outs[-1]])
    prepared = prepare(owner, resident, tail, vwrite, filled)
    filled = [*prepared, *hiddens[1:]]
    scattered = [line, last] if split_last else [line]
    if split_last:
        prompt = hand_on(prompt, [outs[-1]])
        parts = exchange([prompt] * last[0], last)
        prompt = join(turned(parts), 1)
        filled.append(prompt)

    def down_core(target, after):
        return call(
            functools.partial(down_kernel, core, line, line[0], 2, True, (target,), False),
            "down_core",
            [shape((STATE_SIZE, half), BF16)] + [shape((DRAFTS, half), BF16)] * target,
            turned(pieces) + core_parts,
            after=after,
            moved=1,
        )

    sent, gated = down_core(1, filled)
    received_gated, received = swap(gated, "seq", core, 1), swap(sent, "seq", core, 1)
    (received_gated,) = gather_in([received_gated])
    while len(bases) < groups:
        fill([])

    shares = project(
        stages, owner, *hiddens, gated, received_gated, gain, fetched[0], head_count
    )
    (entering,) = down_core(0, shares[:1])
    prefill_out, token = finish(core, reach, reads, entering, received, bases)
    shares = [shares[0]] + [swap(shares[k], "head", (head_count, 1), k) for k in range(1, head_count)]

    prompts = exchange([prompt] * line[0], line)
    first = swap(hand_on(prompt, shares[:1]), "seq", core, 1)
    late = [hand_on(piece, [token, *shares[1:]]) for piece in prompts[1:]]
    prompts += [first] + [swap(piece, "seq", core, 1) for piece in late]
    new_state, state_slice, verify_out = states(
        stages, scattered, prepared, prompts, shares, seq_count
    )
    return (
        prefill_out,
        new_state.reshape(1, heads, HEAD_DIM, STATE_SIZE),
        verify_out,
        state_slice,
    )


def solution(mesh):
    return jax.shard_map(
        on_device,
        mesh=mesh,
        in_specs=(
            P("seq", "head"),
            P("seq", "head"),
            P("seq", "head"),
            P("seq", "head"),
            P("head"),
            P("head"),
            P("seq", "head", None, None),
            P(),
            P(),
            P(),
            P("seq", "head"),
            P("seq", "head"),
            P("seq", "head"),
            P("seq", "head"),
            P("seq", "head"),
            P("head"),
            P("head", "seq"),
        ),
        out_specs=(
            P("seq", "head"),
            P("seq", "head", None, None),
            P("head", "seq"),
            P("head", "seq"),
        ),
        check_vma=False,
    )
```

```python
import functools

import jax
import jax.numpy as jnp
from jax import lax
from jax.experimental import pallas as pl
from jax.experimental.pallas import tpu as pltpu
from jax.sharding import PartitionSpec as P

HEAD_DIM = 64
STATE_SIZE = 128
BLOCK_LEN = 256
DRAFTS = 8
EPSILON = 1e-05
EXTRA = 32
UP_ROWS = STATE_SIZE + EXTRA
READ_AT = STATE_SIZE + 16
LOG_AT = STATE_SIZE + 24
DOWN_ROWS = STATE_SIZE + 8

F32 = jnp.float32
BF16 = jnp.bfloat16


def tree_stages(count):
    factors, rest = [], count
    if rest > 1:
        factors.append(2)
        rest //= 2
    inner = 1
    while inner * inner * 4 <= rest:
        inner *= 2
    factors += [inner, rest // inner]
    stages, stride = [], 1
    for factor in factors:
        stages.append((factor, stride))
        stride *= factor
    assert stride == count
    return stages


def swap(value, axis, stage, offset):
    count, stride = lax.axis_size(axis), stage[1]
    return lax.ppermute(value, axis, [(k, k ^ (offset * stride)) for k in range(count)])


def place_of(stage):
    factor, stride = stage
    return lax.rem(lax.div(lax.axis_index("seq"), stride), factor)


def dot(a, b, dims=((1,), (0,))):
    return lax.dot_general(a, b, (dims, ((), ())), preferred_element_type=F32)


def split(value, parts):
    found = []
    for _ in range(parts):
        part = value.astype(BF16).astype(F32)
        found.append(part)
        value = value - part
    return found


def head_mask(rows, heads, lanes, lane0):
    row = lax.broadcasted_iota(jnp.int32, (rows, lanes), 0) & (heads - 1)
    head = lax.shift_right_logical(lax.broadcasted_iota(jnp.int32, (rows, lanes), 1) + lane0, 6)
    return jnp.where(row == head, 1.0, 0.0).astype(BF16)


def window(start, size):
    return pl.ds(pl.multiple_of(start, size), size)


def ordered(kernel, count):
    return lambda *refs: kernel(*refs[count:])


ANYWHERE = pl.BlockSpec(memory_space=pl.ANY)
WHOLE = pl.BlockSpec(memory_space=pltpu.VMEM)
IN_HBM = pl.BlockSpec(memory_space=pltpu.HBM)


def call(
    kernel, name, outs, args, specs=None, out_specs=None, grid=(), after=(), scratch=(), alias=None,
    flops=0, exps=0, moved=None, vmem=32,
):
    if specs is None:
        specs = [WHOLE] * len(args)
    if out_specs is None:
        out_specs = [WHOLE] * len(outs)
    if moved is None:
        moved = sum(a.size * a.dtype.itemsize for a in (*args, *outs))
    first = len(after)
    return pl.pallas_call(
        ordered(kernel, first),
        name=name,
        grid=grid,
        out_shape=outs,
        in_specs=[ANYWHERE] * first + specs,
        out_specs=out_specs,
        scratch_shapes=list(scratch),
        input_output_aliases={first + k: v for k, v in (alias or {}).items()},
        compiler_params=pltpu.CompilerParams(vmem_limit_bytes=vmem * 1024 * 1024),
        cost_estimate=pl.CostEstimate(flops=flops, bytes_accessed=moved, transcendentals=exps),
    )(*after, *args)


def in_hbm(value):
    return pltpu.with_memory_space_constraint(value, pltpu.HBM)


def shape(dims, dtype):
    return jax.ShapeDtypeStruct(dims, dtype)


def open_kernel(stage, count, passed, *refs):
    sources, rest = refs[:count], refs[count:]
    outs, scratch = rest[: 9 + passed], rest[9 + passed :]
    outs, later = outs[:9], list(outs[9:])
    sent_ref, run_ref, runt_ref, stept_ref, reach_ref, end_ref, pick_ref, kept_out, owner_out = outs
    sems, held = scratch[0], [*scratch[1:], *later]
    here = lax.axis_index("seq")
    place = place_of(stage)
    early = count - passed
    half = sent_ref.shape[1]

    def fetch(k, at=None):
        if at is None:
            return pltpu.make_async_copy(sources[k], held[k], sems.at[k])
        sem = sems.at[k if at == 1 else count]
        lanes = window((place ^ at) * half, half)
        return pltpu.make_async_copy(sources[k].at[:, lanes], held[k].at[:, lanes], sem)

    first = [fetch(k) for k in range(early + 1)] + [fetch(early + 1, 1)]
    rest = [fetch(early + 1, 0)] + [fetch(k) for k in range(early + 2, count)]
    for copy in first:
        copy.start()
    for copy in first[:early]:
        copy.wait()
    for copy in rest:
        copy.start()
    turned_ref, rate_ref, owner_ref, ids_ref, kept_ref, write_ref, x_ref = held[:7]
    heads, span = turned_ref.shape
    groups = write_ref.shape[1] // STATE_SIZE
    per_group = heads // groups

    step_rows = turned_ref[...]
    stept_ref[...] = step_rows
    pad = (-heads) % 128
    if pad:
        step_rows = jnp.concatenate([step_rows, jnp.zeros((pad, span), F32)], axis=0)
    step = step_rows.T[:, :heads]
    log_decay = -step * rate_ref[...]
    lower = lax.broadcasted_iota(jnp.int32, (span, span), 0) >= lax.broadcasted_iota(
        jnp.int32, (span, span), 1
    )
    lower = jnp.where(lower, 1.0, 0.0).astype(BF16)
    running = sum(dot(lower, part.astype(BF16)) for part in split(log_decay, 3))
    to_end = jnp.exp(running[span - 1 : span, :] - running) * step
    end_ref[...] = jnp.concatenate(split(to_end, 2), axis=1).astype(BF16)

    for copy in first[early:]:
        copy.wait()
    fill_message(place ^ 1, end_ref, x_ref, write_ref, sent_ref)

    wide_run = running
    if pad:
        wide_run = jnp.concatenate([running, jnp.zeros((span, pad), F32)], axis=1)
    runt_ref[...] = wide_run.T[:heads]
    for g in range(groups):
        run_ref[g] = running[:, g * per_group : (g + 1) * per_group]
    reach_ref[...] = jnp.concatenate(split(jnp.exp(running), 2), axis=1).astype(BF16)

    slots = owner_ref.shape[0]
    request = lax.fori_loop(
        0, slots, lambda r, found: jnp.where(owner_ref[r] == here, r, found), jnp.int32(0)
    )
    row = lax.broadcasted_iota(jnp.int32, pick_ref.shape, 0)
    col = lax.broadcasted_iota(jnp.int32, pick_ref.shape, 1)
    pick = jnp.zeros(pick_ref.shape, F32)
    for i in range(DRAFTS):
        pick = jnp.where((row == i) & (col == ids_ref[i, request]), 1.0, pick)
    pick_ref[...] = pick
    kept_out[...] = jnp.zeros(kept_out.shape, jnp.int32) + kept_ref[request]
    owner_out[...] = jnp.zeros(owner_out.shape, jnp.int32) + owner_ref[0]
    for copy in rest:
        copy.wait()


def draft_kernel(
    stage,
    pick_ref,
    kept_ref,
    owner_ref,
    runt_ref,
    rate_ref,
    skip_ref,
    din_ref,
    dgate_ref,
    dwrite_ref,
    dread_ref,
    dstep_ref,
    own_ref,
    sent_ref,
    skip_out,
    q1_ref,
    q2_ref,
    vread_ref,
    vwrite_ref,
    tail_ref,
    extra_ref,
):
    heads, span = runt_ref.shape
    lanes = din_ref.shape[1]
    groups = dwrite_ref.shape[1] // STATE_SIZE
    wide = lanes // groups
    here = lax.axis_index("seq")
    place = place_of(stage)
    pick = pick_ref[...].astype(BF16)
    vin = dot(pick, din_ref[...])
    vgate = dot(pick, dgate_ref[...])
    vwrite = dot(pick, dwrite_ref[...]).astype(BF16)
    vread = dot(pick, dread_ref[...]).astype(BF16)
    vwrite_ref[...] = vwrite
    vread_ref[...] = vread
    vstep = sum(dot(pick, part.astype(BF16)) for part in split(dstep_ref[...], 3))
    vlog = -vstep * rate_ref[...]
    index = lax.broadcasted_iota(jnp.int32, (DRAFTS, heads), 0)
    kept_heads = kept_ref[:, :1]
    acc = jnp.zeros((1, heads), F32)
    vrun = jnp.zeros((DRAFTS, heads), F32)
    reach = jnp.zeros((1, heads), F32)
    for i in range(DRAFTS):
        acc = acc + vlog[i : i + 1]
        vrun = jnp.where(index == i, acc, vrun)
        reach = jnp.where(i < kept_heads[0:1], acc, reach)
    total = runt_ref[:, span - 128 :]
    if heads < 128:
        total = jnp.concatenate([total, jnp.zeros((128 - heads, 128), F32)], axis=0)
    total = total.T[127:128, :heads]
    others = jnp.where(index == 0, total, jnp.where(index == 1, skip_ref[...], reach))
    stacked = split(jnp.concatenate([vrun, vstep, others], axis=0), 3)
    stacked = jnp.concatenate(stacked, axis=0).astype(BF16)
    row = lax.broadcasted_iota(jnp.int32, (DRAFTS, wide), 0)
    kept = kept_ref[:, :1]
    is_owner = owner_ref[0:1, :1] == here
    for g in range(groups):
        at = slice(g * wide, (g + 1) * wide)
        spread = dot(stacked, head_mask(heads, heads, wide, g * wide))
        spread = spread[0:24] + spread[24:48] + spread[48:72]
        vrun_l, vstep_l = spread[0:8], spread[8:16]
        total_l, skip_l, reach_l = spread[16:17], spread[17:18], spread[18:19]
        skip_out[:, at] = skip_l
        vin_g = vin[:, at]
        vr = vread[:, g * STATE_SIZE : (g + 1) * STATE_SIZE]
        vw = vwrite[:, g * STATE_SIZE : (g + 1) * STATE_SIZE]
        scores = dot(vr, vw, ((1,), (1,)))
        direct = skip_l * vin_g
        for j in range(DRAFTS):
            decay = jnp.exp(jnp.where(row >= j, vrun_l - vrun_l[j : j + 1], -jnp.inf))
            direct = direct + decay * scores[:, j : j + 1] * (vstep_l[j : j + 1] * vin_g[j : j + 1])
        gate = vgate[:, at]
        gate = gate / (1.0 + jnp.exp(-gate))
        q1 = direct * gate
        q2 = jnp.exp(vrun_l) * gate
        q1_ref[:, at] = q1
        q2_ref[:, at] = q2
        live = jnp.exp(jnp.where(row < kept, reach_l - vrun_l, -jnp.inf)) * vstep_l * vin_g
        keep_l = jnp.concatenate(
            split(jnp.exp(reach_l), 3) + [jnp.zeros((5, wide), F32)], axis=0
        )
        tail_ref[:, at] = jnp.concatenate(split(live, 3) + [keep_l], axis=0).astype(BF16)
        read_l = jnp.concatenate([vr.astype(F32)] * (wide // STATE_SIZE), axis=1)
        mine = jnp.concatenate([q1, q2, read_l], axis=0)
        mine = jnp.where(is_owner, mine, 0.0)
        logs = jnp.concatenate(split(total_l, 3) + [jnp.zeros((5, wide), F32)], axis=0)
        extra_ref[:, at] = jnp.concatenate([mine, logs], axis=0).astype(BF16)
    half = lanes // 2
    own_ref[...] = extra_ref[:, window(place * half, half)]
    sent_ref[...] = extra_ref[:, window((place ^ 1) * half, half)]


def fill_message(side, end_ref, x_ref, write_ref, out_ref):
    heads = end_ref.shape[1] // 2
    half = out_ref.shape[1]
    wide = 2 * half // (write_ref.shape[1] // STATE_SIZE)
    chunk = min(wide, half)
    start = side * half
    for at in range(0, half, chunk):
        lane0 = start + at
        group = lax.div(lane0, wide)
        scale = dot(end_ref[...], head_mask(2 * heads, heads, chunk, lane0))
        weighted = (x_ref[:, window(lane0, chunk)].astype(F32) * scale).astype(BF16)
        writes = write_ref[:, window(group * STATE_SIZE, STATE_SIZE)]
        writes = writes.astype(F32).T.astype(BF16)
        out_ref[:, at : at + chunk] = dot(writes, weighted).astype(BF16)


def own_kernel(stage, end_ref, x_ref, write_ref, out_ref):
    fill_message(place_of(stage), end_ref, x_ref, write_ref, out_ref)


def state_of(part, at):
    return part[0][:STATE_SIZE, at].astype(F32)


def extra_of(part, at):
    return (part[1][:, at] if part[2] else part[0][STATE_SIZE:UP_ROWS, at]).astype(F32)


def logs_of(part, at):
    found = extra_of(part, at)[LOG_AT - STATE_SIZE :]
    return found[0:1] + found[1:2] + found[2:3]


def turned(parts):
    return [parts[0], *parts[:0:-1]]


def paired(refs, apart):
    if apart:
        return [(refs[k], refs[k + 1], True) for k in range(0, len(refs), 2)]
    return [(ref, None, False) for ref in refs]


def weights_of(logs, place, target):
    spots = [place ^ k for k in range(len(logs))]
    found = []
    for k, spot in enumerate(spots):
        between = jnp.zeros_like(logs[0])
        for other, log in zip(spots, logs):
            if other is not spot:
                between = between + jnp.where((spot < other) & (other < target), log, 0.0)
        found.append(jnp.where(spot < target, jnp.exp(between), 0.0))
    return found


def carry_of(logs, place, target):
    ahead = jnp.zeros_like(logs[0])
    for k, log in enumerate(logs):
        ahead = ahead + jnp.where((place ^ k) < target, log, 0.0)
    return jnp.exp(ahead)


def up_kernel(stage, following, count, apart, *refs):
    taken = 2 * count if apart else count
    parts, outs = paired(refs[:taken], apart), refs[taken:]
    place, target = place_of(stage), place_of(following)
    width = outs[0].shape[1]
    chunk = min(256, width)
    order = list(range(1, len(outs))) + [0]
    for k in order:
        for at in range(0, width, chunk):
            start = at if len(outs) == 1 else (target ^ k) * width + at
            at_in = window(start, chunk)
            logs = [logs_of(part, at_in) for part in parts]
            scale = weights_of(logs, place, count)
            state = sum(w * state_of(part, at_in) for w, part in zip(scale, parts))
            outs[k][:STATE_SIZE, at : at + chunk] = state.astype(BF16)
            mine = sum(extra_of(part, at_in) for part in parts)
            total = jnp.concatenate(
                split(sum(logs), 3) + [jnp.zeros((5, chunk), F32)], axis=0
            )
            outs[k][STATE_SIZE:, at : at + chunk] = jnp.concatenate(
                [mine[:24], total], axis=0
            ).astype(BF16)


def top_kernel(stage, count, *refs):
    parts, outs, prompt_ref = paired(turned(refs[:count]), False), refs[count:-1], refs[-1]
    whole = slice(None)
    place = place_of(stage)
    width = prompt_ref.shape[1]
    logs = [logs_of(part, whole) for part in parts]
    states = [state_of(part, whole) for part in parts]
    final = sum(w * s for w, s in zip(weights_of(logs, place, count), states)).astype(BF16)
    prompt_ref[...] = final
    mine = sum(extra_of(part, whole) for part in parts)
    reads = mine[16:24, :STATE_SIZE].astype(BF16)
    gated = mine[0:8] + mine[8:16] * dot(reads, final)
    gated = gated.astype(BF16)
    for k in list(range(1, len(outs))) + [0]:
        scale = weights_of(logs, place, place ^ k)
        outs[k][:STATE_SIZE, :] = sum(w * s for w, s in zip(scale, states)).astype(BF16)
        outs[k][STATE_SIZE:, :] = gated


def down_kernel(stage, above, above_count, count, apart, targets, handed, *refs):
    end = above_count + (2 * count if apart else count)
    pieces, outs = turned(refs[:above_count]), refs[end:]
    parts = paired(refs[above_count:end], apart)
    if handed:
        outs[-1][...] = outs[0][...]
        outs = outs[1:-1]
    place, source = place_of(stage), place_of(above)
    width = pieces[0].shape[1]
    chunk = min(256, width)
    gated_ref = outs[1] if apart and len(outs) > 1 else None
    for k, out_ref in zip(targets, outs):
        for piece in range(above_count):
            for at in range(0, width, chunk):
                start = at if above_count == 1 else (source ^ piece) * width + at
                at_out = window(start, chunk)
                block = pieces[piece][:, at : at + chunk]
                logs = [logs_of(part, at_out) for part in parts]
                state = carry_of(logs, place, place ^ k) * block[:STATE_SIZE].astype(F32)
                for w, part in zip(weights_of(logs, place, place ^ k), parts):
                    state = state + w * state_of(part, at_out)
                out_ref[:STATE_SIZE, at_out] = state.astype(BF16)
                if gated_ref is not None:
                    gated_ref[:, at_out] = block[STATE_SIZE:]
                elif out_ref.shape[0] > STATE_SIZE:
                    out_ref[STATE_SIZE:, at_out] = block[STATE_SIZE:]


def intra_kernel(group, run_ref, runt_ref, stept_ref, skip_ref, x_ref, write_ref, read_ref, *refs):
    fetch = None
    out_ref = refs[0]
    if len(refs) > 1:
        source_ref, out_ref, held_ref, sem = refs
        fetch = pltpu.make_async_copy(source_ref, held_ref, sem)
        fetch.start()
    span, heads = run_ref.shape[1:]
    mid = span // 2
    states = slice(group * STATE_SIZE, (group + 1) * STATE_SIZE)
    scores = dot(read_ref[:, states], write_ref[:, states], ((1,), (1,)))
    row = lax.broadcasted_iota(jnp.int32, (mid, mid), 0)
    causal = row >= lax.broadcasted_iota(jnp.int32, (mid, mid), 1)
    running = run_ref[group]
    low, high = slice(0, mid), slice(mid, span)
    for pair in range(heads // 2):
        found = []
        for k in (2 * pair, 2 * pair + 1):
            h = group * heads + k
            x = x_ref[:, h * HEAD_DIM : (h + 1) * HEAD_DIM]
            t_run, j_run = running[:, k : k + 1], runt_ref[h : h + 1, :]
            step = stept_ref[h : h + 1, :]

            def mixed(rows, cols, masked):
                gap = t_run[rows] - j_run[:, cols]
                if masked:
                    gap = jnp.where(causal, gap, -jnp.inf)
                return (scores[rows, cols] * jnp.exp(gap) * step[:, cols]).astype(BF16)

            top = dot(mixed(low, low, True), x[low])
            bottom = dot(mixed(high, low, False), x[low]) + dot(mixed(high, high, True), x[high])
            found.append(jnp.concatenate([top, bottom], axis=0))
        at = slice(pair * 2 * HEAD_DIM, (pair + 1) * 2 * HEAD_DIM)
        lanes = slice((group * heads + 2 * pair) * HEAD_DIM, (group * heads + 2 * pair + 2) * HEAD_DIM)
        both = jnp.concatenate(found, axis=1)
        out_ref[:, at] = both + skip_ref[:, lanes] * x_ref[:, lanes].astype(F32)
    if fetch is not None:
        fetch.wait()


def intra(group, run, runt, stept, skip, x, write, read, after, wanted=()):
    span, per_group = run.shape[1:]
    wide = per_group * HEAD_DIM
    return call(
        functools.partial(intra_kernel, group),
        "intra",
        [shape((span, wide), F32)] + [shape(value.shape, value.dtype) for value in wanted],
        (run, runt, stept, skip, x, write, read, *map(in_hbm, wanted)),
        specs=[WHOLE] * 7 + [IN_HBM] * len(wanted),
        scratch=[pltpu.SemaphoreType.DMA] * len(wanted),
        after=after,
        flops=per_group * span * span * HEAD_DIM * 2,
        moved=wide * span * 6,
        exps=per_group * span * span * 3 // 4,
    )


def finish_kernel(stage, reach_ref, read_ref, own_ref, got_ref, *refs):
    base_refs, (out_ref, token_ref, held_ref, sems) = refs[:-4], refs[-4:]
    token_ref[...] = jnp.zeros_like(token_ref)
    place = place_of(stage)
    heads = reach_ref.shape[1] // 2
    lanes = held_ref.shape[1]
    wide = lanes // len(base_refs)
    half = lanes // 2
    chunk = lanes // sems.shape[0]
    copies = []
    for k, lane0 in enumerate(range(0, lanes, chunk)):
        group, at = lane0 // wide, lane0 % half
        at_in, at_out = slice(at, at + chunk), slice(lane0, lane0 + chunk)
        entering = jnp.where(place == lane0 // half, own_ref[:, at_in], got_ref[:, at_in])
        inter = dot(read_ref[:, group * STATE_SIZE : (group + 1) * STATE_SIZE], entering)
        inter = inter * dot(reach_ref[...], head_mask(2 * heads, heads, chunk, lane0))
        base = base_refs[group][:, lane0 % wide : lane0 % wide + chunk]
        held_ref[:, at_out] = (inter + base).astype(BF16)
        copies.append(
            pltpu.make_async_copy(held_ref.at[:, at_out], out_ref.at[:, at_out], sems.at[k])
        )
        copies[-1].start()
    for copy in copies:
        copy.wait()


def finish(stage, reach, read, own, got, bases):
    span = read.shape[0]
    lanes = 2 * own.shape[1]
    chunk = min(512, own.shape[1])
    return call(
        functools.partial(finish_kernel, stage),
        "finish",
        [shape((span, lanes), BF16), shape((8, 128), F32)],
        (reach, read, own, got, *bases),
        out_specs=[IN_HBM, WHOLE],
        scratch=[pltpu.VMEM((span, lanes), BF16), pltpu.SemaphoreType.DMA((lanes // chunk,))],
        moved=1,
    )


def resident_kernel(state_ref, vread_ref, q1_ref, q2_ref, gain_ref, out_ref):
    groups = vread_ref.shape[1] // STATE_SIZE
    wide = state_ref.shape[0] // groups
    for g in range(groups):
        at = slice(g * wide, (g + 1) * wide)
        reads = vread_ref[:, g * STATE_SIZE : (g + 1) * STATE_SIZE]
        drawn = dot(reads, state_ref[at, :], ((1,), (1,)))
        gated = q1_ref[:, at] + q2_ref[:, at] * drawn
        out_ref[:, at] = normed(gated, gain_ref[:, at]).astype(BF16)


def normed(gated, gain):
    mean_square = jnp.mean(gated * gated, axis=1, keepdims=True)
    return gated * lax.rsqrt(mean_square + EPSILON) * gain


def resident_hidden(state, vread, q1, q2, gain, after):
    lanes = state.shape[0]
    return call(
        resident_kernel,
        "resident_hidden",
        [shape((DRAFTS, lanes), BF16)],
        (state, vread, q1, q2, gain),
        after=after,
        flops=2 * DRAFTS * lanes * STATE_SIZE,
    )[0]


def hand_on(value, after):
    def copy(value_ref, out_ref):
        out_ref[...] = value_ref[...]

    return call(copy, "hand_on", [shape(value.shape, value.dtype)], [value], after=after)[0]


def gather_in(values, after=()):
    def copy(*refs):
        for k in range(len(values)):
            refs[len(values) + k][...] = refs[k][...]

    return call(
        copy, "gather_in", [shape(v.shape, v.dtype) for v in values], values, after=after,
        flops=10**10, moved=1,
    )


def join_kernel(axis, *refs):
    out_ref = refs[-1]
    for k, ref in enumerate(refs[:-1]):
        size = ref.shape[axis]
        at = slice(k * size, (k + 1) * size)
        if axis == 0:
            out_ref[at, :] = ref[...]
        else:
            out_ref[:, at] = ref[...]


def join(parts, axis, after=()):
    dims = list(parts[0].shape)
    dims[axis] *= len(parts)
    return call(
        functools.partial(join_kernel, axis), "join", [shape(tuple(dims), parts[0].dtype)], parts, after=after, moved=1
    )[0]


def project_kernel(stages, head_count, *refs):
    owner_ref, own_rows, got_rows, own_ref, got_ref, gain_ref, weight_ref = refs[:7]
    outs = refs[7 : 7 + head_count]
    gated_ref, left_ref, total_ref = refs[7 + head_count :]
    here, head = lax.axis_index("seq"), lax.axis_index("head")
    place = place_of(stages[0])
    half = own_ref.shape[1]
    lanes = weight_ref.shape[0]
    wide = min(1024, lanes)
    rows = own_rows.shape[0]
    for k, ref in enumerate((own_ref, got_ref)):
        gated_ref[:, window((place ^ k) * half, half)] = ref[...].astype(F32)
    left_ref[0:rows, :] = own_rows[...]
    left_ref[rows : 2 * rows, :] = got_rows[...]
    for lane0 in range(0, lanes, wide):
        at = slice(lane0, lane0 + wide)
        hidden = normed(gated_ref[:, at], gain_ref[:, at])
        hidden = jnp.concatenate([hidden, jnp.zeros_like(hidden)], axis=0)
        left_ref[2 * rows :, at] = hidden.astype(BF16)
    total_ref[...] = dot(left_ref[...], weight_ref[...])

    per_head = 2 * rows // DRAFTS // head_count
    offsets = [0]
    for factor, stride in reversed(stages):
        offsets = [a + k * stride for k in range(factor) for a in offsets]
    owner = owner_ref[...]
    tail = total_ref[2 * rows : 2 * rows + DRAFTS, :]
    for k in list(range(1, head_count)) + [0]:
        first = (head ^ k) * per_head
        for slot in range(per_head):
            at = slice(slot * DRAFTS, (slot + 1) * DRAFTS)
            offset = here ^ (first + slot)
            block = jnp.int32(0)
            for position, value in enumerate(offsets):
                block = jnp.where(offset == value, position, block)
            drawn = total_ref[window(block * DRAFTS, DRAFTS), :]
            drawn = jnp.where(owner == first + slot, tail, drawn)
            outs[k][at, :] = drawn.astype(outs[k].dtype)


def project(stages, owner, own_rows, got_rows, own, got, gain, weight, head_count):
    lanes, cols = weight.shape
    rows = 2 * own_rows.shape[0]
    return call(
        functools.partial(project_kernel, stages, head_count),
        "project",
        [shape((rows // head_count, cols), BF16 if k else F32) for k in range(head_count)],
        (owner, own_rows, got_rows, own, got, gain, weight),
        scratch=[
            pltpu.VMEM((DRAFTS, lanes), F32),
            pltpu.VMEM((rows + 16, lanes), BF16),
            pltpu.VMEM((rows + 16, cols), F32),
        ],
        moved=1,
    )


def prepare_kernel(owner_ref, resident_ref, tail_ref, vwrite_ref, base_ref, factor_ref):
    here = lax.axis_index("seq")
    lanes = resident_ref.shape[0]
    wide = lanes // (vwrite_ref.shape[1] // STATE_SIZE)
    chunk = min(512, wide)
    is_owner = owner_ref[0:1, :STATE_SIZE] == here
    row = lax.broadcasted_iota(jnp.int32, (32, STATE_SIZE), 0)
    ones = jnp.where((row >= 24) & (row < 27), 1.0, 0.0)
    for start in range(0, lanes, chunk):
        rows, group = slice(start, start + chunk), start // wide
        writes = vwrite_ref[:, group * STATE_SIZE : (group + 1) * STATE_SIZE].astype(F32)
        writes = jnp.concatenate([writes, writes, writes, jnp.zeros_like(writes)], axis=0)
        right = jnp.concatenate([writes, ones], axis=1).astype(BF16)
        left = tail_ref[:, rows].astype(F32).T.astype(BF16)
        both = dot(left, right)
        added, decay = both[:, :STATE_SIZE], both[:, STATE_SIZE:]
        kept = decay * resident_ref[rows, :].astype(F32)
        base_ref[rows, :] = added + jnp.where(is_owner, 0.0, kept)
        factor_ref[rows, :] = jnp.where(is_owner, decay, 0.0)


def prepare(owner, resident, tail, vwrite, after):
    return call(
        prepare_kernel,
        "prepare_states",
        [shape(resident.shape, F32)] * 2,
        (owner, resident, tail, vwrite),
        after=after,
        moved=1,
    )


def states_kernel(stages, scattered, pieces, offsets, ending, *refs):
    base_ref, factor_ref = refs[:2]
    count = len(offsets)
    prompt_refs, refs = refs[2 : 2 + count], refs[2 + count :]
    new_ref, *slice_refs, turned_ref, held_ref, sems = refs[-4 - count :] if not ending else refs[-6:]
    here = lax.axis_index("seq")
    core, line, last = stages
    lanes = base_ref.shape[0]
    part = lanes // pieces
    width = part // (last[0] if len(scattered) > 1 else 1)

    def piece_at(spot):
        return (spot // line[0] ^ place_of(core)) * line[0] + (spot % line[0] ^ place_of(line))

    def spot_of(offset):
        return (offset // line[0] ^ place_of(core)) * line[0] + (offset % line[0] ^ place_of(line))

    copies, found = [], []
    chunk = part // 2 if part >= 512 else part
    per_slice = HEAD_DIM // (core[0] * line[0] * last[0])
    for index, (offset, prompt_ref) in enumerate(zip(offsets, prompt_refs)):
        start = spot_of(offset) * part
        for at in range(0, part, chunk):
            inner = index * part + at
            for lane in range(at, at + chunk, width):
                position = jnp.int32(0)
                if len(scattered) > 1:
                    apart = lane // width ^ place_of(last)
                    position = jnp.where(apart == 0, 0, last[0] - apart)
                block = prompt_ref[:, window(position * width, width)].astype(F32).T
                turned_ref[index * part + lane : index * part + lane + width, :] = block
            rows = window(start + at, chunk)
            mine = slice(inner, inner + chunk)
            new = factor_ref[rows, :] * turned_ref[mine, :] + base_ref[rows, :]
            held_ref[mine, :] = new.astype(BF16)
            copies.append(
                pltpu.make_async_copy(
                    held_ref.at[mine, :], new_ref.at[rows, :], sems.at[len(copies)]
                )
            )
            copies[-1].start()
        heads = part // HEAD_DIM
        picked = [
            turned_ref[pl.ds(index * part + here * per_slice + k, heads, stride=HEAD_DIM), :]
            for k in range(per_slice)
        ]
        found.append(jnp.concatenate(picked, axis=1))
    if ending:
        others, shares = refs[: pieces - count], refs[pieces - count : -7]
        slice_ref, verify_ref = slice_refs
        verify_ref[...] = sum(ref[...].astype(F32) for ref in shares).astype(BF16)
        every = dict(zip(offsets, found))
        rest = [k for k in range(pieces) if k not in offsets]
        every.update(zip(rest, (ref[...] for ref in others)))
        rows = []
        for spot in range(pieces):
            chosen = every[0]
            for k in range(1, pieces):
                chosen = jnp.where(piece_at(spot) == k, every[k], chosen)
            rows.append(chosen)
        slice_ref[...] = jnp.concatenate(rows, axis=0).astype(BF16)
    else:
        for ref, value in zip(slice_refs, found):
            ref[...] = value
    for copy in copies:
        copy.wait()


def states(stages, scattered, prepared, pieces, offsets, prompts, new, slices, shares, after=()):
    lanes = prepared[0].shape[0]
    part = lanes // pieces
    count = len(offsets)
    cols = HEAD_DIM // (stages[2][0] * stages[2][1]) * STATE_SIZE
    ending = bool(shares)
    args = [*prepared, *prompts]
    if ending:
        args += [slices[k] for k in range(pieces) if k not in offsets] + shares
    specs = [WHOLE] * len(args)
    alias = None
    if new is not None:
        alias = {len(args): 0}
        args.append(new)
        specs.append(IN_HBM)
    outs = [shape((lanes, STATE_SIZE), BF16)]
    if ending:
        outs += [shape((lanes // HEAD_DIM, cols), BF16), shape(shares[0].shape, BF16)]
    else:
        outs += [shape((part // HEAD_DIM, cols), F32)] * count
    return call(
        functools.partial(states_kernel, stages, scattered, pieces, offsets, ending),
        "states",
        outs,
        args,
        specs=specs,
        out_specs=[IN_HBM] + [WHOLE] * (len(outs) - 1),
        after=after,
        alias=alias,
        scratch=[
            pltpu.VMEM((count * part, STATE_SIZE), F32),
            pltpu.VMEM((count * part, STATE_SIZE), BF16),
            pltpu.SemaphoreType.DMA((2 * count,)),
        ],
        moved=1,
    )


def on_device(
    prefill_input,
    prefill_step,
    write_proj,
    read_proj,
    decay_rate,
    skip_gain,
    resident_state,
    owner_slot,
    draft_ids,
    accepted_len,
    draft_input,
    draft_gate,
    draft_write,
    draft_read,
    draft_step,
    norm_gain,
    out_weight,
):
    span, lanes = prefill_input.shape
    assert span == BLOCK_LEN
    heads = decay_rate.shape[0]
    groups = write_proj.shape[1] // STATE_SIZE
    per_group = heads // groups
    half = lanes // 2
    seq_count, head_count = lax.axis_size("seq"), lax.axis_size("head")
    stages = tree_stages(seq_count)
    core, line, last = stages
    slots = owner_slot.shape[0]
    assert core[0] == 2 and slots == seq_count
    rate, skip, gain = decay_rate[None], skip_gain[None], norm_gain[None]
    resident = resident_state.reshape(lanes, STATE_SIZE)

    inputs = [
        in_hbm(value)
        for value in (
            prefill_step.T, rate, owner_slot, draft_ids.T, accepted_len, write_proj, prefill_input,
            draft_input, draft_gate, draft_write, draft_read, draft_step, skip, rate, read_proj, resident,
            gain,
        )
    ]
    passed = 12
    opened = call(
        functools.partial(open_kernel, core, len(inputs), passed),
        "open_block",
        [
            shape((STATE_SIZE, half), BF16),
            shape((groups, span, per_group), F32),
            shape((heads, span), F32),
            shape((heads, span), F32),
            shape((span, 2 * heads), BF16),
            shape((span, 2 * heads), BF16),
            shape((DRAFTS, draft_input.shape[0]), F32),
            shape((DRAFTS, 128), jnp.int32),
            shape((DRAFTS, out_weight.shape[1]), jnp.int32),
        ]
        + [shape(value.shape, value.dtype) for value in inputs[-passed:]],
        inputs,
        specs=[IN_HBM] * len(inputs),
        scratch=[pltpu.SemaphoreType.DMA((len(inputs) + 1,))]
        + [
            (pltpu.SMEM if value.dtype == jnp.int32 else pltpu.VMEM)(value.shape, value.dtype)
            for value in inputs[:-passed]
        ],
        flops=span * lanes * STATE_SIZE * 2,
    )
    sent, run, runt, stept, reach, end, pick, kept, owner = opened[:9]
    writes, x, din, dgate, dwrite, dread, dstep, skip, rate, reads, resident, gain = opened[9:]
    received = swap(sent, "seq", core, 1)
    own_extra, sent_extra, skip_lanes, q1, q2, vread, vwrite, tail = call(
        functools.partial(draft_kernel, core),
        "draft_rows",
        [
            shape((EXTRA, half), BF16),
            shape((EXTRA, half), BF16),
            shape((1, lanes), F32),
            shape((DRAFTS, lanes), F32),
            shape((DRAFTS, lanes), F32),
            shape((DRAFTS, groups * STATE_SIZE), BF16),
            shape((DRAFTS, groups * STATE_SIZE), BF16),
            shape((32, lanes), BF16),
        ],
        (pick, kept, owner, runt, rate, skip, din, dgate, dwrite, dread, dstep),
        after=[sent],
        scratch=[pltpu.VMEM((EXTRA, lanes), BF16)],
        flops=DRAFTS * lanes * 100,
    )
    received_extra = swap(sent_extra, "seq", core, 1)
    (own,) = call(
        functools.partial(own_kernel, core),
        "own_message",
        [shape((STATE_SIZE, half), BF16)],
        (end, x, writes),
        after=[sent_extra],
        flops=span * lanes * STATE_SIZE,
    )
    core_parts = [own, own_extra, received, received_extra]

    bases, fetched = [], []

    def fill(after):
        if len(bases) < groups:
            wanted = [out_weight] if len(bases) == min(1, groups - 1) else []
            base, *found = intra(
                len(bases), run, runt, stept, skip_lanes, x, writes, reads, after, wanted
            )
            bases.append(base)
            fetched.extend(found)
        return bases[-1:]

    def exchange(parts, stage):
        got = {k: swap(parts[k], "seq", stage, k) for k in range(1, stage[0])}
        return [parts[0]] + [got[k] for k in range(1, stage[0])]

    line_width = half // line[0]
    split_last = line_width % (last[0] * 128) == 0
    last_width = line_width // last[0] if split_last else line_width
    outs = call(
        functools.partial(up_kernel, core, line, 2, True),
        "up_line",
        [shape((UP_ROWS, line_width), BF16)] * line[0],
        core_parts,
        flops=half * UP_ROWS * 4,
    )
    line_parts = exchange(outs, line)
    hidden = resident_hidden(resident, vread, q1, q2, gain, [outs[-1]])
    hiddens = exchange([hidden] * last[0], last)
    filled = fill([outs[-1]])
    outs = call(
        functools.partial(up_kernel, line, last, line[0], False),
        "up_last",
        [shape((UP_ROWS, last_width), BF16)] * (last[0] if split_last else 1),
        line_parts,
        after=filled + hiddens[:0:-1],
        flops=line_width * UP_ROWS * 4,
    )
    last_parts = exchange(outs if split_last else outs * last[0], last)
    hidden = join(hiddens, 0, [outs[-1]])
    hiddens = exchange([hidden] * line[0], line)
    filled = fill([outs[-1]])
    last_parts = last_parts[:1] + list(gather_in(last_parts[:0:-1], filled))[::-1]
    *outs, prompt = call(
        functools.partial(top_kernel, last, last[0]),
        "top",
        [shape((DOWN_ROWS, last_width), BF16)] * (last[0] if split_last else 1)
        + [shape((STATE_SIZE, last_width), BF16)],
        turned(last_parts),
        after=filled,
        flops=last_width * UP_ROWS * 16,
    )

    pieces = exchange(outs, last) if split_last else outs
    hidden = join(hiddens, 0, [outs[-1]])
    filled = fill([outs[-1], hidden])
    if split_last:
        pieces = pieces[:1] + list(gather_in(pieces[:0:-1], filled))[::-1]
    outs = call(
        functools.partial(down_kernel, line, last, len(pieces), line[0], False, range(line[0]), False),
        "down_line",
        [shape((DOWN_ROWS, line_width), BF16)] * line[0],
        [*turned(pieces), *line_parts],
        after=filled,
        flops=line_width * UP_ROWS * 8,
    )
    pieces = exchange(outs, line)
    hiddens = [hidden, swap(hidden, "seq", core, 1)]
    filled = fill([outs[-1]])
    prepared = prepare(owner, resident, tail, vwrite, filled)
    filled = [*prepared, *hiddens[1:]]
    scattered = [line, last] if split_last else [line]
    if split_last:
        prompt = hand_on(prompt, [outs[-1]])
        parts = exchange([prompt] * last[0], last)
        prompt = join(turned(parts), 1)
        filled.append(prompt)

    def down_core(target, after):
        return call(
            functools.partial(down_kernel, core, line, line[0], 2, True, (target,), False),
            "down_core",
            [shape((STATE_SIZE, half), BF16)] + [shape((DRAFTS, half), BF16)] * target,
            turned(pieces) + core_parts,
            after=after,
            moved=1,
        )

    sent, gated = down_core(1, filled)
    received_gated, received = swap(gated, "seq", core, 1), swap(sent, "seq", core, 1)
    (received_gated,) = gather_in([received_gated])
    while len(bases) < groups:
        fill([])

    shares = project(
        stages, owner, *hiddens, gated, received_gated, gain, fetched[0], head_count
    )
    (entering,) = down_core(0, shares[:1])
    prefill_out, token = finish(core, reach, reads, entering, received, bases)
    shares = [shares[0]] + [swap(shares[k], "head", (head_count, 1), k) for k in range(1, head_count)]

    prompts = exchange([prompt] * line[0], line)
    pieces = 2 * line[0]
    crossed = swap(hand_on(prompt, shares[:1]), "seq", core, 1)
    late = gather_in(prompts[1:], [token, *shares[1:]])
    slices = {}
    new_state, slices[0], slices[line[0]] = states(
        stages, scattered, prepared, pieces, (0, line[0]), (prompt, crossed), None, None, (), late[:1]
    )
    offsets = (*range(1, line[0]), *range(line[0] + 1, pieces))
    prompts = prompts[1:] + [swap(piece, "seq", core, 1) for piece in late]
    new_state, state_slice, verify_out = states(
        stages, scattered, prepared, pieces, offsets, prompts, new_state, slices, shares
    )
    return (
        prefill_out,
        new_state.reshape(1, heads, HEAD_DIM, STATE_SIZE),
        verify_out,
        state_slice,
    )


def solution(mesh):
    return jax.shard_map(
        on_device,
        mesh=mesh,
        in_specs=(
            P("seq", "head"),
            P("seq", "head"),
            P("seq", "head"),
            P("seq", "head"),
            P("head"),
            P("head"),
            P("seq", "head", None, None),
            P(),
            P(),
            P(),
            P("seq", "head"),
            P("seq", "head"),
            P("seq", "head"),
            P("seq", "head"),
            P("seq", "head"),
            P("head"),
            P("head", "seq"),
        ),
        out_specs=(
            P("seq", "head"),
            P("seq", "head", None, None),
            P("head", "seq"),
            P("head", "seq"),
        ),
        check_vma=False,
    )
```

```python
import functools

import jax
import jax.numpy as jnp
from jax import lax
from jax.experimental import pallas as pl
from jax.experimental.pallas import tpu as pltpu
from jax.sharding import PartitionSpec as P

HEAD_DIM = 64
STATE_SIZE = 128
BLOCK_LEN = 256
DRAFTS = 8
EPSILON = 1e-05
EXTRA = 32
UP_ROWS = STATE_SIZE + EXTRA
READ_AT = STATE_SIZE + 16
LOG_AT = STATE_SIZE + 24
DOWN_ROWS = STATE_SIZE + 8

F32 = jnp.float32
BF16 = jnp.bfloat16


def tree_stages(count):
    factors, rest = [], count
    if rest > 1:
        factors.append(2)
        rest //= 2
    inner = 1
    while inner * inner * 4 <= rest:
        inner *= 2
    factors += [inner, rest // inner]
    stages, stride = [], 1
    for factor in factors:
        stages.append((factor, stride))
        stride *= factor
    assert stride == count
    return stages


def swap(value, axis, stage, offset):
    count, stride = lax.axis_size(axis), stage[1]
    return lax.ppermute(value, axis, [(k, k ^ (offset * stride)) for k in range(count)])


def place_of(stage):
    factor, stride = stage
    return lax.rem(lax.div(lax.axis_index("seq"), stride), factor)


def dot(a, b, dims=((1,), (0,))):
    return lax.dot_general(a, b, (dims, ((), ())), preferred_element_type=F32)


def split(value, parts):
    found = []
    for _ in range(parts):
        part = value.astype(BF16).astype(F32)
        found.append(part)
        value = value - part
    return found


def head_mask(rows, heads, lanes, lane0):
    row = lax.broadcasted_iota(jnp.int32, (rows, lanes), 0) & (heads - 1)
    head = lax.shift_right_logical(lax.broadcasted_iota(jnp.int32, (rows, lanes), 1) + lane0, 6)
    return jnp.where(row == head, 1.0, 0.0).astype(BF16)


def window(start, size):
    return pl.ds(pl.multiple_of(start, size), size)


def ordered(kernel, count):
    return lambda *refs: kernel(*refs[count:])


ANYWHERE = pl.BlockSpec(memory_space=pl.ANY)
WHOLE = pl.BlockSpec(memory_space=pltpu.VMEM)
IN_HBM = pl.BlockSpec(memory_space=pltpu.HBM)


def call(
    kernel, name, outs, args, specs=None, out_specs=None, grid=(), after=(), scratch=(), alias=None,
    flops=0, exps=0, moved=None, vmem=32,
):
    if specs is None:
        specs = [WHOLE] * len(args)
    if out_specs is None:
        out_specs = [WHOLE] * len(outs)
    if moved is None:
        moved = sum(a.size * a.dtype.itemsize for a in (*args, *outs))
    first = len(after)
    return pl.pallas_call(
        ordered(kernel, first),
        name=name,
        grid=grid,
        out_shape=outs,
        in_specs=[ANYWHERE] * first + specs,
        out_specs=out_specs,
        scratch_shapes=list(scratch),
        input_output_aliases={first + k: v for k, v in (alias or {}).items()},
        compiler_params=pltpu.CompilerParams(vmem_limit_bytes=vmem * 1024 * 1024),
        cost_estimate=pl.CostEstimate(flops=flops, bytes_accessed=moved, transcendentals=exps),
    )(*after, *args)


def in_hbm(value):
    return pltpu.with_memory_space_constraint(value, pltpu.HBM)


def shape(dims, dtype):
    return jax.ShapeDtypeStruct(dims, dtype)


def open_kernel(stage, count, passed, *refs):
    sources, rest = refs[:count], refs[count:]
    outs, scratch = rest[: 9 + passed], rest[9 + passed :]
    outs, later = outs[:9], list(outs[9:])
    sent_ref, run_ref, runt_ref, stept_ref, reach_ref, end_ref, pick_ref, kept_out, owner_out = outs
    sems, held = scratch[0], [*scratch[1:], *later]
    here = lax.axis_index("seq")
    place = place_of(stage)
    early = count - passed
    half = sent_ref.shape[1]

    def fetch(k, at=None):
        if at is None:
            return pltpu.make_async_copy(sources[k], held[k], sems.at[k])
        sem = sems.at[k if at == 1 else count]
        lanes = window((place ^ at) * half, half)
        return pltpu.make_async_copy(sources[k].at[:, lanes], held[k].at[:, lanes], sem)

    first = [fetch(k) for k in range(early + 1)] + [fetch(early + 1, 1)]
    rest = [fetch(early + 1, 0)] + [fetch(k) for k in range(early + 2, count)]
    for copy in first:
        copy.start()
    for copy in first[:early]:
        copy.wait()
    for copy in rest:
        copy.start()
    turned_ref, rate_ref, owner_ref, ids_ref, kept_ref, write_ref, x_ref = held[:7]
    heads, span = turned_ref.shape
    groups = write_ref.shape[1] // STATE_SIZE
    per_group = heads // groups

    step_rows = turned_ref[...]
    stept_ref[...] = step_rows
    pad = (-heads) % 128
    if pad:
        step_rows = jnp.concatenate([step_rows, jnp.zeros((pad, span), F32)], axis=0)
    step = step_rows.T[:, :heads]
    log_decay = -step * rate_ref[...]
    lower = lax.broadcasted_iota(jnp.int32, (span, span), 0) >= lax.broadcasted_iota(
        jnp.int32, (span, span), 1
    )
    lower = jnp.where(lower, 1.0, 0.0).astype(BF16)
    running = sum(dot(lower, part.astype(BF16)) for part in split(log_decay, 3))
    to_end = jnp.exp(running[span - 1 : span, :] - running) * step
    end_ref[...] = jnp.concatenate(split(to_end, 2), axis=1).astype(BF16)

    for copy in first[early:]:
        copy.wait()
    fill_message(place ^ 1, end_ref, x_ref, write_ref, sent_ref)

    wide_run = running
    if pad:
        wide_run = jnp.concatenate([running, jnp.zeros((span, pad), F32)], axis=1)
    runt_ref[...] = wide_run.T[:heads]
    for g in range(groups):
        run_ref[g] = running[:, g * per_group : (g + 1) * per_group]
    reach_ref[...] = jnp.concatenate(split(jnp.exp(running), 2), axis=1).astype(BF16)

    slots = owner_ref.shape[0]
    request = lax.fori_loop(
        0, slots, lambda r, found: jnp.where(owner_ref[r] == here, r, found), jnp.int32(0)
    )
    row = lax.broadcasted_iota(jnp.int32, pick_ref.shape, 0)
    col = lax.broadcasted_iota(jnp.int32, pick_ref.shape, 1)
    pick = jnp.zeros(pick_ref.shape, F32)
    for i in range(DRAFTS):
        pick = jnp.where((row == i) & (col == ids_ref[i, request]), 1.0, pick)
    pick_ref[...] = pick
    kept_out[...] = jnp.zeros(kept_out.shape, jnp.int32) + kept_ref[request]
    owner_out[...] = jnp.zeros(owner_out.shape, jnp.int32) + owner_ref[0]
    for copy in rest:
        copy.wait()


def draft_kernel(
    stage,
    pick_ref,
    kept_ref,
    owner_ref,
    runt_ref,
    rate_ref,
    skip_ref,
    din_ref,
    dgate_ref,
    dwrite_ref,
    dread_ref,
    dstep_ref,
    own_ref,
    sent_ref,
    skip_out,
    q1_ref,
    q2_ref,
    vread_ref,
    vwrite_ref,
    tail_ref,
    extra_ref,
):
    heads, span = runt_ref.shape
    lanes = din_ref.shape[1]
    groups = dwrite_ref.shape[1] // STATE_SIZE
    wide = lanes // groups
    here = lax.axis_index("seq")
    place = place_of(stage)
    pick = pick_ref[...].astype(BF16)
    vin = dot(pick, din_ref[...])
    vgate = dot(pick, dgate_ref[...])
    vwrite = dot(pick, dwrite_ref[...]).astype(BF16)
    vread = dot(pick, dread_ref[...]).astype(BF16)
    vwrite_ref[...] = vwrite
    vread_ref[...] = vread
    vstep = sum(dot(pick, part.astype(BF16)) for part in split(dstep_ref[...], 3))
    vlog = -vstep * rate_ref[...]
    index = lax.broadcasted_iota(jnp.int32, (DRAFTS, heads), 0)
    kept_heads = kept_ref[:, :1]
    acc = jnp.zeros((1, heads), F32)
    vrun = jnp.zeros((DRAFTS, heads), F32)
    reach = jnp.zeros((1, heads), F32)
    for i in range(DRAFTS):
        acc = acc + vlog[i : i + 1]
        vrun = jnp.where(index == i, acc, vrun)
        reach = jnp.where(i < kept_heads[0:1], acc, reach)
    total = runt_ref[:, span - 128 :]
    if heads < 128:
        total = jnp.concatenate([total, jnp.zeros((128 - heads, 128), F32)], axis=0)
    total = total.T[127:128, :heads]
    others = jnp.where(index == 0, total, jnp.where(index == 1, skip_ref[...], reach))
    stacked = split(jnp.concatenate([vrun, vstep, others], axis=0), 3)
    stacked = jnp.concatenate(stacked, axis=0).astype(BF16)
    row = lax.broadcasted_iota(jnp.int32, (DRAFTS, wide), 0)
    kept = kept_ref[:, :1]
    is_owner = owner_ref[0:1, :1] == here
    for g in range(groups):
        at = slice(g * wide, (g + 1) * wide)
        spread = dot(stacked, head_mask(heads, heads, wide, g * wide))
        spread = spread[0:24] + spread[24:48] + spread[48:72]
        vrun_l, vstep_l = spread[0:8], spread[8:16]
        total_l, skip_l, reach_l = spread[16:17], spread[17:18], spread[18:19]
        skip_out[:, at] = skip_l
        vin_g = vin[:, at]
        vr = vread[:, g * STATE_SIZE : (g + 1) * STATE_SIZE]
        vw = vwrite[:, g * STATE_SIZE : (g + 1) * STATE_SIZE]
        scores = dot(vr, vw, ((1,), (1,)))
        direct = skip_l * vin_g
        for j in range(DRAFTS):
            decay = jnp.exp(jnp.where(row >= j, vrun_l - vrun_l[j : j + 1], -jnp.inf))
            direct = direct + decay * scores[:, j : j + 1] * (vstep_l[j : j + 1] * vin_g[j : j + 1])
        gate = vgate[:, at]
        gate = gate / (1.0 + jnp.exp(-gate))
        q1 = direct * gate
        q2 = jnp.exp(vrun_l) * gate
        q1_ref[:, at] = q1
        q2_ref[:, at] = q2
        live = jnp.exp(jnp.where(row < kept, reach_l - vrun_l, -jnp.inf)) * vstep_l * vin_g
        keep_l = jnp.concatenate(
            split(jnp.exp(reach_l), 3) + [jnp.zeros((5, wide), F32)], axis=0
        )
        tail_ref[:, at] = jnp.concatenate(split(live, 3) + [keep_l], axis=0).astype(BF16)
        read_l = jnp.concatenate([vr.astype(F32)] * (wide // STATE_SIZE), axis=1)
        mine = jnp.concatenate([q1, q2, read_l], axis=0)
        mine = jnp.where(is_owner, mine, 0.0)
        logs = jnp.concatenate(split(total_l, 3) + [jnp.zeros((5, wide), F32)], axis=0)
        extra_ref[:, at] = jnp.concatenate([mine, logs], axis=0).astype(BF16)
    half = lanes // 2
    own_ref[...] = extra_ref[:, window(place * half, half)]
    sent_ref[...] = extra_ref[:, window((place ^ 1) * half, half)]


def fill_message(side, end_ref, x_ref, write_ref, out_ref):
    heads = end_ref.shape[1] // 2
    half = out_ref.shape[1]
    wide = 2 * half // (write_ref.shape[1] // STATE_SIZE)
    chunk = min(wide, half)
    start = side * half
    for at in range(0, half, chunk):
        lane0 = start + at
        group = lax.div(lane0, wide)
        scale = dot(end_ref[...], head_mask(2 * heads, heads, chunk, lane0))
        weighted = (x_ref[:, window(lane0, chunk)].astype(F32) * scale).astype(BF16)
        writes = write_ref[:, window(group * STATE_SIZE, STATE_SIZE)]
        writes = writes.astype(F32).T.astype(BF16)
        out_ref[:, at : at + chunk] = dot(writes, weighted).astype(BF16)


def own_kernel(stage, end_ref, x_ref, write_ref, out_ref):
    fill_message(place_of(stage), end_ref, x_ref, write_ref, out_ref)


def state_of(part, at):
    return part[0][:STATE_SIZE, at].astype(F32)


def extra_of(part, at):
    return (part[1][:, at] if part[2] else part[0][STATE_SIZE:UP_ROWS, at]).astype(F32)


def logs_of(part, at):
    found = extra_of(part, at)[LOG_AT - STATE_SIZE :]
    return found[0:1] + found[1:2] + found[2:3]


def turned(parts):
    return [parts[0], *parts[:0:-1]]


def paired(refs, apart):
    if apart:
        return [(refs[k], refs[k + 1], True) for k in range(0, len(refs), 2)]
    return [(ref, None, False) for ref in refs]


def weights_of(logs, place, target):
    spots = [place ^ k for k in range(len(logs))]
    found = []
    for k, spot in enumerate(spots):
        between = jnp.zeros_like(logs[0])
        for other, log in zip(spots, logs):
            if other is not spot:
                between = between + jnp.where((spot < other) & (other < target), log, 0.0)
        found.append(jnp.where(spot < target, jnp.exp(between), 0.0))
    return found


def carry_of(logs, place, target):
    ahead = jnp.zeros_like(logs[0])
    for k, log in enumerate(logs):
        ahead = ahead + jnp.where((place ^ k) < target, log, 0.0)
    return jnp.exp(ahead)


def up_kernel(stage, following, count, apart, *refs):
    taken = 2 * count if apart else count
    parts, outs = paired(refs[:taken], apart), refs[taken:]
    place, target = place_of(stage), place_of(following)
    width = outs[0].shape[1]
    chunk = min(256, width)
    order = list(range(1, len(outs))) + [0]
    for k in order:
        for at in range(0, width, chunk):
            start = at if len(outs) == 1 else (target ^ k) * width + at
            at_in = window(start, chunk)
            logs = [logs_of(part, at_in) for part in parts]
            scale = weights_of(logs, place, count)
            state = sum(w * state_of(part, at_in) for w, part in zip(scale, parts))
            outs[k][:STATE_SIZE, at : at + chunk] = state.astype(BF16)
            mine = sum(extra_of(part, at_in) for part in parts)
            total = jnp.concatenate(
                split(sum(logs), 3) + [jnp.zeros((5, chunk), F32)], axis=0
            )
            outs[k][STATE_SIZE:, at : at + chunk] = jnp.concatenate(
                [mine[:24], total], axis=0
            ).astype(BF16)


def top_kernel(stage, count, *refs):
    parts, outs, prompt_ref = paired(turned(refs[:count]), False), refs[count:-1], refs[-1]
    whole = slice(None)
    place = place_of(stage)
    width = prompt_ref.shape[1]
    logs = [logs_of(part, whole) for part in parts]
    states = [state_of(part, whole) for part in parts]
    final = sum(w * s for w, s in zip(weights_of(logs, place, count), states)).astype(BF16)
    prompt_ref[...] = final
    mine = sum(extra_of(part, whole) for part in parts)
    reads = mine[16:24, :STATE_SIZE].astype(BF16)
    gated = mine[0:8] + mine[8:16] * dot(reads, final)
    gated = gated.astype(BF16)
    for k in list(range(1, len(outs))) + [0]:
        scale = weights_of(logs, place, place ^ k)
        outs[k][:STATE_SIZE, :] = sum(w * s for w, s in zip(scale, states)).astype(BF16)
        outs[k][STATE_SIZE:, :] = gated


def down_kernel(stage, above, above_count, count, apart, targets, handed, *refs):
    end = above_count + (2 * count if apart else count)
    pieces, outs = turned(refs[:above_count]), refs[end:]
    parts = paired(refs[above_count:end], apart)
    if handed:
        outs[-1][...] = outs[0][...]
        outs = outs[1:-1]
    place, source = place_of(stage), place_of(above)
    width = pieces[0].shape[1]
    chunk = min(256, width)
    gated_ref = outs[1] if apart and len(outs) > 1 else None
    for k, out_ref in zip(targets, outs):
        for piece in range(above_count):
            for at in range(0, width, chunk):
                start = at if above_count == 1 else (source ^ piece) * width + at
                at_out = window(start, chunk)
                block = pieces[piece][:, at : at + chunk]
                logs = [logs_of(part, at_out) for part in parts]
                state = carry_of(logs, place, place ^ k) * block[:STATE_SIZE].astype(F32)
                for w, part in zip(weights_of(logs, place, place ^ k), parts):
                    state = state + w * state_of(part, at_out)
                out_ref[:STATE_SIZE, at_out] = state.astype(BF16)
                if gated_ref is not None:
                    gated_ref[:, at_out] = block[STATE_SIZE:]
                elif out_ref.shape[0] > STATE_SIZE:
                    out_ref[STATE_SIZE:, at_out] = block[STATE_SIZE:]


def intra_kernel(group, run_ref, runt_ref, stept_ref, skip_ref, x_ref, write_ref, read_ref, *refs):
    fetch = None
    out_ref = refs[0]
    if len(refs) > 1:
        source_ref, out_ref, held_ref, sem = refs
        fetch = pltpu.make_async_copy(source_ref, held_ref, sem)
        fetch.start()
    span, heads = run_ref.shape[1:]
    mid = span // 2
    states = slice(group * STATE_SIZE, (group + 1) * STATE_SIZE)
    scores = dot(read_ref[:, states], write_ref[:, states], ((1,), (1,)))
    row = lax.broadcasted_iota(jnp.int32, (mid, mid), 0)
    causal = row >= lax.broadcasted_iota(jnp.int32, (mid, mid), 1)
    running = run_ref[group]
    low, high = slice(0, mid), slice(mid, span)
    for pair in range(heads // 2):
        found = []
        for k in (2 * pair, 2 * pair + 1):
            h = group * heads + k
            x = x_ref[:, h * HEAD_DIM : (h + 1) * HEAD_DIM]
            t_run, j_run = running[:, k : k + 1], runt_ref[h : h + 1, :]
            step = stept_ref[h : h + 1, :]

            def mixed(rows, cols, masked):
                gap = t_run[rows] - j_run[:, cols]
                if masked:
                    gap = jnp.where(causal, gap, -jnp.inf)
                return (scores[rows, cols] * jnp.exp(gap) * step[:, cols]).astype(BF16)

            top = dot(mixed(low, low, True), x[low])
            bottom = dot(mixed(high, low, False), x[low]) + dot(mixed(high, high, True), x[high])
            found.append(jnp.concatenate([top, bottom], axis=0))
        at = slice(pair * 2 * HEAD_DIM, (pair + 1) * 2 * HEAD_DIM)
        lanes = slice((group * heads + 2 * pair) * HEAD_DIM, (group * heads + 2 * pair + 2) * HEAD_DIM)
        both = jnp.concatenate(found, axis=1)
        out_ref[:, at] = both + skip_ref[:, lanes] * x_ref[:, lanes].astype(F32)
    if fetch is not None:
        fetch.wait()


def intra(group, run, runt, stept, skip, x, write, read, after, wanted=()):
    span, per_group = run.shape[1:]
    wide = per_group * HEAD_DIM
    return call(
        functools.partial(intra_kernel, group),
        "intra",
        [shape((span, wide), F32)] + [shape(value.shape, value.dtype) for value in wanted],
        (run, runt, stept, skip, x, write, read, *map(in_hbm, wanted)),
        specs=[WHOLE] * 7 + [IN_HBM] * len(wanted),
        scratch=[pltpu.SemaphoreType.DMA] * len(wanted),
        after=after,
        flops=per_group * span * span * HEAD_DIM * 2,
        moved=wide * span * 6,
        exps=per_group * span * span * 3 // 4,
    )


def finish_kernel(stage, reach_ref, read_ref, own_ref, got_ref, *refs):
    base_refs, (out_ref, token_ref, held_ref, sems) = refs[:-4], refs[-4:]
    token_ref[...] = jnp.zeros_like(token_ref)
    place = place_of(stage)
    heads = reach_ref.shape[1] // 2
    lanes = held_ref.shape[1]
    wide = lanes // len(base_refs)
    half = lanes // 2
    chunk = lanes // sems.shape[0]
    copies = []
    for k, lane0 in enumerate(range(0, lanes, chunk)):
        group, at = lane0 // wide, lane0 % half
        at_in, at_out = slice(at, at + chunk), slice(lane0, lane0 + chunk)
        entering = jnp.where(place == lane0 // half, own_ref[:, at_in], got_ref[:, at_in])
        inter = dot(read_ref[:, group * STATE_SIZE : (group + 1) * STATE_SIZE], entering)
        inter = inter * dot(reach_ref[...], head_mask(2 * heads, heads, chunk, lane0))
        base = base_refs[group][:, lane0 % wide : lane0 % wide + chunk]
        held_ref[:, at_out] = (inter + base).astype(BF16)
        copies.append(
            pltpu.make_async_copy(held_ref.at[:, at_out], out_ref.at[:, at_out], sems.at[k])
        )
        copies[-1].start()
    for copy in copies:
        copy.wait()


def finish(stage, reach, read, own, got, bases):
    span = read.shape[0]
    lanes = 2 * own.shape[1]
    chunk = min(512, own.shape[1])
    return call(
        functools.partial(finish_kernel, stage),
        "finish",
        [shape((span, lanes), BF16), shape((8, 128), F32)],
        (reach, read, own, got, *bases),
        out_specs=[IN_HBM, WHOLE],
        scratch=[pltpu.VMEM((span, lanes), BF16), pltpu.SemaphoreType.DMA((lanes // chunk,))],
        moved=1,
    )


def resident_kernel(state_ref, vread_ref, q1_ref, q2_ref, gain_ref, out_ref):
    groups = vread_ref.shape[1] // STATE_SIZE
    wide = state_ref.shape[0] // groups
    for g in range(groups):
        at = slice(g * wide, (g + 1) * wide)
        reads = vread_ref[:, g * STATE_SIZE : (g + 1) * STATE_SIZE]
        drawn = dot(reads, state_ref[at, :], ((1,), (1,)))
        gated = q1_ref[:, at] + q2_ref[:, at] * drawn
        out_ref[:, at] = normed(gated, gain_ref[:, at]).astype(BF16)


def normed(gated, gain):
    mean_square = jnp.mean(gated * gated, axis=1, keepdims=True)
    return gated * lax.rsqrt(mean_square + EPSILON) * gain


def resident_hidden(state, vread, q1, q2, gain, after):
    lanes = state.shape[0]
    return call(
        resident_kernel,
        "resident_hidden",
        [shape((DRAFTS, lanes), BF16)],
        (state, vread, q1, q2, gain),
        after=after,
        flops=2 * DRAFTS * lanes * STATE_SIZE,
    )[0]


def hand_on(value, after):
    def copy(value_ref, out_ref):
        out_ref[...] = value_ref[...]

    return call(copy, "hand_on", [shape(value.shape, value.dtype)], [value], after=after)[0]


def gather_in(values, after=()):
    def copy(*refs):
        for k in range(len(values)):
            refs[len(values) + k][...] = refs[k][...]

    return call(
        copy, "gather_in", [shape(v.shape, v.dtype) for v in values], values, after=after,
        flops=10**10, moved=1,
    )


def join_kernel(axis, *refs):
    out_ref, start = refs[-1], 0
    for ref in refs[:-1]:
        at = slice(start, start + ref.shape[axis])
        start = at.stop
        if axis == 0:
            out_ref[at, :] = ref[...]
        else:
            out_ref[:, at] = ref[...]


def join(parts, axis, after=(), flops=0):
    dims = list(parts[0].shape)
    dims[axis] = sum(part.shape[axis] for part in parts)
    return call(
        functools.partial(join_kernel, axis), "join", [shape(tuple(dims), parts[0].dtype)], parts, after=after, moved=1, flops=flops
    )[0]


def project_kernel(stages, head_count, *refs):
    owner_ref, own_rows, got_rows, own_ref, got_ref, gain_ref, weight_ref = refs[:7]
    outs = refs[7 : 7 + head_count]
    gated_ref, left_ref, total_ref = refs[7 + head_count :]
    here, head = lax.axis_index("seq"), lax.axis_index("head")
    place = place_of(stages[0])
    half = own_ref.shape[1]
    lanes = weight_ref.shape[0]
    wide = min(1024, lanes)
    rows = own_rows.shape[0]
    for k, ref in enumerate((own_ref, got_ref)):
        gated_ref[:, window((place ^ k) * half, half)] = ref[...].astype(F32)
    left_ref[0:rows, :] = own_rows[...]
    left_ref[rows : 2 * rows, :] = got_rows[...]
    for lane0 in range(0, lanes, wide):
        at = slice(lane0, lane0 + wide)
        hidden = normed(gated_ref[:, at], gain_ref[:, at])
        hidden = jnp.concatenate([hidden, jnp.zeros_like(hidden)], axis=0)
        left_ref[2 * rows :, at] = hidden.astype(BF16)
    total_ref[...] = dot(left_ref[...], weight_ref[...])

    per_head = 2 * rows // DRAFTS // head_count
    offsets = [0]
    for factor, stride in reversed(stages):
        offsets = [a + k * stride for k in range(factor) for a in offsets]
    owner = owner_ref[...]
    tail = total_ref[2 * rows : 2 * rows + DRAFTS, :]
    for k in list(range(1, head_count)) + [0]:
        first = (head ^ k) * per_head
        for slot in range(per_head):
            at = slice(slot * DRAFTS, (slot + 1) * DRAFTS)
            offset = here ^ (first + slot)
            block = jnp.int32(0)
            for position, value in enumerate(offsets):
                block = jnp.where(offset == value, position, block)
            drawn = total_ref[window(block * DRAFTS, DRAFTS), :]
            drawn = jnp.where(owner == first + slot, tail, drawn)
            outs[k][at, :] = drawn.astype(outs[k].dtype)


def project(stages, owner, own_rows, got_rows, own, got, gain, weight, head_count):
    lanes, cols = weight.shape
    rows = 2 * own_rows.shape[0]
    return call(
        functools.partial(project_kernel, stages, head_count),
        "project",
        [shape((rows // head_count, cols), BF16 if k else F32) for k in range(head_count)],
        (owner, own_rows, got_rows, own, got, gain, weight),
        scratch=[
            pltpu.VMEM((DRAFTS, lanes), F32),
            pltpu.VMEM((rows + 16, lanes), BF16),
            pltpu.VMEM((rows + 16, cols), F32),
        ],
        moved=1,
    )


def prepare_kernel(owner_ref, resident_ref, tail_ref, vwrite_ref, base_ref, factor_ref):
    here = lax.axis_index("seq")
    lanes = resident_ref.shape[0]
    wide = lanes // (vwrite_ref.shape[1] // STATE_SIZE)
    chunk = min(512, wide)
    is_owner = owner_ref[0:1, :STATE_SIZE] == here
    row = lax.broadcasted_iota(jnp.int32, (32, STATE_SIZE), 0)
    ones = jnp.where((row >= 24) & (row < 27), 1.0, 0.0)
    for start in range(0, lanes, chunk):
        rows, group = slice(start, start + chunk), start // wide
        writes = vwrite_ref[:, group * STATE_SIZE : (group + 1) * STATE_SIZE].astype(F32)
        writes = jnp.concatenate([writes, writes, writes, jnp.zeros_like(writes)], axis=0)
        right = jnp.concatenate([writes, ones], axis=1).astype(BF16)
        left = tail_ref[:, rows].astype(F32).T.astype(BF16)
        both = dot(left, right)
        added, decay = both[:, :STATE_SIZE], both[:, STATE_SIZE:]
        kept = decay * resident_ref[rows, :].astype(F32)
        base_ref[rows, :] = added + jnp.where(is_owner, 0.0, kept)
        factor_ref[rows, :] = jnp.where(is_owner, decay, 0.0)


def prepare(owner, resident, tail, vwrite, after):
    return call(
        prepare_kernel,
        "prepare_states",
        [shape(resident.shape, F32)] * 2,
        (owner, resident, tail, vwrite),
        after=after,
        moved=1,
    )


def states_kernel(stages, scattered, pieces, offsets, ending, *refs):
    base_ref, factor_ref = refs[:2]
    count = len(offsets)
    prompt_refs, refs = refs[2 : 2 + count], refs[2 + count :]
    new_ref, *slice_refs, turned_ref, held_ref, sems = refs[-4 - count :] if not ending else refs[-6:]
    here = lax.axis_index("seq")
    core, line, last = stages
    lanes = base_ref.shape[0]
    part = lanes // pieces
    width = part // (last[0] if len(scattered) > 1 else 1)

    def piece_at(spot):
        return (spot // line[0] ^ place_of(core)) * line[0] + (spot % line[0] ^ place_of(line))

    def spot_of(offset):
        return (offset // line[0] ^ place_of(core)) * line[0] + (offset % line[0] ^ place_of(line))

    copies, found = [], []
    chunk = part // 2 if part >= 512 else part
    per_slice = HEAD_DIM // (core[0] * line[0] * last[0])
    for index, (offset, prompt_ref) in enumerate(zip(offsets, prompt_refs)):
        start = spot_of(offset) * part
        for at in range(0, part, chunk):
            inner = index * part + at
            for lane in range(at, at + chunk, width):
                position = jnp.int32(0)
                if len(scattered) > 1:
                    apart = lane // width ^ place_of(last)
                    position = jnp.where(apart == 0, 0, last[0] - apart)
                block = prompt_ref[:, window(position * width, width)].astype(F32).T
                turned_ref[index * part + lane : index * part + lane + width, :] = block
            rows = window(start + at, chunk)
            mine = slice(inner, inner + chunk)
            new = factor_ref[rows, :] * turned_ref[mine, :] + base_ref[rows, :]
            held_ref[mine, :] = new.astype(BF16)
            copies.append(
                pltpu.make_async_copy(
                    held_ref.at[mine, :], new_ref.at[rows, :], sems.at[len(copies)]
                )
            )
            copies[-1].start()
        heads = part // HEAD_DIM
        picked = [
            turned_ref[pl.ds(index * part + here * per_slice + k, heads, stride=HEAD_DIM), :]
            for k in range(per_slice)
        ]
        found.append(jnp.concatenate(picked, axis=1))
    if ending:
        others, shares = refs[: pieces - count], refs[pieces - count : -7]
        slice_ref, verify_ref = slice_refs
        verify_ref[...] = sum(ref[...].astype(F32) for ref in shares).astype(BF16)
        every = dict(zip(offsets, found))
        rest = [k for k in range(pieces) if k not in offsets]
        every.update(zip(rest, (ref[...] for ref in others)))
        rows = []
        for spot in range(pieces):
            chosen = every[0]
            for k in range(1, pieces):
                chosen = jnp.where(piece_at(spot) == k, every[k], chosen)
            rows.append(chosen)
        slice_ref[...] = jnp.concatenate(rows, axis=0).astype(BF16)
    else:
        for ref, value in zip(slice_refs, found):
            ref[...] = value
    for copy in copies:
        copy.wait()


def states(stages, scattered, prepared, pieces, offsets, prompts, new, slices, shares, after=()):
    lanes = prepared[0].shape[0]
    part = lanes // pieces
    count = len(offsets)
    cols = HEAD_DIM // (stages[2][0] * stages[2][1]) * STATE_SIZE
    ending = bool(shares)
    args = [*prepared, *prompts]
    if ending:
        args += [slices[k] for k in range(pieces) if k not in offsets] + shares
    specs = [WHOLE] * len(args)
    alias = None
    if new is not None:
        alias = {len(args): 0}
        args.append(new)
        specs.append(IN_HBM)
    outs = [shape((lanes, STATE_SIZE), BF16)]
    if ending:
        outs += [shape((lanes // HEAD_DIM, cols), BF16), shape(shares[0].shape, BF16)]
    else:
        outs += [shape((part // HEAD_DIM, cols), F32)] * count
    return call(
        functools.partial(states_kernel, stages, scattered, pieces, offsets, ending),
        "states",
        outs,
        args,
        specs=specs,
        out_specs=[IN_HBM] + [WHOLE] * (len(outs) - 1),
        after=after,
        alias=alias,
        scratch=[
            pltpu.VMEM((count * part, STATE_SIZE), F32),
            pltpu.VMEM((count * part, STATE_SIZE), BF16),
            pltpu.SemaphoreType.DMA((2 * count,)),
        ],
        moved=1,
    )


def on_device(
    prefill_input,
    prefill_step,
    write_proj,
    read_proj,
    decay_rate,
    skip_gain,
    resident_state,
    owner_slot,
    draft_ids,
    accepted_len,
    draft_input,
    draft_gate,
    draft_write,
    draft_read,
    draft_step,
    norm_gain,
    out_weight,
):
    span, lanes = prefill_input.shape
    assert span == BLOCK_LEN
    heads = decay_rate.shape[0]
    groups = write_proj.shape[1] // STATE_SIZE
    per_group = heads // groups
    half = lanes // 2
    seq_count, head_count = lax.axis_size("seq"), lax.axis_size("head")
    stages = tree_stages(seq_count)
    core, line, last = stages
    slots = owner_slot.shape[0]
    assert core[0] == 2 and slots == seq_count
    rate, skip, gain = decay_rate[None], skip_gain[None], norm_gain[None]
    resident = resident_state.reshape(lanes, STATE_SIZE)

    inputs = [
        in_hbm(value)
        for value in (
            prefill_step.T, rate, owner_slot, draft_ids.T, accepted_len, write_proj, prefill_input,
            draft_input, draft_gate, draft_write, draft_read, draft_step, skip, rate, read_proj, resident,
            gain,
        )
    ]
    passed = 12
    opened = call(
        functools.partial(open_kernel, core, len(inputs), passed),
        "open_block",
        [
            shape((STATE_SIZE, half), BF16),
            shape((groups, span, per_group), F32),
            shape((heads, span), F32),
            shape((heads, span), F32),
            shape((span, 2 * heads), BF16),
            shape((span, 2 * heads), BF16),
            shape((DRAFTS, draft_input.shape[0]), F32),
            shape((DRAFTS, 128), jnp.int32),
            shape((DRAFTS, out_weight.shape[1]), jnp.int32),
        ]
        + [shape(value.shape, value.dtype) for value in inputs[-passed:]],
        inputs,
        specs=[IN_HBM] * len(inputs),
        scratch=[pltpu.SemaphoreType.DMA((len(inputs) + 1,))]
        + [
            (pltpu.SMEM if value.dtype == jnp.int32 else pltpu.VMEM)(value.shape, value.dtype)
            for value in inputs[:-passed]
        ],
        flops=span * lanes * STATE_SIZE * 2,
    )
    sent, run, runt, stept, reach, end, pick, kept, owner = opened[:9]
    writes, x, din, dgate, dwrite, dread, dstep, skip, rate, reads, resident, gain = opened[9:]
    received = swap(sent, "seq", core, 1)
    own_extra, sent_extra, skip_lanes, q1, q2, vread, vwrite, tail = call(
        functools.partial(draft_kernel, core),
        "draft_rows",
        [
            shape((EXTRA, half), BF16),
            shape((EXTRA, half), BF16),
            shape((1, lanes), F32),
            shape((DRAFTS, lanes), F32),
            shape((DRAFTS, lanes), F32),
            shape((DRAFTS, groups * STATE_SIZE), BF16),
            shape((DRAFTS, groups * STATE_SIZE), BF16),
            shape((32, lanes), BF16),
        ],
        (pick, kept, owner, runt, rate, skip, din, dgate, dwrite, dread, dstep),
        after=[sent],
        scratch=[pltpu.VMEM((EXTRA, lanes), BF16)],
        flops=DRAFTS * lanes * 100,
    )
    received_extra = swap(sent_extra, "seq", core, 1)
    (own,) = call(
        functools.partial(own_kernel, core),
        "own_message",
        [shape((STATE_SIZE, half), BF16)],
        (end, x, writes),
        after=[sent_extra],
        flops=span * lanes * STATE_SIZE,
    )
    core_parts = [own, own_extra, received, received_extra]

    bases, fetched = [], []

    def fill(after):
        if len(bases) < groups:
            wanted = [out_weight] if len(bases) == min(1, groups - 1) else []
            base, *found = intra(
                len(bases), run, runt, stept, skip_lanes, x, writes, reads, after, wanted
            )
            bases.append(base)
            fetched.extend(found)
        return bases[-1:]

    def exchange(parts, stage):
        got = {k: swap(parts[k], "seq", stage, k) for k in range(1, stage[0])}
        return [parts[0]] + [got[k] for k in range(1, stage[0])]

    line_width = half // line[0]
    split_last = line_width % (last[0] * 128) == 0
    last_width = line_width // last[0] if split_last else line_width
    outs = call(
        functools.partial(up_kernel, core, line, 2, True),
        "up_line",
        [shape((UP_ROWS, line_width), BF16)] * line[0],
        core_parts,
        flops=half * UP_ROWS * 4,
    )
    line_parts = exchange(outs, line)
    hidden = resident_hidden(resident, vread, q1, q2, gain, [outs[-1]])
    hiddens = exchange([hidden] * last[0], last)
    filled = fill([outs[-1]])
    outs = call(
        functools.partial(up_kernel, line, last, line[0], False),
        "up_last",
        [shape((UP_ROWS, last_width), BF16)] * (last[0] if split_last else 1),
        line_parts,
        after=filled + hiddens[:0:-1],
        flops=line_width * UP_ROWS * 4,
    )
    last_parts = exchange(outs if split_last else outs * last[0], last)
    hidden = join(hiddens, 0, [outs[-1]])
    hiddens = exchange([hidden] * line[0], line)
    filled = fill([outs[-1]])
    last_parts = last_parts[:1] + list(gather_in(last_parts[:0:-1], filled))[::-1]
    *outs, prompt = call(
        functools.partial(top_kernel, last, last[0]),
        "top",
        [shape((DOWN_ROWS, last_width), BF16)] * (last[0] if split_last else 1)
        + [shape((STATE_SIZE, last_width), BF16)],
        turned(last_parts),
        after=filled,
        flops=last_width * UP_ROWS * 16,
    )

    pieces = exchange(outs, last) if split_last else outs
    hidden = join(hiddens, 0, [outs[-1]])
    filled = fill([outs[-1], hidden])
    ahead = exchange([prompt] * line[0], line)
    if split_last:
        pieces = pieces[:1] + list(gather_in(pieces[:0:-1], filled))[::-1]
    outs = call(
        functools.partial(down_kernel, line, last, len(pieces), line[0], False, range(line[0]), False),
        "down_line",
        [shape((DOWN_ROWS, line_width), BF16)] * line[0],
        [*turned(pieces), *line_parts],
        after=filled + ahead[1:],
        flops=line_width * UP_ROWS * 8,
    )
    pieces = exchange(outs, line)
    hiddens = [hidden, swap(hidden, "seq", core, 1)]
    filled = fill([outs[-1]])
    prepared = prepare(owner, resident, tail, vwrite, filled)
    filled = [*prepared, *hiddens[1:]]
    scattered = [line, last] if split_last else [line]
    if split_last:
        prompt = hand_on(prompt, [outs[-1]])
        parts = exchange([prompt] * last[0], last)
        others = join(turned(parts)[1:], 1)
        filled.append(others)

    def down_core(target, after):
        return call(
            functools.partial(down_kernel, core, line, line[0], 2, True, (target,), False),
            "down_core",
            [shape((STATE_SIZE, half), BF16)] + [shape((DRAFTS, half), BF16)] * target,
            turned(pieces) + core_parts,
            after=after,
            moved=1,
        )

    sent, gated = down_core(1, filled)
    received_gated, received = swap(gated, "seq", core, 1), swap(sent, "seq", core, 1)
    (received_gated,) = gather_in([received_gated])
    while len(bases) < groups:
        fill([])

    shares = project(
        stages, owner, *hiddens, gated, received_gated, gain, fetched[0], head_count
    )
    (entering,) = down_core(0, shares[:1])
    prefill_out, token = finish(core, reach, reads, entering, received, bases)
    shares = [shares[0]] + [swap(shares[k], "head", (head_count, 1), k) for k in range(1, head_count)]

    pieces = 2 * line[0]
    late = ahead[1:]
    if split_last:
        behind = exchange([others] * line[0], line)
        prompt = join([prompt, others], 1, shares[:1])
        late = [
            join(pair, 1, [token, *shares[1:]], flops=10**10) for pair in zip(late, behind[1:])
        ]
    crossed = swap(prompt, "seq", core, 1)
    slices = {}
    new_state, slices[0], slices[line[0]] = states(
        stages, scattered, prepared, pieces, (0, line[0]), (prompt, crossed), None, None, (), late[:1]
    )
    offsets = (*range(1, line[0]), *range(line[0] + 1, pieces))
    prompts = late + [swap(piece, "seq", core, 1) for piece in late]
    new_state, state_slice, verify_out = states(
        stages, scattered, prepared, pieces, offsets, prompts, new_state, slices, shares
    )
    return (
        prefill_out,
        new_state.reshape(1, heads, HEAD_DIM, STATE_SIZE),
        verify_out,
        state_slice,
    )


def solution(mesh):
    return jax.shard_map(
        on_device,
        mesh=mesh,
        in_specs=(
            P("seq", "head"),
            P("seq", "head"),
            P("seq", "head"),
            P("seq", "head"),
            P("head"),
            P("head"),
            P("seq", "head", None, None),
            P(),
            P(),
            P(),
            P("seq", "head"),
            P("seq", "head"),
            P("seq", "head"),
            P("seq", "head"),
            P("seq", "head"),
            P("head"),
            P("head", "seq"),
        ),
        out_specs=(
            P("seq", "head"),
            P("seq", "head", None, None),
            P("head", "seq"),
            P("head", "seq"),
        ),
        check_vma=False,
    )
```

```python
import functools

import jax
import jax.numpy as jnp
from jax import lax
from jax.experimental import pallas as pl
from jax.experimental.pallas import tpu as pltpu
from jax.sharding import PartitionSpec as P

HEAD_DIM = 64
STATE_SIZE = 128
BLOCK_LEN = 256
DRAFTS = 8
EPSILON = 1e-05
EXTRA = 32
UP_ROWS = STATE_SIZE + EXTRA
READ_AT = STATE_SIZE + 16
LOG_AT = STATE_SIZE + 24
DOWN_ROWS = STATE_SIZE + 8

F32 = jnp.float32
BF16 = jnp.bfloat16


def tree_stages(count):
    factors, rest = [], count
    if rest > 1:
        factors.append(2)
        rest //= 2
    inner = 1
    while inner * inner * 4 <= rest:
        inner *= 2
    factors += [inner, rest // inner]
    stages, stride = [], 1
    for factor in factors:
        stages.append((factor, stride))
        stride *= factor
    assert stride == count
    return stages


def swap(value, axis, stage, offset):
    count, stride = lax.axis_size(axis), stage[1]
    return lax.ppermute(value, axis, [(k, k ^ (offset * stride)) for k in range(count)])


def place_of(stage):
    factor, stride = stage
    return lax.rem(lax.div(lax.axis_index("seq"), stride), factor)


def dot(a, b, dims=((1,), (0,))):
    return lax.dot_general(a, b, (dims, ((), ())), preferred_element_type=F32)


def split(value, parts):
    found = []
    for _ in range(parts):
        part = value.astype(BF16).astype(F32)
        found.append(part)
        value = value - part
    return found


def head_mask(rows, heads, lanes, lane0):
    row = lax.broadcasted_iota(jnp.int32, (rows, lanes), 0) & (heads - 1)
    head = lax.shift_right_logical(lax.broadcasted_iota(jnp.int32, (rows, lanes), 1) + lane0, 6)
    return jnp.where(row == head, 1.0, 0.0).astype(BF16)


def window(start, size):
    return pl.ds(pl.multiple_of(start, size), size)


def ordered(kernel, count):
    return lambda *refs: kernel(*refs[count:])


ANYWHERE = pl.BlockSpec(memory_space=pl.ANY)
WHOLE = pl.BlockSpec(memory_space=pltpu.VMEM)
IN_HBM = pl.BlockSpec(memory_space=pltpu.HBM)


def call(
    kernel, name, outs, args, specs=None, out_specs=None, grid=(), after=(), scratch=(), alias=None,
    flops=0, exps=0, moved=None, vmem=32,
):
    if specs is None:
        specs = [WHOLE] * len(args)
    if out_specs is None:
        out_specs = [WHOLE] * len(outs)
    if moved is None:
        moved = sum(a.size * a.dtype.itemsize for a in (*args, *outs))
    first = len(after)
    return pl.pallas_call(
        ordered(kernel, first),
        name=name,
        grid=grid,
        out_shape=outs,
        in_specs=[ANYWHERE] * first + specs,
        out_specs=out_specs,
        scratch_shapes=list(scratch),
        input_output_aliases={first + k: v for k, v in (alias or {}).items()},
        compiler_params=pltpu.CompilerParams(vmem_limit_bytes=vmem * 1024 * 1024),
        cost_estimate=pl.CostEstimate(flops=flops, bytes_accessed=moved, transcendentals=exps),
    )(*after, *args)


def in_hbm(value):
    return pltpu.with_memory_space_constraint(value, pltpu.HBM)


def shape(dims, dtype):
    return jax.ShapeDtypeStruct(dims, dtype)


def open_kernel(stage, count, passed, *refs):
    sources, rest = refs[:count], refs[count:]
    outs, scratch = rest[: 9 + passed], rest[9 + passed :]
    outs, later = outs[:9], list(outs[9:])
    sent_ref, run_ref, runt_ref, stept_ref, reach_ref, end_ref, pick_ref, kept_out, owner_out = outs
    sems, held = scratch[0], [*scratch[1:], *later]
    here = lax.axis_index("seq")
    place = place_of(stage)
    early = count - passed
    half = sent_ref.shape[1]

    def fetch(k, at=None):
        if at is None:
            return pltpu.make_async_copy(sources[k], held[k], sems.at[k])
        sem = sems.at[k if at == 1 else count]
        lanes = window((place ^ at) * half, half)
        return pltpu.make_async_copy(sources[k].at[:, lanes], held[k].at[:, lanes], sem)

    first = [fetch(k) for k in range(early + 1)] + [fetch(early + 1, 1)]
    rest = [fetch(early + 1, 0)] + [fetch(k) for k in range(early + 2, count)]
    for copy in first:
        copy.start()
    for copy in first[:early]:
        copy.wait()
    for copy in rest:
        copy.start()
    turned_ref, rate_ref, owner_ref, ids_ref, kept_ref, write_ref, x_ref = held[:7]
    heads, span = turned_ref.shape
    groups = write_ref.shape[1] // STATE_SIZE
    per_group = heads // groups

    step_rows = turned_ref[...]
    stept_ref[...] = step_rows
    pad = (-heads) % 128
    if pad:
        step_rows = jnp.concatenate([step_rows, jnp.zeros((pad, span), F32)], axis=0)
    step = step_rows.T[:, :heads]
    log_decay = -step * rate_ref[...]
    lower = lax.broadcasted_iota(jnp.int32, (span, span), 0) >= lax.broadcasted_iota(
        jnp.int32, (span, span), 1
    )
    lower = jnp.where(lower, 1.0, 0.0).astype(BF16)
    running = sum(dot(lower, part.astype(BF16)) for part in split(log_decay, 3))
    to_end = jnp.exp(running[span - 1 : span, :] - running) * step
    end_ref[...] = jnp.concatenate(split(to_end, 2), axis=1).astype(BF16)

    for copy in first[early:]:
        copy.wait()
    fill_message(place ^ 1, end_ref, x_ref, write_ref, sent_ref)

    wide_run = running
    if pad:
        wide_run = jnp.concatenate([running, jnp.zeros((span, pad), F32)], axis=1)
    runt_ref[...] = wide_run.T[:heads]
    for g in range(groups):
        run_ref[g] = running[:, g * per_group : (g + 1) * per_group]
    reach_ref[...] = jnp.concatenate(split(jnp.exp(running), 2), axis=1).astype(BF16)

    slots = owner_ref.shape[0]
    request = lax.fori_loop(
        0, slots, lambda r, found: jnp.where(owner_ref[r] == here, r, found), jnp.int32(0)
    )
    row = lax.broadcasted_iota(jnp.int32, pick_ref.shape, 0)
    col = lax.broadcasted_iota(jnp.int32, pick_ref.shape, 1)
    pick = jnp.zeros(pick_ref.shape, F32)
    for i in range(DRAFTS):
        pick = jnp.where((row == i) & (col == ids_ref[i, request]), 1.0, pick)
    pick_ref[...] = pick
    kept_out[...] = jnp.zeros(kept_out.shape, jnp.int32) + kept_ref[request]
    owner_out[...] = jnp.zeros(owner_out.shape, jnp.int32) + owner_ref[0]
    for copy in rest:
        copy.wait()


def draft_kernel(
    stage,
    pick_ref,
    kept_ref,
    owner_ref,
    runt_ref,
    rate_ref,
    skip_ref,
    din_ref,
    dgate_ref,
    dwrite_ref,
    dread_ref,
    dstep_ref,
    own_ref,
    sent_ref,
    skip_out,
    q1_ref,
    q2_ref,
    vread_ref,
    vwrite_ref,
    tail_ref,
    extra_ref,
):
    heads, span = runt_ref.shape
    lanes = din_ref.shape[1]
    groups = dwrite_ref.shape[1] // STATE_SIZE
    wide = lanes // groups
    here = lax.axis_index("seq")
    place = place_of(stage)
    pick = pick_ref[...].astype(BF16)
    vin = dot(pick, din_ref[...])
    vgate = dot(pick, dgate_ref[...])
    vwrite = dot(pick, dwrite_ref[...]).astype(BF16)
    vread = dot(pick, dread_ref[...]).astype(BF16)
    vwrite_ref[...] = vwrite
    vread_ref[...] = vread
    vstep = sum(dot(pick, part.astype(BF16)) for part in split(dstep_ref[...], 3))
    vlog = -vstep * rate_ref[...]
    index = lax.broadcasted_iota(jnp.int32, (DRAFTS, heads), 0)
    kept_heads = kept_ref[:, :1]
    acc = jnp.zeros((1, heads), F32)
    vrun = jnp.zeros((DRAFTS, heads), F32)
    reach = jnp.zeros((1, heads), F32)
    for i in range(DRAFTS):
        acc = acc + vlog[i : i + 1]
        vrun = jnp.where(index == i, acc, vrun)
        reach = jnp.where(i < kept_heads[0:1], acc, reach)
    total = runt_ref[:, span - 128 :]
    if heads < 128:
        total = jnp.concatenate([total, jnp.zeros((128 - heads, 128), F32)], axis=0)
    total = total.T[127:128, :heads]
    others = jnp.where(index == 0, total, jnp.where(index == 1, skip_ref[...], reach))
    stacked = split(jnp.concatenate([vrun, vstep, others], axis=0), 3)
    stacked = jnp.concatenate(stacked, axis=0).astype(BF16)
    row = lax.broadcasted_iota(jnp.int32, (DRAFTS, wide), 0)
    kept = kept_ref[:, :1]
    is_owner = owner_ref[0:1, :1] == here
    for g in range(groups):
        at = slice(g * wide, (g + 1) * wide)
        spread = dot(stacked, head_mask(heads, heads, wide, g * wide))
        spread = spread[0:24] + spread[24:48] + spread[48:72]
        vrun_l, vstep_l = spread[0:8], spread[8:16]
        total_l, skip_l, reach_l = spread[16:17], spread[17:18], spread[18:19]
        skip_out[:, at] = skip_l
        vin_g = vin[:, at]
        vr = vread[:, g * STATE_SIZE : (g + 1) * STATE_SIZE]
        vw = vwrite[:, g * STATE_SIZE : (g + 1) * STATE_SIZE]
        scores = dot(vr, vw, ((1,), (1,)))
        direct = skip_l * vin_g
        for j in range(DRAFTS):
            decay = jnp.exp(jnp.where(row >= j, vrun_l - vrun_l[j : j + 1], -jnp.inf))
            direct = direct + decay * scores[:, j : j + 1] * (vstep_l[j : j + 1] * vin_g[j : j + 1])
        gate = vgate[:, at]
        gate = gate / (1.0 + jnp.exp(-gate))
        q1 = direct * gate
        q2 = jnp.exp(vrun_l) * gate
        q1_ref[:, at] = q1
        q2_ref[:, at] = q2
        live = jnp.exp(jnp.where(row < kept, reach_l - vrun_l, -jnp.inf)) * vstep_l * vin_g
        keep_l = jnp.concatenate(
            split(jnp.exp(reach_l), 3) + [jnp.zeros((5, wide), F32)], axis=0
        )
        tail_ref[:, at] = jnp.concatenate(split(live, 3) + [keep_l], axis=0).astype(BF16)
        read_l = jnp.concatenate([vr.astype(F32)] * (wide // STATE_SIZE), axis=1)
        mine = jnp.concatenate([q1, q2, read_l], axis=0)
        mine = jnp.where(is_owner, mine, 0.0)
        logs = jnp.concatenate(split(total_l, 3) + [jnp.zeros((5, wide), F32)], axis=0)
        extra_ref[:, at] = jnp.concatenate([mine, logs], axis=0).astype(BF16)
    half = lanes // 2
    own_ref[...] = extra_ref[:, window(place * half, half)]
    sent_ref[...] = extra_ref[:, window((place ^ 1) * half, half)]


def fill_message(side, end_ref, x_ref, write_ref, out_ref):
    heads = end_ref.shape[1] // 2
    half = out_ref.shape[1]
    wide = 2 * half // (write_ref.shape[1] // STATE_SIZE)
    chunk = min(wide, half)
    start = side * half
    for at in range(0, half, chunk):
        lane0 = start + at
        group = lax.div(lane0, wide)
        scale = dot(end_ref[...], head_mask(2 * heads, heads, chunk, lane0))
        weighted = (x_ref[:, window(lane0, chunk)].astype(F32) * scale).astype(BF16)
        writes = write_ref[:, window(group * STATE_SIZE, STATE_SIZE)]
        writes = writes.astype(F32).T.astype(BF16)
        out_ref[:, at : at + chunk] = dot(writes, weighted).astype(BF16)


def own_kernel(stage, end_ref, x_ref, write_ref, out_ref):
    fill_message(place_of(stage), end_ref, x_ref, write_ref, out_ref)


def state_of(part, at):
    return part[0][:STATE_SIZE, at].astype(F32)


def extra_of(part, at):
    return (part[1][:, at] if part[2] else part[0][STATE_SIZE:UP_ROWS, at]).astype(F32)


def logs_of(part, at):
    found = extra_of(part, at)[LOG_AT - STATE_SIZE :]
    return found[0:1] + found[1:2] + found[2:3]


def turned(parts):
    return [parts[0], *parts[:0:-1]]


def paired(refs, apart):
    if apart:
        return [(refs[k], refs[k + 1], True) for k in range(0, len(refs), 2)]
    return [(ref, None, False) for ref in refs]


def weights_of(logs, place, target):
    spots = [place ^ k for k in range(len(logs))]
    found = []
    for k, spot in enumerate(spots):
        between = jnp.zeros_like(logs[0])
        for other, log in zip(spots, logs):
            if other is not spot:
                between = between + jnp.where((spot < other) & (other < target), log, 0.0)
        found.append(jnp.where(spot < target, jnp.exp(between), 0.0))
    return found


def carry_of(logs, place, target):
    ahead = jnp.zeros_like(logs[0])
    for k, log in enumerate(logs):
        ahead = ahead + jnp.where((place ^ k) < target, log, 0.0)
    return jnp.exp(ahead)


def up_kernel(stage, following, count, apart, *refs):
    taken = 2 * count if apart else count
    parts, outs = paired(refs[:taken], apart), refs[taken:]
    place, target = place_of(stage), place_of(following)
    width = outs[0].shape[1]
    chunk = min(256, width)
    order = list(range(1, len(outs))) + [0]
    for k in order:
        for at in range(0, width, chunk):
            start = at if len(outs) == 1 else (target ^ k) * width + at
            at_in = window(start, chunk)
            logs = [logs_of(part, at_in) for part in parts]
            scale = weights_of(logs, place, count)
            state = sum(w * state_of(part, at_in) for w, part in zip(scale, parts))
            outs[k][:STATE_SIZE, at : at + chunk] = state.astype(BF16)
            mine = sum(extra_of(part, at_in) for part in parts)
            total = jnp.concatenate(
                split(sum(logs), 3) + [jnp.zeros((5, chunk), F32)], axis=0
            )
            outs[k][STATE_SIZE:, at : at + chunk] = jnp.concatenate(
                [mine[:24], total], axis=0
            ).astype(BF16)


def top_kernel(stage, count, *refs):
    parts, outs, prompt_ref = paired(turned(refs[:count]), False), refs[count:-1], refs[-1]
    whole = slice(None)
    place = place_of(stage)
    width = prompt_ref.shape[1]
    logs = [logs_of(part, whole) for part in parts]
    states = [state_of(part, whole) for part in parts]
    final = sum(w * s for w, s in zip(weights_of(logs, place, count), states)).astype(BF16)
    prompt_ref[...] = final
    mine = sum(extra_of(part, whole) for part in parts)
    reads = mine[16:24, :STATE_SIZE].astype(BF16)
    gated = mine[0:8] + mine[8:16] * dot(reads, final)
    gated = gated.astype(BF16)
    for k in list(range(1, len(outs))) + [0]:
        scale = weights_of(logs, place, place ^ k)
        outs[k][:STATE_SIZE, :] = sum(w * s for w, s in zip(scale, states)).astype(BF16)
        outs[k][STATE_SIZE:, :] = gated


def down_kernel(stage, above, above_count, count, apart, targets, handed, *refs):
    end = above_count + (2 * count if apart else count)
    pieces, outs = turned(refs[:above_count]), refs[end:]
    parts = paired(refs[above_count:end], apart)
    if handed:
        outs[-1][...] = outs[0][...]
        outs = outs[1:-1]
    place, source = place_of(stage), place_of(above)
    width = pieces[0].shape[1]
    chunk = min(256, width)
    gated_ref = outs[1] if apart and len(outs) > 1 else None
    for k, out_ref in zip(targets, outs):
        for piece in range(above_count):
            for at in range(0, width, chunk):
                start = at if above_count == 1 else (source ^ piece) * width + at
                at_out = window(start, chunk)
                block = pieces[piece][:, at : at + chunk]
                logs = [logs_of(part, at_out) for part in parts]
                state = carry_of(logs, place, place ^ k) * block[:STATE_SIZE].astype(F32)
                for w, part in zip(weights_of(logs, place, place ^ k), parts):
                    state = state + w * state_of(part, at_out)
                out_ref[:STATE_SIZE, at_out] = state.astype(BF16)
                if gated_ref is not None:
                    gated_ref[:, at_out] = block[STATE_SIZE:]
                elif out_ref.shape[0] > STATE_SIZE:
                    out_ref[STATE_SIZE:, at_out] = block[STATE_SIZE:]


def intra_kernel(group, run_ref, runt_ref, stept_ref, skip_ref, x_ref, write_ref, read_ref, *refs):
    fetch = None
    out_ref = refs[0]
    if len(refs) > 1:
        source_ref, out_ref, held_ref, sem = refs
        fetch = pltpu.make_async_copy(source_ref, held_ref, sem)
        fetch.start()
    span, heads = run_ref.shape[1:]
    mid = span // 2
    states = slice(group * STATE_SIZE, (group + 1) * STATE_SIZE)
    scores = dot(read_ref[:, states], write_ref[:, states], ((1,), (1,)))
    row = lax.broadcasted_iota(jnp.int32, (mid, mid), 0)
    causal = row >= lax.broadcasted_iota(jnp.int32, (mid, mid), 1)
    running = run_ref[group]
    low, high = slice(0, mid), slice(mid, span)
    for pair in range(heads // 2):
        found = []
        for k in (2 * pair, 2 * pair + 1):
            h = group * heads + k
            x = x_ref[:, h * HEAD_DIM : (h + 1) * HEAD_DIM]
            t_run, j_run = running[:, k : k + 1], runt_ref[h : h + 1, :]
            step = stept_ref[h : h + 1, :]

            def mixed(rows, cols, masked):
                gap = t_run[rows] - j_run[:, cols]
                if masked:
                    gap = jnp.where(causal, gap, -jnp.inf)
                return (scores[rows, cols] * jnp.exp(gap) * step[:, cols]).astype(BF16)

            top = dot(mixed(low, low, True), x[low])
            bottom = dot(mixed(high, low, False), x[low]) + dot(mixed(high, high, True), x[high])
            found.append(jnp.concatenate([top, bottom], axis=0))
        at = slice(pair * 2 * HEAD_DIM, (pair + 1) * 2 * HEAD_DIM)
        lanes = slice((group * heads + 2 * pair) * HEAD_DIM, (group * heads + 2 * pair + 2) * HEAD_DIM)
        both = jnp.concatenate(found, axis=1)
        out_ref[:, at] = both + skip_ref[:, lanes] * x_ref[:, lanes].astype(F32)
    if fetch is not None:
        fetch.wait()


def intra(group, run, runt, stept, skip, x, write, read, after, wanted=()):
    span, per_group = run.shape[1:]
    wide = per_group * HEAD_DIM
    return call(
        functools.partial(intra_kernel, group),
        "intra",
        [shape((span, wide), F32)] + [shape(value.shape, value.dtype) for value in wanted],
        (run, runt, stept, skip, x, write, read, *map(in_hbm, wanted)),
        specs=[WHOLE] * 7 + [IN_HBM] * len(wanted),
        scratch=[pltpu.SemaphoreType.DMA] * len(wanted),
        after=after,
        flops=per_group * span * span * HEAD_DIM * 2,
        moved=wide * span * 6,
        exps=per_group * span * span * 3 // 4,
    )


def finish_kernel(stage, reach_ref, read_ref, own_ref, got_ref, *refs):
    base_refs, (out_ref, token_ref, held_ref, sems) = refs[:-4], refs[-4:]
    token_ref[...] = jnp.zeros_like(token_ref)
    place = place_of(stage)
    heads = reach_ref.shape[1] // 2
    lanes = held_ref.shape[1]
    wide = lanes // len(base_refs)
    half = lanes // 2
    chunk = lanes // sems.shape[0]
    copies = []
    for k, lane0 in enumerate(range(0, lanes, chunk)):
        group, at = lane0 // wide, lane0 % half
        at_in, at_out = slice(at, at + chunk), slice(lane0, lane0 + chunk)
        entering = jnp.where(place == lane0 // half, own_ref[:, at_in], got_ref[:, at_in])
        inter = dot(read_ref[:, group * STATE_SIZE : (group + 1) * STATE_SIZE], entering)
        inter = inter * dot(reach_ref[...], head_mask(2 * heads, heads, chunk, lane0))
        base = base_refs[group][:, lane0 % wide : lane0 % wide + chunk]
        held_ref[:, at_out] = (inter + base).astype(BF16)
        copies.append(
            pltpu.make_async_copy(held_ref.at[:, at_out], out_ref.at[:, at_out], sems.at[k])
        )
        copies[-1].start()
    for copy in copies:
        copy.wait()


def finish(stage, reach, read, own, got, bases):
    span = read.shape[0]
    lanes = 2 * own.shape[1]
    chunk = min(512, own.shape[1])
    return call(
        functools.partial(finish_kernel, stage),
        "finish",
        [shape((span, lanes), BF16), shape((8, 128), F32)],
        (reach, read, own, got, *bases),
        out_specs=[IN_HBM, WHOLE],
        scratch=[pltpu.VMEM((span, lanes), BF16), pltpu.SemaphoreType.DMA((lanes // chunk,))],
        moved=1,
    )


def resident_kernel(state_ref, vread_ref, q1_ref, q2_ref, gain_ref, out_ref):
    groups = vread_ref.shape[1] // STATE_SIZE
    wide = state_ref.shape[0] // groups
    for g in range(groups):
        at = slice(g * wide, (g + 1) * wide)
        reads = vread_ref[:, g * STATE_SIZE : (g + 1) * STATE_SIZE]
        drawn = dot(reads, state_ref[at, :], ((1,), (1,)))
        gated = q1_ref[:, at] + q2_ref[:, at] * drawn
        out_ref[:, at] = normed(gated, gain_ref[:, at]).astype(BF16)


def normed(gated, gain):
    mean_square = jnp.mean(gated * gated, axis=1, keepdims=True)
    return gated * lax.rsqrt(mean_square + EPSILON) * gain


def resident_hidden(state, vread, q1, q2, gain, after):
    lanes = state.shape[0]
    return call(
        resident_kernel,
        "resident_hidden",
        [shape((DRAFTS, lanes), BF16)],
        (state, vread, q1, q2, gain),
        after=after,
        flops=2 * DRAFTS * lanes * STATE_SIZE,
    )[0]


def hand_on(value, after):
    def copy(value_ref, out_ref):
        out_ref[...] = value_ref[...]

    return call(copy, "hand_on", [shape(value.shape, value.dtype)], [value], after=after)[0]


def gather_in(values, after=()):
    def copy(*refs):
        for k in range(len(values)):
            refs[len(values) + k][...] = refs[k][...]

    return call(
        copy, "gather_in", [shape(v.shape, v.dtype) for v in values], values, after=after,
        flops=10**10, moved=1,
    )


def join_kernel(axis, *refs):
    out_ref, start = refs[-1], 0
    for ref in refs[:-1]:
        at = slice(start, start + ref.shape[axis])
        start = at.stop
        if axis == 0:
            out_ref[at, :] = ref[...]
        else:
            out_ref[:, at] = ref[...]


def join(parts, axis, after=(), flops=0):
    dims = list(parts[0].shape)
    dims[axis] = sum(part.shape[axis] for part in parts)
    return call(
        functools.partial(join_kernel, axis), "join", [shape(tuple(dims), parts[0].dtype)], parts, after=after, moved=1, flops=flops
    )[0]


def project_kernel(stages, head_count, *refs):
    owner_ref, own_rows, got_rows, own_ref, got_ref, gain_ref, weight_ref = refs[:7]
    outs = refs[7 : 7 + head_count]
    gated_ref, left_ref, total_ref = refs[7 + head_count :]
    here, head = lax.axis_index("seq"), lax.axis_index("head")
    place = place_of(stages[0])
    half = own_ref.shape[1]
    lanes = weight_ref.shape[0]
    wide = min(1024, lanes)
    rows = own_rows.shape[0]
    for k, ref in enumerate((own_ref, got_ref)):
        gated_ref[:, window((place ^ k) * half, half)] = ref[...].astype(F32)
    left_ref[0:rows, :] = own_rows[...]
    left_ref[rows : 2 * rows, :] = got_rows[...]
    for lane0 in range(0, lanes, wide):
        at = slice(lane0, lane0 + wide)
        hidden = normed(gated_ref[:, at], gain_ref[:, at])
        hidden = jnp.concatenate([hidden, jnp.zeros_like(hidden)], axis=0)
        left_ref[2 * rows :, at] = hidden.astype(BF16)
    total_ref[...] = dot(left_ref[...], weight_ref[...])

    per_head = 2 * rows // DRAFTS // head_count
    offsets = [0]
    for factor, stride in reversed(stages):
        offsets = [a + k * stride for k in range(factor) for a in offsets]
    owner = owner_ref[...]
    tail = total_ref[2 * rows : 2 * rows + DRAFTS, :]
    for k in list(range(1, head_count)) + [0]:
        first = (head ^ k) * per_head
        for slot in range(per_head):
            at = slice(slot * DRAFTS, (slot + 1) * DRAFTS)
            offset = here ^ (first + slot)
            block = jnp.int32(0)
            for position, value in enumerate(offsets):
                block = jnp.where(offset == value, position, block)
            drawn = total_ref[window(block * DRAFTS, DRAFTS), :]
            drawn = jnp.where(owner == first + slot, tail, drawn)
            outs[k][at, :] = drawn.astype(outs[k].dtype)


def project(stages, owner, own_rows, got_rows, own, got, gain, weight, head_count):
    lanes, cols = weight.shape
    rows = 2 * own_rows.shape[0]
    return call(
        functools.partial(project_kernel, stages, head_count),
        "project",
        [shape((rows // head_count, cols), BF16 if k else F32) for k in range(head_count)],
        (owner, own_rows, got_rows, own, got, gain, weight),
        scratch=[
            pltpu.VMEM((DRAFTS, lanes), F32),
            pltpu.VMEM((rows + 16, lanes), BF16),
            pltpu.VMEM((rows + 16, cols), F32),
        ],
        moved=1,
    )


def prepare_kernel(owner_ref, resident_ref, tail_ref, vwrite_ref, base_ref, factor_ref):
    here = lax.axis_index("seq")
    lanes = resident_ref.shape[0]
    wide = lanes // (vwrite_ref.shape[1] // STATE_SIZE)
    chunk = min(512, wide)
    is_owner = owner_ref[0:1, :STATE_SIZE] == here
    row = lax.broadcasted_iota(jnp.int32, (32, STATE_SIZE), 0)
    ones = jnp.where((row >= 24) & (row < 27), 1.0, 0.0)
    for start in range(0, lanes, chunk):
        rows, group = slice(start, start + chunk), start // wide
        writes = vwrite_ref[:, group * STATE_SIZE : (group + 1) * STATE_SIZE].astype(F32)
        writes = jnp.concatenate([writes, writes, writes, jnp.zeros_like(writes)], axis=0)
        right = jnp.concatenate([writes, ones], axis=1).astype(BF16)
        left = tail_ref[:, rows].astype(F32).T.astype(BF16)
        both = dot(left, right)
        added, decay = both[:, :STATE_SIZE], both[:, STATE_SIZE:]
        kept = decay * resident_ref[rows, :].astype(F32)
        base_ref[rows, :] = added + jnp.where(is_owner, 0.0, kept)
        factor_ref[rows, :] = jnp.where(is_owner, decay, 0.0)


def prepare(owner, resident, tail, vwrite, after):
    return call(
        prepare_kernel,
        "prepare_states",
        [shape(resident.shape, F32)] * 2,
        (owner, resident, tail, vwrite),
        after=after,
        moved=1,
    )


def states_kernel(stages, scattered, pieces, offsets, ending, *refs):
    base_ref, factor_ref = refs[:2]
    count = len(offsets)
    prompt_refs, refs = refs[2 : 2 + count], refs[2 + count :]
    new_ref, *slice_refs, turned_ref, held_ref, sems = refs[-4 - count :] if not ending else refs[-6:]
    here = lax.axis_index("seq")
    core, line, last = stages
    lanes = base_ref.shape[0]
    part = lanes // pieces
    width = part // (last[0] if len(scattered) > 1 else 1)

    def piece_at(spot):
        return (spot // line[0] ^ place_of(core)) * line[0] + (spot % line[0] ^ place_of(line))

    def spot_of(offset):
        return (offset // line[0] ^ place_of(core)) * line[0] + (offset % line[0] ^ place_of(line))

    copies, found = [], []
    chunk = part // 4 if part >= 1024 else part
    per_slice = HEAD_DIM // (core[0] * line[0] * last[0])
    for index, (offset, prompt_ref) in enumerate(zip(offsets, prompt_refs)):
        start = spot_of(offset) * part
        for at in range(0, part, chunk):
            inner = index * part + at
            for lane in range(at, at + chunk, width):
                position = jnp.int32(0)
                if len(scattered) > 1:
                    apart = lane // width ^ place_of(last)
                    position = jnp.where(apart == 0, 0, last[0] - apart)
                block = prompt_ref[:, window(position * width, width)].astype(F32).T
                turned_ref[index * part + lane : index * part + lane + width, :] = block
            rows = window(start + at, chunk)
            mine = slice(inner, inner + chunk)
            new = factor_ref[rows, :] * turned_ref[mine, :] + base_ref[rows, :]
            held_ref[mine, :] = new.astype(BF16)
            copies.append(
                pltpu.make_async_copy(
                    held_ref.at[mine, :], new_ref.at[rows, :], sems.at[len(copies)]
                )
            )
            copies[-1].start()
        heads = part // HEAD_DIM
        picked = [
            turned_ref[pl.ds(index * part + here * per_slice + k, heads, stride=HEAD_DIM), :]
            for k in range(per_slice)
        ]
        found.append(jnp.concatenate(picked, axis=1))
    if ending:
        others, shares = refs[: pieces - count], refs[pieces - count : -7]
        slice_ref, verify_ref = slice_refs
        verify_ref[...] = sum(ref[...].astype(F32) for ref in shares).astype(BF16)
        every = dict(zip(offsets, found))
        rest = [k for k in range(pieces) if k not in offsets]
        every.update(zip(rest, (ref[...] for ref in others)))
        rows = []
        for spot in range(pieces):
            chosen = every[0]
            for k in range(1, pieces):
                chosen = jnp.where(piece_at(spot) == k, every[k], chosen)
            rows.append(chosen)
        slice_ref[...] = jnp.concatenate(rows, axis=0).astype(BF16)
    else:
        for ref, value in zip(slice_refs, found):
            ref[...] = value
    for copy in copies:
        copy.wait()


def states(stages, scattered, prepared, pieces, offsets, prompts, new, slices, shares, after=()):
    lanes = prepared[0].shape[0]
    part = lanes // pieces
    count = len(offsets)
    cols = HEAD_DIM // (stages[2][0] * stages[2][1]) * STATE_SIZE
    ending = bool(shares)
    args = [*prepared, *prompts]
    if ending:
        args += [slices[k] for k in range(pieces) if k not in offsets] + shares
    specs = [WHOLE] * len(args)
    alias = None
    if new is not None:
        alias = {len(args): 0}
        args.append(new)
        specs.append(IN_HBM)
    outs = [shape((lanes, STATE_SIZE), BF16)]
    if ending:
        outs += [shape((lanes // HEAD_DIM, cols), BF16), shape(shares[0].shape, BF16)]
    else:
        outs += [shape((part // HEAD_DIM, cols), F32)] * count
    return call(
        functools.partial(states_kernel, stages, scattered, pieces, offsets, ending),
        "states",
        outs,
        args,
        specs=specs,
        out_specs=[IN_HBM] + [WHOLE] * (len(outs) - 1),
        after=after,
        alias=alias,
        scratch=[
            pltpu.VMEM((count * part, STATE_SIZE), F32),
            pltpu.VMEM((count * part, STATE_SIZE), BF16),
            pltpu.SemaphoreType.DMA((4 * count,)),
        ],
        moved=1,
    )


def on_device(
    prefill_input,
    prefill_step,
    write_proj,
    read_proj,
    decay_rate,
    skip_gain,
    resident_state,
    owner_slot,
    draft_ids,
    accepted_len,
    draft_input,
    draft_gate,
    draft_write,
    draft_read,
    draft_step,
    norm_gain,
    out_weight,
):
    span, lanes = prefill_input.shape
    assert span == BLOCK_LEN
    heads = decay_rate.shape[0]
    groups = write_proj.shape[1] // STATE_SIZE
    per_group = heads // groups
    half = lanes // 2
    seq_count, head_count = lax.axis_size("seq"), lax.axis_size("head")
    stages = tree_stages(seq_count)
    core, line, last = stages
    slots = owner_slot.shape[0]
    assert core[0] == 2 and slots == seq_count
    rate, skip, gain = decay_rate[None], skip_gain[None], norm_gain[None]
    resident = resident_state.reshape(lanes, STATE_SIZE)

    inputs = [
        in_hbm(value)
        for value in (
            prefill_step.T, rate, owner_slot, draft_ids.T, accepted_len, write_proj, prefill_input,
            draft_input, draft_gate, draft_write, draft_read, draft_step, skip, rate, read_proj, resident,
            gain,
        )
    ]
    passed = 12
    opened = call(
        functools.partial(open_kernel, core, len(inputs), passed),
        "open_block",
        [
            shape((STATE_SIZE, half), BF16),
            shape((groups, span, per_group), F32),
            shape((heads, span), F32),
            shape((heads, span), F32),
            shape((span, 2 * heads), BF16),
            shape((span, 2 * heads), BF16),
            shape((DRAFTS, draft_input.shape[0]), F32),
            shape((DRAFTS, 128), jnp.int32),
            shape((DRAFTS, out_weight.shape[1]), jnp.int32),
        ]
        + [shape(value.shape, value.dtype) for value in inputs[-passed:]],
        inputs,
        specs=[IN_HBM] * len(inputs),
        scratch=[pltpu.SemaphoreType.DMA((len(inputs) + 1,))]
        + [
            (pltpu.SMEM if value.dtype == jnp.int32 else pltpu.VMEM)(value.shape, value.dtype)
            for value in inputs[:-passed]
        ],
        flops=span * lanes * STATE_SIZE * 2,
    )
    sent, run, runt, stept, reach, end, pick, kept, owner = opened[:9]
    writes, x, din, dgate, dwrite, dread, dstep, skip, rate, reads, resident, gain = opened[9:]
    received = swap(sent, "seq", core, 1)
    own_extra, sent_extra, skip_lanes, q1, q2, vread, vwrite, tail = call(
        functools.partial(draft_kernel, core),
        "draft_rows",
        [
            shape((EXTRA, half), BF16),
            shape((EXTRA, half), BF16),
            shape((1, lanes), F32),
            shape((DRAFTS, lanes), F32),
            shape((DRAFTS, lanes), F32),
            shape((DRAFTS, groups * STATE_SIZE), BF16),
            shape((DRAFTS, groups * STATE_SIZE), BF16),
            shape((32, lanes), BF16),
        ],
        (pick, kept, owner, runt, rate, skip, din, dgate, dwrite, dread, dstep),
        after=[sent],
        scratch=[pltpu.VMEM((EXTRA, lanes), BF16)],
        flops=DRAFTS * lanes * 100,
    )
    received_extra = swap(sent_extra, "seq", core, 1)
    (own,) = call(
        functools.partial(own_kernel, core),
        "own_message",
        [shape((STATE_SIZE, half), BF16)],
        (end, x, writes),
        after=[sent_extra],
        flops=span * lanes * STATE_SIZE,
    )
    core_parts = [own, own_extra, received, received_extra]

    bases, fetched = [], []

    def fill(after):
        if len(bases) < groups:
            wanted = [out_weight] if len(bases) == min(1, groups - 1) else []
            base, *found = intra(
                len(bases), run, runt, stept, skip_lanes, x, writes, reads, after, wanted
            )
            bases.append(base)
            fetched.extend(found)
        return bases[-1:]

    def exchange(parts, stage):
        got = {k: swap(parts[k], "seq", stage, k) for k in range(1, stage[0])}
        return [parts[0]] + [got[k] for k in range(1, stage[0])]

    line_width = half // line[0]
    split_last = line_width % (last[0] * 128) == 0
    last_width = line_width // last[0] if split_last else line_width
    outs = call(
        functools.partial(up_kernel, core, line, 2, True),
        "up_line",
        [shape((UP_ROWS, line_width), BF16)] * line[0],
        core_parts,
        flops=half * UP_ROWS * 4,
    )
    line_parts = exchange(outs, line)
    hidden = resident_hidden(resident, vread, q1, q2, gain, [outs[-1]])
    hiddens = exchange([hidden] * last[0], last)
    filled = fill([outs[-1]])
    outs = call(
        functools.partial(up_kernel, line, last, line[0], False),
        "up_last",
        [shape((UP_ROWS, last_width), BF16)] * (last[0] if split_last else 1),
        line_parts,
        after=filled + hiddens[:0:-1],
        flops=line_width * UP_ROWS * 4,
    )
    last_parts = exchange(outs if split_last else outs * last[0], last)
    hidden = join(hiddens, 0, [outs[-1]])
    hiddens = exchange([hidden] * line[0], line)
    filled = fill([outs[-1]])
    last_parts = last_parts[:1] + list(gather_in(last_parts[:0:-1], filled))[::-1]
    *outs, prompt = call(
        functools.partial(top_kernel, last, last[0]),
        "top",
        [shape((DOWN_ROWS, last_width), BF16)] * (last[0] if split_last else 1)
        + [shape((STATE_SIZE, last_width), BF16)],
        turned(last_parts),
        after=filled,
        flops=last_width * UP_ROWS * 16,
    )

    pieces = exchange(outs, last) if split_last else outs
    hidden = join(hiddens, 0, [outs[-1]])
    filled = fill([outs[-1], hidden])
    ahead = exchange([prompt] * line[0], line)
    if split_last:
        pieces = pieces[:1] + list(gather_in(pieces[:0:-1], filled))[::-1]
    outs = call(
        functools.partial(down_kernel, line, last, len(pieces), line[0], False, range(line[0]), False),
        "down_line",
        [shape((DOWN_ROWS, line_width), BF16)] * line[0],
        [*turned(pieces), *line_parts],
        after=filled + ahead[1:],
        flops=line_width * UP_ROWS * 8,
    )
    pieces = exchange(outs, line)
    hiddens = [hidden, swap(hidden, "seq", core, 1)]
    filled = fill([outs[-1]])
    prepared = prepare(owner, resident, tail, vwrite, filled)
    filled = [*prepared, *hiddens[1:]]
    scattered = [line, last] if split_last else [line]
    if split_last:
        prompt = hand_on(prompt, [outs[-1]])
        parts = exchange([prompt] * last[0], last)
        others = join(turned(parts)[1:], 1)
        filled.append(others)

    def down_core(target, after):
        return call(
            functools.partial(down_kernel, core, line, line[0], 2, True, (target,), False),
            "down_core",
            [shape((STATE_SIZE, half), BF16)] + [shape((DRAFTS, half), BF16)] * target,
            turned(pieces) + core_parts,
            after=after,
            moved=1,
        )

    sent, gated = down_core(1, filled)
    received_gated, received = swap(gated, "seq", core, 1), swap(sent, "seq", core, 1)
    (received_gated,) = gather_in([received_gated])
    while len(bases) < groups:
        fill([])

    shares = project(
        stages, owner, *hiddens, gated, received_gated, gain, fetched[0], head_count
    )
    (entering,) = down_core(0, shares[:1])
    prefill_out, token = finish(core, reach, reads, entering, received, bases)
    shares = [shares[0]] + [swap(shares[k], "head", (head_count, 1), k) for k in range(1, head_count)]

    pieces = 2 * line[0]
    late = ahead[1:]
    if split_last:
        behind = exchange([others] * line[0], line)
        prompt = join([prompt, others], 1, shares[:1])
        late = [
            join(pair, 1, [token, *shares[1:]], flops=10**10) for pair in zip(late, behind[1:])
        ]
    crossed = swap(prompt, "seq", core, 1)
    early = (0, line[0], *range(1, line[0]))
    new_state, *found = states(
        stages, scattered, prepared, pieces, early, (prompt, crossed, *late), None, None, ()
    )
    slices = dict(zip(early, found))
    offsets = tuple(range(line[0] + 1, pieces))
    prompts = [swap(piece, "seq", core, 1) for piece in late]
    new_state, state_slice, verify_out = states(
        stages, scattered, prepared, pieces, offsets, prompts, new_state, slices, shares
    )
    return (
        prefill_out,
        new_state.reshape(1, heads, HEAD_DIM, STATE_SIZE),
        verify_out,
        state_slice,
    )


def solution(mesh):
    return jax.shard_map(
        on_device,
        mesh=mesh,
        in_specs=(
            P("seq", "head"),
            P("seq", "head"),
            P("seq", "head"),
            P("seq", "head"),
            P("head"),
            P("head"),
            P("seq", "head", None, None),
            P(),
            P(),
            P(),
            P("seq", "head"),
            P("seq", "head"),
            P("seq", "head"),
            P("seq", "head"),
            P("seq", "head"),
            P("head"),
            P("head", "seq"),
        ),
        out_specs=(
            P("seq", "head"),
            P("seq", "head", None, None),
            P("head", "seq"),
            P("head", "seq"),
        ),
        check_vma=False,
    )
```
